128 devices in a mesh: section: 4 (over z), group: 2 (over core), row: 16 (over x, y).
Axes of the slice: x: 4, y: 4, z: 4, core: 2. Of those that a mesh axis runs over, the one named last changes fastest.
Arguments:
- token_ids: int32 [4, 32, 128], P(None, ('group', 'row')), may hold values from 0 to 31999
- segment_ids: int32 [4, 32, 128], P(None, ('group', 'row')), may hold values from 0 to 7, never falling along the last dimension, each value on 1 to 64 neighbouring positions
- noise_input: bfloat16 [4, 32, 128, 256], P(None, ('group', 'row'), None, 'section'), may hold values from -6 to 6
- embed_table: bfloat16 [32000, 256], P(None, 'section'), may hold values from -6 to 6
- input_proj: bfloat16 [256, 1024], P('section'), may hold values from -0.375 to 0.375
- norm_gain: bfloat16 [4, 1024], P('section'), may hold values from 0.5 to 1.5
- lead_weight: bfloat16 [4, 1024, 4096], P('section'), may hold values from -3 to 3
- down_weight: bfloat16 [4, 2048, 1024], P('section'), may hold values from -0.125 to 0.125
- final_gain: bfloat16 [1024], replicated, may hold values from 0.5 to 1.5
- readout_proj: bfloat16 [1024, 256], P(None, 'section'), may hold values from -0.1875 to 0.1875
- head_table: bfloat16 [32000, 256], P('section'), may hold values from -0.75 to 0.75
Outputs:
- noise_grad: float32 [4, 32, 128, 256], P(None, ('group', 'row'), None, 'section')
- embed_grad: float32 [32000, 256], P('row', 'section')
- input_proj_grad: float32 [256, 1024], P(('section', 'row'))
- norm_gain_grad: float32 [4, 1024], P('section', 'row')
- lead_grad: float32 [4, 1024, 4096], P('section', 'row')
- down_grad: float32 [4, 2048, 1024], P('section', 'row')
- final_gain_grad: float32 [1024], P(('section', 'row'))
- readout_grad: float32 [1024, 256], P('row', 'section')
- head_grad: float32 [32000, 256], P(('section', 'row'))
The draws below stay inside these ranges and needn't reach their ends.
Inputs may be any that keep to these rules, and one draw needn't show every extreme that they name: `segment_ids`: along each packed row the numbers never fall; a segment holds at most 64 positions, and in each row some segment holds exactly that many.
All inputs are finite; a program needn't handle non-finite values.
Results may differ from the reference program's by a relative error of at most 0.04.
Values may be sent and summed in bfloat16 or wider, within the bound.
No kernel may reach another device: no remote copies, remote signals or barrier semaphores. Data moves between devices by JAX's collectives and lax.ppermute only.
A program may use at most 320 MiB of HBM per device.

```python
import math
import jax
import jax.numpy as jnp
import numpy as np
from jax import lax

D = 1024
HEADS = 16
HEAD_SIZE = 64
FF = 4096
EMB = 256
VOCAB = 32000
ROW_LEN = 128
MICRO = 4
SEGMENTS = 8
SEG_MOST = 64
LAYERS = 2
ROWS = 32


def draw_lead_weight(key, part):
    values = jax.random.normal(key, (2 * LAYERS, D, FF), jnp.float32)
    values = jnp.clip(values, -6.0, 6.0) * D ** (-0.5)
    attention_rows = (jnp.arange(2 * LAYERS) % 2 == 0)[:, None, None]
    output_columns = (jnp.arange(FF) >= 3 * D)[None, None, :]
    boost = jnp.where(jnp.logical_and(attention_rows, output_columns), 4.0, 1.0)
    return (values * boost).astype(jnp.bfloat16)


def place_ends(values, own_key, smallest, high):
    spot = [jax.random.randint(jax.random.fold_in(own_key, axis), (), 0, length) for axis, length in enumerate(values.shape)]
    main_axis = values.shape.index(max(values.shape))
    next_to = spot[:main_axis] + [(spot[main_axis] + 1) % values.shape[main_axis]] + spot[main_axis + 1:]
    return values.at[tuple(spot)].set(smallest).at[tuple(next_to)].set(high)


def block_levels(stream_key, shape, cuts, low, top_value):
    def one(position, parts):
        heights = jax.random.uniform(jax.random.fold_in(jax.random.fold_in(stream_key, 6), position), (parts,), jnp.float32, low / len(cuts), top_value / len(cuts))
        return jnp.repeat(jnp.exp(heights), shape[position] // parts).reshape((-1,) + (1,) * (len(shape) - position - 1))

    factor_of = one(*cuts[0])
    for cut in cuts[1:]:
        factor_of = factor_of * one(*cut)
    return factor_of


def profile(number_of, total, bound, lean):
    portions = [(1 << 20) // math.isqrt(standing ** lean) + 1 for standing in range(2, number_of + 1)]
    surplus, holding = total - bound - (number_of - 1), [1] * (number_of - 1)
    while surplus > 0:
        candidates = [i for i in range(number_of - 1) if holding[i] < bound]
        whole, left = sum([portions[i] for i in candidates]), surplus
        for i in candidates:
            more = min(bound - holding[i], max(1, left * portions[i] // whole), surplus)
            holding[i] = holding[i] + more
            surplus = surplus - more
    return np.array([bound] + holding)


def ragged_sizes(stream_key, number_of, total, bound, slope):
    if number_of == 2:
        one = jax.random.randint(stream_key, (), max(1, total - bound), min(bound, total - 1) + 1)
        return jnp.stack([one, total - one])
    sizes = jnp.asarray(profile(number_of, total, bound, slope), jnp.int32)
    pairs = (number_of - 1) // 2
    source_of, sink = sizes[1:1 + 2 * pairs:2], sizes[2:2 + 2 * pairs:2]
    room = jnp.minimum(source_of - 1, bound - sink)
    moved = jax.random.randint(jax.random.fold_in(stream_key, 1), (pairs,), 0, 1 << 20) % (room + 1)
    sizes = sizes.at[1:1 + 2 * pairs:2].set(source_of - moved).at[2:2 + 2 * pairs:2].set(sink + moved)
    return sizes[jax.random.permutation(jax.random.fold_in(stream_key, 2), number_of)]


def gaussian(own_key, extent, scale, limit, cuts=(), dtype=jnp.bfloat16):
    array = jax.random.normal(own_key, extent, jnp.float32) * scale
    if len(cuts) > 0:
        array = block_levels(own_key, extent, cuts, -0.22, 0.18) * array
    return jnp.clip(array, min=-limit, max=limit).astype(dtype)


def setup_inputs(seed: int = 0) -> dict:
    key_list = jax.random.split(jax.random.key(seed), 12)
    token_ids = place_ends(jax.random.randint(key_list[0], (MICRO, ROWS, ROW_LEN), 0, VOCAB), jax.random.fold_in(key_list[0], 1), 0, VOCAB - 1).astype(jnp.int32)
    segment_ids = jax.vmap(lambda own: jnp.searchsorted(jnp.cumsum(ragged_sizes(own, SEGMENTS, ROW_LEN, SEG_MOST, 1)), jnp.arange(ROW_LEN), side="right"))(jax.random.split(key_list[1], MICRO * ROWS)).reshape((MICRO, ROWS, ROW_LEN)).astype(jnp.int32)
    noise_input = gaussian(key_list[2], (MICRO, ROWS, ROW_LEN, EMB), 1.0, 6.0, ((1, 32), (3, 4)))
    embed_table = gaussian(key_list[3], (VOCAB, EMB), 1.0, 6.0, ((1, 4),))
    input_proj = gaussian(key_list[4], (EMB, D), EMB ** -0.5, 0.375, ((0, 4),))
    norm_gain = jnp.clip(1.0 + 0.1 * jax.random.normal(key_list[5], (2 * LAYERS, D), jnp.float32), 0.5, 1.5).astype(jnp.bfloat16)
    lead_weight = draw_lead_weight(jax.random.fold_in(key_list[11], 71), 0)
    down_weight = gaussian(key_list[7], (2 * LAYERS, FF // 2, D), (FF // 2) ** -0.5, 0.125, ((0, 4),))
    final_gain = jnp.clip(1.0 + 0.1 * jax.random.normal(key_list[8], (D,), jnp.float32), 0.5, 1.5).astype(jnp.bfloat16)
    readout_proj = gaussian(key_list[9], (D, EMB), D ** -0.5, 0.1875, ((1, 4),))
    head_table = gaussian(key_list[10], (VOCAB, EMB), (EMB // 4) ** -0.5, 0.75, ((0, 4),))
    return {"token_ids": token_ids, "segment_ids": segment_ids, "noise_input": noise_input, "embed_table": embed_table, "input_proj": input_proj, "norm_gain": norm_gain, "lead_weight": lead_weight, "down_weight": down_weight, "final_gain": final_gain, "readout_proj": readout_proj, "head_table": head_table}


EPSILON = 1e-05
MASKED = -1000000000.0
HIGHEST = lax.Precision.HIGHEST

@jax.custom_vjp
def low(v):
    return lax.optimization_barrier(v.astype(jnp.bfloat16)).astype(jnp.float32)

@jax.custom_vjp
def low_back(v):
    return v

def low_keep(v):
    return (low(v), None)

def low_pass(kept, grad):
    return (grad,)

def back_keep(v):
    return (v, None)

def back_low(kept, grad):
    return (low(grad),)
low.defvjp(low_keep, low_pass)
low_back.defvjp(back_keep, back_low)

def product(former, latter):
    return jnp.dot(former, latter, precision=HIGHEST)

def normalize(values, gain_vec):
    centre = lax.optimization_barrier(jnp.mean(values, axis=-1, keepdims=True))
    centred = values - centre
    spread = lax.optimization_barrier(jnp.mean(centred * centred, axis=-1, keepdims=True))
    return centred * lax.rsqrt(spread + EPSILON) * gain_vec

def attention(packed, segments):
    row_count = packed.shape[0]
    pieces_qkv = packed.reshape(row_count, ROW_LEN, 3, HEADS, HEAD_SIZE)
    raw_scores = jnp.einsum('rqhd,rkhd->rhqk', pieces_qkv[:, :, 0], pieces_qkv[:, :, 1], precision=HIGHEST) * HEAD_SIZE ** (-0.5)
    raw_scores = low_back(raw_scores)
    same_segment = segments[:, None, :, None] == segments[:, None, None, :]
    attn_probs = jax.nn.softmax(jnp.where(same_segment, raw_scores, MASKED), axis=-1)
    mixed_heads = jnp.einsum('rhqk,rkhd->rqhd', low(attn_probs), pieces_qkv[:, :, 2], precision=HIGHEST)
    return mixed_heads.reshape(row_count, ROW_LEN, HEADS * HEAD_SIZE)

def attention_pair(row_pair):
    return attention(row_pair[0], row_pair[1])

def attention_half(residual, segment_ids, gain_vec, lead_w):
    normed = low(normalize(residual, gain_vec))
    packed = low_back(low(product(normed, lead_w[:, :3 * D])))
    mixed_heads = low_back(low(lax.map(jax.checkpoint(attention_pair), (packed, segment_ids))))
    return low_back(low(residual + low_back(product(mixed_heads, lead_w[:, 3 * D:]))))

def feed_forward_half(residual, gain_vec, lead_w, down_w):
    normed = low(normalize(residual, gain_vec))
    inner_act = low_back(product(normed, lead_w))
    active = low(jax.nn.gelu(inner_act))
    return low_back(low(residual + low_back(product(active, down_w))))

def reference(token_ids, segment_ids, noise_input, embed_table, input_proj, norm_gain, lead_weight, down_weight, final_gain, readout_proj, head_table):
    inputs = tuple((argument.astype(jnp.float32) for argument in (noise_input, embed_table, input_proj, norm_gain, lead_weight, down_weight, final_gain, readout_proj, head_table)))

    def objective(noise_f, table_f, lift_w, gains, leads, downs, gain_f, readout_w, head_w):
        embedded = table_f[token_ids] + noise_f
        residual = low_back(low(product(low(embedded), lift_w)))
        for half_at in range(2 * LAYERS):
            if half_at % 2 == 0:
                residual = jax.checkpoint(attention_half)(residual, segment_ids, gains[half_at], leads[half_at])
            else:
                down_full = jnp.concatenate((downs[half_at - 1], downs[half_at]), axis=0)
                residual = jax.checkpoint(feed_forward_half)(residual, gains[half_at], leads[half_at], down_full)
        normed = low(normalize(residual, gain_f))
        readout = low_back(low(product(normed, readout_w)))

        def row_loss(row_pair):
            logits = low_back(jnp.dot(row_pair[0], head_w.T, precision=HIGHEST))
            picked = jnp.take_along_axis(logits, row_pair[1][:, None], axis=-1)[:, 0]
            return jnp.sum(jax.nn.logsumexp(logits, axis=-1) - picked)
        losses = lax.map(jax.checkpoint(row_loss), (readout.reshape(-1, ROW_LEN, EMB), token_ids.reshape(-1, ROW_LEN)))
        return jnp.sum(losses)
    total_loss, pullback = jax.vjp(objective, *inputs)
    gradients = pullback(jnp.ones_like(total_loss))
    return (gradients[0], gradients[1], gradients[2], gradients[3], gradients[4], gradients[5], gradients[6], gradients[7], gradients[8])
```

```python
import itertools

import jax
import jax.numpy as jnp
from jax import lax
from jax.experimental import pallas as pl
from jax.experimental.pallas import tpu as pltpu
from jax.sharding import PartitionSpec as P

HEADS = 16
HEAD_SIZE = 64
LOW = jnp.bfloat16
WIDE = jnp.float32
EPSILON = 1e-05
MASKED = -1000000000.0
CHUNK = 512


def matmul(former, latter):
    return jnp.dot(former, latter, preferred_element_type=WIDE)


def matmul_nt(former, latter):
    return lax.dot_general(
        former, latter, (((1,), (1,)), ((), ())), preferred_element_type=WIDE
    )


def matmul_tn(former, latter):
    return lax.dot_general(
        former, latter, (((0,), (0,)), ((), ())), preferred_element_type=WIDE
    )


def layer_norm(values):
    centre = jnp.mean(values, axis=-1, keepdims=True)
    centred = values - centre
    variance = jnp.mean(centred * centred, axis=-1, keepdims=True)
    factor = lax.rsqrt(variance + EPSILON)
    return (centred * factor, factor)


def norm_back(grad_normed, normed, factor):
    first_mean = jnp.mean(grad_normed, axis=-1, keepdims=True)
    second_mean = jnp.mean(grad_normed * normed, axis=-1, keepdims=True)
    return factor * (grad_normed - first_mean - normed * second_mean)


GELU_A = 0.7978845608028654
GELU_B = 0.044715


def gelu(v):
    return 0.5 * v * (1.0 + jnp.tanh(GELU_A * (v + GELU_B * (v * v * v))))


def gelu_slope(v):
    square = v * v
    bend = jnp.tanh(GELU_A * (v + GELU_B * (square * v)))
    return 0.5 * (1.0 + bend) + 0.5 * v * (1.0 - bend * bend) * (
        GELU_A * (1.0 + 3.0 * GELU_B * square)
    )


def head_probs(scores, same):
    scores = jnp.where(same, scores * HEAD_SIZE ** (-0.5), MASKED)
    expo = jnp.exp(scores - jnp.max(scores, axis=-1, keepdims=True))
    return expo / jnp.sum(expo, axis=-1, keepdims=True)


def weight_copies(lead_ref, down_ref, lead_buf, down_buf, sems):
    count = lead_buf.shape[0]
    leads = [
        pltpu.make_async_copy(
            lead_ref.at[:, pl.ds(j * CHUNK, CHUNK)], lead_buf.at[j], sems.at[j]
        )
        for j in range(count)
    ]
    downs = [
        pltpu.make_async_copy(
            down_ref.at[pl.ds(j * CHUNK, CHUNK), :], down_buf.at[j], sems.at[count + j]
        )
        for j in range(count)
    ]
    return leads, downs


def forward_kernel(
    role_ref,
    entry_ref,
    seg_col_ref,
    seg_row_ref,
    gain_ref,
    lead_ref,
    down_ref,
    entries_in,
    normeds_in,
    saved_in,
    inner_in,
    out_ref,
    entries_ref,
    normeds_ref,
    saved_ref,
    inner_ref,
    lead_buf,
    down_buf,
    normed_buf,
    saved_buf,
    inner_buf,
    sems,
    out_sems,
):
    role, slot = role_ref[0], role_ref[1]
    width = entry_ref.shape[1]
    leads, downs = weight_copies(lead_ref, down_ref, lead_buf, down_buf, sems)
    count = len(leads)
    keep_normed = pltpu.make_async_copy(normed_buf, normeds_ref.at[slot], out_sems.at[0])
    keep_saved = pltpu.make_async_copy(saved_buf, saved_ref.at[slot], out_sems.at[1])
    keep_inner = pltpu.make_async_copy(inner_buf, inner_ref.at[slot], out_sems.at[2])
    keep_entry = pltpu.make_async_copy(entry_ref, entries_ref.at[slot], out_sems.at[3])

    @pl.when(role == 0)
    def _():
        out_ref[...] = jnp.zeros_like(out_ref)

    @pl.when(role == 1)
    def _():
        for j in range(count):
            leads[j].start()
        keep_entry.start()
        residual = entry_ref[...].astype(WIDE)
        normed, _ = layer_norm(residual)
        normed_buf[...] = (normed * gain_ref[...]).astype(LOW)
        keep_normed.start()
        qkv = 3 * width // CHUNK
        for j in range(qkv):
            leads[j].wait()
            saved_buf[:, j * CHUNK : (j + 1) * CHUNK] = matmul(
                normed_buf[...], lead_buf[j]
            ).astype(LOW)
        same = seg_col_ref[slot] == seg_row_ref[slot]
        left = lax.broadcasted_iota(jnp.int32, (entry_ref.shape[0], 128), 1) < HEAD_SIZE
        zero = jnp.zeros((entry_ref.shape[0], 128), LOW)
        for pair in range(HEADS // 2):
            at = pair * 128
            query = saved_buf[:, at : at + 128]
            key = saved_buf[:, width + at : width + at + 128]
            value = saved_buf[:, 2 * width + at : 2 * width + at + 128]
            probs_a = head_probs(matmul_nt(jnp.where(left, query, zero), key), same)
            probs_b = head_probs(matmul_nt(jnp.where(left, zero, query), key), same)
            mixed = jnp.where(
                left, matmul(probs_a.astype(LOW), value), matmul(probs_b.astype(LOW), value)
            )
            saved_buf[:, 3 * width + at : 3 * width + at + 128] = mixed.astype(LOW)
        keep_saved.start()
        mixed = saved_buf[:, 3 * width :]
        for j in range(qkv, count):
            leads[j].wait()
            at = (j - qkv) * CHUNK
            out_ref[:, at : at + CHUNK] = (
                entry_ref[:, at : at + CHUNK].astype(WIDE) + matmul(mixed, lead_buf[j])
            ).astype(LOW)
        keep_entry.wait()
        keep_normed.wait()
        keep_saved.wait()

    @pl.when(role == 2)
    def _():
        for j in range(count):
            leads[j].start()
            downs[j].start()
        keep_entry.start()
        residual = entry_ref[...].astype(WIDE)
        normed, _ = layer_norm(residual)
        normed_buf[...] = (normed * gain_ref[...]).astype(LOW)
        keep_normed.start()
        result = residual
        for j in range(count):
            leads[j].wait()
            inner = matmul(normed_buf[...], lead_buf[j])
            inner_buf[:, j * CHUNK : (j + 1) * CHUNK] = inner
            active = gelu(inner).astype(LOW)
            saved_buf[:, j * CHUNK : (j + 1) * CHUNK] = active
            downs[j].wait()
            result = result + matmul(active, down_buf[j])
        keep_saved.start()
        keep_inner.start()
        out_ref[...] = result.astype(LOW)
        keep_entry.wait()
        keep_normed.wait()
        keep_saved.wait()
        keep_inner.wait()


VMEM_SPEC = pl.BlockSpec(memory_space=pltpu.VMEM)
ANY_SPEC = pl.BlockSpec(memory_space=pl.ANY)


def weight_scratch(width, hidden):
    count = hidden // CHUNK
    return [
        pltpu.VMEM((count, width, CHUNK), LOW),
        pltpu.VMEM((count, CHUNK, width), LOW),
    ]


def forward_stage(role, entry, seg_col, seg_row, gain, lead, down, kept):
    tokens, width = entry.shape
    hidden = lead.shape[1]
    return pl.pallas_call(
        forward_kernel,
        out_shape=[jax.ShapeDtypeStruct(entry.shape, LOW)]
        + [jax.ShapeDtypeStruct(k.shape, k.dtype) for k in kept],
        in_specs=[pl.BlockSpec(memory_space=pltpu.SMEM)]
        + [VMEM_SPEC] * 4
        + [ANY_SPEC] * 6,
        out_specs=[VMEM_SPEC] + [ANY_SPEC] * 4,
        scratch_shapes=weight_scratch(width, hidden)
        + [
            pltpu.VMEM((tokens, width), LOW),
            pltpu.VMEM((tokens, hidden), LOW),
            pltpu.VMEM((tokens, hidden), WIDE),
            pltpu.SemaphoreType.DMA((2 * hidden // CHUNK,)),
            pltpu.SemaphoreType.DMA((4,)),
        ],
        input_output_aliases={7: 1, 8: 2, 9: 3, 10: 4},
        compiler_params=pltpu.CompilerParams(vmem_limit_bytes=30 << 20),
        cost_estimate=pl.CostEstimate(
            flops=4 * tokens * width * hidden, bytes_accessed=20 << 20, transcendentals=0
        ),
        name="forward_stage",
    )(role, entry, seg_col, seg_row, gain, lead, down, *kept)


def backward_kernel(
    role_ref,
    grad_ref,
    seg_col_ref,
    seg_row_ref,
    gain_ref,
    lead_ref,
    down_ref,
    entries_ref,
    saved_ref,
    inner_ref,
    nexts_in,
    grads_in,
    gains_in,
    out_ref,
    nexts_ref,
    grads_ref,
    gains_ref,
    lead_buf,
    down_buf,
    saved_buf,
    inner_buf,
    grads_buf,
    mixed_buf,
    gain_buf,
    entry_buf,
    sems,
    in_sems,
    out_sems,
):
    role, slot = role_ref[0], role_ref[1]
    tokens, width = grad_ref.shape
    leads, downs = weight_copies(lead_ref, down_ref, lead_buf, down_buf, sems)
    count = len(leads)
    bring_saved = pltpu.make_async_copy(saved_ref.at[slot], saved_buf, in_sems.at[0])
    bring_inner = pltpu.make_async_copy(inner_ref.at[slot], inner_buf, in_sems.at[1])
    bring_entry = pltpu.make_async_copy(entries_ref.at[slot], entry_buf, in_sems.at[2])
    keep_next = pltpu.make_async_copy(grad_ref, nexts_ref.at[slot], out_sems.at[0])
    keep_grads = pltpu.make_async_copy(grads_buf, grads_ref.at[slot], out_sems.at[1])
    keep_gain = pltpu.make_async_copy(gain_buf, gains_ref.at[slot], out_sems.at[2])
    qkv = 3 * width // CHUNK

    def finish(grad_normed):
        keep_grads.start()
        bring_entry.wait()
        normed, factor = layer_norm(entry_buf[...].astype(WIDE))
        gain_buf[...] = jnp.broadcast_to(
            jnp.sum(grad_normed * normed, axis=0, keepdims=True), gain_buf.shape
        )
        keep_gain.start()
        out_ref[...] = (
            grad_ref[...].astype(WIDE) + norm_back(grad_normed * gain_ref[...], normed, factor)
        ).astype(LOW)
        keep_next.wait()
        keep_grads.wait()
        keep_gain.wait()

    @pl.when(role == 0)
    def _():
        out_ref[...] = jnp.zeros_like(out_ref)

    @pl.when(role == 1)
    def _():
        bring_saved.start()
        for j in list(range(qkv, count)) + list(range(qkv)):
            leads[j].start()
        keep_next.start()
        bring_entry.start()
        grads_buf[:, 3 * width :] = grad_ref[...]
        grad_mixed = jnp.zeros((tokens, width), WIDE)
        for j in range(qkv, count):
            leads[j].wait()
            at = (j - qkv) * CHUNK
            grad_mixed = grad_mixed + matmul_nt(grad_ref[:, at : at + CHUNK], lead_buf[j])
        mixed_buf[...] = grad_mixed.astype(LOW)
        bring_saved.wait()
        same = seg_col_ref[slot] == seg_row_ref[slot]
        left = lax.broadcasted_iota(jnp.int32, (tokens, 128), 1) < HEAD_SIZE
        zero = jnp.zeros((tokens, 128), LOW)
        scale = HEAD_SIZE ** (-0.5)
        for pair in range(HEADS // 2):
            at = pair * 128
            query = saved_buf[:, at : at + 128]
            key = saved_buf[:, width + at : width + at + 128]
            value = saved_buf[:, 2 * width + at : 2 * width + at + 128]
            grad = mixed_buf[:, at : at + 128]
            parts = []
            for own in (0, 1):
                mine = lambda v: jnp.where(left, v, zero) if own == 0 else jnp.where(left, zero, v)
                probs = head_probs(matmul_nt(mine(query), key), same)
                grad_probs = matmul_nt(mine(grad), value)
                grad_scores = probs * (
                    grad_probs - jnp.sum(probs * grad_probs, axis=-1, keepdims=True)
                )
                grad_low = grad_scores.astype(LOW)
                parts.append(
                    (
                        matmul(grad_low, key) * scale,
                        matmul_tn(grad_low, query) * scale,
                        matmul_tn(probs.astype(LOW), grad),
                    )
                )
            for which in range(3):
                spot = which * width + at
                grads_buf[:, spot : spot + 128] = jnp.where(
                    left, parts[0][which], parts[1][which]
                ).astype(LOW)
        grad_normed = jnp.zeros((tokens, width), WIDE)
        for j in range(qkv):
            leads[j].wait()
            grad_normed = grad_normed + matmul_nt(
                grads_buf[:, j * CHUNK : (j + 1) * CHUNK], lead_buf[j]
            )
        finish(grad_normed)

    @pl.when(role == 2)
    def _():
        bring_inner.start()
        for j in range(count):
            downs[j].start()
            leads[j].start()
        keep_next.start()
        bring_entry.start()
        grad_normed = jnp.zeros((tokens, width), WIDE)
        bring_inner.wait()
        for j in range(count):
            at = slice(j * CHUNK, (j + 1) * CHUNK)
            downs[j].wait()
            grad_active = matmul_nt(grad_ref[...], down_buf[j])
            grads_buf[:, at] = (gelu_slope(inner_buf[:, at]) * grad_active).astype(LOW)
            leads[j].wait()
            grad_normed = grad_normed + matmul_nt(grads_buf[:, at], lead_buf[j])
        finish(grad_normed)


def backward_stage(
    role, grad, seg_col, seg_row, gain, lead, down, entries, saved, inner, totals
):
    tokens, width = grad.shape
    hidden = lead.shape[1]
    return pl.pallas_call(
        backward_kernel,
        out_shape=[jax.ShapeDtypeStruct(grad.shape, LOW)]
        + [jax.ShapeDtypeStruct(k.shape, k.dtype) for k in totals],
        in_specs=[pl.BlockSpec(memory_space=pltpu.SMEM)]
        + [VMEM_SPEC] * 4
        + [ANY_SPEC] * 8,
        out_specs=[VMEM_SPEC] + [ANY_SPEC] * 3,
        scratch_shapes=weight_scratch(width, hidden)
        + [
            pltpu.VMEM((tokens, hidden), LOW),
            pltpu.VMEM((tokens, hidden), WIDE),
            pltpu.VMEM((tokens, hidden), LOW),
            pltpu.VMEM((tokens, width), LOW),
            pltpu.VMEM((8, width), WIDE),
            pltpu.VMEM((tokens, width), LOW),
            pltpu.SemaphoreType.DMA((2 * hidden // CHUNK,)),
            pltpu.SemaphoreType.DMA((3,)),
            pltpu.SemaphoreType.DMA((3,)),
        ],
        input_output_aliases={10: 1, 11: 2, 12: 3},
        compiler_params=pltpu.CompilerParams(vmem_limit_bytes=32 << 20),
        cost_estimate=pl.CostEstimate(
            flops=4 * tokens * width * hidden, bytes_accessed=20 << 20, transcendentals=0
        ),
        name="backward_stage",
    )(role, grad, seg_col, seg_row, gain, lead, down, entries, saved, inner, *totals)


def stats_kernel(readout_ref, table_ref, peak_ref, total_ref):
    logits = matmul_nt(table_ref[...], readout_ref[...])
    own_peak = jnp.max(logits, axis=0, keepdims=True)
    own_total = lambda peak: jnp.sum(jnp.exp(logits - peak), axis=0, keepdims=True)

    @pl.when(pl.program_id(0) == 0)
    def _():
        peak_ref[...] = own_peak
        total_ref[...] = own_total(own_peak)

    @pl.when(pl.program_id(0) > 0)
    def _():
        peak = jnp.maximum(peak_ref[...], own_peak)
        total_ref[...] = total_ref[...] * jnp.exp(peak_ref[...] - peak) + own_total(peak)
        peak_ref[...] = peak


def head_stats(readout, table, tile):
    tokens, emb = readout.shape
    vocab = table.shape[0]
    whole = pl.BlockSpec((1, tokens), lambda i: (0, 0))
    return pl.pallas_call(
        stats_kernel,
        out_shape=[jax.ShapeDtypeStruct((1, tokens), WIDE)] * 2,
        grid=(vocab // tile,),
        in_specs=[
            pl.BlockSpec((tokens, emb), lambda i: (0, 0)),
            pl.BlockSpec((tile, emb), lambda i: (i, 0)),
        ],
        out_specs=[whole, whole],
        compiler_params=pltpu.CompilerParams(vmem_limit_bytes=40 << 20),
        cost_estimate=pl.CostEstimate(
            flops=2 * tokens * vocab * emb, bytes_accessed=5 << 20, transcendentals=tokens * vocab
        ),
        name="head_stats",
    )(readout, table)


def head_kernel(base_ref, readout_ref, table_ref, logsum_ref, ids_ref, head_ref, grad_ref):
    tile = table_ref.shape[0]
    logits = matmul_nt(table_ref[...], readout_ref[...])
    ids = ids_ref[...] - (base_ref[0] + pl.program_id(0) * tile)
    hits = lax.broadcasted_iota(jnp.int32, logits.shape, 0) == ids
    probs = jnp.exp(logits - logsum_ref[...])
    grads = jnp.where(hits, probs - 1.0, probs).astype(LOW)
    head_ref[...] = matmul(grads, readout_ref[...]).astype(LOW)
    term = matmul_tn(grads, table_ref[...])

    @pl.when(pl.program_id(0) == 0)
    def _():
        grad_ref[...] = term

    @pl.when(pl.program_id(0) > 0)
    def _():
        grad_ref[...] += term


def head_grads(base, readout, table, logsum, ids, tile):
    tokens, emb = readout.shape
    vocab = table.shape[0]
    row = pl.BlockSpec((1, tokens), lambda i: (0, 0))
    whole = pl.BlockSpec((tokens, emb), lambda i: (0, 0))
    part = pl.BlockSpec((tile, emb), lambda i: (i, 0))
    return pl.pallas_call(
        head_kernel,
        out_shape=[
            jax.ShapeDtypeStruct((vocab, emb), LOW),
            jax.ShapeDtypeStruct((tokens, emb), WIDE),
        ],
        grid=(vocab // tile,),
        in_specs=[pl.BlockSpec(memory_space=pltpu.SMEM), whole, part, row, row],
        out_specs=[part, whole],
        compiler_params=pltpu.CompilerParams(vmem_limit_bytes=40 << 20),
        cost_estimate=pl.CostEstimate(
            flops=6 * tokens * vocab * emb, bytes_accessed=9 << 20, transcendentals=tokens * vocab
        ),
        name="head_grads",
    )(base, readout, table, logsum, ids)


ROW_LEN = 128
SEC, GRP, NX, NY = 4, 2, 4, 4
ALL = ("section", "group", "row")
TURNS = (1, 3, 2)


def route(value, target_of):
    number = lambda s, g, x, y: (s * GRP + g) * NX * NY + x * NY + y
    pairs = []
    for at in itertools.product(range(SEC), range(GRP), range(NX), range(NY)):
        target = target_of(*at)
        if target is not None:
            pairs.append((number(*at), number(*target)))
    return lax.ppermute(value, ALL, pairs)


def link(value, source, target):
    return route(value, lambda s, g, x, y: (target, g, x, y) if s == source else None)


def turn(value, by):
    return route(value, lambda s, g, x, y: ((s + by) % SEC, g, x, y))


def swap_cores(value, sections=range(SEC)):
    return route(value, lambda s, g, x, y: (s, 1 - g, x, y) if s in sections else None)


def plane_route(value, by, first, sections=range(SEC)):
    def target_of(s, g, x, y):
        if s not in sections:
            return None
        if (g == 0) == first:
            return (s, g, (x + by) % NX, y)
        return (s, g, x, (y + by) % NY)

    return route(value, target_of)


def after(value, earlier):
    return lax.optimization_barrier((value, earlier))[0]


def block_of(values, block, count):
    size = values.shape[1] // count
    return lax.dynamic_slice_in_dim(values, block * size, size, 1)


def row_block(values, block, count):
    size = values.shape[0] // count
    return lax.dynamic_slice_in_dim(values, block * size, size, 0)


def by_second(values, unit):
    rows, columns = values.shape
    return values.reshape(rows, NX, NY, unit).transpose(0, 2, 1, 3).reshape(rows, columns)


def reduce_plane(block_for, second, sections=range(SEC)):
    pieces = {by: block_for(by) for by in TURNS + (0,)}
    total = pieces[0].astype(WIDE)
    for by in TURNS:
        total = total + plane_route(pieces[by], by, True, sections).astype(WIDE)
    lowered = total.astype(LOW)
    mine = row_block(total, second, 4)
    for by in TURNS:
        piece = row_block(lowered, (second + by) % 4, 4)
        mine = mine + plane_route(piece, by, False, sections).astype(WIDE)
    return mine.astype(LOW)


def gather_plane(values):
    blocks = jnp.stack([values] + [plane_route(values, by, True) for by in TURNS])
    blocks = jnp.concatenate([blocks] + [plane_route(blocks, by, False) for by in TURNS])
    return jnp.concatenate([blocks, swap_cores(blocks)])


def embed_kernel(base_ref, ids_ref, grad_ref, out_ref):
    @pl.when(pl.program_id(0) == 0)
    def _():
        out_ref[...] = jnp.zeros_like(out_ref)

    tokens = grad_ref.shape[2]
    local = ids_ref[...] - base_ref[0]
    for block in range(grad_ref.shape[0]):
        ids = local[block * tokens : (block + 1) * tokens]
        hits = lax.broadcasted_iota(jnp.int32, (tokens, out_ref.shape[1]), 1) == ids
        hits = jnp.where(hits, 1.0, 0.0).astype(LOW)
        out_ref[...] += jnp.dot(grad_ref[block], hits, preferred_element_type=WIDE)


def embed_sum(base, ids, grads, rows):
    count, parts, tokens = grads.shape
    step = 4
    return pl.pallas_call(
        embed_kernel,
        out_shape=jax.ShapeDtypeStruct((parts, rows), WIDE),
        grid=(count // step,),
        in_specs=[
            pl.BlockSpec(memory_space=pltpu.SMEM),
            pl.BlockSpec((step * tokens, 1), lambda i: (i, 0)),
            pl.BlockSpec((step, parts, tokens), lambda i: (i, 0, 0)),
        ],
        out_specs=pl.BlockSpec((parts, rows), lambda i: (0, 0)),
        compiler_params=pltpu.CompilerParams(vmem_limit_bytes=40 << 20),
        cost_estimate=pl.CostEstimate(
            flops=2 * count * tokens * 256 * rows, bytes_accessed=12 << 20, transcendentals=0
        ),
        name="embed_sum",
    )(base, ids.reshape(count * tokens, 1), grads)


def local(
    token_ids,
    segment_ids,
    noise_input,
    embed_table,
    input_proj,
    norm_gain,
    lead_weight,
    down_weight,
    final_gain,
    readout_proj,
    head_table,
):
    section = lax.axis_index("section")
    core = lax.axis_index("group")
    row = lax.axis_index("row")
    x_at, y_at = row // NY, row % NY
    first_at, second_at = jnp.where(core == 0, x_at, y_at), jnp.where(core == 0, y_at, x_at)
    micro, _, tokens = token_ids.shape
    width = input_proj.shape[1]
    hidden = lead_weight.shape[2]
    half_rows = down_weight.shape[1]
    emb_part = input_proj.shape[0]
    vocab_part, emb = head_table.shape
    vocab = embed_table.shape[0]
    all_tokens = micro * tokens
    last = SEC - 1
    is_mlp = section % 2 == 1
    gain_half = norm_gain.astype(WIDE)
    lead = lead_weight[0]
    own_down = down_weight[0]
    seg_row = segment_ids
    seg_col = segment_ids.reshape(micro, tokens, 1)
    flat_ids = token_ids.reshape(-1)

    small_pack = jnp.concatenate((input_proj, readout_proj.T))
    packs = {by: turn(small_pack, by) for by in TURNS}
    packs[0] = small_pack
    pack_of = lambda s: lax.select_n((section - s) % SEC, *[packs[by] for by in range(SEC)])
    packs = [pack_of(s) for s in range(SEC)]
    input_full = jnp.concatenate([p[:emb_part] for p in packs])
    readout_full = jnp.concatenate([p[emb_part:] for p in packs])
    embedded = (
        embed_table[flat_ids].astype(WIDE) + noise_input.reshape(-1, emb_part).astype(WIDE)
    ).astype(LOW)
    parts = {by: turn(after(embedded, packs[0]), by) for by in TURNS}
    embedded = jnp.concatenate(
        [embedded] + [parts[SEC - s] for s in range(1, SEC)], axis=1
    )
    first_in = matmul(embedded, input_full).astype(LOW).reshape(micro, tokens, width)

    eighth = row_block(row_block(own_down, core, 2), first_at, 4)
    eighth = jnp.where(section == 1, link(eighth, 0, 1), link(eighth, 2, 3))
    upper = jnp.zeros((4,) + eighth.shape, LOW)
    upper = lax.dynamic_update_index_in_dim(upper, eighth, first_at, 0)
    for by in TURNS:
        upper = lax.dynamic_update_index_in_dim(
            upper, plane_route(eighth, by, True), (first_at - by) % 4, 0
        )
    upper = upper.reshape(half_rows // 2, width)
    upper_other = swap_cores(upper)
    full_down = jnp.concatenate(
        (
            jnp.where(core == 0, upper, upper_other),
            jnp.where(core == 0, upper_other, upper),
            own_down,
        )
    )
    all_ids = gather_plane(after(flat_ids, upper_other))

    kept = (
        jnp.zeros((micro, tokens, width), LOW),
        jnp.zeros((micro, tokens, width), LOW),
        jnp.zeros((micro, tokens, hidden), LOW),
        jnp.zeros((micro, tokens, hidden), WIDE),
    )

    def role_at(at):
        live = jnp.logical_and(at >= 0, at < micro)
        role = jnp.where(live, jnp.where(is_mlp, 2, 1), 0)
        return jnp.stack((role, jnp.clip(at, 0, micro - 1))).astype(jnp.int32)

    steps = micro + 2 * last
    outs, hops = [], {}

    def arrived(step, by):
        parts = [
            (s + by, hops[step - 2, s])
            for s in range(SEC)
            if (step - 2, s) in hops
        ]
        value = parts[0][1] if parts else None
        for target, part in parts[1:]:
            value = jnp.where(section == target, part, value)
        return value

    for step in range(steps):
        entry = arrived(step, 1)
        if entry is None:
            entry = first_in[step]
        elif step < micro:
            entry = jnp.where(section == 0, first_in[step], entry)
        out, *kept = forward_stage(
            role_at(step - 2 * section), entry, seg_col, seg_row, gain_half, lead, full_down, kept
        )
        outs.append(out)
        for s in range(last):
            if 0 <= step - 2 * s < micro:
                ready = after(out, hops[step - 1, s]) if (step - 1, s) in hops else out
                hops[step, s] = link(ready, s, s + 1)
    entries, normeds, saved, inner = kept

    final_rows = jnp.concatenate(outs[2 * last :]).astype(WIDE)
    normed_f, factor_f = layer_norm(final_rows)
    gain_f = final_gain.astype(WIDE)
    final_low = (normed_f * gain_f).astype(LOW)
    readout = matmul_nt(final_low, readout_full).astype(LOW)
    sent = [link(readout, last, s) for s in range(last)]
    for s in range(last):
        readout = jnp.where(section == s, sent[s], readout)
    peak, total = head_stats(readout, head_table, 1600)
    stats = jnp.concatenate((peak, total))
    all_stats = jnp.stack([stats] + [turn(stats, by) for by in TURNS])
    peak = jnp.max(all_stats[:, 0], axis=0)
    total = jnp.sum(all_stats[:, 1] * jnp.exp(all_stats[:, 0] - peak), axis=0)
    logsum = (peak + jnp.log(total))[None]
    head_grad, grad_readout = head_grads(
        (section * vocab_part).reshape(1), readout, head_table, logsum, flat_ids[None], 1600
    )
    grad_low = grad_readout.astype(LOW)
    for s in range(last):
        grad_readout = grad_readout + link(grad_low, s, last).astype(WIDE)
    grad_readout = grad_readout.astype(LOW)
    head_grad = lax.psum_scatter(
        head_grad.reshape(NX * NY, vocab_part // (NX * NY), emb), "row", scatter_dimension=0
    )
    readout_grad = matmul_tn(final_low, grad_readout)
    grad_final = matmul(grad_readout, readout_full)
    final_gain_grad = jnp.sum(grad_final * normed_f, axis=0)
    last_grads = norm_back(grad_final * gain_f, normed_f, factor_f).astype(LOW)
    last_grads = last_grads.reshape(micro, tokens, width)

    totals = (
        jnp.zeros((micro, tokens, width), LOW),
        jnp.zeros((micro, tokens, hidden), LOW),
        jnp.zeros((micro, 8, width), WIDE),
    )
    outs, hops = [], {}
    for step in range(steps):
        grad_next = arrived(step, -1)
        if grad_next is None:
            grad_next = last_grads[step]
        elif step < micro:
            grad_next = jnp.where(section == last, last_grads[step], grad_next)
        out, *totals = backward_stage(
            role_at(step - 2 * (last - section)),
            grad_next,
            seg_col,
            seg_row,
            gain_half,
            lead,
            full_down,
            entries,
            saved,
            inner,
            totals,
        )
        outs.append(out)
        for s in range(1, SEC):
            if 0 <= step - 2 * (last - s) < micro:
                ready = after(out, hops[step - 1, s]) if (step - 1, s) in hops else out
                hops[step, s] = link(ready, s, s - 1)

    first_grads = jnp.concatenate(outs[2 * last :])
    noise_grad = matmul_nt(input_full, first_grads).astype(LOW)
    pieces = noise_grad.reshape(SEC, emb_part, all_tokens)
    noise_grad = pieces[0]
    for s in TURNS:
        noise_grad = jnp.where(section == s, turn(pieces[s], s), noise_grad)
    embed_grad = embed_sum(
        (row * (vocab // 16)).reshape(1), all_ids, gather_plane(noise_grad), vocab // 16
    ).T
    noise_out = noise_grad.reshape(emb_part, micro, tokens).transpose(1, 2, 0).astype(WIDE)

    grad_nexts, grads, gain_grads = totals
    gain_grad = jnp.sum(gain_grads[:, 0], axis=0)
    flat = lambda v: v.reshape(all_tokens, v.shape[-1])
    normed, grad_nexts, grads, saved = flat(normeds), flat(grad_nexts), flat(grads), flat(saved)
    tail = jnp.where(is_mlp, normed, saved[:, 3 * width :])
    order = lambda values, which, unit: jnp.where(which == 0, values, by_second(values, unit))
    odd = (1, 3)

    def lead_block(which, spot, by):
        block = (spot + by) % 4
        former = block_of(order(normed, which, 64), block, 4)
        latter = block_of(order(jnp.where(which == 0, normed, tail), which, 64), block, 4)
        part = lax.dynamic_slice_in_dim(grads, which * 2 * width, 2 * width, 1)
        return jnp.concatenate(
            (matmul_tn(former, part[:, :width]), matmul_tn(latter, part[:, width:])), axis=1
        )

    def down_block(which, spot, by):
        block = (spot + by) % 4
        part = lax.dynamic_slice_in_dim(saved, which * half_rows, half_rows, 1)
        return matmul_tn(block_of(order(part, which, 128), block, 4), grad_nexts)

    input_grad = matmul_tn(embedded, first_grads).reshape(SEC, 16, 4, width)
    input_grad = input_grad.transpose(1, 0, 2, 3).reshape(16, 16, width)
    readout_grad = readout_grad.reshape(16, 16, width)
    vectors = jnp.concatenate(
        (
            gain_grad.reshape(16, 64),
            final_gain_grad.reshape(SEC, 16, 16).transpose(1, 0, 2).reshape(16, 64),
            jnp.zeros((16, width - 128), WIDE),
        ),
        axis=1,
    )
    small = jnp.concatenate(
        (
            jnp.where(section == 0, input_grad, readout_grad),
            vectors[:, None],
            jnp.zeros((16, 15, width), WIDE),
        ),
        axis=1,
    ).reshape(NX, NY, 32, GRP, width // GRP)
    smalls = (small, small.swapaxes(0, 1))

    def small_block(which, spot, by):
        part = jnp.where(which == 0, smalls[0][:, :, :, 0], smalls[1][:, :, :, 1])
        part = lax.dynamic_index_in_dim(part, (spot + by) % 4, 0, False)
        return part.reshape(NY * 32, width // GRP)

    def summed(maker, sections=range(SEC)):
        def block_for(by):
            other = maker(1 - core, second_at, by).astype(LOW)
            got = swap_cores(other, sections).astype(WIDE)
            return (maker(core, first_at, by) + got).astype(LOW)

        return reduce_plane(block_for, second_at, sections)

    both = lambda mine, other: jnp.where(
        core == 0,
        jnp.concatenate((mine, other), axis=1),
        jnp.concatenate((other, mine), axis=1),
    )
    lead_part = summed(lead_block)
    lead_out = both(lead_part, swap_cores(lead_part)).astype(WIDE)

    down_part = summed(down_block, odd)
    down_other = swap_cores(down_part, odd)
    upper_part = jnp.where(core == 0, down_part, down_other)
    lower_part = jnp.where(core == 0, down_other, down_part)
    upper_half = lax.dynamic_slice_in_dim(upper_part, core * (width // 2), width // 2, 1)
    upper_half = jnp.where(section == 0, link(upper_half, 1, 0), link(upper_half, 3, 2))
    down_out = jnp.where(is_mlp, lower_part, both(upper_half, swap_cores(upper_half))).astype(WIDE)

    small_part = summed(small_block)
    small = both(small_part, swap_cores(small_part))
    gain_out = small[16, :64].astype(WIDE)
    input_rows = small[:16].reshape(SEC, 4, width)
    readout_rows = small[:16].reshape(64, SEC, 64)
    final_rows = small[16, 64:128].reshape(SEC, 16)

    def sent_part(by):
        target = (section + by) % SEC
        readouts = lax.dynamic_index_in_dim(readout_rows, target, 1, False).reshape(4, width)
        finals = lax.dynamic_index_in_dim(final_rows, target, 0, False)
        finals = jnp.pad(finals, (0, width - 16))[None]
        inputs = lax.dynamic_index_in_dim(input_rows, target, 0, False)
        return jnp.concatenate((jnp.where(section == 0, inputs, readouts), finals))

    input_out = input_rows[0]
    readout_out = readout_rows[:, last]
    final_out = final_rows[last]
    for by in TURNS:
        part = turn(sent_part(by), by)
        input_out = jnp.where(section == by, part[:4], input_out)
        here = section == (last + by) % SEC
        readout_out = jnp.where(here, part[:4].reshape(64, 64), readout_out)
        final_out = jnp.where(here, part[4, :16], final_out)

    head_out = head_grad.astype(WIDE) + swap_cores(head_grad).astype(WIDE)
    return (
        noise_out[:, None],
        embed_grad,
        input_out.astype(WIDE),
        gain_out[None],
        lead_out[None],
        down_out[None],
        final_out.astype(WIDE),
        readout_out.astype(WIDE),
        head_out,
    )


def solution(mesh):
    in_specs = (
        P(None, ("group", "row"), None),
        P(None, ("group", "row"), None),
        P(None, ("group", "row"), None, "section"),
        P(None, "section"),
        P("section", None),
        P("section", None),
        P("section", None, None),
        P("section", None, None),
        P(),
        P(None, "section"),
        P("section", None),
    )
    out_specs = (
        P(None, ("group", "row"), None, "section"),
        P("row", "section"),
        P(("section", "row"), None),
        P("section", "row"),
        P("section", "row", None),
        P("section", "row", None),
        P(("section", "row")),
        P("row", "section"),
        P(("section", "row"), None),
    )
    return jax.shard_map(local, mesh=mesh, in_specs=in_specs, out_specs=out_specs, check_vma=False)
```

```python
import itertools

import jax
import jax.numpy as jnp
from jax import lax
from jax.experimental import pallas as pl
from jax.experimental.pallas import tpu as pltpu
from jax.sharding import PartitionSpec as P

HEADS = 16
HEAD_SIZE = 64
LOW = jnp.bfloat16
WIDE = jnp.float32
EPSILON = 1e-05
MASKED = -1000000000.0
CHUNK = 512
GELU_A = 0.7978845608028654
GELU_B = 0.044715
HBM_SPEC = pl.BlockSpec(memory_space=pltpu.HBM)
VMEM_SPEC = pl.BlockSpec(memory_space=pltpu.VMEM)
SMEM_SPEC = pl.BlockSpec(memory_space=pltpu.SMEM)


def matmul(former, latter):
    return jnp.dot(former, latter, preferred_element_type=WIDE)


def matmul_nt(former, latter):
    return lax.dot_general(
        former, latter, (((1,), (1,)), ((), ())), preferred_element_type=WIDE
    )


def matmul_tn(former, latter):
    return lax.dot_general(
        former, latter, (((0,), (0,)), ((), ())), preferred_element_type=WIDE
    )


def layer_norm(values):
    centre = jnp.mean(values, axis=-1, keepdims=True)
    centred = values - centre
    variance = jnp.mean(centred * centred, axis=-1, keepdims=True)
    factor = lax.rsqrt(variance + EPSILON)
    return (centred * factor, factor)


def norm_back(grad_normed, normed, factor):
    first_mean = jnp.mean(grad_normed, axis=-1, keepdims=True)
    second_mean = jnp.mean(grad_normed * normed, axis=-1, keepdims=True)
    return factor * (grad_normed - first_mean - normed * second_mean)


def gelu(v):
    return 0.5 * v * (1.0 + jnp.tanh(GELU_A * (v + GELU_B * (v * v * v))))


def gelu_slope(v):
    square = v * v
    bend = jnp.tanh(GELU_A * (v + GELU_B * (square * v)))
    return 0.5 * (1.0 + bend) + 0.5 * v * (1.0 - bend * bend) * (
        GELU_A * (1.0 + 3.0 * GELU_B * square)
    )


def head_probs(scores, same):
    scores = jnp.where(same, scores * HEAD_SIZE ** (-0.5), MASKED)
    expo = jnp.exp(scores - jnp.max(scores, axis=-1, keepdims=True))
    return expo * (1.0 / jnp.sum(expo, axis=-1, keepdims=True))


def lanes(at, size):
    return pl.ds(pl.multiple_of(at, 128), size)


def hold_kernel(lead_in, down_in, lead_ref, down_ref, sem):
    copies = [
        pltpu.make_async_copy(lead_in, lead_ref, sem.at[0]),
        pltpu.make_async_copy(down_in, down_ref, sem.at[1]),
    ]
    for copy in copies:
        copy.start()
    for copy in copies:
        copy.wait()


def hold(lead, down):
    return pl.pallas_call(
        hold_kernel,
        out_shape=[pltpu.VMEM(lead.shape, LOW), pltpu.VMEM(down.shape, LOW)],
        in_specs=[HBM_SPEC] * 2,
        out_specs=[VMEM_SPEC] * 2,
        scratch_shapes=[pltpu.SemaphoreType.DMA((2,))],
        compiler_params=pltpu.CompilerParams(vmem_limit_bytes=4 << 20),
        name="hold",
    )(lead, down)


def forward_kernel(
    role_ref,
    entry_ref,
    seg_col_ref,
    seg_row_ref,
    gain_ref,
    lead_ref,
    down_ref,
    entries_in,
    normeds_in,
    saved_in,
    inner_in,
    out_ref,
    entries_ref,
    normeds_ref,
    saved_ref,
    inner_ref,
    normed_buf,
    saved_buf,
    inner_buf,
    result_buf,
    out_sems,
):
    role, slot = role_ref[0], role_ref[1]
    tokens, width = entry_ref.shape
    keeps = [
        pltpu.make_async_copy(entry_ref, entries_ref.at[slot], out_sems.at[0]),
        pltpu.make_async_copy(normed_buf, normeds_ref.at[slot], out_sems.at[1]),
        pltpu.make_async_copy(saved_buf, saved_ref.at[slot], out_sems.at[2]),
    ]
    keep_inner = pltpu.make_async_copy(inner_buf, inner_ref.at[slot], out_sems.at[3])

    @pl.when(role > 0)
    def _():
        normed, _ = layer_norm(entry_ref[...].astype(WIDE))
        normed_buf[...] = (normed * gain_ref[...]).astype(LOW)
        keeps[0].start()
        keeps[1].start()

    @pl.when(role == 1)
    def _():
        @pl.loop(0, 3 * width // CHUNK)
        def _(j):
            at = lanes(j * CHUNK, CHUNK)
            saved_buf[:, at] = matmul(normed_buf[...], lead_ref[:, at]).astype(LOW)

        same = seg_col_ref[slot] == seg_row_ref[slot]
        left = lax.broadcasted_iota(jnp.int32, (tokens, 128), 1) < HEAD_SIZE
        zero = jnp.zeros((tokens, 128), LOW)

        @pl.loop(0, HEADS // 4)
        def _(quad):
            for which in range(2):
                at = quad * 256 + which * 128
                query = saved_buf[:, lanes(at, 128)]
                key = saved_buf[:, lanes(width + at, 128)]
                value = saved_buf[:, lanes(2 * width + at, 128)]
                probs_a = head_probs(matmul_nt(jnp.where(left, query, zero), key), same)
                probs_b = head_probs(matmul_nt(jnp.where(left, zero, query), key), same)
                mixed = jnp.where(
                    left, matmul(probs_a.astype(LOW), value), matmul(probs_b.astype(LOW), value)
                )
                saved_buf[:, lanes(3 * width + at, 128)] = mixed.astype(LOW)

        keeps[2].start()

        @pl.loop(0, width // CHUNK)
        def _(j):
            at = lanes(j * CHUNK, CHUNK)
            term = matmul(saved_buf[:, 3 * width :], lead_ref[:, lanes(3 * width + j * CHUNK, CHUNK)])
            out_ref[:, at] = (entry_ref[:, at].astype(WIDE) + term).astype(LOW)

    @pl.when(role == 2)
    def _():
        result_buf[...] = entry_ref[...].astype(WIDE)

        @pl.loop(0, lead_ref.shape[1] // CHUNK)
        def _(j):
            at = lanes(j * CHUNK, CHUNK)
            inner = matmul(normed_buf[...], lead_ref[:, at])
            inner_buf[:, at] = inner
            active = gelu(inner).astype(LOW)
            saved_buf[:, at] = active
            result_buf[...] += matmul(active, down_ref[pl.ds(j * CHUNK, CHUNK), :])

        keeps[2].start()
        keep_inner.start()
        out_ref[...] = result_buf[...].astype(LOW)
        keep_inner.wait()

    @pl.when(role > 0)
    def _():
        for keep in keeps:
            keep.wait()


def pinned(value):
    return pltpu.with_memory_space_constraint(value, pltpu.VMEM)


def forward_stage(role, entry, seg_col, seg_row, gain, lead, down, kept):
    tokens, width = entry.shape
    hidden = lead.shape[1]
    return pl.pallas_call(
        forward_kernel,
        out_shape=[jax.ShapeDtypeStruct(entry.shape, LOW)]
        + [jax.ShapeDtypeStruct(k.shape, k.dtype) for k in kept],
        in_specs=[SMEM_SPEC] + [VMEM_SPEC] * 6 + [HBM_SPEC] * 4,
        out_specs=[VMEM_SPEC] + [HBM_SPEC] * 4,
        scratch_shapes=[
            pltpu.VMEM((tokens, width), LOW),
            pltpu.VMEM((tokens, hidden), LOW),
            pltpu.VMEM((tokens, hidden), WIDE),
            pltpu.VMEM((tokens, width), WIDE),
            pltpu.SemaphoreType.DMA((4,)),
        ],
        input_output_aliases={7: 1, 8: 2, 9: 3, 10: 4},
        compiler_params=pltpu.CompilerParams(vmem_limit_bytes=14 << 20),
        cost_estimate=pl.CostEstimate(
            flops=4 * tokens * width * hidden, bytes_accessed=20 << 20, transcendentals=0
        ),
        name="forward_stage",
    )(role, entry, seg_col, seg_row, gain, pinned(lead), pinned(down), *kept)


def backward_kernel(
    role_ref,
    grad_ref,
    seg_col_ref,
    seg_row_ref,
    gain_ref,
    lead_ref,
    down_ref,
    entries_ref,
    saved_ref,
    inner_ref,
    nexts_in,
    grads_in,
    gains_in,
    out_ref,
    nexts_ref,
    grads_ref,
    gains_ref,
    saved_buf,
    inner_buf,
    grads_buf,
    mixed_buf,
    gain_buf,
    entry_buf,
    normed_buf,
    in_sems,
    out_sems,
):
    role, slot = role_ref[0], role_ref[1]
    tokens, width = grad_ref.shape
    bring_saved = pltpu.make_async_copy(saved_ref.at[slot], saved_buf, in_sems.at[0])
    bring_inner = pltpu.make_async_copy(inner_ref.at[slot], inner_buf, in_sems.at[1])
    bring_entry = pltpu.make_async_copy(entries_ref.at[slot], entry_buf, in_sems.at[2])
    keep_next = pltpu.make_async_copy(grad_ref, nexts_ref.at[slot], out_sems.at[0])
    keep_grads = pltpu.make_async_copy(grads_buf, grads_ref.at[slot], out_sems.at[1])
    keep_gain = pltpu.make_async_copy(gain_buf, gains_ref.at[slot], out_sems.at[2])

    @pl.when(role > 0)
    def _():
        bring_entry.start()
        keep_next.start()
        normed_buf[...] = jnp.zeros_like(normed_buf)

    @pl.when(role == 1)
    def _():
        bring_saved.start()
        grads_buf[:, 3 * width :] = grad_ref[...]
        mixed_buf[...] = matmul_nt(grad_ref[...], lead_ref[:, 3 * width :]).astype(LOW)
        bring_saved.wait()
        same = seg_col_ref[slot] == seg_row_ref[slot]
        left = lax.broadcasted_iota(jnp.int32, (tokens, 128), 1) < HEAD_SIZE
        zero = jnp.zeros((tokens, 128), LOW)
        scale = HEAD_SIZE ** (-0.5)

        @pl.loop(0, HEADS // 2)
        def _(pair):
            at = pair * 128
            query = saved_buf[:, lanes(at, 128)]
            key = saved_buf[:, lanes(width + at, 128)]
            value = saved_buf[:, lanes(2 * width + at, 128)]
            grad = mixed_buf[:, lanes(at, 128)]
            parts = []
            for own in (0, 1):
                mine = lambda v: jnp.where(left, v, zero) if own == 0 else jnp.where(left, zero, v)
                probs = head_probs(matmul_nt(mine(query), key), same)
                grad_probs = matmul_nt(mine(grad), value)
                grad_scores = probs * (
                    grad_probs - jnp.sum(probs * grad_probs, axis=-1, keepdims=True)
                )
                grad_low = grad_scores.astype(LOW)
                parts.append(
                    (
                        matmul(grad_low, key) * scale,
                        matmul_tn(grad_low, query) * scale,
                        matmul_tn(probs.astype(LOW), grad),
                    )
                )
            for which in range(3):
                grads_buf[:, lanes(which * width + at, 128)] = jnp.where(
                    left, parts[0][which], parts[1][which]
                ).astype(LOW)

        @pl.loop(0, 3 * width // CHUNK)
        def _(j):
            at = lanes(j * CHUNK, CHUNK)
            normed_buf[...] += matmul_nt(grads_buf[:, at], lead_ref[:, at])

    @pl.when(role == 2)
    def _():
        bring_inner.start()
        bring_inner.wait()

        @pl.loop(0, lead_ref.shape[1] // CHUNK)
        def _(j):
            at = lanes(j * CHUNK, CHUNK)
            grad_active = matmul_nt(grad_ref[...], down_ref[pl.ds(j * CHUNK, CHUNK), :])
            grads = (gelu_slope(inner_buf[:, at]) * grad_active).astype(LOW)
            grads_buf[:, at] = grads
            normed_buf[...] += matmul_nt(grads, lead_ref[:, at])

    @pl.when(role > 0)
    def _():
        keep_grads.start()
        bring_entry.wait()
        grad_normed = normed_buf[...]
        normed, factor = layer_norm(entry_buf[...].astype(WIDE))
        gain_buf[...] = jnp.broadcast_to(
            jnp.sum(grad_normed * normed, axis=0, keepdims=True), gain_buf.shape
        )
        keep_gain.start()
        out_ref[...] = (
            grad_ref[...].astype(WIDE) + norm_back(grad_normed * gain_ref[...], normed, factor)
        ).astype(LOW)
        keep_next.wait()
        keep_grads.wait()
        keep_gain.wait()


def backward_stage(
    role, grad, seg_col, seg_row, gain, lead, down, entries, saved, inner, totals
):
    tokens, width = grad.shape
    hidden = lead.shape[1]
    return pl.pallas_call(
        backward_kernel,
        out_shape=[jax.ShapeDtypeStruct(grad.shape, LOW)]
        + [jax.ShapeDtypeStruct(k.shape, k.dtype) for k in totals],
        in_specs=[SMEM_SPEC] + [VMEM_SPEC] * 6 + [HBM_SPEC] * 6,
        out_specs=[VMEM_SPEC] + [HBM_SPEC] * 3,
        scratch_shapes=[
            pltpu.VMEM((tokens, hidden), LOW),
            pltpu.VMEM((tokens, hidden), WIDE),
            pltpu.VMEM((tokens, hidden), LOW),
            pltpu.VMEM((tokens, width), LOW),
            pltpu.VMEM((8, width), WIDE),
            pltpu.VMEM((tokens, width), LOW),
            pltpu.VMEM((tokens, width), WIDE),
            pltpu.SemaphoreType.DMA((3,)),
            pltpu.SemaphoreType.DMA((3,)),
        ],
        input_output_aliases={10: 1, 11: 2, 12: 3},
        compiler_params=pltpu.CompilerParams(vmem_limit_bytes=14 << 20),
        cost_estimate=pl.CostEstimate(
            flops=4 * tokens * width * hidden, bytes_accessed=20 << 20, transcendentals=0
        ),
        name="backward_stage",
    )(
        role,
        grad,
        seg_col,
        seg_row,
        gain,
        pinned(lead),
        pinned(down),
        entries,
        saved,
        inner,
        *totals,
    )


def stats_kernel(readout_ref, table_ref, peak_ref, total_ref):
    logits = matmul_nt(table_ref[...], readout_ref[...])
    own_peak = jnp.max(logits, axis=0, keepdims=True)
    own_total = lambda peak: jnp.sum(jnp.exp(logits - peak), axis=0, keepdims=True)

    @pl.when(pl.program_id(0) == 0)
    def _():
        peak_ref[...] = own_peak
        total_ref[...] = own_total(own_peak)

    @pl.when(pl.program_id(0) > 0)
    def _():
        peak = jnp.maximum(peak_ref[...], own_peak)
        total_ref[...] = total_ref[...] * jnp.exp(peak_ref[...] - peak) + own_total(peak)
        peak_ref[...] = peak


def head_stats(readout, table, tile):
    tokens, emb = readout.shape
    vocab = table.shape[0]
    whole = pl.BlockSpec((1, tokens), lambda i: (0, 0))
    return pl.pallas_call(
        stats_kernel,
        out_shape=[jax.ShapeDtypeStruct((1, tokens), WIDE)] * 2,
        grid=(vocab // tile,),
        in_specs=[
            pl.BlockSpec((tokens, emb), lambda i: (0, 0)),
            pl.BlockSpec((tile, emb), lambda i: (i, 0)),
        ],
        out_specs=[whole, whole],
        compiler_params=pltpu.CompilerParams(vmem_limit_bytes=30 << 20),
        cost_estimate=pl.CostEstimate(
            flops=2 * tokens * vocab * emb, bytes_accessed=5 << 20, transcendentals=tokens * vocab
        ),
        name="head_stats",
    )(readout, table)


def head_kernel(base_ref, readout_ref, table_ref, logsum_ref, ids_ref, head_ref, grad_ref):
    tile = table_ref.shape[0]
    logits = matmul_nt(table_ref[...], readout_ref[...])
    ids = ids_ref[...] - (base_ref[0] + pl.program_id(0) * tile)
    hits = lax.broadcasted_iota(jnp.int32, logits.shape, 0) == ids
    probs = jnp.exp(logits - logsum_ref[...])
    grads = jnp.where(hits, probs - 1.0, probs).astype(LOW)
    head_ref[...] = matmul(grads, readout_ref[...]).astype(LOW)
    term = matmul_tn(grads, table_ref[...])

    @pl.when(pl.program_id(0) == 0)
    def _():
        grad_ref[...] = term

    @pl.when(pl.program_id(0) > 0)
    def _():
        grad_ref[...] += term


def head_grads(base, readout, table, logsum, ids, tile):
    tokens, emb = readout.shape
    vocab = table.shape[0]
    row = pl.BlockSpec((1, tokens), lambda i: (0, 0))
    whole = pl.BlockSpec((tokens, emb), lambda i: (0, 0))
    part = pl.BlockSpec((tile, emb), lambda i: (i, 0))
    return pl.pallas_call(
        head_kernel,
        out_shape=[
            jax.ShapeDtypeStruct((vocab, emb), LOW),
            jax.ShapeDtypeStruct((tokens, emb), WIDE),
        ],
        grid=(vocab // tile,),
        in_specs=[SMEM_SPEC, whole, part, row, row],
        out_specs=[part, whole],
        compiler_params=pltpu.CompilerParams(vmem_limit_bytes=30 << 20),
        cost_estimate=pl.CostEstimate(
            flops=6 * tokens * vocab * emb, bytes_accessed=9 << 20, transcendentals=tokens * vocab
        ),
        name="head_grads",
    )(base, readout, table, logsum, ids)


def lookup_kernel(ids_ref, table_ref, noise_ref, out_ref, total_ref):
    step = pl.program_id(0)
    tile = table_ref.shape[1]
    tokens = ids_ref.shape[1]
    ids = ids_ref[...] - step * tile
    hits = lax.broadcasted_iota(jnp.int32, (tile, tokens), 0) == ids
    hits = jnp.where(hits, 1.0, 0.0).astype(LOW)
    term = matmul(table_ref[...], hits)

    @pl.when(step == 0)
    def _():
        total_ref[...] = term

    @pl.when(step > 0)
    def _():
        total_ref[...] += term

    @pl.when(step == pl.num_programs(0) - 1)
    def _():
        out_ref[...] = (total_ref[...] + noise_ref[...].astype(WIDE)).astype(LOW)


def lookup(ids, table, noise, tile):
    parts, vocab = table.shape
    tokens = ids.shape[1]
    whole = pl.BlockSpec((parts, tokens), lambda i: (0, 0))
    return pl.pallas_call(
        lookup_kernel,
        out_shape=jax.ShapeDtypeStruct((parts, tokens), LOW),
        grid=(vocab // tile,),
        in_specs=[
            pl.BlockSpec((1, tokens), lambda i: (0, 0)),
            pl.BlockSpec((parts, tile), lambda i: (0, i)),
            whole,
        ],
        out_specs=whole,
        scratch_shapes=[pltpu.VMEM((parts, tokens), WIDE)],
        compiler_params=pltpu.CompilerParams(vmem_limit_bytes=30 << 20),
        cost_estimate=pl.CostEstimate(
            flops=2 * 128 * vocab * tokens, bytes_accessed=4 << 20, transcendentals=0
        ),
        name="lookup",
    )(ids, table, noise)


def lead_grad_kernel(where_ref, normed_ref, mixed_ref, grads_ref, out_ref, turned_ref):
    role, half, spot = where_ref[0], where_ref[1], where_ref[2]
    step = pl.program_id(0)
    width = normed_ref.shape[1]
    steps = pl.num_programs(0)
    use_mixed = jnp.logical_and(role == 1, half == 1)

    @pl.when(step == 0)
    def _():
        turned_ref[...] = normed_ref[...].T

    @pl.when(jnp.logical_and(step == steps // 2, use_mixed))
    def _():
        turned_ref[...] = mixed_ref[...].T

    result = matmul(turned_ref[...], grads_ref[...]).astype(LOW)
    unit = width // 16
    for x in range(4):
        for y in range(4):
            part = result[(4 * x + y) * unit : (4 * x + y + 1) * unit]

            @pl.when(half == 0)
            def _():
                out_ref[(x - spot + 4) % 4, y * unit : (y + 1) * unit, :] = part

            @pl.when(half == 1)
            def _():
                out_ref[(y - spot + 4) % 4, x * unit : (x + 1) * unit, :] = part


def lead_grad(where, normed, saved, grads):
    tokens, width = normed.shape
    tile = 512
    return pl.pallas_call(
        lead_grad_kernel,
        out_shape=jax.ShapeDtypeStruct((4, width // 4, 2 * width), LOW),
        grid_spec=pltpu.PrefetchScalarGridSpec(
            num_scalar_prefetch=1,
            grid=(2 * width // tile,),
            in_specs=[
                pl.BlockSpec((tokens, width), lambda i, where: (0, 0)),
                pl.BlockSpec((tokens, width), lambda i, where: (0, 3)),
                pl.BlockSpec((tokens, tile), lambda i, where: (0, where[1] * (2 * width // tile) + i)),
            ],
            out_specs=pl.BlockSpec((4, width // 4, tile), lambda i, where: (0, 0, i)),
            scratch_shapes=[pltpu.VMEM((width, tokens), LOW)],
        ),
        compiler_params=pltpu.CompilerParams(vmem_limit_bytes=24 << 20),
        cost_estimate=pl.CostEstimate(
            flops=4 * tokens * width * width, bytes_accessed=8 << 20, transcendentals=0
        ),
        name="lead_grad",
    )(where, normed, saved, grads)


def down_grad_kernel(where_ref, saved_ref, nexts_ref, out_ref):
    role, half, spot = where_ref[0], where_ref[1], where_ref[2]
    at = pl.program_id(0)
    unit = saved_ref.shape[1] // 4

    @pl.when(role == 2)
    def _():
        result = matmul_tn(saved_ref[...], nexts_ref[...]).astype(LOW)

        @pl.when(half == 0)
        def _():
            out_ref[(at - spot + 4) % 4] = result

        @pl.when(half == 1)
        def _():
            for y in range(4):
                out_ref[
                    (y - spot + 4) % 4, pl.ds(pl.multiple_of(at * unit, unit), unit), :
                ] = result[y * unit : (y + 1) * unit]


def down_grad(where, saved, nexts):
    tokens, hidden = saved.shape
    width = nexts.shape[1]
    rows = hidden // 8
    live = lambda where: jnp.where(where[0] == 2, 1, 0)
    return pl.pallas_call(
        down_grad_kernel,
        out_shape=jax.ShapeDtypeStruct((4, rows, width), LOW),
        grid_spec=pltpu.PrefetchScalarGridSpec(
            num_scalar_prefetch=1,
            grid=(4,),
            in_specs=[
                pl.BlockSpec((tokens, rows), lambda i, where: (0, (where[1] * 4 + i) * live(where))),
                pl.BlockSpec((tokens, width), lambda i, where: (0, 0)),
            ],
            out_specs=pl.BlockSpec((4, rows, width), lambda i, where: (0, 0, 0)),
        ),
        compiler_params=pltpu.CompilerParams(vmem_limit_bytes=24 << 20),
        cost_estimate=pl.CostEstimate(
            flops=2 * tokens * width * hidden // 2, bytes_accessed=8 << 20, transcendentals=0
        ),
        name="down_grad",
    )(where, saved, nexts)


ROW_LEN = 128
SEC, GRP, NX, NY = 4, 2, 4, 4
ALL = ("section", "group", "row")
TURNS = (1, 3, 2)


def route(value, target_of):
    number = lambda s, g, x, y: (s * GRP + g) * NX * NY + x * NY + y
    pairs = []
    for at in itertools.product(range(SEC), range(GRP), range(NX), range(NY)):
        target = target_of(*at)
        if target is not None:
            pairs.append((number(*at), number(*target)))
    return lax.ppermute(value, ALL, pairs)


def link(value, source, target):
    return route(value, lambda s, g, x, y: (target, g, x, y) if s == source else None)


def turn(value, by):
    return route(value, lambda s, g, x, y: ((s + by) % SEC, g, x, y))


def swap_cores(value, sections=range(SEC)):
    return route(value, lambda s, g, x, y: (s, 1 - g, x, y) if s in sections else None)


def plane_route(value, by, first, sections=range(SEC)):
    def target_of(s, g, x, y):
        if s not in sections:
            return None
        if (g == 0) == first:
            return (s, g, (x + by) % NX, y)
        return (s, g, x, (y + by) % NY)

    return route(value, target_of)


def after(value, earlier):
    return lax.optimization_barrier((value, earlier))[0]


def row_block(values, block, count):
    size = values.shape[0] // count
    return lax.dynamic_slice_in_dim(values, block * size, size, 0)


def reduce_plane(mine, got, second, sections=range(SEC)):
    piece = lambda by: mine[by] if got is None else (mine[by].astype(WIDE) + got[by].astype(WIDE))
    total = piece(0).astype(WIDE)
    for by in TURNS:
        total = total + plane_route(piece(by).astype(LOW), by, True, sections).astype(WIDE)
    lowered = total.astype(LOW)
    result = row_block(total, second, 4)
    for by in TURNS:
        block = row_block(lowered, (second + by) % 4, 4)
        result = result + plane_route(block, by, False, sections).astype(WIDE)
    return result.astype(LOW)


def gather_plane(values):
    blocks = jnp.stack([values] + [plane_route(values, by, True) for by in TURNS])
    blocks = jnp.concatenate([blocks] + [plane_route(blocks, by, False) for by in TURNS])
    return jnp.concatenate([blocks, swap_cores(blocks)])


def empty(*kinds):
    return pl.pallas_call(
        lambda *refs: None,
        out_shape=[jax.ShapeDtypeStruct(shape, dtype) for shape, dtype in kinds],
        out_specs=[HBM_SPEC] * len(kinds),
        name="empty",
    )()


def embed_kernel(base_ref, ids_ref, grad_ref, out_ref):
    @pl.when(pl.program_id(0) == 0)
    def _():
        out_ref[...] = jnp.zeros_like(out_ref)

    tokens = grad_ref.shape[2]
    local = ids_ref[...] - base_ref[0]
    for block in range(grad_ref.shape[0]):
        ids = local[block * tokens : (block + 1) * tokens]
        hits = lax.broadcasted_iota(jnp.int32, (tokens, out_ref.shape[1]), 1) == ids
        hits = jnp.where(hits, 1.0, 0.0).astype(LOW)
        out_ref[...] += jnp.dot(grad_ref[block], hits, preferred_element_type=WIDE)


def embed_sum(base, ids, grads, rows):
    count, parts, tokens = grads.shape
    step = 4
    return pl.pallas_call(
        embed_kernel,
        out_shape=jax.ShapeDtypeStruct((parts, rows), WIDE),
        grid=(count // step,),
        in_specs=[
            pl.BlockSpec(memory_space=pltpu.SMEM),
            pl.BlockSpec((step * tokens, 1), lambda i: (i, 0)),
            pl.BlockSpec((step, parts, tokens), lambda i: (i, 0, 0)),
        ],
        out_specs=pl.BlockSpec((parts, rows), lambda i: (0, 0)),
        compiler_params=pltpu.CompilerParams(vmem_limit_bytes=40 << 20),
        cost_estimate=pl.CostEstimate(
            flops=2 * count * tokens * 256 * rows, bytes_accessed=12 << 20, transcendentals=0
        ),
        name="embed_sum",
    )(base, ids.reshape(count * tokens, 1), grads)


def local(
    token_ids,
    segment_ids,
    noise_input,
    embed_table,
    input_proj,
    norm_gain,
    lead_weight,
    down_weight,
    final_gain,
    readout_proj,
    head_table,
):
    section = lax.axis_index("section")
    core = lax.axis_index("group")
    row = lax.axis_index("row")
    x_at, y_at = row // NY, row % NY
    first_at, second_at = jnp.where(core == 0, x_at, y_at), jnp.where(core == 0, y_at, x_at)
    micro, _, tokens = token_ids.shape
    width = input_proj.shape[1]
    hidden = lead_weight.shape[2]
    half_rows = down_weight.shape[1]
    emb_part = input_proj.shape[0]
    vocab_part, emb = head_table.shape
    vocab = embed_table.shape[0]
    all_tokens = micro * tokens
    last = SEC - 1
    is_mlp = section % 2 == 1
    gain_half = norm_gain.astype(WIDE)
    lead = lead_weight[0]
    own_down = down_weight[0]
    seg_row = segment_ids
    seg_col = segment_ids.reshape(micro, tokens, 1)
    flat_ids = token_ids.reshape(-1)

    noise = noise_input[:, 0].transpose(2, 0, 1).reshape(emb_part, -1)
    own_embedded = lookup(flat_ids[None], embed_table.T, noise, 3200)
    small_pack = jnp.concatenate((input_proj, readout_proj.T))
    packs = {by: turn(small_pack, by) for by in TURNS}
    packs[0] = small_pack
    pack_of = lambda s: lax.select_n((section - s) % SEC, *[packs[by] for by in range(SEC)])
    packed = [pack_of(s) for s in range(SEC)]
    input_full = jnp.concatenate([p[:emb_part] for p in packed])
    readout_full = jnp.concatenate([p[emb_part:] for p in packed])
    parts = {by: turn(after(own_embedded, packs[by]), by) for by in TURNS}
    embedded = jnp.concatenate(
        [own_embedded] + [parts[SEC - s] for s in range(1, SEC)]
    )
    first_in = matmul_tn(embedded, input_full).astype(LOW).reshape(micro, tokens, width)

    eighth = row_block(row_block(own_down, core, 2), first_at, 4)
    eighth = jnp.where(section == 1, link(eighth, 0, 1), link(eighth, 2, 3))
    upper = jnp.zeros((4,) + eighth.shape, LOW)
    upper = lax.dynamic_update_index_in_dim(upper, eighth, first_at, 0)
    for by in TURNS:
        upper = lax.dynamic_update_index_in_dim(
            upper, plane_route(eighth, by, True), (first_at - by) % 4, 0
        )
    upper = upper.reshape(half_rows // 2, width)
    upper_other = swap_cores(upper)
    full_down = jnp.concatenate(
        (
            jnp.where(core == 0, upper, upper_other),
            jnp.where(core == 0, upper_other, upper),
            own_down,
        )
    )
    all_ids = gather_plane(after(flat_ids, upper_other))
    held = hold(lead, full_down)

    kept = empty(
        ((micro, tokens, width), LOW),
        ((micro, tokens, width), LOW),
        ((micro, tokens, hidden), LOW),
        ((micro, tokens, hidden), WIDE),
    )

    def role_at(at):
        live = jnp.logical_and(at >= 0, at < micro)
        role = jnp.where(live, jnp.where(is_mlp, 2, 1), 0)
        return jnp.stack((role, jnp.clip(at, 0, micro - 1))).astype(jnp.int32)

    steps = micro + 2 * last
    outs, hops = [], {}

    def arrived(step, by):
        parts = [
            (s + by, hops[step - 2, s])
            for s in range(SEC)
            if (step - 2, s) in hops
        ]
        value = parts[0][1] if parts else None
        for target, part in parts[1:]:
            value = jnp.where(section == target, part, value)
        return value

    for step in range(steps):
        entry = arrived(step, 1)
        if entry is None:
            entry = first_in[step]
        elif step < micro:
            entry = jnp.where(section == 0, first_in[step], entry)
        out, *kept = forward_stage(
            role_at(step - 2 * section), entry, seg_col, seg_row, gain_half, *held, kept
        )
        outs.append(out)
        for s in range(last):
            if 0 <= step - 2 * s < micro:
                ready = after(out, hops[step - 1, s]) if (step - 1, s) in hops else out
                hops[step, s] = link(ready, s, s + 1)
    entries, normeds, saved, inner = kept

    final_rows = jnp.concatenate(outs[2 * last :]).astype(WIDE)
    normed_f, factor_f = layer_norm(final_rows)
    gain_f = final_gain.astype(WIDE)
    final_low = (normed_f * gain_f).astype(LOW)
    readout = matmul_nt(final_low, readout_full).astype(LOW)
    sent = [link(readout, last, s) for s in range(last)]
    for s in range(last):
        readout = jnp.where(section == s, sent[s], readout)
    peak, total = head_stats(readout, head_table, 1600)
    stats = jnp.concatenate((peak, total))
    all_stats = jnp.stack([stats] + [turn(stats, by) for by in TURNS])
    peak = jnp.max(all_stats[:, 0], axis=0)
    total = jnp.sum(all_stats[:, 1] * jnp.exp(all_stats[:, 0] - peak), axis=0)
    logsum = (peak + jnp.log(total))[None]
    head_grad, grad_readout = head_grads(
        (section * vocab_part).reshape(1), readout, head_table, logsum, flat_ids[None], 1600
    )
    grad_low = grad_readout.astype(LOW)
    for s in range(last):
        grad_readout = grad_readout + link(grad_low, s, last).astype(WIDE)
    grad_readout = grad_readout.astype(LOW)
    head_grad = lax.psum_scatter(
        head_grad.reshape(NX * NY, vocab_part // (NX * NY), emb), "row", scatter_dimension=0
    )
    readout_grad = matmul_tn(final_low, grad_readout)
    grad_final = matmul(grad_readout, readout_full)
    final_gain_grad = jnp.sum(grad_final * normed_f, axis=0)
    last_grads = norm_back(grad_final * gain_f, normed_f, factor_f).astype(LOW)
    last_grads = last_grads.reshape(micro, tokens, width)

    totals = empty(
        ((micro, tokens, width), LOW),
        ((micro, tokens, hidden), LOW),
        ((micro, 8, width), WIDE),
    )
    outs, hops = [], {}
    for step in range(steps):
        grad_next = arrived(step, -1)
        if grad_next is None:
            grad_next = last_grads[step]
        elif step < micro:
            grad_next = jnp.where(section == last, last_grads[step], grad_next)
        out, *totals = backward_stage(
            role_at(step - 2 * (last - section)),
            grad_next,
            seg_col,
            seg_row,
            gain_half,
            *held,
            entries,
            saved,
            inner,
            totals,
        )
        outs.append(out)
        for s in range(1, SEC):
            if 0 <= step - 2 * (last - s) < micro:
                ready = after(out, hops[step - 1, s]) if (step - 1, s) in hops else out
                hops[step, s] = link(ready, s, s - 1)

    first_grads = jnp.concatenate(outs[2 * last :])
    noise_grad = matmul_nt(input_full, first_grads).astype(LOW)
    pieces = noise_grad.reshape(SEC, emb_part, all_tokens)
    noise_grad = pieces[0]
    for s in TURNS:
        noise_grad = jnp.where(section == s, turn(pieces[s], s), noise_grad)
    embed_grad = embed_sum(
        (row * (vocab // 16)).reshape(1), all_ids, gather_plane(noise_grad), vocab // 16
    ).T
    noise_out = noise_grad.reshape(emb_part, micro, tokens).transpose(1, 2, 0).astype(WIDE)

    grad_nexts, grads, gain_grads = totals
    gain_grad = jnp.sum(gain_grads[:, 0], axis=0)
    flat = lambda v: v.reshape(all_tokens, v.shape[-1])
    normed, grad_nexts, grads, saved = flat(normeds), flat(grad_nexts), flat(grads), flat(saved)
    odd = (1, 3)
    role = jnp.where(is_mlp, 2, 1)
    where_other = jnp.stack((role, 1 - core, second_at)).astype(jnp.int32)
    where_mine = jnp.stack((role, core, first_at)).astype(jnp.int32)
    both = lambda mine, other: jnp.where(
        core == 0,
        jnp.concatenate((mine, other), axis=1),
        jnp.concatenate((other, mine), axis=1),
    )
    lead_got = swap_cores(lead_grad(where_other, normed, saved, grads))
    lead_mine = lead_grad(where_mine, normed, saved, grads)
    down_got = swap_cores(down_grad(where_other, saved, grad_nexts), odd)
    down_mine = down_grad(where_mine, saved, grad_nexts)
    lead_part = reduce_plane(lead_mine, lead_got, second_at)
    down_part = reduce_plane(down_mine, down_got, second_at, odd)
    lead_out = both(lead_part, swap_cores(lead_part)).astype(WIDE)

    down_other = swap_cores(down_part, odd)
    upper_part = jnp.where(core == 0, down_part, down_other)
    lower_part = jnp.where(core == 0, down_other, down_part)
    upper_half = lax.dynamic_slice_in_dim(upper_part, core * (width // 2), width // 2, 1)
    upper_half = jnp.where(section == 0, link(upper_half, 1, 0), link(upper_half, 3, 2))
    down_out = jnp.where(is_mlp, lower_part, both(upper_half, swap_cores(upper_half))).astype(WIDE)

    input_grad = matmul(embedded, first_grads).reshape(SEC, 16, 4, width)
    input_grad = input_grad.transpose(1, 0, 2, 3).reshape(16, 16, width)
    readout_grad = readout_grad.reshape(16, 16, width)
    vectors = jnp.concatenate(
        (
            gain_grad.reshape(16, 64),
            final_gain_grad.reshape(SEC, 16, 16).transpose(1, 0, 2).reshape(16, 64),
            jnp.zeros((16, width - 128), WIDE),
        ),
        axis=1,
    )
    small = jnp.concatenate(
        (
            jnp.where(section == 0, input_grad, readout_grad),
            vectors[:, None],
            jnp.zeros((16, 15, width), WIDE),
        ),
        axis=1,
    ).astype(LOW)
    half_of = lambda which: lax.dynamic_slice_in_dim(small, which * (width // 2), width // 2, 2)
    small = half_of(core).astype(WIDE) + swap_cores(half_of(1 - core)).astype(WIDE)
    small = small.astype(LOW).reshape(NX, NY, 32, width // 2)
    small = jnp.where(core == 0, small, small.swapaxes(0, 1))
    small = jnp.stack(
        [lax.dynamic_index_in_dim(small, (first_at + by) % 4, 0, False) for by in range(4)]
    )
    small_part = reduce_plane(small.reshape(4, NY * 32, width // 2), None, second_at)
    small = both(small_part, swap_cores(small_part))
    gain_out = small[16, :64].astype(WIDE)
    input_rows = small[:16].reshape(SEC, 4, width)
    readout_rows = small[:16].reshape(64, SEC, 64)
    final_rows = small[16, 64:128].reshape(SEC, 16)

    def sent_part(by):
        target = (section + by) % SEC
        readouts = lax.dynamic_index_in_dim(readout_rows, target, 1, False).reshape(4, width)
        finals = lax.dynamic_index_in_dim(final_rows, target, 0, False)
        finals = jnp.pad(finals, (0, width - 16))[None]
        inputs = lax.dynamic_index_in_dim(input_rows, target, 0, False)
        return jnp.concatenate((jnp.where(section == 0, inputs, readouts), finals))

    input_out = input_rows[0]
    readout_out = readout_rows[:, last]
    final_out = final_rows[last]
    for by in TURNS:
        part = turn(sent_part(by), by)
        input_out = jnp.where(section == by, part[:4], input_out)
        here = section == (last + by) % SEC
        readout_out = jnp.where(here, part[:4].reshape(64, 64), readout_out)
        final_out = jnp.where(here, part[4, :16], final_out)

    head_out = head_grad.astype(WIDE) + swap_cores(head_grad).astype(WIDE)
    return (
        noise_out[:, None],
        embed_grad,
        input_out.astype(WIDE),
        gain_out[None],
        lead_out[None],
        down_out[None],
        final_out.astype(WIDE),
        readout_out.astype(WIDE),
        head_out,
    )


def solution(mesh):
    in_specs = (
        P(None, ("group", "row"), None),
        P(None, ("group", "row"), None),
        P(None, ("group", "row"), None, "section"),
        P(None, "section"),
        P("section", None),
        P("section", None),
        P("section", None, None),
        P("section", None, None),
        P(),
        P(None, "section"),
        P("section", None),
    )
    out_specs = (
        P(None, ("group", "row"), None, "section"),
        P("row", "section"),
        P(("section", "row"), None),
        P("section", "row"),
        P("section", "row", None),
        P("section", "row", None),
        P(("section", "row")),
        P("row", "section"),
        P(("section", "row"), None),
    )
    return jax.shard_map(local, mesh=mesh, in_specs=in_specs, out_specs=out_specs, check_vma=False)
```

```python
import functools
import itertools

import jax
import jax.numpy as jnp
from jax import lax
from jax.experimental import pallas as pl
from jax.experimental.pallas import tpu as pltpu
from jax.sharding import PartitionSpec as P

HEADS = 16
HEAD_SIZE = 64
LOW = jnp.bfloat16
WIDE = jnp.float32
EPSILON = 1e-05
MASKED = -1000000000.0
CHUNK = 512
GELU_A = 0.7978845608028654
GELU_B = 0.044715
HBM_SPEC = pl.BlockSpec(memory_space=pltpu.HBM)
VMEM_SPEC = pl.BlockSpec(memory_space=pltpu.VMEM)
SMEM_SPEC = pl.BlockSpec(memory_space=pltpu.SMEM)


def matmul(former, latter):
    return jnp.dot(former, latter, preferred_element_type=WIDE)


def matmul_nt(former, latter):
    return lax.dot_general(
        former, latter, (((1,), (1,)), ((), ())), preferred_element_type=WIDE
    )


def matmul_tn(former, latter):
    return lax.dot_general(
        former, latter, (((0,), (0,)), ((), ())), preferred_element_type=WIDE
    )


def layer_norm(values):
    centre = jnp.mean(values, axis=-1, keepdims=True)
    centred = values - centre
    variance = jnp.mean(centred * centred, axis=-1, keepdims=True)
    factor = lax.rsqrt(variance + EPSILON)
    return (centred * factor, factor)


def norm_back(grad_normed, normed, factor):
    first_mean = jnp.mean(grad_normed, axis=-1, keepdims=True)
    second_mean = jnp.mean(grad_normed * normed, axis=-1, keepdims=True)
    return factor * (grad_normed - first_mean - normed * second_mean)


def gelu(v):
    return 0.5 * v * (1.0 + jnp.tanh(GELU_A * (v + GELU_B * (v * v * v))))


def gelu_slope(v):
    square = v * v
    bend = jnp.tanh(GELU_A * (v + GELU_B * (square * v)))
    return 0.5 * (1.0 + bend) + 0.5 * v * (1.0 - bend * bend) * (
        GELU_A * (1.0 + 3.0 * GELU_B * square)
    )


def head_probs(scores, same):
    scores = jnp.where(same, scores * HEAD_SIZE ** (-0.5), MASKED)
    expo = jnp.exp(scores - jnp.max(scores, axis=-1, keepdims=True))
    return expo * (1.0 / jnp.sum(expo, axis=-1, keepdims=True))


def lanes(at, size):
    return pl.ds(pl.multiple_of(at, 128), size)


def hold_kernel(source_ref, held_ref, sem):
    copy = pltpu.make_async_copy(source_ref, held_ref, sem)
    copy.start()
    copy.wait()


def hold(value):
    return pl.pallas_call(
        hold_kernel,
        out_shape=pltpu.VMEM(value.shape, value.dtype),
        in_specs=[HBM_SPEC],
        out_specs=VMEM_SPEC,
        scratch_shapes=[pltpu.SemaphoreType.DMA],
        compiler_params=pltpu.CompilerParams(vmem_limit_bytes=4 << 20),
        name="hold",
    )(far(value))


def forward_kernel(with_down, *refs):
    if not with_down:
        refs = refs[:6] + (None,) + refs[6:]
    forward_body(*refs)


def forward_body(
    role_ref,
    entry_ref,
    seg_col_ref,
    seg_row_ref,
    gain_ref,
    lead_ref,
    down_ref,
    entries_in,
    normeds_in,
    saved_in,
    inner_in,
    out_ref,
    entries_ref,
    normeds_ref,
    saved_ref,
    inner_ref,
    normed_buf,
    saved_buf,
    inner_buf,
    result_buf,
    scores_buf,
    probs_buf,
    out_sems,
):
    role, slot = role_ref[0], role_ref[1]
    tokens, width = entry_ref.shape
    keeps = [
        pltpu.make_async_copy(entry_ref, entries_ref.at[slot], out_sems.at[0]),
        pltpu.make_async_copy(normed_buf, normeds_ref.at[slot], out_sems.at[1]),
        pltpu.make_async_copy(saved_buf, saved_ref.at[slot], out_sems.at[2]),
    ]
    keep_inner = pltpu.make_async_copy(inner_buf, inner_ref.at[slot], out_sems.at[3])

    @pl.when(role > 0)
    def _():
        normed, _ = layer_norm(entry_ref[...].astype(WIDE))
        normed_buf[...] = (normed * gain_ref[...]).astype(LOW)
        keeps[0].start()
        keeps[1].start()

    @pl.when(role == 1)
    def _():
        @pl.loop(0, 3 * width // CHUNK, unroll=2)
        def _(j):
            at = lanes(j * CHUNK, CHUNK)
            saved_buf[:, at] = matmul(normed_buf[...], lead_ref[:, at]).astype(LOW)

        left = lax.broadcasted_iota(jnp.int32, (tokens, 128), 1) < HEAD_SIZE
        zero = jnp.zeros((tokens, 128), LOW)

        @pl.loop(0, HEADS // 8)
        def _(group):
            for pair in range(4):
                at = group * 512 + pair * 128
                query = saved_buf[:, lanes(at, 128)]
                key = saved_buf[:, lanes(width + at, 128)]
                scores_buf[group * 8 + 2 * pair] = matmul_nt(jnp.where(left, query, zero), key)
                scores_buf[group * 8 + 2 * pair + 1] = matmul_nt(jnp.where(left, zero, query), key)

        @pl.loop(0, HEADS // 4)
        def _(group):
            same = seg_col_ref[slot] == seg_row_ref[slot]
            for head in range(4):
                at = group * 4 + head
                probs_buf[at] = head_probs(scores_buf[at], same).astype(LOW)

        @pl.loop(0, HEADS // 8)
        def _(group):
            for pair in range(4):
                at = group * 512 + pair * 128
                value = saved_buf[:, lanes(2 * width + at, 128)]
                mixed = jnp.where(
                    left,
                    matmul(probs_buf[group * 8 + 2 * pair], value),
                    matmul(probs_buf[group * 8 + 2 * pair + 1], value),
                )
                saved_buf[:, lanes(3 * width + at, 128)] = mixed.astype(LOW)

        keeps[2].start()

        @pl.loop(0, width // CHUNK)
        def _(j):
            at = lanes(j * CHUNK, CHUNK)
            term = matmul(saved_buf[:, 3 * width :], lead_ref[:, lanes(3 * width + j * CHUNK, CHUNK)])
            out_ref[:, at] = (entry_ref[:, at].astype(WIDE) + term).astype(LOW)

    def feed_forward():
        result_buf[...] = entry_ref[...].astype(WIDE)

        @pl.loop(0, lead_ref.shape[1] // CHUNK, unroll=2)
        def _(j):
            at = lanes(j * CHUNK, CHUNK)
            inner = matmul(normed_buf[...], lead_ref[:, at])
            inner_buf[:, at] = inner
            active = gelu(inner).astype(LOW)
            saved_buf[:, at] = active
            result_buf[...] += matmul(active, down_ref[pl.ds(j * CHUNK, CHUNK), :])

        keeps[2].start()
        keep_inner.start()
        out_ref[...] = result_buf[...].astype(LOW)
        keep_inner.wait()

    if down_ref is not None:
        pl.when(role == 2)(feed_forward)

    @pl.when(role > 0)
    def _():
        for keep in keeps:
            keep.wait()


def pinned(value):
    return pltpu.with_memory_space_constraint(value, pltpu.VMEM)


def far(value):
    return pltpu.with_memory_space_constraint(value, pltpu.HBM)


def forward_stage(role, entry, seg_col, seg_row, gain, lead, down, kept):
    tokens, width = entry.shape
    hidden = lead.shape[1]
    count = 5 if down is None else 6
    return pl.pallas_call(
        functools.partial(forward_kernel, down is not None),
        out_shape=[jax.ShapeDtypeStruct(entry.shape, LOW)]
        + [jax.ShapeDtypeStruct(k.shape, k.dtype) for k in kept],
        in_specs=[SMEM_SPEC] + [VMEM_SPEC] * count + [HBM_SPEC] * 4,
        out_specs=[VMEM_SPEC] + [HBM_SPEC] * 4,
        scratch_shapes=[
            pltpu.VMEM((tokens, width), LOW),
            pltpu.VMEM((tokens, hidden), LOW),
            pltpu.VMEM((tokens, hidden), WIDE),
            pltpu.VMEM((tokens, width), WIDE),
            pltpu.VMEM((HEADS, tokens, tokens), WIDE),
            pltpu.VMEM((HEADS, tokens, tokens), LOW),
            pltpu.SemaphoreType.DMA((4,)),
        ],
        input_output_aliases={count + 1 + i: 1 + i for i in range(4)},
        compiler_params=pltpu.CompilerParams(vmem_limit_bytes=18 << 20),
        cost_estimate=pl.CostEstimate(
            flops=4 * tokens * width * hidden, bytes_accessed=20 << 20, transcendentals=0
        ),
        name="forward_stage",
    )(role, entry, seg_col, seg_row, gain, pinned(lead), *([pinned(down)] if down is not None else []), *map(far, kept))


def backward_kernel(
    role_ref,
    grad_ref,
    seg_col_ref,
    seg_row_ref,
    gain_ref,
    lead_ref,
    down_ref,
    entries_ref,
    saved_ref,
    inner_ref,
    nexts_in,
    grads_in,
    gains_in,
    out_ref,
    nexts_ref,
    grads_ref,
    gains_ref,
    saved_buf,
    inner_buf,
    grads_buf,
    mixed_buf,
    gain_buf,
    entry_buf,
    normed_buf,
    scores_buf,
    probs_grad_buf,
    probs_buf,
    scores_grad_buf,
    in_sems,
    out_sems,
):
    role, slot = role_ref[0], role_ref[1]
    tokens, width = grad_ref.shape
    bring_saved = pltpu.make_async_copy(saved_ref.at[slot], saved_buf, in_sems.at[0])
    bring_inner = pltpu.make_async_copy(inner_ref.at[slot], inner_buf, in_sems.at[1])
    bring_entry = pltpu.make_async_copy(entries_ref.at[slot], entry_buf, in_sems.at[2])
    keep_next = pltpu.make_async_copy(grad_ref, nexts_ref.at[slot], out_sems.at[0])
    keep_grads = pltpu.make_async_copy(grads_buf, grads_ref.at[slot], out_sems.at[1])
    keep_gain = pltpu.make_async_copy(gain_buf, gains_ref.at[slot], out_sems.at[2])

    @pl.when(role == 2)
    def _():
        bring_inner.start()

    @pl.when(role == 1)
    def _():
        bring_saved.start()

    @pl.when(role > 0)
    def _():
        bring_entry.start()
        keep_next.start()
        normed_buf[...] = jnp.zeros_like(normed_buf)

    @pl.when(role == 1)
    def _():
        grads_buf[:, 3 * width :] = grad_ref[...]
        mixed_buf[...] = matmul_nt(grad_ref[...], lead_ref[:, 3 * width :]).astype(LOW)
        bring_saved.wait()
        left = lax.broadcasted_iota(jnp.int32, (tokens, 128), 1) < HEAD_SIZE
        zero = jnp.zeros((tokens, 128), LOW)
        scale = HEAD_SIZE ** (-0.5)

        @pl.loop(0, HEADS // 8)
        def _(group):
            for pair in range(4):
                at = group * 512 + pair * 128
                query = saved_buf[:, lanes(at, 128)]
                key = saved_buf[:, lanes(width + at, 128)]
                value = saved_buf[:, lanes(2 * width + at, 128)]
                grad = mixed_buf[:, lanes(at, 128)]
                for own in (0, 1):
                    mine = lambda v: jnp.where(left, v, zero) if own == 0 else jnp.where(left, zero, v)
                    scores_buf[group * 8 + 2 * pair + own] = matmul_nt(mine(query), key)
                    probs_grad_buf[group * 8 + 2 * pair + own] = matmul_nt(mine(grad), value)

        @pl.loop(0, HEADS // 4)
        def _(group):
            same = seg_col_ref[slot] == seg_row_ref[slot]
            for head in range(4):
                at = group * 4 + head
                probs = head_probs(scores_buf[at], same)
                probs_buf[at] = probs.astype(LOW)
                grad_probs = probs_grad_buf[at]
                scores_grad_buf[at] = (
                    probs * (grad_probs - jnp.sum(probs * grad_probs, axis=-1, keepdims=True))
                ).astype(LOW)

        @pl.loop(0, HEADS // 4)
        def _(group):
            for pair in range(2):
                at = group * 256 + pair * 128
                query = saved_buf[:, lanes(at, 128)]
                key = saved_buf[:, lanes(width + at, 128)]
                grad = mixed_buf[:, lanes(at, 128)]
                parts = []
                for own in (0, 1):
                    probs = probs_buf[group * 4 + 2 * pair + own]
                    grad_low = scores_grad_buf[group * 4 + 2 * pair + own]
                    parts.append(
                        (
                            matmul(grad_low, key) * scale,
                            matmul_tn(grad_low, query) * scale,
                            matmul_tn(probs, grad),
                        )
                    )
                for which in range(3):
                    grads_buf[:, lanes(which * width + at, 128)] = jnp.where(
                        left, parts[0][which], parts[1][which]
                    ).astype(LOW)

        @pl.loop(0, 3 * width // CHUNK, unroll=2)
        def _(j):
            at = lanes(j * CHUNK, CHUNK)
            normed_buf[...] += matmul_nt(grads_buf[:, at], lead_ref[:, at])

    @pl.when(role == 2)
    def _():
        bring_inner.wait()

        @pl.loop(0, lead_ref.shape[1] // CHUNK, unroll=2)
        def _(j):
            at = lanes(j * CHUNK, CHUNK)
            grad_active = matmul_nt(grad_ref[...], down_ref[pl.ds(j * CHUNK, CHUNK), :])
            grads = (gelu_slope(inner_buf[:, at]) * grad_active).astype(LOW)
            grads_buf[:, at] = grads
            normed_buf[...] += matmul_nt(grads, lead_ref[:, at])

    @pl.when(role > 0)
    def _():
        keep_grads.start()
        bring_entry.wait()
        grad_normed = normed_buf[...]
        normed, factor = layer_norm(entry_buf[...].astype(WIDE))
        gain_buf[...] = jnp.broadcast_to(
            jnp.sum(grad_normed * normed, axis=0, keepdims=True), gain_buf.shape
        )
        keep_gain.start()
        out_ref[...] = (
            grad_ref[...].astype(WIDE) + norm_back(grad_normed * gain_ref[...], normed, factor)
        ).astype(LOW)
        keep_next.wait()
        keep_grads.wait()
        keep_gain.wait()


def backward_stage(
    role, grad, seg_col, seg_row, gain, lead, down, entries, saved, inner, totals
):
    tokens, width = grad.shape
    hidden = lead.shape[1]
    return pl.pallas_call(
        backward_kernel,
        out_shape=[jax.ShapeDtypeStruct(grad.shape, LOW)]
        + [jax.ShapeDtypeStruct(k.shape, k.dtype) for k in totals],
        in_specs=[SMEM_SPEC] + [VMEM_SPEC] * 6 + [HBM_SPEC] * 6,
        out_specs=[VMEM_SPEC] + [HBM_SPEC] * 3,
        scratch_shapes=[
            pltpu.VMEM((tokens, hidden), LOW),
            pltpu.VMEM((tokens, hidden), WIDE),
            pltpu.VMEM((tokens, hidden), LOW),
            pltpu.VMEM((tokens, width), LOW),
            pltpu.VMEM((8, width), WIDE),
            pltpu.VMEM((tokens, width), LOW),
            pltpu.VMEM((tokens, width), WIDE),
            pltpu.VMEM((HEADS, tokens, tokens), WIDE),
            pltpu.VMEM((HEADS, tokens, tokens), WIDE),
            pltpu.VMEM((HEADS, tokens, tokens), LOW),
            pltpu.VMEM((HEADS, tokens, tokens), LOW),
            pltpu.SemaphoreType.DMA((3,)),
            pltpu.SemaphoreType.DMA((3,)),
        ],
        input_output_aliases={10: 1, 11: 2, 12: 3},
        compiler_params=pltpu.CompilerParams(vmem_limit_bytes=18 << 20),
        cost_estimate=pl.CostEstimate(
            flops=4 * tokens * width * hidden, bytes_accessed=20 << 20, transcendentals=0
        ),
        name="backward_stage",
    )(
        role,
        grad,
        seg_col,
        seg_row,
        gain,
        pinned(lead),
        pinned(down),
        far(entries),
        far(saved),
        far(inner),
        *map(far, totals),
    )


def stats_kernel(readout_ref, table_ref, peak_ref, total_ref):
    logits = matmul_nt(table_ref[...], readout_ref[...])
    own_peak = jnp.max(logits, axis=0, keepdims=True)
    own_total = lambda peak: jnp.sum(jnp.exp(logits - peak), axis=0, keepdims=True)

    @pl.when(pl.program_id(0) == 0)
    def _():
        peak_ref[...] = own_peak
        total_ref[...] = own_total(own_peak)

    @pl.when(pl.program_id(0) > 0)
    def _():
        peak = jnp.maximum(peak_ref[...], own_peak)
        total_ref[...] = total_ref[...] * jnp.exp(peak_ref[...] - peak) + own_total(peak)
        peak_ref[...] = peak


def head_stats(readout, table, tile):
    tokens, emb = readout.shape
    vocab = table.shape[0]
    whole = pl.BlockSpec((1, tokens), lambda i: (0, 0))
    return pl.pallas_call(
        stats_kernel,
        out_shape=[jax.ShapeDtypeStruct((1, tokens), WIDE)] * 2,
        grid=(vocab // tile,),
        in_specs=[
            pl.BlockSpec((tokens, emb), lambda i: (0, 0)),
            pl.BlockSpec((tile, emb), lambda i: (i, 0)),
        ],
        out_specs=[whole, whole],
        compiler_params=pltpu.CompilerParams(vmem_limit_bytes=32 << 20),
        cost_estimate=pl.CostEstimate(
            flops=2 * tokens * vocab * emb, bytes_accessed=5 << 20, transcendentals=tokens * vocab
        ),
        name="head_stats",
    )(readout, far(table))


def head_kernel(base_ref, readout_ref, table_ref, logsum_ref, ids_ref, head_ref, grad_ref):
    tile = table_ref.shape[0]
    logits = matmul_nt(table_ref[...], readout_ref[...])
    ids = ids_ref[...] - (base_ref[0] + pl.program_id(0) * tile)
    hits = lax.broadcasted_iota(jnp.int32, logits.shape, 0) == ids
    probs = jnp.exp(logits - logsum_ref[...])
    grads = jnp.where(hits, probs - 1.0, probs).astype(LOW)
    head = matmul(grads, readout_ref[...])
    unit = tile // 4
    for shard in range(4):
        head_ref[shard, :unit] = head[shard * unit : (shard + 1) * unit].astype(LOW)
    term = matmul_tn(grads, table_ref[...])

    @pl.when(pl.program_id(0) == 0)
    def _():
        grad_ref[...] = term

    @pl.when(pl.program_id(0) > 0)
    def _():
        grad_ref[...] += term


def head_grads(base, readout, table, logsum, ids):
    tokens, emb = readout.shape
    vocab = table.shape[0]
    row = pl.BlockSpec((1, tokens), lambda i: (0, 0))
    whole = pl.BlockSpec((tokens, emb), lambda i: (0, 0))
    part = pl.BlockSpec((vocab // 4, emb), lambda i: (i, 0))
    return pl.pallas_call(
        head_kernel,
        out_shape=[
            jax.ShapeDtypeStruct((16, 512, emb), LOW),
            jax.ShapeDtypeStruct((tokens, emb), WIDE),
        ],
        grid=(4,),
        in_specs=[SMEM_SPEC, whole, part, row, row],
        out_specs=[pl.BlockSpec((4, 512, emb), lambda i: (i, 0, 0)), whole],
        compiler_params=pltpu.CompilerParams(vmem_limit_bytes=32 << 20),
        cost_estimate=pl.CostEstimate(
            flops=6 * tokens * vocab * emb, bytes_accessed=9 << 20, transcendentals=tokens * vocab
        ),
        name="head_grads",
    )(base, readout, far(table), logsum, ids)


def pair_kernel(former_ref, latter_ref, out_ref):
    rows = out_ref.shape[0]
    out_ref[...] = former_ref[:rows].astype(WIDE) + latter_ref[:rows].astype(WIDE)


def pair_sum(former, latter, rows):
    return pl.pallas_call(
        pair_kernel,
        out_shape=jax.ShapeDtypeStruct((rows, former.shape[1]), WIDE),
        in_specs=[VMEM_SPEC] * 2,
        out_specs=VMEM_SPEC,
        compiler_params=pltpu.CompilerParams(vmem_limit_bytes=8 << 20),
        name="pair_sum",
    )(former, latter)


def lookup_kernel(ids_ref, table_ref, noise_ref, out_ref, total_ref, low_ref):
    step = pl.program_id(0)
    parts, tile = table_ref.shape
    tokens = ids_ref.shape[1]
    blocks = tile // 128

    @pl.when(step == 0)
    def _():
        lane = jnp.bitwise_and(ids_ref[...], 127)
        hits = lax.broadcasted_iota(jnp.int32, (128, tokens), 0) == lane
        low_ref[...] = jnp.where(hits, 1.0, 0.0).astype(LOW)
        total_ref[...] = noise_ref[...].astype(WIDE)

    stacked = jnp.concatenate(
        [table_ref[:, block * 128 : (block + 1) * 128] for block in range(blocks)]
    )
    found = matmul(stacked, low_ref[...])
    own = jnp.right_shift(ids_ref[...], 7) - step * blocks
    total = jnp.zeros_like(total_ref)
    for block in range(blocks):
        total = jnp.where(own == block, found[block * parts : (block + 1) * parts], total)
    total_ref[...] += total

    @pl.when(step == pl.num_programs(0) - 1)
    def _():
        out_ref[...] = total_ref[...].astype(LOW)


def lookup(ids, table, noise, tile):
    parts, vocab = table.shape
    tokens = ids.shape[1]
    whole = pl.BlockSpec((parts, tokens), lambda i: (0, 0))
    return pl.pallas_call(
        lookup_kernel,
        out_shape=jax.ShapeDtypeStruct((parts, tokens), LOW),
        grid=(vocab // tile,),
        in_specs=[
            pl.BlockSpec((1, tokens), lambda i: (0, 0)),
            pl.BlockSpec((parts, tile), lambda i: (0, i)),
            whole,
        ],
        out_specs=whole,
        scratch_shapes=[pltpu.VMEM((parts, tokens), WIDE), pltpu.VMEM((128, tokens), LOW)],
        compiler_params=pltpu.CompilerParams(vmem_limit_bytes=32 << 20),
        cost_estimate=pl.CostEstimate(
            flops=2 * 128 * vocab * tokens, bytes_accessed=4 << 20, transcendentals=0
        ),
        name="lookup",
    )(ids, far(table), noise)


def lead_grad_kernel(where_ref, normed_ref, mixed_ref, grads_ref, out_ref, turned_ref):
    role, half, spot = where_ref[0], where_ref[1], where_ref[2]
    step = pl.program_id(0)
    width = normed_ref.shape[1]
    steps = pl.num_programs(0)
    use_mixed = jnp.logical_and(role == 1, half == 1)

    @pl.when(step == 0)
    def _():
        turned_ref[...] = normed_ref[...].T

    @pl.when(jnp.logical_and(step == steps // 2, use_mixed))
    def _():
        turned_ref[...] = mixed_ref[...].T

    result = matmul(turned_ref[...], grads_ref[...]).astype(LOW)
    unit = width // 16
    for x in range(4):
        for y in range(4):
            part = result[(4 * x + y) * unit : (4 * x + y + 1) * unit]

            @pl.when(half == 0)
            def _():
                out_ref[(x - spot + 4) % 4, y * unit : (y + 1) * unit, :] = part

            @pl.when(half == 1)
            def _():
                out_ref[(y - spot + 4) % 4, x * unit : (x + 1) * unit, :] = part


def lead_grad(where, normed, saved, grads):
    tokens, width = normed.shape
    tile = 512
    return pl.pallas_call(
        lead_grad_kernel,
        out_shape=jax.ShapeDtypeStruct((4, width // 4, 2 * width), LOW),
        grid_spec=pltpu.PrefetchScalarGridSpec(
            num_scalar_prefetch=1,
            grid=(2 * width // tile,),
            in_specs=[
                pl.BlockSpec((tokens, width), lambda i, where: (0, 0)),
                pl.BlockSpec((tokens, width), lambda i, where: (0, 3)),
                pl.BlockSpec((tokens, tile), lambda i, where: (0, where[1] * (2 * width // tile) + i)),
            ],
            out_specs=pl.BlockSpec((4, width // 4, tile), lambda i, where: (0, 0, i)),
            scratch_shapes=[pltpu.VMEM((width, tokens), LOW)],
        ),
        compiler_params=pltpu.CompilerParams(vmem_limit_bytes=24 << 20),
        cost_estimate=pl.CostEstimate(
            flops=4 * tokens * width * width, bytes_accessed=8 << 20, transcendentals=0
        ),
        name="lead_grad",
    )(where, far(normed), far(saved), far(grads))


def down_grad_kernel(where_ref, saved_ref, nexts_ref, out_ref):
    role, half, spot = where_ref[0], where_ref[1], where_ref[2]
    at = pl.program_id(0)
    unit = saved_ref.shape[1] // 4

    @pl.when(role == 2)
    def _():
        result = matmul_tn(saved_ref[...], nexts_ref[...]).astype(LOW)

        @pl.when(half == 0)
        def _():
            out_ref[(at - spot + 4) % 4] = result

        @pl.when(half == 1)
        def _():
            for y in range(4):
                out_ref[
                    (y - spot + 4) % 4, pl.ds(pl.multiple_of(at * unit, unit), unit), :
                ] = result[y * unit : (y + 1) * unit]


def down_grad(where, saved, nexts):
    tokens, hidden = saved.shape
    width = nexts.shape[1]
    rows = hidden // 8
    live = lambda where: jnp.where(where[0] == 2, 1, 0)
    return pl.pallas_call(
        down_grad_kernel,
        out_shape=jax.ShapeDtypeStruct((4, rows, width), LOW),
        grid_spec=pltpu.PrefetchScalarGridSpec(
            num_scalar_prefetch=1,
            grid=(4,),
            in_specs=[
                pl.BlockSpec((tokens, rows), lambda i, where: (0, (where[1] * 4 + i) * live(where))),
                pl.BlockSpec((tokens, width), lambda i, where: (0, 0)),
            ],
            out_specs=pl.BlockSpec((4, rows, width), lambda i, where: (0, 0, 0)),
        ),
        compiler_params=pltpu.CompilerParams(vmem_limit_bytes=24 << 20),
        cost_estimate=pl.CostEstimate(
            flops=2 * tokens * width * hidden // 2, bytes_accessed=8 << 20, transcendentals=0
        ),
        name="down_grad",
    )(where, far(saved), far(nexts))


def embed_kernel(base_ref, ids_ref, grad_ref, out_ref, total_ref):
    step = pl.program_id(0)
    count, parts, tokens = grad_ref.shape
    blocks = total_ref.shape[0] // parts
    term = None
    for at in range(count):
        ids = ids_ref[at] - base_ref[0]
        lane = jnp.bitwise_and(ids, 127)
        hits = lax.broadcasted_iota(jnp.int32, (128, tokens), 0) == lane
        hits = jnp.where(hits, 1.0, 0.0).astype(LOW)
        own = jnp.right_shift(ids, 7)
        grads = grad_ref[at]
        masked = jnp.concatenate(
            [grads * jnp.where(own == block, 1.0, 0.0).astype(LOW) for block in range(blocks)]
        )
        part = matmul_nt(masked, hits)
        term = part if term is None else term + part

    @pl.when(step == 0)
    def _():
        total_ref[...] = term

    @pl.when(step > 0)
    def _():
        total_ref[...] += term

    @pl.when(step == pl.num_programs(0) - 1)
    def _():
        rows = out_ref.shape[1]
        for block in range(blocks):
            size = min(128, rows - block * 128)
            out_ref[:, block * 128 : block * 128 + size] = total_ref[
                block * parts : (block + 1) * parts, :size
            ]


def embed_sum(base, ids, grads, rows):
    count, parts, tokens = grads.shape
    step = 4
    blocks = -(-rows // 128)
    return pl.pallas_call(
        embed_kernel,
        out_shape=jax.ShapeDtypeStruct((parts, rows), WIDE),
        grid=(count // step,),
        in_specs=[
            SMEM_SPEC,
            pl.BlockSpec((step, 1, tokens), lambda i: (i, 0, 0)),
            pl.BlockSpec((step, parts, tokens), lambda i: (i, 0, 0)),
        ],
        out_specs=pl.BlockSpec((parts, rows), lambda i: (0, 0)),
        scratch_shapes=[pltpu.VMEM((blocks * parts, 128), WIDE)],
        compiler_params=pltpu.CompilerParams(vmem_limit_bytes=32 << 20),
        cost_estimate=pl.CostEstimate(
            flops=2 * count * tokens * parts * rows, bytes_accessed=3 << 20, transcendentals=0
        ),
        name="embed_sum",
    )(base, ids.reshape(count, 1, tokens), grads)


ROW_LEN = 128
SEC, GRP, NX, NY = 4, 2, 4, 4
ALL = ("section", "group", "row")
TURNS = (1, 3, 2)


def route(value, target_of):
    number = lambda s, g, x, y: (s * GRP + g) * NX * NY + x * NY + y
    pairs = []
    for at in itertools.product(range(SEC), range(GRP), range(NX), range(NY)):
        target = target_of(*at)
        if target is not None:
            pairs.append((number(*at), number(*target)))
    return lax.ppermute(value, ALL, pairs)


def link(value, source, target):
    return route(value, lambda s, g, x, y: (target, g, x, y) if s == source else None)


def turn(value, by):
    return route(value, lambda s, g, x, y: ((s + by) % SEC, g, x, y))


def swap_cores(value, sections=range(SEC)):
    return route(value, lambda s, g, x, y: (s, 1 - g, x, y) if s in sections else None)


def plane_route(value, by, first, sections=range(SEC)):
    def target_of(s, g, x, y):
        if s not in sections:
            return None
        if (g == 0) == first:
            return (s, g, (x + by) % NX, y)
        return (s, g, x, (y + by) % NY)

    return route(value, target_of)


def after(value, earlier):
    return lax.optimization_barrier((value, earlier))[0]


def row_block(values, block, count):
    size = values.shape[0] // count
    return lax.dynamic_slice_in_dim(values, block * size, size, 0)


def plane_first(mine, got, sections=range(SEC)):
    piece = lambda by: mine[by] if got is None else (mine[by].astype(WIDE) + got[by].astype(WIDE))
    pieces = [piece(by).astype(LOW) for by in range(4)]
    return (pieces, [plane_route(pieces[by], by, True, sections) for by in TURNS])


def plane_second(first, second, sections=range(SEC)):
    pieces, arrived = first
    total = pieces[0].astype(WIDE)
    for piece in arrived:
        total = total + piece.astype(WIDE)
    total = total.astype(LOW)
    result = row_block(total, second, 4).astype(WIDE)
    for by in TURNS:
        block = row_block(total, (second + by) % 4, 4)
        result = result + plane_route(block, by, False, sections).astype(WIDE)
    return result.astype(LOW)


def gather_own(values):
    blocks = jnp.stack([values] + [plane_route(values, by, True) for by in TURNS])
    return jnp.concatenate([blocks] + [plane_route(blocks, by, False) for by in TURNS])


def gather_plane(values):
    blocks = gather_own(values)
    return jnp.concatenate([blocks, swap_cores(blocks)])


def empty(*kinds):
    return pl.pallas_call(
        lambda *refs: None,
        out_shape=[jax.ShapeDtypeStruct(shape, dtype) for shape, dtype in kinds],
        out_specs=[HBM_SPEC] * len(kinds),
        name="empty",
    )()


def local(
    token_ids,
    segment_ids,
    noise_input,
    embed_table,
    input_proj,
    norm_gain,
    lead_weight,
    down_weight,
    final_gain,
    readout_proj,
    head_table,
):
    section = lax.axis_index("section")
    core = lax.axis_index("group")
    row = lax.axis_index("row")
    x_at, y_at = row // NY, row % NY
    first_at, second_at = jnp.where(core == 0, x_at, y_at), jnp.where(core == 0, y_at, x_at)
    micro, _, tokens = token_ids.shape
    width = input_proj.shape[1]
    hidden = lead_weight.shape[2]
    half_rows = down_weight.shape[1]
    emb_part = input_proj.shape[0]
    vocab_part, emb = head_table.shape
    vocab = embed_table.shape[0]
    all_tokens = micro * tokens
    last = SEC - 1
    is_mlp = section % 2 == 1
    gain_half = norm_gain.astype(WIDE)
    lead = lead_weight[0]
    own_down = down_weight[0]
    seg_row = segment_ids
    seg_col = segment_ids.reshape(micro, tokens, 1)
    flat_ids = token_ids.reshape(-1)

    to_first = lambda v: [v] + [link(v, s, 0) for s in range(1, SEC)]
    eighth = row_block(row_block(own_down, core, 2), first_at, 4)
    eighth = jnp.where(section == 1, link(eighth, 0, 1), link(eighth, 2, 3))
    noise = noise_input[:, 0].transpose(2, 0, 1).reshape(emb_part, -1)
    own_embedded = lookup(flat_ids[None], embed_table.T, noise, 3200)
    inputs = to_first(input_proj)
    input_full = jnp.concatenate(inputs)
    embedded = jnp.concatenate(
        [own_embedded] + [link(after(own_embedded, inputs[s]), s, 0) for s in range(1, SEC)]
    )
    first_in = matmul_tn(embedded, input_full).astype(LOW).reshape(micro, tokens, width)
    held_lead = hold(lead)
    readout_own = after(readout_proj.T, first_in)
    readout_full = jnp.concatenate(
        [link(readout_own, s, last) for s in range(last)] + [readout_own]
    )

    eighth = after(eighth, own_embedded)
    upper = jnp.zeros((4,) + eighth.shape, LOW)
    upper = lax.dynamic_update_index_in_dim(upper, eighth, first_at, 0)
    for by in TURNS:
        upper = lax.dynamic_update_index_in_dim(
            upper, plane_route(eighth, by, True), (first_at - by) % 4, 0
        )
    upper = upper.reshape(half_rows // 2, width)
    upper_other = swap_cores(upper)
    held_down = hold(
        jnp.concatenate(
            (
                jnp.where(core == 0, upper, upper_other),
                jnp.where(core == 0, upper_other, upper),
                own_down,
            )
        )
    )
    all_ids = gather_plane(after(flat_ids, upper_other))

    kept = empty(
        ((micro, tokens, width), LOW),
        ((micro, tokens, width), LOW),
        ((micro, tokens, hidden), LOW),
        ((micro, tokens, hidden), WIDE),
    )

    def role_at(at):
        live = jnp.logical_and(at >= 0, at < micro)
        role = jnp.where(live, jnp.where(is_mlp, 2, 1), 0)
        return jnp.stack((role, jnp.clip(at, 0, micro - 1))).astype(jnp.int32)

    steps = micro + 2 * last
    outs, hops = [], {}

    def arrived(step, by):
        parts = [
            (s + by, hops[step - 2, s])
            for s in range(SEC)
            if (step - 2, s) in hops
        ]
        value = parts[0][1] if parts else None
        for target, part in parts[1:]:
            value = jnp.where(section == target, part, value)
        return value

    for step in range(steps):
        entry = arrived(step, 1)
        if entry is None:
            entry = first_in[step]
        elif step < micro:
            entry = jnp.where(section == 0, first_in[step], entry)
        if step == 5:
            entry = after(entry, all_ids)
        out, *kept = forward_stage(
            role_at(step - 2 * section),
            entry,
            seg_col,
            seg_row,
            gain_half,
            held_lead,
            held_down if step > 1 else None,
            kept,
        )
        outs.append(out)
        for s in range(last):
            if 0 <= step - 2 * s < micro:
                ready = after(out, hops[step - 1, s]) if (step - 1, s) in hops else out
                hops[step, s] = link(ready, s, s + 1)
    entries, normeds, saved, inner = kept

    final_rows = jnp.concatenate(outs[2 * last :]).astype(WIDE)
    normed_f, factor_f = layer_norm(final_rows)
    gain_f = final_gain.astype(WIDE)
    final_low = (normed_f * gain_f).astype(LOW)
    readout = matmul_nt(final_low, readout_full).astype(LOW)
    sent = [link(readout, last, s) for s in range(last)]
    for s in range(last):
        readout = jnp.where(section == s, sent[s], readout)
    peak, total = head_stats(readout, head_table, 2000)
    stats = jnp.concatenate((peak, total))
    all_stats = jnp.stack([stats] + [turn(stats, by) for by in TURNS])
    peak = jnp.max(all_stats[:, 0], axis=0)
    total = jnp.sum(all_stats[:, 1] * jnp.exp(all_stats[:, 0] - peak), axis=0)
    logsum = (peak + jnp.log(total))[None]
    head_grad, grad_readout = head_grads(
        (section * vocab_part).reshape(1), readout, head_table, logsum, flat_ids[None]
    )
    grad_low = grad_readout.astype(LOW)
    for s in range(last):
        grad_readout = grad_readout + link(grad_low, s, last).astype(WIDE)
    grad_readout = grad_readout.astype(LOW)
    head_grad = lax.psum_scatter(head_grad, "row", scatter_dimension=0)
    readout_grad = matmul_tn(final_low, grad_readout)
    grad_final = matmul(grad_readout, readout_full)
    final_gain_grad = jnp.sum(grad_final * normed_f, axis=0)
    last_grads = norm_back(grad_final * gain_f, normed_f, factor_f).astype(LOW)
    last_grads = last_grads.reshape(micro, tokens, width)

    totals = empty(
        ((micro, tokens, width), LOW),
        ((micro, tokens, hidden), LOW),
        ((micro, 8, width), WIDE),
    )
    outs, hops = [], {}
    for step in range(steps):
        grad_next = arrived(step, -1)
        if grad_next is None:
            grad_next = last_grads[step]
        elif step < micro:
            grad_next = jnp.where(section == last, last_grads[step], grad_next)
        if step == steps - 1:
            grad_next = after(grad_next, head_grad)
        out, *totals = backward_stage(
            role_at(step - 2 * (last - section)),
            grad_next,
            seg_col,
            seg_row,
            gain_half,
            held_lead,
            held_down,
            entries,
            saved,
            inner,
            totals,
        )
        outs.append(out)
        for s in range(1, SEC):
            if 0 <= step - 2 * (last - s) < micro:
                ready = after(out, hops[step - 1, s]) if (step - 1, s) in hops else out
                hops[step, s] = link(ready, s, s - 1)

    first_grads = jnp.concatenate(outs[2 * last :])
    noise_grad = matmul_nt(input_full, first_grads).astype(LOW)
    pieces = noise_grad.reshape(SEC, emb_part, all_tokens)
    sent = [link(pieces[s], 0, s) for s in range(1, SEC)]

    grad_nexts, grads, gain_grads = totals
    gain_grad = jnp.sum(gain_grads[:, 0], axis=0)
    flat = lambda v: v.reshape(all_tokens, v.shape[-1])
    normed, grad_nexts, grads, saved = flat(normeds), flat(grad_nexts), flat(grads), flat(saved)
    odd = (1, 3)
    role = jnp.where(is_mlp, 2, 1)
    where_other = jnp.stack((role, 1 - core, second_at)).astype(jnp.int32)
    where_mine = jnp.stack((role, core, first_at)).astype(jnp.int32)
    both = lambda mine, other: jnp.where(
        core == 0,
        jnp.concatenate((mine, other), axis=1),
        jnp.concatenate((other, mine), axis=1),
    )
    lead_got = swap_cores(lead_grad(where_other, normed, saved, grads))
    lead_mine = lead_grad(where_mine, normed, saved, grads)
    down_got = swap_cores(down_grad(where_other, saved, grad_nexts), odd)
    down_mine = down_grad(where_mine, saved, grad_nexts)
    lead_first = plane_first(lead_mine, lead_got)
    down_first = plane_first(down_mine, down_got, odd)
    noise_grad = pieces[0]
    for s in range(1, SEC):
        noise_grad = jnp.where(section == s, sent[s - 1], noise_grad)
    blocks = gather_own(after(noise_grad, (lead_first[0], down_first[0])))
    lead_part = plane_second(lead_first, second_at)
    down_part = plane_second(down_first, second_at, odd)
    lead_out = both(lead_part, swap_cores(lead_part)).astype(WIDE)
    blocks = jnp.concatenate([blocks, swap_cores(blocks)])
    embed_grad = embed_sum((row * (vocab // 16)).reshape(1), all_ids, blocks, vocab // 16).T
    noise_out = noise_grad.reshape(emb_part, micro, tokens).transpose(1, 2, 0).astype(WIDE)

    down_other = swap_cores(down_part, odd)
    upper_part = jnp.where(core == 0, down_part, down_other)
    lower_part = jnp.where(core == 0, down_other, down_part)
    upper_half = lax.dynamic_slice_in_dim(upper_part, core * (width // 2), width // 2, 1)
    upper_half = jnp.where(section == 0, link(upper_half, 1, 0), link(upper_half, 3, 2))
    down_out = jnp.where(is_mlp, lower_part, both(upper_half, swap_cores(upper_half))).astype(WIDE)

    input_grad = matmul(embedded, first_grads).reshape(SEC, 16, 4, width)
    input_grad = input_grad.transpose(1, 0, 2, 3).reshape(16, 16, width)
    readout_grad = readout_grad.reshape(16, 16, width)
    vectors = jnp.concatenate(
        (
            gain_grad.reshape(16, 64),
            final_gain_grad.reshape(SEC, 16, 16).transpose(1, 0, 2).reshape(16, 64),
            jnp.zeros((16, width - 128), WIDE),
        ),
        axis=1,
    )
    small = jnp.concatenate(
        (
            jnp.where(section == 0, input_grad, readout_grad),
            vectors[:, None],
            jnp.zeros((16, 15, width), WIDE),
        ),
        axis=1,
    ).astype(LOW)
    half_of = lambda which: lax.dynamic_slice_in_dim(small, which * (width // 2), width // 2, 2)
    small = half_of(core).astype(WIDE) + swap_cores(half_of(1 - core)).astype(WIDE)
    small = small.astype(LOW).reshape(NX, NY, 32, width // 2)
    small = jnp.where(core == 0, small, small.swapaxes(0, 1))
    small = jnp.stack(
        [lax.dynamic_index_in_dim(small, (first_at + by) % 4, 0, False) for by in range(4)]
    )
    small = after(small, (lead_part, down_part)).reshape(4, NY * 32, width // 2)
    small_part = plane_second(plane_first(small, None), second_at)
    small = both(small_part, swap_cores(small_part))
    gain_out = small[16, :64].astype(WIDE)
    input_rows = small[:16].reshape(SEC, 4, width)
    readout_rows = small[:16].reshape(64, SEC, 64)
    final_rows = small[16, 64:128].reshape(SEC, 16)

    def sent_part(by):
        target = (section + by) % SEC
        readouts = lax.dynamic_index_in_dim(readout_rows, target, 1, False).reshape(4, width)
        finals = lax.dynamic_index_in_dim(final_rows, target, 0, False)
        finals = jnp.pad(finals, (0, width - 16))[None]
        inputs = lax.dynamic_index_in_dim(input_rows, target, 0, False)
        return jnp.concatenate((jnp.where(section == 0, inputs, readouts), finals))

    input_out = input_rows[0]
    readout_out = readout_rows[:, last]
    final_out = final_rows[last]
    for by in TURNS:
        part = turn(sent_part(by), by)
        input_out = jnp.where(section == by, part[:4], input_out)
        here = section == (last + by) % SEC
        readout_out = jnp.where(here, part[:4].reshape(64, 64), readout_out)
        final_out = jnp.where(here, part[4, :16], final_out)

    head_out = pair_sum(head_grad, swap_cores(head_grad), vocab_part // (NX * NY))
    return (
        noise_out[:, None],
        embed_grad,
        input_out.astype(WIDE),
        gain_out[None],
        lead_out[None],
        down_out[None],
        final_out.astype(WIDE),
        readout_out.astype(WIDE),
        head_out,
    )


def solution(mesh):
    in_specs = (
        P(None, ("group", "row"), None),
        P(None, ("group", "row"), None),
        P(None, ("group", "row"), None, "section"),
        P(None, "section"),
        P("section", None),
        P("section", None),
        P("section", None, None),
        P("section", None, None),
        P(),
        P(None, "section"),
        P("section", None),
    )
    out_specs = (
        P(None, ("group", "row"), None, "section"),
        P("row", "section"),
        P(("section", "row"), None),
        P("section", "row"),
        P("section", "row", None),
        P("section", "row", None),
        P(("section", "row")),
        P("row", "section"),
        P(("section", "row"), None),
    )
    return jax.shard_map(local, mesh=mesh, in_specs=in_specs, out_specs=out_specs, check_vma=False)
```

```python
import functools
import itertools

import jax
import jax.numpy as jnp
import numpy as np
from jax import lax
from jax.experimental import pallas as pl
from jax.experimental.pallas import tpu as pltpu
from jax.sharding import PartitionSpec as P

HEADS = 16
HEAD_SIZE = 64
LOW = jnp.bfloat16
WIDE = jnp.float32
EPSILON = 1e-05
MASKED = -1000000000.0
CHUNK = 512
GELU_A = 0.7978845608028654
GELU_B = 0.044715
HBM_SPEC = pl.BlockSpec(memory_space=pltpu.HBM)
VMEM_SPEC = pl.BlockSpec(memory_space=pltpu.VMEM)
SMEM_SPEC = pl.BlockSpec(memory_space=pltpu.SMEM)


def matmul(former, latter):
    return jnp.dot(former, latter, preferred_element_type=WIDE)


def matmul_nt(former, latter):
    return lax.dot_general(
        former, latter, (((1,), (1,)), ((), ())), preferred_element_type=WIDE
    )


def matmul_tn(former, latter):
    return lax.dot_general(
        former, latter, (((0,), (0,)), ((), ())), preferred_element_type=WIDE
    )


def layer_norm(values):
    centre = jnp.mean(values, axis=-1, keepdims=True)
    centred = values - centre
    variance = jnp.mean(centred * centred, axis=-1, keepdims=True)
    factor = lax.rsqrt(variance + EPSILON)
    return (centred * factor, factor)


def norm_back(grad_normed, normed, factor):
    first_mean = jnp.mean(grad_normed, axis=-1, keepdims=True)
    second_mean = jnp.mean(grad_normed * normed, axis=-1, keepdims=True)
    return factor * (grad_normed - first_mean - normed * second_mean)


def gelu(v):
    return 0.5 * v * (1.0 + jnp.tanh(GELU_A * (v + GELU_B * (v * v * v))))


def gelu_slope(v):
    square = v * v
    bend = jnp.tanh(GELU_A * (v + GELU_B * (square * v)))
    return 0.5 * (1.0 + bend) + 0.5 * v * (1.0 - bend * bend) * (
        GELU_A * (1.0 + 3.0 * GELU_B * square)
    )


def head_probs(scores, same):
    scores = jnp.where(same, scores * HEAD_SIZE ** (-0.5), MASKED)
    expo = jnp.exp(scores - jnp.max(scores, axis=-1, keepdims=True))
    return expo * (1.0 / jnp.sum(expo, axis=-1, keepdims=True))


def same_segment(row):
    across = jnp.broadcast_to(row.astype(WIDE), (row.shape[1], row.shape[1]))
    return across.T == across


def lanes(at, size):
    return pl.ds(pl.multiple_of(at, 128), size)


def hold_kernel(source_ref, held_ref, sem):
    copy = pltpu.make_async_copy(source_ref, held_ref, sem)
    copy.start()
    copy.wait()


def hold(value):
    return pl.pallas_call(
        hold_kernel,
        out_shape=pltpu.VMEM(value.shape, value.dtype),
        in_specs=[HBM_SPEC],
        out_specs=VMEM_SPEC,
        scratch_shapes=[pltpu.SemaphoreType.DMA],
        compiler_params=pltpu.CompilerParams(vmem_limit_bytes=4 << 20),
        name="hold",
    )(far(value))


def chosen(choice, candidates, buffer):
    for at, candidate in enumerate(candidates):

        @pl.when(choice == at)
        def _():
            buffer[...] = candidate[...]


def forward_kernel(spot, with_down, count, *refs):
    table_ref, candidates, refs = refs[0], refs[1 : 1 + count], refs[1 + count :]
    if not with_down:
        refs = refs[:3] + (None,) + refs[3:]
    forward_body(spot, table_ref, candidates, *refs)


def forward_body(
    spot,
    table_ref,
    candidates,
    seg_row_ref,
    gain_ref,
    lead_ref,
    down_ref,
    entries_in,
    normeds_in,
    saved_in,
    inner_in,
    out_ref,
    entries_ref,
    normeds_ref,
    saved_ref,
    inner_ref,
    normed_buf,
    saved_buf,
    inner_buf,
    result_buf,
    scores_buf,
    probs_buf,
    entry_ref,
    out_sems,
):
    role, slot = table_ref[spot], table_ref[spot + 1]
    tokens, width = entry_ref.shape
    keeps = [
        pltpu.make_async_copy(entry_ref, entries_ref.at[slot], out_sems.at[0]),
        pltpu.make_async_copy(normed_buf, normeds_ref.at[slot], out_sems.at[1]),
        pltpu.make_async_copy(saved_buf, saved_ref.at[slot], out_sems.at[2]),
    ]
    keep_inner = pltpu.make_async_copy(inner_buf, inner_ref.at[slot], out_sems.at[3])

    @pl.when(role > 0)
    def _():
        chosen(table_ref[spot + 2], candidates, entry_ref)
        normed, _ = layer_norm(entry_ref[...].astype(WIDE))
        normed_buf[...] = (normed * gain_ref[...]).astype(LOW)
        keeps[0].start()
        keeps[1].start()

    @pl.when(role == 1)
    def _():
        @pl.loop(0, 3 * width // CHUNK, unroll=2)
        def _(j):
            at = lanes(j * CHUNK, CHUNK)
            saved_buf[:, at] = matmul(normed_buf[...], lead_ref[:, at]).astype(LOW)

        left = lax.broadcasted_iota(jnp.int32, (tokens, 128), 1) < HEAD_SIZE
        zero = jnp.zeros((tokens, 128), LOW)

        @pl.loop(0, HEADS // 8)
        def _(group):
            for pair in range(4):
                at = group * 512 + pair * 128
                query = saved_buf[:, lanes(at, 128)]
                key = saved_buf[:, lanes(width + at, 128)]
                scores_buf[group * 8 + 2 * pair] = matmul_nt(jnp.where(left, query, zero), key)
                scores_buf[group * 8 + 2 * pair + 1] = matmul_nt(jnp.where(left, zero, query), key)

        @pl.loop(0, HEADS // 4)
        def _(group):
            same = same_segment(seg_row_ref[slot])
            for head in range(4):
                at = group * 4 + head
                probs_buf[at] = head_probs(scores_buf[at], same).astype(LOW)

        @pl.loop(0, HEADS // 8)
        def _(group):
            for pair in range(4):
                at = group * 512 + pair * 128
                value = saved_buf[:, lanes(2 * width + at, 128)]
                mixed = jnp.where(
                    left,
                    matmul(probs_buf[group * 8 + 2 * pair], value),
                    matmul(probs_buf[group * 8 + 2 * pair + 1], value),
                )
                saved_buf[:, lanes(3 * width + at, 128)] = mixed.astype(LOW)

        keeps[2].start()

        @pl.loop(0, width // CHUNK)
        def _(j):
            at = lanes(j * CHUNK, CHUNK)
            term = matmul(saved_buf[:, 3 * width :], lead_ref[:, lanes(3 * width + j * CHUNK, CHUNK)])
            out_ref[:, at] = (entry_ref[:, at].astype(WIDE) + term).astype(LOW)

    def feed_forward():
        result_buf[...] = entry_ref[...].astype(WIDE)

        @pl.loop(0, lead_ref.shape[1] // CHUNK, unroll=2)
        def _(j):
            at = lanes(j * CHUNK, CHUNK)
            inner = matmul(normed_buf[...], lead_ref[:, at])
            inner_buf[:, at] = inner
            active = gelu(inner).astype(LOW)
            saved_buf[:, at] = active
            result_buf[...] += matmul(active, down_ref[pl.ds(j * CHUNK, CHUNK), :])

        keeps[2].start()
        keep_inner.start()
        out_ref[...] = result_buf[...].astype(LOW)
        keep_inner.wait()

    if down_ref is not None:
        pl.when(role == 2)(feed_forward)

    @pl.when(role > 0)
    def _():
        for keep in keeps:
            keep.wait()


def pinned(value):
    return pltpu.with_memory_space_constraint(value, pltpu.VMEM)


def far(value):
    return pltpu.with_memory_space_constraint(value, pltpu.HBM)


def forward_stage(spot, table, entries, seg_row, gain, lead, down, kept):
    tokens, width = entries[0].shape
    hidden = lead.shape[1]
    count = len(entries) + (3 if down is None else 4)
    return pl.pallas_call(
        functools.partial(forward_kernel, spot, down is not None, len(entries)),
        out_shape=[jax.ShapeDtypeStruct((tokens, width), LOW)]
        + [jax.ShapeDtypeStruct(k.shape, k.dtype) for k in kept],
        in_specs=[SMEM_SPEC] + [VMEM_SPEC] * count + [HBM_SPEC] * 4,
        out_specs=[VMEM_SPEC] + [HBM_SPEC] * 4,
        scratch_shapes=[
            pltpu.VMEM((tokens, width), LOW),
            pltpu.VMEM((tokens, hidden), LOW),
            pltpu.VMEM((tokens, hidden), WIDE),
            pltpu.VMEM((tokens, width), WIDE),
            pltpu.VMEM((HEADS, tokens, tokens), WIDE),
            pltpu.VMEM((HEADS, tokens, tokens), LOW),
            pltpu.VMEM((tokens, width), LOW),
            pltpu.SemaphoreType.DMA((4,)),
        ],
        input_output_aliases={count + 1 + i: 1 + i for i in range(4)},
        compiler_params=pltpu.CompilerParams(vmem_limit_bytes=18 << 20),
        cost_estimate=pl.CostEstimate(
            flops=4 * tokens * width * hidden, bytes_accessed=20 << 20, transcendentals=0
        ),
        name="forward_stage",
    )(table, *entries, seg_row, gain, pinned(lead), *([pinned(down)] if down is not None else []), *map(far, kept))


def backward_kernel(spot, count, *refs):
    backward_body(spot, refs[0], refs[1 : 1 + count], *refs[1 + count :])


def backward_body(
    spot,
    table_ref,
    candidates,
    seg_row_ref,
    gain_ref,
    lead_ref,
    down_ref,
    entries_ref,
    saved_ref,
    inner_ref,
    nexts_in,
    grads_in,
    gains_in,
    out_ref,
    nexts_ref,
    grads_ref,
    gains_ref,
    saved_buf,
    inner_buf,
    grads_buf,
    mixed_buf,
    gain_buf,
    entry_buf,
    normed_buf,
    scores_buf,
    probs_grad_buf,
    probs_buf,
    scores_grad_buf,
    grad_ref,
    in_sems,
    out_sems,
):
    role, slot = table_ref[spot], table_ref[spot + 1]
    tokens, width = grad_ref.shape
    bring_saved = pltpu.make_async_copy(saved_ref.at[slot], saved_buf, in_sems.at[0])
    bring_inner = pltpu.make_async_copy(inner_ref.at[slot], inner_buf, in_sems.at[1])
    bring_entry = pltpu.make_async_copy(entries_ref.at[slot], entry_buf, in_sems.at[2])
    keep_next = pltpu.make_async_copy(grad_ref, nexts_ref.at[slot], out_sems.at[0])
    keep_grads = pltpu.make_async_copy(grads_buf, grads_ref.at[slot], out_sems.at[1])
    keep_gain = pltpu.make_async_copy(gain_buf, gains_ref.at[slot], out_sems.at[2])

    @pl.when(role == 2)
    def _():
        bring_inner.start()

    @pl.when(role == 1)
    def _():
        bring_saved.start()

    @pl.when(role > 0)
    def _():
        bring_entry.start()
        chosen(table_ref[spot + 2], candidates, grad_ref)
        keep_next.start()
        normed_buf[...] = jnp.zeros_like(normed_buf)

    @pl.when(role == 1)
    def _():
        grads_buf[:, 3 * width :] = grad_ref[...]
        mixed_buf[...] = matmul_nt(grad_ref[...], lead_ref[:, 3 * width :]).astype(LOW)
        bring_saved.wait()
        left = lax.broadcasted_iota(jnp.int32, (tokens, 128), 1) < HEAD_SIZE
        zero = jnp.zeros((tokens, 128), LOW)
        scale = HEAD_SIZE ** (-0.5)

        @pl.loop(0, HEADS // 8)
        def _(group):
            for pair in range(4):
                at = group * 512 + pair * 128
                query = saved_buf[:, lanes(at, 128)]
                key = saved_buf[:, lanes(width + at, 128)]
                value = saved_buf[:, lanes(2 * width + at, 128)]
                grad = mixed_buf[:, lanes(at, 128)]
                for own in (0, 1):
                    mine = lambda v: jnp.where(left, v, zero) if own == 0 else jnp.where(left, zero, v)
                    scores_buf[group * 8 + 2 * pair + own] = matmul_nt(mine(query), key)
                    probs_grad_buf[group * 8 + 2 * pair + own] = matmul_nt(mine(grad), value)

        @pl.loop(0, HEADS // 4)
        def _(group):
            same = same_segment(seg_row_ref[slot])
            for head in range(4):
                at = group * 4 + head
                probs = head_probs(scores_buf[at], same)
                probs_buf[at] = probs.astype(LOW)
                grad_probs = probs_grad_buf[at]
                scores_grad_buf[at] = (
                    probs * (grad_probs - jnp.sum(probs * grad_probs, axis=-1, keepdims=True))
                ).astype(LOW)

        @pl.loop(0, HEADS // 4)
        def _(group):
            for pair in range(2):
                at = group * 256 + pair * 128
                query = saved_buf[:, lanes(at, 128)]
                key = saved_buf[:, lanes(width + at, 128)]
                grad = mixed_buf[:, lanes(at, 128)]
                parts = []
                for own in (0, 1):
                    probs = probs_buf[group * 4 + 2 * pair + own]
                    grad_low = scores_grad_buf[group * 4 + 2 * pair + own]
                    parts.append(
                        (
                            matmul(grad_low, key) * scale,
                            matmul_tn(grad_low, query) * scale,
                            matmul_tn(probs, grad),
                        )
                    )
                for which in range(3):
                    grads_buf[:, lanes(which * width + at, 128)] = jnp.where(
                        left, parts[0][which], parts[1][which]
                    ).astype(LOW)

        @pl.loop(0, 3 * width // CHUNK, unroll=2)
        def _(j):
            at = lanes(j * CHUNK, CHUNK)
            normed_buf[...] += matmul_nt(grads_buf[:, at], lead_ref[:, at])

    @pl.when(role == 2)
    def _():
        bring_inner.wait()

        @pl.loop(0, lead_ref.shape[1] // CHUNK, unroll=2)
        def _(j):
            at = lanes(j * CHUNK, CHUNK)
            grad_active = matmul_nt(grad_ref[...], down_ref[pl.ds(j * CHUNK, CHUNK), :])
            grads = (gelu_slope(inner_buf[:, at]) * grad_active).astype(LOW)
            grads_buf[:, at] = grads
            normed_buf[...] += matmul_nt(grads, lead_ref[:, at])

    @pl.when(role > 0)
    def _():
        keep_grads.start()
        bring_entry.wait()
        grad_normed = normed_buf[...]
        normed, factor = layer_norm(entry_buf[...].astype(WIDE))
        gain_buf[...] = jnp.broadcast_to(
            jnp.sum(grad_normed * normed, axis=0, keepdims=True), gain_buf.shape
        )
        keep_gain.start()
        out_ref[...] = (
            grad_ref[...].astype(WIDE) + norm_back(grad_normed * gain_ref[...], normed, factor)
        ).astype(LOW)
        keep_next.wait()
        keep_grads.wait()
        keep_gain.wait()


def backward_stage(
    spot, table, nexts, seg_row, gain, lead, down, entries, saved, inner, totals
):
    tokens, width = nexts[0].shape
    count = len(nexts)
    hidden = lead.shape[1]
    return pl.pallas_call(
        functools.partial(backward_kernel, spot, count),
        out_shape=[jax.ShapeDtypeStruct((tokens, width), LOW)]
        + [jax.ShapeDtypeStruct(k.shape, k.dtype) for k in totals],
        in_specs=[SMEM_SPEC] + [VMEM_SPEC] * (count + 4) + [HBM_SPEC] * 6,
        out_specs=[VMEM_SPEC] + [HBM_SPEC] * 3,
        scratch_shapes=[
            pltpu.VMEM((tokens, hidden), LOW),
            pltpu.VMEM((tokens, hidden), WIDE),
            pltpu.VMEM((tokens, hidden), LOW),
            pltpu.VMEM((tokens, width), LOW),
            pltpu.VMEM((8, width), WIDE),
            pltpu.VMEM((tokens, width), LOW),
            pltpu.VMEM((tokens, width), WIDE),
            pltpu.VMEM((HEADS, tokens, tokens), WIDE),
            pltpu.VMEM((HEADS, tokens, tokens), WIDE),
            pltpu.VMEM((HEADS, tokens, tokens), LOW),
            pltpu.VMEM((HEADS, tokens, tokens), LOW),
            pltpu.VMEM((tokens, width), LOW),
            pltpu.SemaphoreType.DMA((3,)),
            pltpu.SemaphoreType.DMA((3,)),
        ],
        input_output_aliases={count + 8 + i: 1 + i for i in range(3)},
        compiler_params=pltpu.CompilerParams(vmem_limit_bytes=18 << 20),
        cost_estimate=pl.CostEstimate(
            flops=4 * tokens * width * hidden, bytes_accessed=20 << 20, transcendentals=0
        ),
        name="backward_stage",
    )(
        table,
        *nexts,
        seg_row,
        gain,
        pinned(lead),
        pinned(down),
        far(entries),
        far(saved),
        far(inner),
        *map(far, totals),
    )


def stats_kernel(spot, plan_ref, *refs):
    candidates, (table_ref, readout_ref, peak_ref, total_ref) = refs[:-4], refs[-4:]
    step = pl.program_id(0)

    @pl.when(step == 0)
    def _():
        chosen(plan_ref[spot], candidates, readout_ref)

    logits = matmul_nt(table_ref[...], readout_ref[...])
    own_peak = jnp.max(logits, axis=0, keepdims=True)
    own_total = lambda peak: jnp.sum(jnp.exp(logits - peak), axis=0, keepdims=True)

    @pl.when(step == 0)
    def _():
        peak_ref[...] = own_peak
        total_ref[...] = own_total(own_peak)

    @pl.when(step > 0)
    def _():
        peak = jnp.maximum(peak_ref[...], own_peak)
        total_ref[...] = total_ref[...] * jnp.exp(peak_ref[...] - peak) + own_total(peak)
        peak_ref[...] = peak


def head_stats(spot, plan, readouts, table, tile):
    tokens, emb = readouts[0].shape
    vocab = table.shape[0]
    whole = pl.BlockSpec((1, tokens), lambda i: (0, 0))
    rows = pl.BlockSpec((tokens, emb), lambda i: (0, 0))
    return pl.pallas_call(
        functools.partial(stats_kernel, spot),
        out_shape=[jax.ShapeDtypeStruct((tokens, emb), LOW)]
        + [jax.ShapeDtypeStruct((1, tokens), WIDE)] * 2,
        grid=(vocab // tile,),
        in_specs=[SMEM_SPEC]
        + [rows] * len(readouts)
        + [pl.BlockSpec((tile, emb), lambda i: (i, 0))],
        out_specs=[rows, whole, whole],
        compiler_params=pltpu.CompilerParams(vmem_limit_bytes=32 << 20),
        cost_estimate=pl.CostEstimate(
            flops=2 * tokens * vocab * emb, bytes_accessed=5 << 20, transcendentals=tokens * vocab
        ),
        name="head_stats",
    )(plan, *readouts, far(table))


def head_kernel(spot, table_base_ref, readout_ref, table_ref, logsum_ref, ids_ref, head_ref, grad_ref):
    tile = table_ref.shape[0]
    logits = matmul_nt(table_ref[...], readout_ref[...])
    ids = ids_ref[...] - (table_base_ref[spot] + pl.program_id(0) * tile)
    hits = lax.broadcasted_iota(jnp.int32, logits.shape, 0) == ids
    probs = jnp.exp(logits - logsum_ref[...])
    grads = jnp.where(hits, probs - 1.0, probs).astype(LOW)
    head = matmul(grads, readout_ref[...])
    unit = tile // 4
    for shard in range(4):
        head_ref[shard, :unit] = head[shard * unit : (shard + 1) * unit].astype(LOW)
    term = matmul_tn(grads, table_ref[...])

    @pl.when(pl.program_id(0) == 0)
    def _():
        grad_ref[...] = term

    @pl.when(pl.program_id(0) > 0)
    def _():
        grad_ref[...] += term


def head_grads(spot, base, readout, table, logsum, ids):
    tokens, emb = readout.shape
    vocab = table.shape[0]
    row = pl.BlockSpec((1, tokens), lambda i: (0, 0))
    whole = pl.BlockSpec((tokens, emb), lambda i: (0, 0))
    part = pl.BlockSpec((vocab // 4, emb), lambda i: (i, 0))
    return pl.pallas_call(
        functools.partial(head_kernel, spot),
        out_shape=[
            pltpu.HBM((16, 512, emb), LOW),
            jax.ShapeDtypeStruct((tokens, emb), WIDE),
        ],
        grid=(4,),
        in_specs=[SMEM_SPEC, whole, part, row, row],
        out_specs=[pl.BlockSpec((4, 512, emb), lambda i: (i, 0, 0)), whole],
        compiler_params=pltpu.CompilerParams(vmem_limit_bytes=32 << 20),
        cost_estimate=pl.CostEstimate(
            flops=6 * tokens * vocab * emb, bytes_accessed=9 << 20, transcendentals=tokens * vocab
        ),
        name="head_grads",
    )(base, readout, far(table), logsum, ids)


def pair_kernel(former_ref, latter_ref, out_ref):
    rows = out_ref.shape[0]
    out_ref[...] = former_ref[:rows].astype(WIDE) + latter_ref[:rows].astype(WIDE)


def pair_sum(former, latter, rows):
    return pl.pallas_call(
        pair_kernel,
        out_shape=jax.ShapeDtypeStruct((rows, former.shape[1]), WIDE),
        in_specs=[VMEM_SPEC] * 2,
        out_specs=VMEM_SPEC,
        compiler_params=pltpu.CompilerParams(vmem_limit_bytes=8 << 20),
        name="pair_sum",
    )(former, latter)


def lookup_kernel(ids_ref, table_ref, noise_ref, out_ref, total_ref, low_ref):
    step = pl.program_id(0)
    parts, tile = table_ref.shape
    tokens = ids_ref.shape[1]
    blocks = tile // 128

    @pl.when(step == 0)
    def _():
        lane = jnp.bitwise_and(ids_ref[...], 127)
        hits = lax.broadcasted_iota(jnp.int32, (128, tokens), 0) == lane
        low_ref[...] = jnp.where(hits, 1.0, 0.0).astype(LOW)
        total_ref[...] = noise_ref[...].astype(WIDE)

    stacked = jnp.concatenate(
        [table_ref[:, block * 128 : (block + 1) * 128] for block in range(blocks)]
    )
    found = matmul(stacked, low_ref[...])
    own = jnp.right_shift(ids_ref[...], 7) - step * blocks
    total = jnp.zeros_like(total_ref)
    for block in range(blocks):
        total = jnp.where(own == block, found[block * parts : (block + 1) * parts], total)
    total_ref[...] += total

    @pl.when(step == pl.num_programs(0) - 1)
    def _():
        out_ref[...] = total_ref[...].astype(LOW)


def lookup(ids, table, noise, tile):
    parts, vocab = table.shape
    tokens = ids.shape[1]
    whole = pl.BlockSpec((parts, tokens), lambda i: (0, 0))
    return pl.pallas_call(
        lookup_kernel,
        out_shape=jax.ShapeDtypeStruct((parts, tokens), LOW),
        grid=(vocab // tile,),
        in_specs=[
            pl.BlockSpec((1, tokens), lambda i: (0, 0)),
            pl.BlockSpec((parts, tile), lambda i: (0, i)),
            whole,
        ],
        out_specs=whole,
        scratch_shapes=[pltpu.VMEM((parts, tokens), WIDE), pltpu.VMEM((128, tokens), LOW)],
        compiler_params=pltpu.CompilerParams(vmem_limit_bytes=32 << 20),
        cost_estimate=pl.CostEstimate(
            flops=2 * 128 * vocab * tokens, bytes_accessed=4 << 20, transcendentals=0
        ),
        name="lookup",
    )(ids, far(table), noise)


def lead_grad_kernel(where_ref, normed_ref, mixed_ref, grads_ref, out_ref, turned_ref):
    role, half, spot = where_ref[0], where_ref[1], where_ref[2]
    step = pl.program_id(0)
    width = normed_ref.shape[1]
    steps = pl.num_programs(0)
    use_mixed = jnp.logical_and(role == 1, half == 1)

    @pl.when(step == 0)
    def _():
        turned_ref[...] = normed_ref[...].T

    @pl.when(jnp.logical_and(step == steps // 2, use_mixed))
    def _():
        turned_ref[...] = mixed_ref[...].T

    result = matmul(turned_ref[...], grads_ref[...]).astype(LOW)
    unit = width // 16
    for x in range(4):
        for y in range(4):
            part = result[(4 * x + y) * unit : (4 * x + y + 1) * unit]

            @pl.when(half == 0)
            def _():
                out_ref[(x - spot + 4) % 4, y * unit : (y + 1) * unit, :] = part

            @pl.when(half == 1)
            def _():
                out_ref[(y - spot + 4) % 4, x * unit : (x + 1) * unit, :] = part


def lead_grad(where, normed, saved, grads):
    tokens, width = normed.shape
    tile = 512
    return pl.pallas_call(
        lead_grad_kernel,
        out_shape=jax.ShapeDtypeStruct((4, width // 4, 2 * width), LOW),
        grid_spec=pltpu.PrefetchScalarGridSpec(
            num_scalar_prefetch=1,
            grid=(2 * width // tile,),
            in_specs=[
                pl.BlockSpec((tokens, width), lambda i, where: (0, 0)),
                pl.BlockSpec((tokens, width), lambda i, where: (0, 3)),
                pl.BlockSpec((tokens, tile), lambda i, where: (0, where[1] * (2 * width // tile) + i)),
            ],
            out_specs=pl.BlockSpec((4, width // 4, tile), lambda i, where: (0, 0, i)),
            scratch_shapes=[pltpu.VMEM((width, tokens), LOW)],
        ),
        compiler_params=pltpu.CompilerParams(vmem_limit_bytes=24 << 20),
        cost_estimate=pl.CostEstimate(
            flops=4 * tokens * width * width, bytes_accessed=8 << 20, transcendentals=0
        ),
        name="lead_grad",
    )(where, far(normed), far(saved), far(grads))


def down_grad_kernel(where_ref, saved_ref, nexts_ref, out_ref, buf_ref, sem):
    role, half, spot = where_ref[0], where_ref[1], where_ref[2]
    at = pl.program_id(0)
    unit = saved_ref.shape[1] // 4

    @pl.when(role == 2)
    def _():
        result = matmul_tn(saved_ref[...], nexts_ref[...]).astype(LOW)

        @pl.when(half == 0)
        def _():
            buf_ref[(at - spot + 4) % 4] = result

        @pl.when(half == 1)
        def _():
            for y in range(4):
                buf_ref[
                    (y - spot + 4) % 4, pl.ds(pl.multiple_of(at * unit, unit), unit), :
                ] = result[y * unit : (y + 1) * unit]

        @pl.when(at == pl.num_programs(0) - 1)
        def _():
            copy = pltpu.make_async_copy(buf_ref, out_ref, sem)
            copy.start()
            copy.wait()


def down_grad(where, saved, nexts):
    tokens, hidden = saved.shape
    width = nexts.shape[1]
    rows = hidden // 8
    live = lambda where: jnp.where(where[0] == 2, 1, 0)
    return pl.pallas_call(
        down_grad_kernel,
        out_shape=pltpu.HBM((4, rows, width), LOW),
        grid_spec=pltpu.PrefetchScalarGridSpec(
            num_scalar_prefetch=1,
            grid=(4,),
            in_specs=[
                pl.BlockSpec((tokens, rows), lambda i, where: (0, (where[1] * 4 + i) * live(where))),
                pl.BlockSpec((tokens, width), lambda i, where: (0, 0)),
            ],
            out_specs=HBM_SPEC,
            scratch_shapes=[pltpu.VMEM((4, rows, width), LOW), pltpu.SemaphoreType.DMA],
        ),
        compiler_params=pltpu.CompilerParams(vmem_limit_bytes=24 << 20),
        cost_estimate=pl.CostEstimate(
            flops=2 * tokens * width * hidden // 2, bytes_accessed=8 << 20, transcendentals=0
        ),
        name="down_grad",
    )(where, far(saved), far(nexts))


def upper_kernel(where_ref, *refs):
    out_ref, sems = refs[4], refs[5]
    rows = refs[0].shape[0]
    copies = []
    for at, part in enumerate(refs[:4]):
        place = (where_ref[0] - at + 4) % 4
        copies.append(
            pltpu.make_async_copy(
                part, out_ref.at[pl.ds(pl.multiple_of(place * rows, rows), rows), :], sems.at[at]
            )
        )
        copies[-1].start()
    for copy in copies:
        copy.wait()


def upper_half(where, parts):
    rows, width = parts[0].shape
    return pl.pallas_call(
        upper_kernel,
        out_shape=pltpu.HBM((4 * rows, width), LOW),
        in_specs=[SMEM_SPEC] + [HBM_SPEC] * 4,
        out_specs=HBM_SPEC,
        scratch_shapes=[pltpu.SemaphoreType.DMA((4,))],
        compiler_params=pltpu.CompilerParams(vmem_limit_bytes=4 << 20),
        name="upper_half",
    )(where, *map(far, parts))


def hold_down_kernel(where_ref, mine_ref, other_ref, own_ref, out_ref, sems):
    rows = mine_ref.shape[0]
    core = where_ref[1]
    spot = lambda at: out_ref.at[pl.ds(pl.multiple_of(at * rows, rows), rows), :]
    copies = [
        pltpu.make_async_copy(mine_ref, spot(core), sems.at[0]),
        pltpu.make_async_copy(other_ref, spot(1 - core), sems.at[1]),
        pltpu.make_async_copy(own_ref, out_ref.at[pl.ds(2 * rows, 2 * rows), :], sems.at[2]),
    ]
    for copy in copies:
        copy.start()
    for copy in copies:
        copy.wait()


def hold_down(where, mine, other, own):
    rows, width = mine.shape
    return pl.pallas_call(
        hold_down_kernel,
        out_shape=pltpu.VMEM((4 * rows, width), LOW),
        in_specs=[SMEM_SPEC] + [HBM_SPEC] * 3,
        out_specs=VMEM_SPEC,
        scratch_shapes=[pltpu.SemaphoreType.DMA((3,))],
        compiler_params=pltpu.CompilerParams(vmem_limit_bytes=4 << 20),
        name="hold_down",
    )(where, far(mine), far(other), far(own))


def noise_kernel(spot, plan_ref, ids_ref, *refs):
    candidates, (packed_ref, noise_ref, buf_ref) = refs[:-3], refs[-3:]
    parts = noise_ref.shape[0]
    chosen(plan_ref[spot], candidates, buf_ref)
    packed_ref[:parts] = buf_ref[...]
    noise_ref[...] = buf_ref[...].astype(WIDE)
    ids = ids_ref[...]
    high = jnp.right_shift(ids, 8).astype(WIDE)
    low = jnp.bitwise_and(ids, 255).astype(WIDE)
    at = lax.broadcasted_iota(jnp.int32, (16, ids.shape[1]), 0)
    split = jnp.where(at == 0, high, jnp.where(at == 1, low, 0.0))
    packed_ref[parts:] = split.astype(LOW)


def noise_pack(spot, plan, ids, candidates):
    parts, tokens = candidates[0].shape
    return pl.pallas_call(
        functools.partial(noise_kernel, spot),
        out_shape=[
            jax.ShapeDtypeStruct((parts + 16, tokens), LOW),
            jax.ShapeDtypeStruct((parts, tokens), WIDE),
        ],
        in_specs=[SMEM_SPEC] + [VMEM_SPEC] * (1 + len(candidates)),
        out_specs=[VMEM_SPEC] * 2,
        scratch_shapes=[pltpu.VMEM((parts, tokens), LOW)],
        compiler_params=pltpu.CompilerParams(vmem_limit_bytes=8 << 20),
        name="noise_pack",
    )(plan, ids, *candidates)


def embed_kernel(base_ref, mine_ref, other_ref, out_ref, total_ref):
    step = pl.program_id(0)
    steps = pl.num_programs(0)
    parts = out_ref.shape[0]
    blocks = total_ref.shape[0] // parts

    def add(gathered_ref):
        count, _, tokens = gathered_ref.shape
        term = None
        for at in range(count):
            split = gathered_ref[at, parts : parts + 16].astype(WIDE)
            ids = (split[0:1] * 256.0 + split[1:2]).astype(jnp.int32) - base_ref[0]
            lane = jnp.bitwise_and(ids, 127)
            hits = lax.broadcasted_iota(jnp.int32, (128, tokens), 0) == lane
            hits = jnp.where(hits, 1.0, 0.0).astype(LOW)
            own = jnp.right_shift(ids, 7)
            grads = gathered_ref[at, :parts]
            masked = jnp.concatenate(
                [grads * jnp.where(own == block, 1.0, 0.0).astype(LOW) for block in range(blocks)]
            )
            part = matmul_nt(masked, hits)
            term = part if term is None else term + part

        @pl.when(step == 0)
        def _():
            total_ref[...] = term

        @pl.when(step > 0)
        def _():
            total_ref[...] += term

    pl.when(step < steps // 2)(lambda: add(mine_ref))
    pl.when(step >= steps // 2)(lambda: add(other_ref))

    @pl.when(step == steps - 1)
    def _():
        rows = out_ref.shape[1]
        for block in range(blocks):
            size = min(128, rows - block * 128)
            out_ref[:, block * 128 : block * 128 + size] = total_ref[
                block * parts : (block + 1) * parts, :size
            ]


def embed_sum(base, mine, other, parts, rows):
    count, deep, tokens = mine.shape
    step = 4
    half = count // step
    blocks = -(-rows // 128)
    return pl.pallas_call(
        embed_kernel,
        out_shape=jax.ShapeDtypeStruct((parts, rows), WIDE),
        grid=(2 * half,),
        in_specs=[
            SMEM_SPEC,
            pl.BlockSpec((step, deep, tokens), lambda i: (jnp.minimum(i, half - 1), 0, 0)),
            pl.BlockSpec((step, deep, tokens), lambda i: (jnp.maximum(i - half, 0), 0, 0)),
        ],
        out_specs=pl.BlockSpec((parts, rows), lambda i: (0, 0)),
        scratch_shapes=[pltpu.VMEM((blocks * parts, 128), WIDE)],
        compiler_params=pltpu.CompilerParams(vmem_limit_bytes=32 << 20),
        cost_estimate=pl.CostEstimate(
            flops=4 * count * tokens * parts * rows, bytes_accessed=3 << 20, transcendentals=0
        ),
        name="embed_sum",
    )(base, mine, other)


def empty(*kinds):
    return pl.pallas_call(
        lambda *refs: None,
        out_shape=[pltpu.HBM(shape, dtype) for shape, dtype in kinds],
        out_specs=[HBM_SPEC] * len(kinds),
        compiler_params=pltpu.CompilerParams(vmem_limit_bytes=1 << 20),
        name="empty",
    )()


ROW_LEN = 128
SEC, GRP, NX, NY = 4, 2, 4, 4
ALL = ("section", "group", "row")
TURNS = (1, 3, 2)


def route(value, target_of):
    number = lambda s, g, x, y: (s * GRP + g) * NX * NY + x * NY + y
    pairs = []
    for at in itertools.product(range(SEC), range(GRP), range(NX), range(NY)):
        target = target_of(*at)
        if target is not None:
            pairs.append((number(*at), number(*target)))
    return lax.ppermute(value, ALL, pairs)


def link(value, source, target):
    return route(value, lambda s, g, x, y: (target, g, x, y) if s == source else None)


def turn(value, by):
    return route(value, lambda s, g, x, y: ((s + by) % SEC, g, x, y))


def swap_cores(value, sections=range(SEC)):
    return route(value, lambda s, g, x, y: (s, 1 - g, x, y) if s in sections else None)


def plane_route(value, by, first, sections=range(SEC)):
    def target_of(s, g, x, y):
        if s not in sections:
            return None
        if (g == 0) == first:
            return (s, g, (x + by) % NX, y)
        return (s, g, x, (y + by) % NY)

    return route(value, target_of)


def after(value, earlier):
    return lax.optimization_barrier((value, earlier))[0]


def row_block(values, block, count):
    size = values.shape[0] // count
    return lax.dynamic_slice_in_dim(values, block * size, size, 0)


def plane_first(mine, got, sections=range(SEC)):
    piece = lambda by: mine[by] if got is None else (mine[by].astype(WIDE) + got[by].astype(WIDE))
    pieces = [piece(by).astype(LOW) for by in range(4)]
    return (pieces, [plane_route(pieces[by], by, True, sections) for by in TURNS])


def plane_sum(pieces):
    total = pieces[0].astype(WIDE)
    for piece in pieces[1:]:
        total = total + piece.astype(WIDE)
    return total.astype(LOW)


def plane_second(pieces, arrived, second, sections=range(SEC)):
    total = plane_sum([pieces[0]] + arrived)
    return [row_block(total, second, 4)] + [
        plane_route(row_block(total, (second + by) % 4, 4), by, False, sections) for by in TURNS
    ]


def group_exchange(values, first):
    number = lambda s, g, x, y: (s * GRP + g) * NX * NY + x * NY + y
    groups = []
    for s in range(SEC):
        for g in range(GRP):
            along_x = (g == 0) == first
            for at in range(4):
                groups.append(
                    [number(s, g, i, at) if along_x else number(s, g, at, i) for i in range(4)]
                )
    return lax.all_to_all(values, ALL, 0, 0, axis_index_groups=groups, tiled=True)


def section_exchange(values):
    return lax.all_to_all(values, "section", 0, 0, tiled=True)


def plans(micro, vocab_part):
    last = SEC - 1
    steps = micro + 2 * last
    table = np.zeros((SEC, 6 * steps + 2), np.int32)
    for s in range(SEC):
        for way in range(2):
            depth = s if way == 0 else last - s
            for step in range(steps):
                at = step - 2 * depth
                if 0 <= at < micro:
                    sources = ([0] if step < micro else []) + [
                        d + 1 for d in range(last) if 0 <= step - 2 - 2 * d < micro
                    ]
                    spot = 3 * (way * steps + step)
                    table[s, spot : spot + 3] = (1 + s % 2, at, sources.index(depth))
        table[s, 6 * steps :] = (s * vocab_part, s)
    return table


def local(
    token_ids,
    segment_ids,
    noise_input,
    embed_table,
    input_proj,
    norm_gain,
    lead_weight,
    down_weight,
    final_gain,
    readout_proj,
    head_table,
):
    section = lax.axis_index("section")
    core = lax.axis_index("group")
    row = lax.axis_index("row")
    x_at, y_at = row // NY, row % NY
    first_at = jnp.where(core == 0, x_at, y_at)
    micro, _, tokens = token_ids.shape
    width = input_proj.shape[1]
    hidden = lead_weight.shape[2]
    half_rows = down_weight.shape[1]
    emb_part = input_proj.shape[0]
    vocab_part, emb = head_table.shape
    vocab = embed_table.shape[0]
    all_tokens = micro * tokens
    last = SEC - 1
    gain_half = norm_gain.astype(WIDE)
    lead = lead_weight[0]
    own_down = down_weight[0]
    seg_row = segment_ids
    flat_ids = token_ids.reshape(-1)

    plan = plans(micro, vocab_part)
    steps = micro + 2 * last
    table = lax.dynamic_index_in_dim(jnp.asarray(plan), section, 0, False)
    where_start = jnp.stack((first_at, core)).astype(jnp.int32)
    to_first = lambda v: [v] + [link(v, s, 0) for s in range(1, SEC)]
    eighth = row_block(row_block(own_down, core, 2), first_at, 4)
    eighth = jnp.where(section == 1, link(eighth, 0, 1), link(eighth, 2, 3))
    noise = noise_input[:, 0].transpose(2, 0, 1).reshape(emb_part, -1)
    own_embedded = lookup(flat_ids[None], embed_table.T, noise, 3200)
    inputs = to_first(input_proj)
    input_full = jnp.concatenate(inputs)
    embedded = jnp.concatenate(
        [own_embedded] + [link(own_embedded, s, 0) for s in range(1, SEC)]
    )
    first_in = matmul_tn(embedded, input_full).astype(LOW).reshape(micro, tokens, width)
    held_lead = hold(lead)
    eighth = after(eighth, own_embedded)
    eighths = [eighth] + [plane_route(eighth, by, True) for by in (1, 2, 3)]
    upper = upper_half(where_start, [after(part, first_in) for part in eighths])
    held_down = hold_down(where_start, upper, swap_cores(upper), own_down)

    kept = empty(
        ((micro, tokens, width), LOW),
        ((micro, tokens, width), LOW),
        ((micro, tokens, hidden), LOW),
        ((micro, tokens, hidden), WIDE),
    )

    def sources(first, step, hops, order):
        arrived = [hops[step - 2, s] for s in order if (step - 2, s) in hops]
        return ([first[step]] if step < micro else []) + arrived

    outs, hops = [], {}
    for step in range(steps):
        out, *kept = forward_stage(
            3 * step,
            table,
            sources(first_in, step, hops, range(SEC)),
            seg_row,
            gain_half,
            held_lead,
            held_down if step > 1 else None,
            kept,
        )
        outs.append(out)
        for s in range(last):
            if 0 <= step - 2 * s < micro:
                ready = after(out, hops[step - 1, s]) if (step - 1, s) in hops else out
                hops[step, s] = link(ready, s, s + 1)
        if step == 2:
            readout_own = after(readout_proj.T, out)
            readout_full = jnp.concatenate(
                [link(readout_own, s, last) for s in range(last)] + [readout_own]
            )
    entries, normeds, saved, inner = kept

    final_rows = jnp.concatenate(outs[2 * last :]).astype(WIDE)
    normed_f, factor_f = layer_norm(final_rows)
    gain_f = final_gain.astype(WIDE)
    final_low = (normed_f * gain_f).astype(LOW)
    readout = matmul_nt(final_low, readout_full).astype(LOW)
    sent = [link(readout, last, s) for s in range(last)]
    readout, peak, total = head_stats(6 * steps + 1, table, sent + [readout], head_table, 2000)
    stats = jnp.concatenate((peak, total))
    all_stats = section_exchange(jnp.tile(stats, (SEC, 1))).reshape(SEC, 2, all_tokens)
    peak = jnp.max(all_stats[:, 0], axis=0)
    total = jnp.sum(all_stats[:, 1] * jnp.exp(all_stats[:, 0] - peak), axis=0)
    logsum = (peak + jnp.log(total))[None]
    head_grad, grad_readout = head_grads(
        6 * steps, table, readout, head_table, logsum, flat_ids[None]
    )
    grad_low = grad_readout.astype(LOW)
    for s in range(last):
        grad_readout = grad_readout + link(grad_low, s, last).astype(WIDE)
    grad_readout = grad_readout.astype(LOW)
    head_grad = lax.psum_scatter(head_grad, "row", scatter_dimension=0)
    readout_grad = matmul_tn(final_low, grad_readout)
    grad_final = matmul(grad_readout, readout_full)
    final_gain_grad = jnp.sum(grad_final * normed_f, axis=0)
    last_grads = norm_back(grad_final * gain_f, normed_f, factor_f).astype(LOW)
    last_grads = last_grads.reshape(micro, tokens, width)

    totals = empty(
        ((micro, tokens, width), LOW),
        ((micro, tokens, hidden), LOW),
        ((micro, 8, width), WIDE),
    )
    outs, hops = [], {}
    for step in range(steps):
        out, *totals = backward_stage(
            3 * (steps + step),
            table,
            sources(last_grads, step, hops, range(SEC - 1, -1, -1)),
            seg_row,
            gain_half,
            held_lead,
            held_down,
            entries,
            saved,
            inner,
            totals,
        )
        outs.append(out)
        for s in range(1, SEC):
            if 0 <= step - 2 * (last - s) < micro:
                ready = after(out, hops[step - 1, s]) if (step - 1, s) in hops else out
                hops[step, s] = link(ready, s, s - 1)
    section, core, row = lax.optimization_barrier((section, core, row, out))[:3]
    x_at, y_at = row // NY, row % NY
    first_at, second_at = jnp.where(core == 0, x_at, y_at), jnp.where(core == 0, y_at, x_at)
    is_mlp = section % 2 == 1

    first_grads = jnp.concatenate(outs[2 * last :])
    noise_grad = matmul_nt(input_full, first_grads).astype(LOW)
    pieces = noise_grad.reshape(SEC, emb_part, all_tokens)
    sent = [link(pieces[s], 0, s) for s in range(1, SEC)]

    grad_nexts, grads, gain_grads = totals
    gain_grad = jnp.sum(gain_grads[:, 0], axis=0)
    flat = lambda v: v.reshape(all_tokens, v.shape[-1])
    grads = after(grads, head_grad)
    normed, grad_nexts, grads, saved = flat(normeds), flat(grad_nexts), flat(grads), flat(saved)
    odd = (1, 3)
    role = jnp.where(is_mlp, 2, 1)
    where_other = jnp.stack((role, 1 - core, second_at)).astype(jnp.int32)
    where_mine = jnp.stack((role, core, first_at)).astype(jnp.int32)
    both = lambda mine, other: jnp.where(
        core == 0,
        jnp.concatenate((mine, other), axis=1),
        jnp.concatenate((other, mine), axis=1),
    )
    down_got = swap_cores(down_grad(where_other, saved, grad_nexts), odd)
    down_mine = down_grad(where_mine, saved, grad_nexts)
    lead_got = swap_cores(lead_grad(after(where_other, down_mine), normed, saved, grads))
    packed, noise_wide = noise_pack(6 * steps + 1, table, flat_ids[None], [pieces[0]] + sent)
    down_first = plane_first(down_mine, down_got, odd)
    lead_mine = lead_grad(after(where_mine, (packed, down_first[0])), normed, saved, grads)
    lead_first = plane_first(lead_mine, lead_got)

    input_grad = matmul(embedded, first_grads).reshape(SEC, 16, 4, width)
    input_grad = input_grad.transpose(1, 0, 2, 3).reshape(16, 16, width)
    readout_grad = readout_grad.reshape(16, 16, width)
    vectors = jnp.concatenate(
        (
            gain_grad.reshape(16, 64),
            final_gain_grad.reshape(SEC, 16, 16).transpose(1, 0, 2).reshape(16, 64),
            jnp.zeros((16, width - 128), WIDE),
        ),
        axis=1,
    )
    small = jnp.concatenate(
        (
            jnp.where(section == 0, input_grad, readout_grad),
            vectors[:, None],
            jnp.zeros((16, 15, width), WIDE),
        ),
        axis=1,
    ).astype(LOW)
    small = after(small, lead_first[0])
    half_of = lambda which: lax.dynamic_slice_in_dim(small, which * (width // 2), width // 2, 2)
    small = half_of(core).astype(WIDE) + swap_cores(half_of(1 - core)).astype(WIDE)
    small = small.astype(LOW).reshape(NX, NY, 32, width // 2)
    small = jnp.where(core == 0, small, small.swapaxes(0, 1)).reshape(4, NY * 32, width // 2)
    deep = emb_part + 16

    def exchange(blocks, packed, first):
        rows = blocks.shape[1]
        everywhere = jnp.broadcast_to(packed, (4,) + packed.shape)
        got = group_exchange(jnp.concatenate((blocks, everywhere), axis=1), first)
        return jnp.sum(got[:, :rows].astype(WIDE), axis=0).astype(LOW), got[:, rows:]

    small, packed = exchange(small, packed, True)
    small, packed = exchange(
        small.reshape(4, 32, width // 2), packed.reshape(4 * deep, all_tokens), False
    )
    packed = packed.reshape(16, deep, all_tokens)
    packed_other = swap_cores(packed)
    small = both(small, swap_cores(small))
    down_second = plane_second(after(down_first[0], packed), down_first[1], second_at, odd)
    lead_second = plane_second(after(lead_first[0], packed), lead_first[1], second_at)
    embed_grad = embed_sum(
        (row * (vocab // 16)).reshape(1), packed, packed_other, emb_part, vocab // 16
    )
    down_part = plane_sum(after(down_second, embed_grad))
    lead_part = plane_sum(after(lead_second, embed_grad))
    noise_out = noise_wide.reshape(emb_part, micro, tokens).transpose(1, 2, 0)
    lead_out = both(lead_part, swap_cores(lead_part)).astype(WIDE)

    def first_target(s, g, x, y):
        if s % 2 == 0:
            return None
        return (s - 1, 0, x, y) if g == 0 else (s, 0, x, y)

    def second_target(s, g, x, y):
        return (s - 1, 1, x, y) if s % 2 == 1 and g == 0 else None

    to_core_0 = route(down_part, first_target)
    to_core_1 = route(down_part, second_target)
    down_out = jnp.where(
        core == 0, to_core_0, jnp.where(is_mlp, down_part, to_core_1)
    ).astype(WIDE)

    gain_out = small[16, :64].astype(WIDE)
    input_rows = small[:16].reshape(SEC, 4, width)
    readout_rows = small[:16].reshape(64, SEC, 64)
    final_rows = small[16, 64:128].reshape(SEC, 16)

    finals = jnp.pad(final_rows, ((0, 0), (0, width - 16)))[:, None]
    mine = jnp.where(
        section == 0, input_rows, readout_rows.transpose(1, 0, 2).reshape(SEC, 4, width)
    )
    shared = section_exchange(
        jnp.concatenate((mine, finals, jnp.zeros((SEC, 3, width), LOW)), axis=1)
    )
    input_out = shared[0, :4]
    readout_out = shared[last, :4].reshape(64, 64)
    final_out = shared[last, 4, :16]

    head_out = pair_sum(head_grad, swap_cores(head_grad), vocab_part // (NX * NY))
    return (
        noise_out[:, None],
        embed_grad.T,
        input_out.astype(WIDE),
        gain_out[None],
        lead_out[None],
        down_out[None],
        final_out.astype(WIDE),
        readout_out.astype(WIDE),
        head_out,
    )


def solution(mesh):
    in_specs = (
        P(None, ("group", "row"), None),
        P(None, ("group", "row"), None),
        P(None, ("group", "row"), None, "section"),
        P(None, "section"),
        P("section", None),
        P("section", None),
        P("section", None, None),
        P("section", None, None),
        P(),
        P(None, "section"),
        P("section", None),
    )
    out_specs = (
        P(None, ("group", "row"), None, "section"),
        P("row", "section"),
        P(("section", "row"), None),
        P("section", "row"),
        P("section", "row", None),
        P("section", "row", None),
        P(("section", "row")),
        P("row", "section"),
        P(("section", "row"), None),
    )
    return jax.shard_map(local, mesh=mesh, in_specs=in_specs, out_specs=out_specs, check_vma=False)
```

```python
import functools
import itertools

import jax
import jax.numpy as jnp
import numpy as np
from jax import lax
from jax.experimental import pallas as pl
from jax.experimental.pallas import tpu as pltpu
from jax.sharding import PartitionSpec as P

HEADS = 16
HEAD_SIZE = 64
LOW = jnp.bfloat16
WIDE = jnp.float32
EPSILON = 1e-05
MASKED = -1000000000.0
CHUNK = 512
GELU_A = 0.7978845608028654
GELU_B = 0.044715
HBM_SPEC = pl.BlockSpec(memory_space=pltpu.HBM)
VMEM_SPEC = pl.BlockSpec(memory_space=pltpu.VMEM)
SMEM_SPEC = pl.BlockSpec(memory_space=pltpu.SMEM)


def matmul(former, latter):
    return jnp.dot(former, latter, preferred_element_type=WIDE)


def matmul_nt(former, latter):
    return lax.dot_general(
        former, latter, (((1,), (1,)), ((), ())), preferred_element_type=WIDE
    )


def matmul_tn(former, latter):
    return lax.dot_general(
        former, latter, (((0,), (0,)), ((), ())), preferred_element_type=WIDE
    )


def layer_norm(values):
    centre = jnp.mean(values, axis=-1, keepdims=True)
    centred = values - centre
    variance = jnp.mean(centred * centred, axis=-1, keepdims=True)
    factor = lax.rsqrt(variance + EPSILON)
    return (centred * factor, factor)


def norm_back(grad_normed, normed, factor):
    first_mean = jnp.mean(grad_normed, axis=-1, keepdims=True)
    second_mean = jnp.mean(grad_normed * normed, axis=-1, keepdims=True)
    return factor * (grad_normed - first_mean - normed * second_mean)


def gelu(v):
    return 0.5 * v * (1.0 + jnp.tanh(GELU_A * (v + GELU_B * (v * v * v))))


def gelu_slope(v):
    square = v * v
    bend = jnp.tanh(GELU_A * (v + GELU_B * (square * v)))
    return 0.5 * (1.0 + bend) + 0.5 * v * (1.0 - bend * bend) * (
        GELU_A * (1.0 + 3.0 * GELU_B * square)
    )


def head_probs(scores, same):
    scores = jnp.where(same, scores * HEAD_SIZE ** (-0.5), MASKED)
    expo = jnp.exp(scores - jnp.max(scores, axis=-1, keepdims=True))
    return expo * (1.0 / jnp.sum(expo, axis=-1, keepdims=True))


def same_segment(row):
    across = jnp.broadcast_to(row.astype(WIDE), (row.shape[1], row.shape[1]))
    return across.T == across


def lanes(at, size):
    return pl.ds(pl.multiple_of(at, 128), size)


def hold_kernel(source_ref, held_ref, sem):
    copy = pltpu.make_async_copy(source_ref, held_ref, sem)
    copy.start()
    copy.wait()


def hold(value):
    return pl.pallas_call(
        hold_kernel,
        out_shape=pltpu.VMEM(value.shape, value.dtype),
        in_specs=[HBM_SPEC],
        out_specs=VMEM_SPEC,
        scratch_shapes=[pltpu.SemaphoreType.DMA],
        compiler_params=pltpu.CompilerParams(vmem_limit_bytes=4 << 20),
        name="hold",
    )(far(value))


def chosen(choice, candidates, buffer):
    for at, candidate in enumerate(candidates):

        @pl.when(choice == at)
        def _():
            buffer[...] = candidate[...]


def forward_kernel(spot, with_down, count, *refs):
    table_ref, candidates, refs = refs[0], refs[1 : 1 + count], refs[1 + count :]
    if not with_down:
        refs = refs[:3] + (None,) + refs[3:]
    forward_body(spot, table_ref, candidates, *refs)


def forward_body(
    spot,
    table_ref,
    candidates,
    seg_row_ref,
    gain_ref,
    lead_ref,
    down_ref,
    entries_in,
    normeds_in,
    saved_in,
    inner_in,
    out_ref,
    entries_ref,
    normeds_ref,
    saved_ref,
    inner_ref,
    normed_buf,
    saved_buf,
    inner_buf,
    result_buf,
    scores_buf,
    probs_buf,
    entry_ref,
    out_sems,
):
    role, slot = table_ref[spot], table_ref[spot + 1]
    tokens, width = entry_ref.shape
    keeps = [
        pltpu.make_async_copy(entry_ref, entries_ref.at[slot], out_sems.at[0]),
        pltpu.make_async_copy(normed_buf, normeds_ref.at[slot], out_sems.at[1]),
        pltpu.make_async_copy(saved_buf, saved_ref.at[slot], out_sems.at[2]),
    ]
    keep_inner = pltpu.make_async_copy(inner_buf, inner_ref.at[slot], out_sems.at[3])

    @pl.when(role > 0)
    def _():
        chosen(table_ref[spot + 2], candidates, entry_ref)
        normed, _ = layer_norm(entry_ref[...].astype(WIDE))
        normed_buf[...] = (normed * gain_ref[...]).astype(LOW)
        keeps[0].start()
        keeps[1].start()

    @pl.when(role == 1)
    def _():
        @pl.loop(0, 3 * width // CHUNK, unroll=2)
        def _(j):
            at = lanes(j * CHUNK, CHUNK)
            saved_buf[:, at] = matmul(normed_buf[...], lead_ref[:, at]).astype(LOW)

        left = lax.broadcasted_iota(jnp.int32, (tokens, 128), 1) < HEAD_SIZE
        zero = jnp.zeros((tokens, 128), LOW)

        @pl.loop(0, HEADS // 8)
        def _(group):
            for pair in range(4):
                at = group * 512 + pair * 128
                query = saved_buf[:, lanes(at, 128)]
                key = saved_buf[:, lanes(width + at, 128)]
                scores_buf[group * 8 + 2 * pair] = matmul_nt(jnp.where(left, query, zero), key)
                scores_buf[group * 8 + 2 * pair + 1] = matmul_nt(jnp.where(left, zero, query), key)

        @pl.loop(0, HEADS // 4)
        def _(group):
            same = same_segment(seg_row_ref[slot])
            for head in range(4):
                at = group * 4 + head
                probs_buf[at] = head_probs(scores_buf[at], same).astype(LOW)

        @pl.loop(0, HEADS // 8)
        def _(group):
            for pair in range(4):
                at = group * 512 + pair * 128
                value = saved_buf[:, lanes(2 * width + at, 128)]
                mixed = jnp.where(
                    left,
                    matmul(probs_buf[group * 8 + 2 * pair], value),
                    matmul(probs_buf[group * 8 + 2 * pair + 1], value),
                )
                saved_buf[:, lanes(3 * width + at, 128)] = mixed.astype(LOW)

        keeps[2].start()

        @pl.loop(0, width // CHUNK)
        def _(j):
            at = lanes(j * CHUNK, CHUNK)
            term = matmul(saved_buf[:, 3 * width :], lead_ref[:, lanes(3 * width + j * CHUNK, CHUNK)])
            out_ref[:, at] = (entry_ref[:, at].astype(WIDE) + term).astype(LOW)

    def feed_forward():
        result_buf[...] = entry_ref[...].astype(WIDE)

        @pl.loop(0, lead_ref.shape[1] // CHUNK, unroll=2)
        def _(j):
            at = lanes(j * CHUNK, CHUNK)
            inner = matmul(normed_buf[...], lead_ref[:, at])
            inner_buf[:, at] = inner
            active = gelu(inner).astype(LOW)
            saved_buf[:, at] = active
            result_buf[...] += matmul(active, down_ref[pl.ds(j * CHUNK, CHUNK), :])

        keeps[2].start()
        keep_inner.start()
        out_ref[...] = result_buf[...].astype(LOW)
        keep_inner.wait()

    if down_ref is not None:
        pl.when(role == 2)(feed_forward)

    @pl.when(role > 0)
    def _():
        for keep in keeps:
            keep.wait()


def pinned(value):
    return pltpu.with_memory_space_constraint(value, pltpu.VMEM)


def far(value):
    return pltpu.with_memory_space_constraint(value, pltpu.HBM)


def forward_stage(spot, table, entries, seg_row, gain, lead, down, kept):
    tokens, width = entries[0].shape
    hidden = lead.shape[1]
    count = len(entries) + (3 if down is None else 4)
    return pl.pallas_call(
        functools.partial(forward_kernel, spot, down is not None, len(entries)),
        out_shape=[jax.ShapeDtypeStruct((tokens, width), LOW)]
        + [jax.ShapeDtypeStruct(k.shape, k.dtype) for k in kept],
        in_specs=[SMEM_SPEC] + [VMEM_SPEC] * count + [HBM_SPEC] * 4,
        out_specs=[VMEM_SPEC] + [HBM_SPEC] * 4,
        scratch_shapes=[
            pltpu.VMEM((tokens, width), LOW),
            pltpu.VMEM((tokens, hidden), LOW),
            pltpu.VMEM((tokens, hidden), WIDE),
            pltpu.VMEM((tokens, width), WIDE),
            pltpu.VMEM((HEADS, tokens, tokens), WIDE),
            pltpu.VMEM((HEADS, tokens, tokens), LOW),
            pltpu.VMEM((tokens, width), LOW),
            pltpu.SemaphoreType.DMA((4,)),
        ],
        input_output_aliases={count + 1 + i: 1 + i for i in range(4)},
        compiler_params=pltpu.CompilerParams(vmem_limit_bytes=18 << 20),
        cost_estimate=pl.CostEstimate(
            flops=4 * tokens * width * hidden, bytes_accessed=20 << 20, transcendentals=0
        ),
        name="forward_stage",
    )(table, *entries, seg_row, gain, pinned(lead), *([pinned(down)] if down is not None else []), *map(far, kept))


def backward_kernel(spot, count, *refs):
    backward_body(spot, refs[0], refs[1 : 1 + count], *refs[1 + count :])


def backward_body(
    spot,
    table_ref,
    candidates,
    seg_row_ref,
    gain_ref,
    lead_ref,
    down_ref,
    entries_ref,
    saved_ref,
    inner_ref,
    nexts_in,
    grads_in,
    gains_in,
    out_ref,
    nexts_ref,
    grads_ref,
    gains_ref,
    saved_buf,
    inner_buf,
    grads_buf,
    mixed_buf,
    gain_buf,
    entry_buf,
    normed_buf,
    scores_buf,
    probs_grad_buf,
    probs_buf,
    scores_grad_buf,
    grad_ref,
    in_sems,
    out_sems,
):
    role, slot = table_ref[spot], table_ref[spot + 1]
    tokens, width = grad_ref.shape
    bring_saved = pltpu.make_async_copy(saved_ref.at[slot], saved_buf, in_sems.at[0])
    bring_inner = pltpu.make_async_copy(inner_ref.at[slot], inner_buf, in_sems.at[1])
    bring_entry = pltpu.make_async_copy(entries_ref.at[slot], entry_buf, in_sems.at[2])
    keep_next = pltpu.make_async_copy(grad_ref, nexts_ref.at[slot], out_sems.at[0])
    keep_grads = pltpu.make_async_copy(grads_buf, grads_ref.at[slot], out_sems.at[1])
    keep_gain = pltpu.make_async_copy(gain_buf, gains_ref.at[slot], out_sems.at[2])

    @pl.when(role == 2)
    def _():
        bring_inner.start()

    @pl.when(role == 1)
    def _():
        bring_saved.start()

    @pl.when(role > 0)
    def _():
        bring_entry.start()
        chosen(table_ref[spot + 2], candidates, grad_ref)
        keep_next.start()
        normed_buf[...] = jnp.zeros_like(normed_buf)

    @pl.when(role == 1)
    def _():
        grads_buf[:, 3 * width :] = grad_ref[...]
        mixed_buf[...] = matmul_nt(grad_ref[...], lead_ref[:, 3 * width :]).astype(LOW)
        bring_saved.wait()
        left = lax.broadcasted_iota(jnp.int32, (tokens, 128), 1) < HEAD_SIZE
        zero = jnp.zeros((tokens, 128), LOW)
        scale = HEAD_SIZE ** (-0.5)

        @pl.loop(0, HEADS // 8)
        def _(group):
            for pair in range(4):
                at = group * 512 + pair * 128
                query = saved_buf[:, lanes(at, 128)]
                key = saved_buf[:, lanes(width + at, 128)]
                value = saved_buf[:, lanes(2 * width + at, 128)]
                grad = mixed_buf[:, lanes(at, 128)]
                for own in (0, 1):
                    mine = lambda v: jnp.where(left, v, zero) if own == 0 else jnp.where(left, zero, v)
                    scores_buf[group * 8 + 2 * pair + own] = matmul_nt(mine(query), key)
                    probs_grad_buf[group * 8 + 2 * pair + own] = matmul_nt(mine(grad), value)

        @pl.loop(0, HEADS // 4)
        def _(group):
            same = same_segment(seg_row_ref[slot])
            for head in range(4):
                at = group * 4 + head
                probs = head_probs(scores_buf[at], same)
                probs_buf[at] = probs.astype(LOW)
                grad_probs = probs_grad_buf[at]
                scores_grad_buf[at] = (
                    probs * (grad_probs - jnp.sum(probs * grad_probs, axis=-1, keepdims=True))
                ).astype(LOW)

        @pl.loop(0, HEADS // 4)
        def _(group):
            for pair in range(2):
                at = group * 256 + pair * 128
                query = saved_buf[:, lanes(at, 128)]
                key = saved_buf[:, lanes(width + at, 128)]
                grad = mixed_buf[:, lanes(at, 128)]
                parts = []
                for own in (0, 1):
                    probs = probs_buf[group * 4 + 2 * pair + own]
                    grad_low = scores_grad_buf[group * 4 + 2 * pair + own]
                    parts.append(
                        (
                            matmul(grad_low, key) * scale,
                            matmul_tn(grad_low, query) * scale,
                            matmul_tn(probs, grad),
                        )
                    )
                for which in range(3):
                    grads_buf[:, lanes(which * width + at, 128)] = jnp.where(
                        left, parts[0][which], parts[1][which]
                    ).astype(LOW)

        @pl.loop(0, 3 * width // CHUNK, unroll=2)
        def _(j):
            at = lanes(j * CHUNK, CHUNK)
            normed_buf[...] += matmul_nt(grads_buf[:, at], lead_ref[:, at])

    @pl.when(role == 2)
    def _():
        bring_inner.wait()

        @pl.loop(0, lead_ref.shape[1] // CHUNK, unroll=2)
        def _(j):
            at = lanes(j * CHUNK, CHUNK)
            grad_active = matmul_nt(grad_ref[...], down_ref[pl.ds(j * CHUNK, CHUNK), :])
            grads = (gelu_slope(inner_buf[:, at]) * grad_active).astype(LOW)
            grads_buf[:, at] = grads
            normed_buf[...] += matmul_nt(grads, lead_ref[:, at])

    @pl.when(role > 0)
    def _():
        keep_grads.start()
        bring_entry.wait()
        grad_normed = normed_buf[...]
        normed, factor = layer_norm(entry_buf[...].astype(WIDE))
        gain_buf[...] = jnp.broadcast_to(
            jnp.sum(grad_normed * normed, axis=0, keepdims=True), gain_buf.shape
        )
        keep_gain.start()
        out_ref[...] = (
            grad_ref[...].astype(WIDE) + norm_back(grad_normed * gain_ref[...], normed, factor)
        ).astype(LOW)
        keep_next.wait()
        keep_grads.wait()
        keep_gain.wait()


def backward_stage(
    spot, table, nexts, seg_row, gain, lead, down, entries, saved, inner, totals
):
    tokens, width = nexts[0].shape
    count = len(nexts)
    hidden = lead.shape[1]
    return pl.pallas_call(
        functools.partial(backward_kernel, spot, count),
        out_shape=[jax.ShapeDtypeStruct((tokens, width), LOW)]
        + [jax.ShapeDtypeStruct(k.shape, k.dtype) for k in totals],
        in_specs=[SMEM_SPEC] + [VMEM_SPEC] * (count + 4) + [HBM_SPEC] * 6,
        out_specs=[VMEM_SPEC] + [HBM_SPEC] * 3,
        scratch_shapes=[
            pltpu.VMEM((tokens, hidden), LOW),
            pltpu.VMEM((tokens, hidden), WIDE),
            pltpu.VMEM((tokens, hidden), LOW),
            pltpu.VMEM((tokens, width), LOW),
            pltpu.VMEM((8, width), WIDE),
            pltpu.VMEM((tokens, width), LOW),
            pltpu.VMEM((tokens, width), WIDE),
            pltpu.VMEM((HEADS, tokens, tokens), WIDE),
            pltpu.VMEM((HEADS, tokens, tokens), WIDE),
            pltpu.VMEM((HEADS, tokens, tokens), LOW),
            pltpu.VMEM((HEADS, tokens, tokens), LOW),
            pltpu.VMEM((tokens, width), LOW),
            pltpu.SemaphoreType.DMA((3,)),
            pltpu.SemaphoreType.DMA((3,)),
        ],
        input_output_aliases={count + 8 + i: 1 + i for i in range(3)},
        compiler_params=pltpu.CompilerParams(vmem_limit_bytes=18 << 20),
        cost_estimate=pl.CostEstimate(
            flops=4 * tokens * width * hidden, bytes_accessed=20 << 20, transcendentals=0
        ),
        name="backward_stage",
    )(
        table,
        *nexts,
        seg_row,
        gain,
        pinned(lead),
        pinned(down),
        far(entries),
        far(saved),
        far(inner),
        *map(far, totals),
    )


def stats_kernel(spot, plan_ref, *refs):
    candidates, (table_ref, readout_ref, peak_ref, total_ref) = refs[:-4], refs[-4:]
    step = pl.program_id(0)

    @pl.when(step == 0)
    def _():
        chosen(plan_ref[spot], candidates, readout_ref)

    logits = matmul_nt(table_ref[...], readout_ref[...])
    own_peak = jnp.max(logits, axis=0, keepdims=True)
    own_total = lambda peak: jnp.sum(jnp.exp(logits - peak), axis=0, keepdims=True)

    @pl.when(step == 0)
    def _():
        peak_ref[...] = own_peak
        total_ref[...] = own_total(own_peak)

    @pl.when(step > 0)
    def _():
        peak = jnp.maximum(peak_ref[...], own_peak)
        total_ref[...] = total_ref[...] * jnp.exp(peak_ref[...] - peak) + own_total(peak)
        peak_ref[...] = peak


def head_stats(spot, plan, readouts, table, tile):
    tokens, emb = readouts[0].shape
    vocab = table.shape[0]
    whole = pl.BlockSpec((1, tokens), lambda i: (0, 0))
    rows = pl.BlockSpec((tokens, emb), lambda i: (0, 0))
    return pl.pallas_call(
        functools.partial(stats_kernel, spot),
        out_shape=[jax.ShapeDtypeStruct((tokens, emb), LOW)]
        + [jax.ShapeDtypeStruct((1, tokens), WIDE)] * 2,
        grid=(vocab // tile,),
        in_specs=[SMEM_SPEC]
        + [rows] * len(readouts)
        + [pl.BlockSpec((tile, emb), lambda i: (i, 0))],
        out_specs=[rows, whole, whole],
        compiler_params=pltpu.CompilerParams(vmem_limit_bytes=32 << 20),
        cost_estimate=pl.CostEstimate(
            flops=2 * tokens * vocab * emb, bytes_accessed=5 << 20, transcendentals=tokens * vocab
        ),
        name="head_stats",
    )(plan, *readouts, far(table))


def head_kernel(spot, table_base_ref, readout_ref, table_ref, logsum_ref, ids_ref, head_ref, grad_ref):
    tile = table_ref.shape[0]
    logits = matmul_nt(table_ref[...], readout_ref[...])
    ids = ids_ref[...] - (table_base_ref[spot] + pl.program_id(0) * tile)
    hits = lax.broadcasted_iota(jnp.int32, logits.shape, 0) == ids
    probs = jnp.exp(logits - logsum_ref[...])
    grads = jnp.where(hits, probs - 1.0, probs).astype(LOW)
    head = matmul(grads, readout_ref[...])
    unit = tile // 4
    for shard in range(4):
        head_ref[shard, :unit] = head[shard * unit : (shard + 1) * unit].astype(LOW)
    term = matmul_tn(grads, table_ref[...])

    @pl.when(pl.program_id(0) == 0)
    def _():
        grad_ref[...] = term

    @pl.when(pl.program_id(0) > 0)
    def _():
        grad_ref[...] += term


def head_grads(spot, base, readout, table, logsum, ids):
    tokens, emb = readout.shape
    vocab = table.shape[0]
    row = pl.BlockSpec((1, tokens), lambda i: (0, 0))
    whole = pl.BlockSpec((tokens, emb), lambda i: (0, 0))
    part = pl.BlockSpec((vocab // 4, emb), lambda i: (i, 0))
    return pl.pallas_call(
        functools.partial(head_kernel, spot),
        out_shape=[
            pltpu.HBM((16, 512, emb), LOW),
            jax.ShapeDtypeStruct((tokens, emb), WIDE),
        ],
        grid=(4,),
        in_specs=[SMEM_SPEC, whole, part, row, row],
        out_specs=[pl.BlockSpec((4, 512, emb), lambda i: (i, 0, 0)), whole],
        compiler_params=pltpu.CompilerParams(vmem_limit_bytes=32 << 20),
        cost_estimate=pl.CostEstimate(
            flops=6 * tokens * vocab * emb, bytes_accessed=9 << 20, transcendentals=tokens * vocab
        ),
        name="head_grads",
    )(base, readout, far(table), logsum, ids)


def pair_kernel(former_ref, latter_ref, out_ref):
    rows = out_ref.shape[0]
    out_ref[...] = former_ref[:rows].astype(WIDE) + latter_ref[:rows].astype(WIDE)


def pair_sum(former, latter, rows):
    return pl.pallas_call(
        pair_kernel,
        out_shape=jax.ShapeDtypeStruct((rows, former.shape[1]), WIDE),
        in_specs=[VMEM_SPEC] * 2,
        out_specs=VMEM_SPEC,
        compiler_params=pltpu.CompilerParams(vmem_limit_bytes=8 << 20),
        name="pair_sum",
    )(former, latter)


def lookup_kernel(ids_ref, table_ref, noise_ref, out_ref, total_ref, low_ref):
    step = pl.program_id(0)
    parts, tile = table_ref.shape
    tokens = ids_ref.shape[1]
    blocks = tile // 128

    @pl.when(step == 0)
    def _():
        lane = jnp.bitwise_and(ids_ref[...], 127)
        hits = lax.broadcasted_iota(jnp.int32, (128, tokens), 0) == lane
        low_ref[...] = jnp.where(hits, 1.0, 0.0).astype(LOW)
        total_ref[...] = noise_ref[...].astype(WIDE)

    stacked = jnp.concatenate(
        [table_ref[:, block * 128 : (block + 1) * 128] for block in range(blocks)]
    )
    found = matmul(stacked, low_ref[...])
    own = jnp.right_shift(ids_ref[...], 7) - step * blocks
    total = jnp.zeros_like(total_ref)
    for block in range(blocks):
        total = jnp.where(own == block, found[block * parts : (block + 1) * parts], total)
    total_ref[...] += total

    @pl.when(step == pl.num_programs(0) - 1)
    def _():
        out_ref[...] = total_ref[...].astype(LOW)


def lookup(ids, table, noise, tile):
    parts, vocab = table.shape
    tokens = ids.shape[1]
    whole = pl.BlockSpec((parts, tokens), lambda i: (0, 0))
    return pl.pallas_call(
        lookup_kernel,
        out_shape=jax.ShapeDtypeStruct((parts, tokens), LOW),
        grid=(vocab // tile,),
        in_specs=[
            pl.BlockSpec((1, tokens), lambda i: (0, 0)),
            pl.BlockSpec((parts, tile), lambda i: (0, i)),
            whole,
        ],
        out_specs=whole,
        scratch_shapes=[pltpu.VMEM((parts, tokens), WIDE), pltpu.VMEM((128, tokens), LOW)],
        compiler_params=pltpu.CompilerParams(vmem_limit_bytes=32 << 20),
        cost_estimate=pl.CostEstimate(
            flops=2 * 128 * vocab * tokens, bytes_accessed=4 << 20, transcendentals=0
        ),
        name="lookup",
    )(ids, far(table), noise)


def lead_grad_kernel(where_ref, normed_ref, mixed_ref, grads_ref, *refs):
    got_ref, (out_ref, turned_ref) = (refs[0] if len(refs) == 3 else None), refs[-2:]
    role, half, spot = where_ref[0], where_ref[1], where_ref[2]
    step = pl.program_id(0)
    width = normed_ref.shape[1]
    steps = pl.num_programs(0)
    use_mixed = jnp.logical_and(role == 1, half == 1)

    @pl.when(step == 0)
    def _():
        turned_ref[...] = normed_ref[...].T

    @pl.when(jnp.logical_and(step == steps // 2, use_mixed))
    def _():
        turned_ref[...] = mixed_ref[...].T

    result = matmul(turned_ref[...], grads_ref[...])
    unit = width // 16

    def put(block, rows, part):
        if got_ref is not None:
            part = part + got_ref[block, rows, :].astype(WIDE)
        out_ref[block, rows, :] = part.astype(LOW)

    for x in range(4):
        for y in range(4):
            part = result[(4 * x + y) * unit : (4 * x + y + 1) * unit]

            @pl.when(half == 0)
            def _():
                put((x - spot + 4) % 4, slice(y * unit, (y + 1) * unit), part)

            @pl.when(half == 1)
            def _():
                put((y - spot + 4) % 4, slice(x * unit, (x + 1) * unit), part)


def lead_grad(where, normed, saved, grads, got=None):
    tokens, width = normed.shape
    tile = 512
    blocks = pl.BlockSpec((4, width // 4, tile), lambda i, where: (0, 0, i))
    return pl.pallas_call(
        lead_grad_kernel,
        out_shape=jax.ShapeDtypeStruct((4, width // 4, 2 * width), LOW),
        grid_spec=pltpu.PrefetchScalarGridSpec(
            num_scalar_prefetch=1,
            grid=(2 * width // tile,),
            in_specs=[
                pl.BlockSpec((tokens, width), lambda i, where: (0, 0)),
                pl.BlockSpec((tokens, width), lambda i, where: (0, 3)),
                pl.BlockSpec((tokens, tile), lambda i, where: (0, where[1] * (2 * width // tile) + i)),
            ]
            + ([] if got is None else [blocks]),
            out_specs=blocks,
            scratch_shapes=[pltpu.VMEM((width, tokens), LOW)],
        ),
        compiler_params=pltpu.CompilerParams(vmem_limit_bytes=24 << 20),
        cost_estimate=pl.CostEstimate(
            flops=4 * tokens * width * width, bytes_accessed=8 << 20, transcendentals=0
        ),
        name="lead_grad",
    )(where, far(normed), far(saved), far(grads), *([] if got is None else [got]))


def down_grad_kernel(where_ref, saved_ref, nexts_ref, *refs):
    got_ref, (out_ref, buf_ref, got_buf, sems) = (refs[0] if len(refs) == 5 else None), refs[-4:]
    role, half, spot = where_ref[0], where_ref[1], where_ref[2]
    at = pl.program_id(0)
    unit = saved_ref.shape[1] // 4

    @pl.when(role == 2)
    def _():
        if got_ref is not None:
            bring = pltpu.make_async_copy(got_ref, got_buf, sems.at[1])
            pl.when(at == 0)(bring.start)
        result = matmul_tn(saved_ref[...], nexts_ref[...])
        if got_ref is not None:
            pl.when(at == 0)(bring.wait)

        def put(block, rows, part):
            if got_ref is not None:
                part = part + got_buf[block, rows, :].astype(WIDE)
            buf_ref[block, rows, :] = part.astype(LOW)

        @pl.when(half == 0)
        def _():
            put((at - spot + 4) % 4, slice(None), result)

        @pl.when(half == 1)
        def _():
            rows = pl.ds(pl.multiple_of(at * unit, unit), unit)
            for y in range(4):
                put((y - spot + 4) % 4, rows, result[y * unit : (y + 1) * unit])

        @pl.when(at == pl.num_programs(0) - 1)
        def _():
            copy = pltpu.make_async_copy(buf_ref, out_ref, sems.at[0])
            copy.start()
            copy.wait()


def down_grad(where, saved, nexts, got=None):
    tokens, hidden = saved.shape
    width = nexts.shape[1]
    rows = hidden // 8
    live = lambda where: jnp.where(where[0] == 2, 1, 0)
    small = (8, 128)
    return pl.pallas_call(
        down_grad_kernel,
        out_shape=pltpu.HBM((4, rows, width), LOW),
        grid_spec=pltpu.PrefetchScalarGridSpec(
            num_scalar_prefetch=1,
            grid=(4,),
            in_specs=[
                pl.BlockSpec((tokens, rows), lambda i, where: (0, (where[1] * 4 + i) * live(where))),
                pl.BlockSpec((tokens, width), lambda i, where: (0, 0)),
            ]
            + ([] if got is None else [HBM_SPEC]),
            out_specs=HBM_SPEC,
            scratch_shapes=[
                pltpu.VMEM((4, rows, width), LOW),
                pltpu.VMEM(small if got is None else (4, rows, width), LOW),
                pltpu.SemaphoreType.DMA((2,)),
            ],
        ),
        compiler_params=pltpu.CompilerParams(vmem_limit_bytes=28 << 20),
        cost_estimate=pl.CostEstimate(
            flops=2 * tokens * width * hidden // 2, bytes_accessed=8 << 20, transcendentals=0
        ),
        name="down_grad",
    )(where, far(saved), far(nexts), *([] if got is None else [far(got)]))


def upper_kernel(where_ref, *refs):
    out_ref = refs[4]
    rows = refs[0].shape[0]
    for at, part in enumerate(refs[:4]):
        place = (where_ref[0] - at + 4) % 4
        out_ref[pl.ds(pl.multiple_of(place * rows, rows), rows), :] = part[...]


def upper_half(where, parts):
    rows, width = parts[0].shape
    return pl.pallas_call(
        upper_kernel,
        out_shape=jax.ShapeDtypeStruct((4 * rows, width), LOW),
        in_specs=[SMEM_SPEC] + [VMEM_SPEC] * 4,
        out_specs=VMEM_SPEC,
        compiler_params=pltpu.CompilerParams(vmem_limit_bytes=8 << 20),
        name="upper_half",
    )(where, *parts)


def hold_down_kernel(where_ref, mine_ref, other_ref, own_ref, out_ref, sems):
    rows = mine_ref.shape[0]
    core = where_ref[1]
    spot = lambda at: out_ref.at[pl.ds(pl.multiple_of(at * rows, rows), rows), :]
    copies = [
        pltpu.make_async_copy(mine_ref, spot(core), sems.at[0]),
        pltpu.make_async_copy(other_ref, spot(1 - core), sems.at[1]),
        pltpu.make_async_copy(own_ref, out_ref.at[pl.ds(2 * rows, 2 * rows), :], sems.at[2]),
    ]
    for copy in copies:
        copy.start()
    for copy in copies:
        copy.wait()


def hold_down(where, mine, other, own):
    rows, width = mine.shape
    return pl.pallas_call(
        hold_down_kernel,
        out_shape=pltpu.VMEM((4 * rows, width), LOW),
        in_specs=[SMEM_SPEC] + [VMEM_SPEC] * 2 + [HBM_SPEC],
        out_specs=VMEM_SPEC,
        scratch_shapes=[pltpu.SemaphoreType.DMA((3,))],
        compiler_params=pltpu.CompilerParams(vmem_limit_bytes=8 << 20),
        name="hold_down",
    )(where, mine, other, far(own))


def noise_kernel(spot, plan_ref, ids_ref, *refs):
    candidates, (packed_ref, noise_ref, buf_ref) = refs[:-3], refs[-3:]
    parts = noise_ref.shape[0]
    chosen(plan_ref[spot], candidates, buf_ref)
    packed_ref[:parts] = buf_ref[...]
    noise_ref[...] = buf_ref[...].astype(WIDE)
    ids = ids_ref[...]
    high = jnp.right_shift(ids, 8).astype(WIDE)
    low = jnp.bitwise_and(ids, 255).astype(WIDE)
    at = lax.broadcasted_iota(jnp.int32, (16, ids.shape[1]), 0)
    split = jnp.where(at == 0, high, jnp.where(at == 1, low, 0.0))
    packed_ref[parts:] = split.astype(LOW)


def noise_pack(spot, plan, ids, candidates):
    parts, tokens = candidates[0].shape
    return pl.pallas_call(
        functools.partial(noise_kernel, spot),
        out_shape=[
            jax.ShapeDtypeStruct((parts + 16, tokens), LOW),
            jax.ShapeDtypeStruct((parts, tokens), WIDE),
        ],
        in_specs=[SMEM_SPEC] + [VMEM_SPEC] * (1 + len(candidates)),
        out_specs=[VMEM_SPEC] * 2,
        scratch_shapes=[pltpu.VMEM((parts, tokens), LOW)],
        compiler_params=pltpu.CompilerParams(vmem_limit_bytes=8 << 20),
        name="noise_pack",
    )(plan, ids, *candidates)


def embed_kernel(base_ref, mine_ref, other_ref, out_ref, total_ref):
    step = pl.program_id(0)
    steps = pl.num_programs(0)
    parts = out_ref.shape[0]
    blocks = total_ref.shape[0] // parts

    def add(gathered_ref):
        count, _, tokens = gathered_ref.shape
        term = None
        for at in range(count):
            split = gathered_ref[at, parts : parts + 16].astype(WIDE)
            ids = (split[0:1] * 256.0 + split[1:2]).astype(jnp.int32) - base_ref[0]
            lane = jnp.bitwise_and(ids, 127)
            hits = lax.broadcasted_iota(jnp.int32, (128, tokens), 0) == lane
            hits = jnp.where(hits, 1.0, 0.0).astype(LOW)
            own = jnp.right_shift(ids, 7)
            grads = gathered_ref[at, :parts]
            masked = jnp.concatenate(
                [grads * jnp.where(own == block, 1.0, 0.0).astype(LOW) for block in range(blocks)]
            )
            part = matmul_nt(masked, hits)
            term = part if term is None else term + part

        @pl.when(step == 0)
        def _():
            total_ref[...] = term

        @pl.when(step > 0)
        def _():
            total_ref[...] += term

    pl.when(step < steps // 2)(lambda: add(mine_ref))
    pl.when(step >= steps // 2)(lambda: add(other_ref))

    @pl.when(step == steps - 1)
    def _():
        rows = out_ref.shape[1]
        for block in range(blocks):
            size = min(128, rows - block * 128)
            out_ref[:, block * 128 : block * 128 + size] = total_ref[
                block * parts : (block + 1) * parts, :size
            ]


def embed_sum(base, mine, other, parts, rows):
    count, deep, tokens = mine.shape
    step = 4
    half = count // step
    blocks = -(-rows // 128)
    return pl.pallas_call(
        embed_kernel,
        out_shape=jax.ShapeDtypeStruct((parts, rows), WIDE),
        grid=(2 * half,),
        in_specs=[
            SMEM_SPEC,
            pl.BlockSpec((step, deep, tokens), lambda i: (jnp.minimum(i, half - 1), 0, 0)),
            pl.BlockSpec((step, deep, tokens), lambda i: (jnp.maximum(i - half, 0), 0, 0)),
        ],
        out_specs=pl.BlockSpec((parts, rows), lambda i: (0, 0)),
        scratch_shapes=[pltpu.VMEM((blocks * parts, 128), WIDE)],
        compiler_params=pltpu.CompilerParams(vmem_limit_bytes=32 << 20),
        cost_estimate=pl.CostEstimate(
            flops=tokens * parts, bytes_accessed=1 << 16, transcendentals=0
        ),
        name="embed_sum",
    )(base, mine, other)


def empty(*kinds):
    return pl.pallas_call(
        lambda *refs: None,
        out_shape=[pltpu.HBM(shape, dtype) for shape, dtype in kinds],
        out_specs=[HBM_SPEC] * len(kinds),
        compiler_params=pltpu.CompilerParams(vmem_limit_bytes=1 << 20),
        name="empty",
    )()


ROW_LEN = 128
SEC, GRP, NX, NY = 4, 2, 4, 4
ALL = ("section", "group", "row")
TURNS = (1, 3, 2)


def route(value, target_of):
    number = lambda s, g, x, y: (s * GRP + g) * NX * NY + x * NY + y
    pairs = []
    for at in itertools.product(range(SEC), range(GRP), range(NX), range(NY)):
        target = target_of(*at)
        if target is not None:
            pairs.append((number(*at), number(*target)))
    return lax.ppermute(value, ALL, pairs)


def link(value, source, target):
    return route(value, lambda s, g, x, y: (target, g, x, y) if s == source else None)


def turn(value, by):
    return route(value, lambda s, g, x, y: ((s + by) % SEC, g, x, y))


def swap_cores(value, sections=range(SEC)):
    return route(value, lambda s, g, x, y: (s, 1 - g, x, y) if s in sections else None)


def plane_route(value, by, first, sections=range(SEC)):
    def target_of(s, g, x, y):
        if s not in sections:
            return None
        if (g == 0) == first:
            return (s, g, (x + by) % NX, y)
        return (s, g, x, (y + by) % NY)

    return route(value, target_of)


def after(value, earlier):
    return lax.optimization_barrier((value, earlier))[0]


def row_block(values, block, count):
    size = values.shape[0] // count
    return lax.dynamic_slice_in_dim(values, block * size, size, 0)


def plane_first(mine, sections=range(SEC)):
    return [mine[0]] + [plane_route(mine[by], by, True, sections) for by in TURNS]


def plane_sum(pieces):
    total = pieces[0].astype(WIDE)
    for piece in pieces[1:]:
        total = total + piece.astype(WIDE)
    return total.astype(LOW)


def plane_second(pieces, second, sections=range(SEC)):
    total = plane_sum(pieces)
    return [row_block(total, second, 4)] + [
        plane_route(row_block(total, (second + by) % 4, 4), by, False, sections) for by in TURNS
    ]


def group_exchange(values, first):
    number = lambda s, g, x, y: (s * GRP + g) * NX * NY + x * NY + y
    groups = []
    for s in range(SEC):
        for g in range(GRP):
            along_x = (g == 0) == first
            for at in range(4):
                groups.append(
                    [number(s, g, i, at) if along_x else number(s, g, at, i) for i in range(4)]
                )
    return lax.all_to_all(values, ALL, 0, 0, axis_index_groups=groups, tiled=True)


def section_exchange(values):
    return lax.all_to_all(values, "section", 0, 0, tiled=True)


def plans(micro, vocab_part):
    last = SEC - 1
    steps = micro + 2 * last
    table = np.zeros((SEC, 6 * steps + 2), np.int32)
    for s in range(SEC):
        for way in range(2):
            depth = s if way == 0 else last - s
            for step in range(steps):
                at = step - 2 * depth
                if 0 <= at < micro:
                    sources = ([0] if step < micro else []) + [
                        d + 1 for d in range(last) if 0 <= step - 2 - 2 * d < micro
                    ]
                    spot = 3 * (way * steps + step)
                    table[s, spot : spot + 3] = (1 + s % 2, at, sources.index(depth))
        table[s, 6 * steps :] = (s * vocab_part, s)
    return table


def local(
    token_ids,
    segment_ids,
    noise_input,
    embed_table,
    input_proj,
    norm_gain,
    lead_weight,
    down_weight,
    final_gain,
    readout_proj,
    head_table,
):
    section = lax.axis_index("section")
    core = lax.axis_index("group")
    row = lax.axis_index("row")
    x_at, y_at = row // NY, row % NY
    first_at = jnp.where(core == 0, x_at, y_at)
    micro, _, tokens = token_ids.shape
    width = input_proj.shape[1]
    hidden = lead_weight.shape[2]
    half_rows = down_weight.shape[1]
    emb_part = input_proj.shape[0]
    vocab_part, emb = head_table.shape
    vocab = embed_table.shape[0]
    all_tokens = micro * tokens
    last = SEC - 1
    gain_half = norm_gain.astype(WIDE)
    lead = lead_weight[0]
    own_down = down_weight[0]
    seg_row = segment_ids
    flat_ids = token_ids.reshape(-1)

    plan = plans(micro, vocab_part)
    steps = micro + 2 * last
    table = lax.dynamic_index_in_dim(jnp.asarray(plan), section, 0, False)
    flat_ids = after(flat_ids, table)
    where_start = jnp.stack((first_at, core)).astype(jnp.int32)
    to_first = lambda v: [v] + [link(v, s, 0) for s in range(1, SEC)]
    eighth = row_block(row_block(own_down, core, 2), first_at, 4)
    eighth = jnp.where(section == 1, link(eighth, 0, 1), link(eighth, 2, 3))
    noise = noise_input[:, 0].transpose(2, 0, 1).reshape(emb_part, -1)
    own_embedded = lookup(flat_ids[None], embed_table.T, noise, 3200)
    inputs = to_first(input_proj)
    input_full = jnp.concatenate(inputs)
    embedded = jnp.concatenate(
        [own_embedded] + [link(own_embedded, s, 0) for s in range(1, SEC)]
    )
    first_in = matmul_tn(embedded, input_full).astype(LOW).reshape(micro, tokens, width)
    held_lead = hold(lead)
    eighth = after(eighth, own_embedded)
    eighths = [eighth] + [plane_route(eighth, by, True) for by in (1, 2, 3)]
    upper = upper_half(where_start, [after(part, first_in) for part in eighths])
    held_down = hold_down(where_start, upper, swap_cores(upper), own_down)

    kept = empty(
        ((micro, tokens, width), LOW),
        ((micro, tokens, width), LOW),
        ((micro, tokens, hidden), LOW),
        ((micro, tokens, hidden), WIDE),
    )

    def sources(first, step, hops, order):
        arrived = [hops[step - 2, s] for s in order if (step - 2, s) in hops]
        return ([first[step]] if step < micro else []) + arrived

    outs, hops = [], {}
    for step in range(steps):
        out, *kept = forward_stage(
            3 * step,
            table,
            sources(first_in, step, hops, range(SEC)),
            seg_row,
            gain_half,
            held_lead,
            held_down if step > 1 else None,
            kept,
        )
        outs.append(out)
        for s in range(last):
            if 0 <= step - 2 * s < micro:
                ready = after(out, hops[step - 1, s]) if (step - 1, s) in hops else out
                hops[step, s] = link(ready, s, s + 1)
        if step == 2:
            readout_own = after(readout_proj.T, out)
            readout_full = jnp.concatenate(
                [link(readout_own, s, last) for s in range(last)] + [readout_own]
            )
    entries, normeds, saved, inner = kept

    final_rows = jnp.concatenate(outs[2 * last :]).astype(WIDE)
    normed_f, factor_f = layer_norm(final_rows)
    gain_f = final_gain.astype(WIDE)
    final_low = (normed_f * gain_f).astype(LOW)
    readout = matmul_nt(final_low, readout_full).astype(LOW)
    sent = [link(readout, last, s) for s in range(last)]
    readout, peak, total = head_stats(6 * steps + 1, table, sent + [readout], head_table, 2000)
    stats = jnp.concatenate((peak, total))
    all_stats = section_exchange(jnp.tile(stats, (SEC, 1))).reshape(SEC, 2, all_tokens)
    peak = jnp.max(all_stats[:, 0], axis=0)
    total = jnp.sum(all_stats[:, 1] * jnp.exp(all_stats[:, 0] - peak), axis=0)
    logsum = (peak + jnp.log(total))[None]
    head_grad, grad_readout = head_grads(
        6 * steps, table, readout, head_table, logsum, flat_ids[None]
    )
    grad_low = grad_readout.astype(LOW)
    for s in range(last):
        grad_readout = grad_readout + link(grad_low, s, last).astype(WIDE)
    grad_readout = grad_readout.astype(LOW)
    head_grad = lax.psum_scatter(head_grad, "row", scatter_dimension=0)
    readout_grad = matmul_tn(final_low, grad_readout)
    grad_final = matmul(grad_readout, readout_full)
    final_gain_grad = jnp.sum(grad_final * normed_f, axis=0)
    last_grads = norm_back(grad_final * gain_f, normed_f, factor_f).astype(LOW)
    last_grads = last_grads.reshape(micro, tokens, width)

    totals = empty(
        ((micro, tokens, width), LOW),
        ((micro, tokens, hidden), LOW),
        ((micro, 8, width), WIDE),
    )
    outs, hops = [], {}
    for step in range(steps):
        out, *totals = backward_stage(
            3 * (steps + step),
            table,
            sources(last_grads, step, hops, range(SEC - 1, -1, -1)),
            seg_row,
            gain_half,
            held_lead,
            held_down,
            entries,
            saved,
            inner,
            totals,
        )
        outs.append(out)
        for s in range(1, SEC):
            if 0 <= step - 2 * (last - s) < micro:
                ready = after(out, hops[step - 1, s]) if (step - 1, s) in hops else out
                hops[step, s] = link(ready, s, s - 1)
    section, core, row = lax.optimization_barrier((section, core, row, out))[:3]
    x_at, y_at = row // NY, row % NY
    first_at, second_at = jnp.where(core == 0, x_at, y_at), jnp.where(core == 0, y_at, x_at)
    is_mlp = section % 2 == 1

    first_grads = jnp.concatenate(outs[2 * last :])
    noise_grad = matmul_nt(input_full, first_grads).astype(LOW)
    pieces = noise_grad.reshape(SEC, emb_part, all_tokens)
    sent = [link(pieces[s], 0, s) for s in range(1, SEC)]

    grad_nexts, grads, gain_grads = totals
    gain_grad = jnp.sum(gain_grads[:, 0], axis=0)
    flat = lambda v: v.reshape(all_tokens, v.shape[-1])
    grads = after(grads, head_grad)
    normed, grad_nexts, grads, saved = flat(normeds), flat(grad_nexts), flat(grads), flat(saved)
    odd = (1, 3)
    role = jnp.where(is_mlp, 2, 1)
    where_other = jnp.stack((role, 1 - core, second_at)).astype(jnp.int32)
    where_mine = jnp.stack((role, core, first_at)).astype(jnp.int32)
    both = lambda mine, other: jnp.where(
        core == 0,
        jnp.concatenate((mine, other), axis=1),
        jnp.concatenate((other, mine), axis=1),
    )
    down_got = swap_cores(down_grad(where_other, saved, grad_nexts), odd)
    lead_got = swap_cores(lead_grad(where_other, normed, saved, grads))
    down_mine = down_grad(where_mine, saved, grad_nexts, down_got)
    down_first = plane_first(down_mine, odd)

    input_grad = matmul(embedded, first_grads).reshape(SEC, 16, 4, width)
    input_grad = input_grad.transpose(1, 0, 2, 3).reshape(16, 16, width)
    readout_grad = readout_grad.reshape(16, 16, width)
    vectors = jnp.concatenate(
        (
            gain_grad.reshape(16, 64),
            final_gain_grad.reshape(SEC, 16, 16).transpose(1, 0, 2).reshape(16, 64),
            jnp.zeros((16, width - 128), WIDE),
        ),
        axis=1,
    )
    small = jnp.concatenate(
        (
            jnp.where(section == 0, input_grad, readout_grad),
            vectors[:, None],
            jnp.zeros((16, 15, width), WIDE),
        ),
        axis=1,
    ).astype(LOW)
    late_ids = after(flat_ids, down_mine)[None]
    packed, noise_wide = noise_pack(6 * steps + 1, table, late_ids, [pieces[0]] + sent)
    half_of = lambda which: lax.dynamic_slice_in_dim(small, which * (width // 2), width // 2, 2)
    small = half_of(core).astype(WIDE) + swap_cores(half_of(1 - core)).astype(WIDE)
    small = small.astype(LOW).reshape(NX, NY, 32, width // 2)
    small = jnp.where(core == 0, small, small.swapaxes(0, 1)).reshape(4, NY * 32, width // 2)
    deep = emb_part + 16

    def exchange(blocks, packed, first):
        rows = blocks.shape[1]
        everywhere = jnp.broadcast_to(packed, (4,) + packed.shape)
        got = group_exchange(jnp.concatenate((blocks, everywhere), axis=1), first)
        return jnp.sum(got[:, :rows].astype(WIDE), axis=0).astype(LOW), got[:, rows:]

    small, packed = exchange(small, packed, True)
    small, packed = exchange(
        small.reshape(4, 32, width // 2), packed.reshape(4 * deep, all_tokens), False
    )
    packed = packed.reshape(16, deep, all_tokens)
    packed_other = swap_cores(packed)
    small = both(small, swap_cores(small))
    down_second = plane_second(after(down_first, packed), second_at, odd)
    where_mine = after(where_mine, (packed, down_second[0]))
    lead_mine = lead_grad(where_mine, normed, saved, grads, lead_got)
    lead_first = plane_first(lead_mine)
    embed_grad = embed_sum(
        (row * (vocab // 16)).reshape(1), packed, packed_other, emb_part, vocab // 16
    )
    gain_out = small[16, :64].astype(WIDE)
    input_rows = small[:16].reshape(SEC, 4, width)
    readout_rows = small[:16].reshape(64, SEC, 64)
    final_rows = small[16, 64:128].reshape(SEC, 16)

    finals = jnp.pad(final_rows, ((0, 0), (0, width - 16)))[:, None]
    mine = jnp.where(
        section == 0, input_rows, readout_rows.transpose(1, 0, 2).reshape(SEC, 4, width)
    )
    shared = section_exchange(
        jnp.concatenate((mine, finals, jnp.zeros((SEC, 3, width), LOW)), axis=1)
    )
    input_out = shared[0, :4]
    readout_out = shared[last, :4].reshape(64, 64)
    final_out = shared[last, 4, :16]

    ready = (embed_grad, shared)
    lead_second = plane_second(after(lead_first, ready), second_at)
    down_part = plane_sum(after(down_second, ready))
    lead_part = plane_sum(lead_second)
    noise_out = noise_wide.reshape(emb_part, micro, tokens).transpose(1, 2, 0)
    lead_out = both(lead_part, swap_cores(lead_part)).astype(WIDE)

    def first_target(s, g, x, y):
        if s % 2 == 0:
            return None
        return (s - 1, 0, x, y) if g == 0 else (s, 0, x, y)

    def second_target(s, g, x, y):
        return (s - 1, 1, x, y) if s % 2 == 1 and g == 0 else None

    to_core_0 = route(down_part, first_target)
    to_core_1 = route(down_part, second_target)
    down_out = jnp.where(
        core == 0, to_core_0, jnp.where(is_mlp, down_part, to_core_1)
    ).astype(WIDE)

    head_out = pair_sum(head_grad, swap_cores(head_grad), vocab_part // (NX * NY))
    return (
        noise_out[:, None],
        embed_grad.T,
        input_out.astype(WIDE),
        gain_out[None],
        lead_out[None],
        down_out[None],
        final_out.astype(WIDE),
        readout_out.astype(WIDE),
        head_out,
    )


def solution(mesh):
    in_specs = (
        P(None, ("group", "row"), None),
        P(None, ("group", "row"), None),
        P(None, ("group", "row"), None, "section"),
        P(None, "section"),
        P("section", None),
        P("section", None),
        P("section", None, None),
        P("section", None, None),
        P(),
        P(None, "section"),
        P("section", None),
    )
    out_specs = (
        P(None, ("group", "row"), None, "section"),
        P("row", "section"),
        P(("section", "row"), None),
        P("section", "row"),
        P("section", "row", None),
        P("section", "row", None),
        P(("section", "row")),
        P("row", "section"),
        P(("section", "row"), None),
    )
    return jax.shard_map(local, mesh=mesh, in_specs=in_specs, out_specs=out_specs, check_vma=False)
```

```python
import functools
import itertools

import jax
import jax.numpy as jnp
import numpy as np
from jax import lax
from jax.experimental import pallas as pl
from jax.experimental.pallas import tpu as pltpu
from jax.sharding import PartitionSpec as P

HEADS = 16
HEAD_SIZE = 64
LOW = jnp.bfloat16
WIDE = jnp.float32
EPSILON = 1e-05
MASKED = -1000000000.0
CHUNK = 512
GELU_A = 0.7978845608028654
GELU_B = 0.044715
HBM_SPEC = pl.BlockSpec(memory_space=pltpu.HBM)
VMEM_SPEC = pl.BlockSpec(memory_space=pltpu.VMEM)
SMEM_SPEC = pl.BlockSpec(memory_space=pltpu.SMEM)


def matmul(former, latter):
    return jnp.dot(former, latter, preferred_element_type=WIDE)


def matmul_nt(former, latter):
    return lax.dot_general(
        former, latter, (((1,), (1,)), ((), ())), preferred_element_type=WIDE
    )


def matmul_tn(former, latter):
    return lax.dot_general(
        former, latter, (((0,), (0,)), ((), ())), preferred_element_type=WIDE
    )


def layer_norm(values):
    centre = jnp.mean(values, axis=-1, keepdims=True)
    centred = values - centre
    variance = jnp.mean(centred * centred, axis=-1, keepdims=True)
    factor = lax.rsqrt(variance + EPSILON)
    return (centred * factor, factor)


def norm_back(grad_normed, normed, factor):
    first_mean = jnp.mean(grad_normed, axis=-1, keepdims=True)
    second_mean = jnp.mean(grad_normed * normed, axis=-1, keepdims=True)
    return factor * (grad_normed - first_mean - normed * second_mean)


def gelu(v):
    return 0.5 * v * (1.0 + jnp.tanh(GELU_A * (v + GELU_B * (v * v * v))))


def gelu_slope(v):
    square = v * v
    bend = jnp.tanh(GELU_A * (v + GELU_B * (square * v)))
    return 0.5 * (1.0 + bend) + 0.5 * v * (1.0 - bend * bend) * (
        GELU_A * (1.0 + 3.0 * GELU_B * square)
    )


def head_probs(scores, same):
    scores = jnp.where(same, scores * HEAD_SIZE ** (-0.5), MASKED)
    expo = jnp.exp(scores - jnp.max(scores, axis=-1, keepdims=True))
    return expo * (1.0 / jnp.sum(expo, axis=-1, keepdims=True))


def same_segment(row):
    across = jnp.broadcast_to(row.astype(WIDE), (row.shape[1], row.shape[1]))
    return across.T == across


def lanes(at, size):
    return pl.ds(pl.multiple_of(at, 128), size)


def chosen(choice, candidates, buffer):
    for at, candidate in enumerate(candidates):

        @pl.when(choice == at)
        def _():
            buffer[...] = candidate[...]


def forward_kernel(spot, with_down, loads, count, *refs):
    table_ref, candidates, refs = refs[0], refs[1 : 1 + count], refs[1 + count :]
    if not with_down:
        refs = refs[:3] + (None,) + refs[3:]
    source_ref = load_sems = None
    if loads:
        source_ref, load_sems = refs[2], refs[-1]
        refs = refs[:2] + (refs[13],) + refs[3:13] + refs[14:-1]
    forward_body(spot, table_ref, candidates, source_ref, load_sems, *refs)


def forward_body(
    spot,
    table_ref,
    candidates,
    source_ref,
    load_sems,
    seg_row_ref,
    gain_ref,
    lead_ref,
    down_ref,
    entries_in,
    normeds_in,
    saved_in,
    inner_in,
    out_ref,
    entries_ref,
    normeds_ref,
    saved_ref,
    inner_ref,
    normed_buf,
    saved_buf,
    inner_buf,
    result_buf,
    scores_buf,
    probs_buf,
    entry_ref,
    out_sems,
):
    role, slot = table_ref[spot], table_ref[spot + 1]
    tokens, width = entry_ref.shape
    keeps = [
        pltpu.make_async_copy(entry_ref, entries_ref.at[slot], out_sems.at[0]),
        pltpu.make_async_copy(normed_buf, normeds_ref.at[slot], out_sems.at[1]),
        pltpu.make_async_copy(saved_buf, saved_ref.at[slot], out_sems.at[2]),
    ]
    keep_inner = pltpu.make_async_copy(inner_buf, inner_ref.at[slot], out_sems.at[3])

    def load(j):
        at = lanes(j * CHUNK, CHUNK)
        return pltpu.make_async_copy(source_ref.at[:, at], lead_ref.at[:, at], load_sems.at[j])

    def loaded(j):
        if source_ref is not None:
            load(j).wait()

    if source_ref is not None:
        for j in range(lead_ref.shape[1] // CHUNK):
            load(j).start()

        @pl.when(role != 1)
        def _():
            pl.loop(0, lead_ref.shape[1] // CHUNK)(loaded)

    @pl.when(role > 0)
    def _():
        chosen(table_ref[spot + 2], candidates, entry_ref)
        normed, _ = layer_norm(entry_ref[...].astype(WIDE))
        normed_buf[...] = (normed * gain_ref[...]).astype(LOW)
        keeps[0].start()
        keeps[1].start()

    @pl.when(role == 1)
    def _():
        @pl.loop(0, 3 * width // CHUNK, unroll=2)
        def _(j):
            at = lanes(j * CHUNK, CHUNK)
            loaded(j)
            saved_buf[:, at] = matmul(normed_buf[...], lead_ref[:, at]).astype(LOW)

        left = lax.broadcasted_iota(jnp.int32, (tokens, 128), 1) < HEAD_SIZE
        zero = jnp.zeros((tokens, 128), LOW)

        @pl.loop(0, HEADS // 8)
        def _(group):
            for pair in range(4):
                at = group * 512 + pair * 128
                query = saved_buf[:, lanes(at, 128)]
                key = saved_buf[:, lanes(width + at, 128)]
                scores_buf[group * 8 + 2 * pair] = matmul_nt(jnp.where(left, query, zero), key)
                scores_buf[group * 8 + 2 * pair + 1] = matmul_nt(jnp.where(left, zero, query), key)

        @pl.loop(0, HEADS // 4)
        def _(group):
            same = same_segment(seg_row_ref[slot])
            for head in range(4):
                at = group * 4 + head
                probs_buf[at] = head_probs(scores_buf[at], same).astype(LOW)

        @pl.loop(0, HEADS // 8)
        def _(group):
            for pair in range(4):
                at = group * 512 + pair * 128
                value = saved_buf[:, lanes(2 * width + at, 128)]
                mixed = jnp.where(
                    left,
                    matmul(probs_buf[group * 8 + 2 * pair], value),
                    matmul(probs_buf[group * 8 + 2 * pair + 1], value),
                )
                saved_buf[:, lanes(3 * width + at, 128)] = mixed.astype(LOW)

        keeps[2].start()

        @pl.loop(0, width // CHUNK)
        def _(j):
            at = lanes(j * CHUNK, CHUNK)
            loaded(3 * width // CHUNK + j)
            term = matmul(saved_buf[:, 3 * width :], lead_ref[:, lanes(3 * width + j * CHUNK, CHUNK)])
            out_ref[:, at] = (entry_ref[:, at].astype(WIDE) + term).astype(LOW)

    def feed_forward():
        result_buf[...] = entry_ref[...].astype(WIDE)

        @pl.loop(0, lead_ref.shape[1] // CHUNK, unroll=2)
        def _(j):
            at = lanes(j * CHUNK, CHUNK)
            inner = matmul(normed_buf[...], lead_ref[:, at])
            inner_buf[:, at] = inner
            active = gelu(inner).astype(LOW)
            saved_buf[:, at] = active
            result_buf[...] += matmul(active, down_ref[pl.ds(j * CHUNK, CHUNK), :])

        keeps[2].start()
        keep_inner.start()
        out_ref[...] = result_buf[...].astype(LOW)
        keep_inner.wait()

    if down_ref is not None:
        pl.when(role == 2)(feed_forward)

    @pl.when(role > 0)
    def _():
        for keep in keeps:
            keep.wait()


def pinned(value):
    return pltpu.with_memory_space_constraint(value, pltpu.VMEM)


def far(value):
    return pltpu.with_memory_space_constraint(value, pltpu.HBM)


def forward_stage(spot, table, entries, seg_row, gain, lead, down, kept, loads=False):
    tokens, width = entries[0].shape
    hidden = lead.shape[1]
    count = len(entries) + (3 if down is None else 4)
    given = [VMEM_SPEC] * (len(entries) + 2) + [HBM_SPEC if loads else VMEM_SPEC]
    return pl.pallas_call(
        functools.partial(forward_kernel, spot, down is not None, loads, len(entries)),
        out_shape=[jax.ShapeDtypeStruct((tokens, width), LOW)]
        + [jax.ShapeDtypeStruct(k.shape, k.dtype) for k in kept]
        + ([pltpu.VMEM(lead.shape, LOW)] if loads else []),
        in_specs=[SMEM_SPEC] + given + [VMEM_SPEC] * (down is not None) + [HBM_SPEC] * 4,
        out_specs=[VMEM_SPEC] + [HBM_SPEC] * 4 + [VMEM_SPEC] * loads,
        scratch_shapes=[
            pltpu.VMEM((tokens, width), LOW),
            pltpu.VMEM((tokens, hidden), LOW),
            pltpu.VMEM((tokens, hidden), WIDE),
            pltpu.VMEM((tokens, width), WIDE),
            pltpu.VMEM((HEADS, tokens, tokens), WIDE),
            pltpu.VMEM((HEADS, tokens, tokens), LOW),
            pltpu.VMEM((tokens, width), LOW),
            pltpu.SemaphoreType.DMA((4,)),
        ]
        + ([pltpu.SemaphoreType.DMA((hidden // CHUNK,))] if loads else []),
        input_output_aliases={count + 1 + i: 1 + i for i in range(4)},
        compiler_params=pltpu.CompilerParams(vmem_limit_bytes=18 << 20),
        cost_estimate=pl.CostEstimate(
            flops=4 * tokens * width * hidden, bytes_accessed=20 << 20, transcendentals=0
        ),
        name="forward_stage",
    )(
        table,
        *entries,
        seg_row,
        gain,
        (far if loads else pinned)(lead),
        *([pinned(down)] if down is not None else []),
        *map(far, kept),
    )


def backward_kernel(spot, count, *refs):
    backward_body(spot, refs[0], refs[1 : 1 + count], *refs[1 + count :])


def backward_body(
    spot,
    table_ref,
    candidates,
    seg_row_ref,
    gain_ref,
    lead_ref,
    down_ref,
    entries_ref,
    saved_ref,
    inner_ref,
    nexts_in,
    grads_in,
    gains_in,
    out_ref,
    nexts_ref,
    grads_ref,
    gains_ref,
    saved_buf,
    inner_buf,
    grads_buf,
    mixed_buf,
    gain_buf,
    entry_buf,
    normed_buf,
    scores_buf,
    probs_grad_buf,
    probs_buf,
    scores_grad_buf,
    grad_ref,
    in_sems,
    out_sems,
):
    role, slot = table_ref[spot], table_ref[spot + 1]
    tokens, width = grad_ref.shape
    bring_saved = pltpu.make_async_copy(saved_ref.at[slot], saved_buf, in_sems.at[0])
    bring_inner = pltpu.make_async_copy(inner_ref.at[slot], inner_buf, in_sems.at[1])
    bring_entry = pltpu.make_async_copy(entries_ref.at[slot], entry_buf, in_sems.at[2])
    keep_next = pltpu.make_async_copy(grad_ref, nexts_ref.at[slot], out_sems.at[0])
    keep_grads = pltpu.make_async_copy(grads_buf, grads_ref.at[slot], out_sems.at[1])
    keep_gain = pltpu.make_async_copy(gain_buf, gains_ref.at[slot], out_sems.at[2])

    @pl.when(role == 2)
    def _():
        bring_inner.start()

    @pl.when(role == 1)
    def _():
        bring_saved.start()

    @pl.when(role > 0)
    def _():
        bring_entry.start()
        chosen(table_ref[spot + 2], candidates, grad_ref)
        keep_next.start()
        normed_buf[...] = jnp.zeros_like(normed_buf)

    @pl.when(role == 1)
    def _():
        grads_buf[:, 3 * width :] = grad_ref[...]
        mixed_buf[...] = matmul_nt(grad_ref[...], lead_ref[:, 3 * width :]).astype(LOW)
        bring_saved.wait()
        left = lax.broadcasted_iota(jnp.int32, (tokens, 128), 1) < HEAD_SIZE
        zero = jnp.zeros((tokens, 128), LOW)
        scale = HEAD_SIZE ** (-0.5)

        @pl.loop(0, HEADS // 8)
        def _(group):
            for pair in range(4):
                at = group * 512 + pair * 128
                query = saved_buf[:, lanes(at, 128)]
                key = saved_buf[:, lanes(width + at, 128)]
                value = saved_buf[:, lanes(2 * width + at, 128)]
                grad = mixed_buf[:, lanes(at, 128)]
                for own in (0, 1):
                    mine = lambda v: jnp.where(left, v, zero) if own == 0 else jnp.where(left, zero, v)
                    scores_buf[group * 8 + 2 * pair + own] = matmul_nt(mine(query), key)
                    probs_grad_buf[group * 8 + 2 * pair + own] = matmul_nt(mine(grad), value)

        @pl.loop(0, HEADS // 4)
        def _(group):
            same = same_segment(seg_row_ref[slot])
            for head in range(4):
                at = group * 4 + head
                probs = head_probs(scores_buf[at], same)
                probs_buf[at] = probs.astype(LOW)
                grad_probs = probs_grad_buf[at]
                scores_grad_buf[at] = (
                    probs * (grad_probs - jnp.sum(probs * grad_probs, axis=-1, keepdims=True))
                ).astype(LOW)

        @pl.loop(0, HEADS // 4)
        def _(group):
            for pair in range(2):
                at = group * 256 + pair * 128
                query = saved_buf[:, lanes(at, 128)]
                key = saved_buf[:, lanes(width + at, 128)]
                grad = mixed_buf[:, lanes(at, 128)]
                parts = []
                for own in (0, 1):
                    probs = probs_buf[group * 4 + 2 * pair + own]
                    grad_low = scores_grad_buf[group * 4 + 2 * pair + own]
                    parts.append(
                        (
                            matmul(grad_low, key) * scale,
                            matmul_tn(grad_low, query) * scale,
                            matmul_tn(probs, grad),
                        )
                    )
                for which in range(3):
                    grads_buf[:, lanes(which * width + at, 128)] = jnp.where(
                        left, parts[0][which], parts[1][which]
                    ).astype(LOW)

        @pl.loop(0, 3 * width // CHUNK, unroll=2)
        def _(j):
            at = lanes(j * CHUNK, CHUNK)
            normed_buf[...] += matmul_nt(grads_buf[:, at], lead_ref[:, at])

    @pl.when(role == 2)
    def _():
        bring_inner.wait()

        @pl.loop(0, lead_ref.shape[1] // CHUNK, unroll=2)
        def _(j):
            at = lanes(j * CHUNK, CHUNK)
            grad_active = matmul_nt(grad_ref[...], down_ref[pl.ds(j * CHUNK, CHUNK), :])
            grads = (gelu_slope(inner_buf[:, at]) * grad_active).astype(LOW)
            grads_buf[:, at] = grads
            normed_buf[...] += matmul_nt(grads, lead_ref[:, at])

    @pl.when(role > 0)
    def _():
        keep_grads.start()
        bring_entry.wait()
        grad_normed = normed_buf[...]
        normed, factor = layer_norm(entry_buf[...].astype(WIDE))
        gain_buf[...] = jnp.broadcast_to(
            jnp.sum(grad_normed * normed, axis=0, keepdims=True), gain_buf.shape
        )
        keep_gain.start()
        out_ref[...] = (
            grad_ref[...].astype(WIDE) + norm_back(grad_normed * gain_ref[...], normed, factor)
        ).astype(LOW)
        keep_next.wait()
        keep_grads.wait()
        keep_gain.wait()


def backward_stage(
    spot, table, nexts, seg_row, gain, lead, down, entries, saved, inner, totals
):
    tokens, width = nexts[0].shape
    count = len(nexts)
    hidden = lead.shape[1]
    return pl.pallas_call(
        functools.partial(backward_kernel, spot, count),
        out_shape=[jax.ShapeDtypeStruct((tokens, width), LOW)]
        + [jax.ShapeDtypeStruct(k.shape, k.dtype) for k in totals],
        in_specs=[SMEM_SPEC] + [VMEM_SPEC] * (count + 4) + [HBM_SPEC] * 6,
        out_specs=[VMEM_SPEC] + [HBM_SPEC] * 3,
        scratch_shapes=[
            pltpu.VMEM((tokens, hidden), LOW),
            pltpu.VMEM((tokens, hidden), WIDE),
            pltpu.VMEM((tokens, hidden), LOW),
            pltpu.VMEM((tokens, width), LOW),
            pltpu.VMEM((8, width), WIDE),
            pltpu.VMEM((tokens, width), LOW),
            pltpu.VMEM((tokens, width), WIDE),
            pltpu.VMEM((HEADS, tokens, tokens), WIDE),
            pltpu.VMEM((HEADS, tokens, tokens), WIDE),
            pltpu.VMEM((HEADS, tokens, tokens), LOW),
            pltpu.VMEM((HEADS, tokens, tokens), LOW),
            pltpu.VMEM((tokens, width), LOW),
            pltpu.SemaphoreType.DMA((3,)),
            pltpu.SemaphoreType.DMA((3,)),
        ],
        input_output_aliases={count + 8 + i: 1 + i for i in range(3)},
        compiler_params=pltpu.CompilerParams(vmem_limit_bytes=18 << 20),
        cost_estimate=pl.CostEstimate(
            flops=4 * tokens * width * hidden, bytes_accessed=20 << 20, transcendentals=0
        ),
        name="backward_stage",
    )(
        table,
        *nexts,
        seg_row,
        gain,
        pinned(lead),
        pinned(down),
        far(entries),
        far(saved),
        far(inner),
        *map(far, totals),
    )


def stats_kernel(spot, plan_ref, *refs):
    candidates, (table_ref, readout_ref, peak_ref, total_ref) = refs[:-4], refs[-4:]
    step = pl.program_id(0)

    @pl.when(step == 0)
    def _():
        chosen(plan_ref[spot], candidates, readout_ref)

    logits = matmul_nt(table_ref[...], readout_ref[...])
    own_peak = jnp.max(logits, axis=0, keepdims=True)
    own_total = lambda peak: jnp.sum(jnp.exp(logits - peak), axis=0, keepdims=True)

    @pl.when(step == 0)
    def _():
        peak_ref[...] = own_peak
        total_ref[...] = own_total(own_peak)

    @pl.when(step > 0)
    def _():
        peak = jnp.maximum(peak_ref[...], own_peak)
        total_ref[...] = total_ref[...] * jnp.exp(peak_ref[...] - peak) + own_total(peak)
        peak_ref[...] = peak


def head_stats(spot, plan, readouts, table, tile):
    tokens, emb = readouts[0].shape
    vocab = table.shape[0]
    whole = pl.BlockSpec((1, tokens), lambda i: (0, 0))
    rows = pl.BlockSpec((tokens, emb), lambda i: (0, 0))
    return pl.pallas_call(
        functools.partial(stats_kernel, spot),
        out_shape=[jax.ShapeDtypeStruct((tokens, emb), LOW)]
        + [jax.ShapeDtypeStruct((1, tokens), WIDE)] * 2,
        grid=(vocab // tile,),
        in_specs=[SMEM_SPEC]
        + [rows] * len(readouts)
        + [pl.BlockSpec((tile, emb), lambda i: (i, 0))],
        out_specs=[rows, whole, whole],
        compiler_params=pltpu.CompilerParams(vmem_limit_bytes=32 << 20),
        cost_estimate=pl.CostEstimate(
            flops=2 * tokens * vocab * emb, bytes_accessed=5 << 20, transcendentals=tokens * vocab
        ),
        name="head_stats",
    )(plan, *readouts, far(table))


def head_kernel(spot, table_base_ref, readout_ref, table_ref, logsum_ref, ids_ref, head_ref, grad_ref):
    tile = table_ref.shape[0]
    logits = matmul_nt(table_ref[...], readout_ref[...])
    ids = ids_ref[...] - (table_base_ref[spot] + pl.program_id(0) * tile)
    hits = lax.broadcasted_iota(jnp.int32, logits.shape, 0) == ids
    probs = jnp.exp(logits - logsum_ref[...])
    grads = jnp.where(hits, probs - 1.0, probs).astype(LOW)
    head = matmul(grads, readout_ref[...])
    unit = tile // 4
    for shard in range(4):
        head_ref[shard, :unit] = head[shard * unit : (shard + 1) * unit].astype(LOW)
    term = matmul_tn(grads, table_ref[...])

    @pl.when(pl.program_id(0) == 0)
    def _():
        grad_ref[...] = term

    @pl.when(pl.program_id(0) > 0)
    def _():
        grad_ref[...] += term


def head_grads(spot, base, readout, table, logsum, ids):
    tokens, emb = readout.shape
    vocab = table.shape[0]
    row = pl.BlockSpec((1, tokens), lambda i: (0, 0))
    whole = pl.BlockSpec((tokens, emb), lambda i: (0, 0))
    part = pl.BlockSpec((vocab // 4, emb), lambda i: (i, 0))
    return pl.pallas_call(
        functools.partial(head_kernel, spot),
        out_shape=[
            pltpu.HBM((16, 512, emb), LOW),
            jax.ShapeDtypeStruct((tokens, emb), WIDE),
        ],
        grid=(4,),
        in_specs=[SMEM_SPEC, whole, part, row, row],
        out_specs=[pl.BlockSpec((4, 512, emb), lambda i: (i, 0, 0)), whole],
        compiler_params=pltpu.CompilerParams(vmem_limit_bytes=32 << 20),
        cost_estimate=pl.CostEstimate(
            flops=6 * tokens * vocab * emb, bytes_accessed=9 << 20, transcendentals=tokens * vocab
        ),
        name="head_grads",
    )(base, readout, far(table), logsum, ids)


def pair_kernel(former_ref, latter_ref, out_ref):
    rows = out_ref.shape[0]
    out_ref[...] = former_ref[:rows].astype(WIDE) + latter_ref[:rows].astype(WIDE)


def pair_sum(former, latter, rows):
    return pl.pallas_call(
        pair_kernel,
        out_shape=jax.ShapeDtypeStruct((rows, former.shape[1]), WIDE),
        in_specs=[VMEM_SPEC] * 2,
        out_specs=VMEM_SPEC,
        compiler_params=pltpu.CompilerParams(vmem_limit_bytes=8 << 20),
        name="pair_sum",
    )(former, latter)


def lookup_kernel(ids_ref, table_ref, noise_ref, out_ref, total_ref, low_ref):
    step = pl.program_id(0)
    parts, tile = table_ref.shape
    tokens = ids_ref.shape[1]
    blocks = tile // 128

    @pl.when(step == 0)
    def _():
        lane = jnp.bitwise_and(ids_ref[...], 127)
        hits = lax.broadcasted_iota(jnp.int32, (128, tokens), 0) == lane
        low_ref[...] = jnp.where(hits, 1.0, 0.0).astype(LOW)
        total_ref[...] = noise_ref[...].astype(WIDE)

    stacked = jnp.concatenate(
        [table_ref[:, block * 128 : (block + 1) * 128] for block in range(blocks)]
    )
    found = matmul(stacked, low_ref[...])
    own = jnp.right_shift(ids_ref[...], 7) - step * blocks
    total = jnp.zeros_like(total_ref)
    for block in range(blocks):
        total = jnp.where(own == block, found[block * parts : (block + 1) * parts], total)
    total_ref[...] += total

    @pl.when(step == pl.num_programs(0) - 1)
    def _():
        out_ref[...] = total_ref[...].astype(LOW)


def lookup(ids, table, noise, tile):
    parts, vocab = table.shape
    tokens = ids.shape[1]
    whole = pl.BlockSpec((parts, tokens), lambda i: (0, 0))
    return pl.pallas_call(
        lookup_kernel,
        out_shape=jax.ShapeDtypeStruct((parts, tokens), LOW),
        grid=(vocab // tile,),
        in_specs=[
            pl.BlockSpec((1, tokens), lambda i: (0, 0)),
            pl.BlockSpec((parts, tile), lambda i: (0, i)),
            whole,
        ],
        out_specs=whole,
        scratch_shapes=[pltpu.VMEM((parts, tokens), WIDE), pltpu.VMEM((128, tokens), LOW)],
        compiler_params=pltpu.CompilerParams(vmem_limit_bytes=32 << 20),
        cost_estimate=pl.CostEstimate(
            flops=2 * 128 * vocab * tokens, bytes_accessed=4 << 20, transcendentals=0
        ),
        name="lookup",
    )(ids, far(table), noise)


def lead_grad_kernel(where_ref, normed_ref, mixed_ref, grads_ref, *refs):
    got_ref, (out_ref, turned_ref) = (refs[0] if len(refs) == 3 else None), refs[-2:]
    role, half, spot = where_ref[0], where_ref[1], where_ref[2]
    step = pl.program_id(0)
    width = normed_ref.shape[1]
    steps = pl.num_programs(0)
    use_mixed = jnp.logical_and(role == 1, half == 1)

    @pl.when(step == 0)
    def _():
        turned_ref[...] = normed_ref[...].T

    @pl.when(jnp.logical_and(step == steps // 2, use_mixed))
    def _():
        turned_ref[...] = mixed_ref[...].T

    result = matmul(turned_ref[...], grads_ref[...])
    unit = width // 16

    def put(block, rows, part):
        if got_ref is not None:
            part = part + got_ref[block, rows, :].astype(WIDE)
        out_ref[block, rows, :] = part.astype(LOW)

    for x in range(4):
        for y in range(4):
            part = result[(4 * x + y) * unit : (4 * x + y + 1) * unit]

            @pl.when(half == 0)
            def _():
                put((x - spot + 4) % 4, slice(y * unit, (y + 1) * unit), part)

            @pl.when(half == 1)
            def _():
                put((y - spot + 4) % 4, slice(x * unit, (x + 1) * unit), part)


def lead_grad(where, normed, saved, grads, got=None):
    tokens, width = normed.shape
    tile = 512
    blocks = pl.BlockSpec((4, width // 4, tile), lambda i, where: (0, 0, i))
    return pl.pallas_call(
        lead_grad_kernel,
        out_shape=jax.ShapeDtypeStruct((4, width // 4, 2 * width), LOW),
        grid_spec=pltpu.PrefetchScalarGridSpec(
            num_scalar_prefetch=1,
            grid=(2 * width // tile,),
            in_specs=[
                pl.BlockSpec((tokens, width), lambda i, where: (0, 0)),
                pl.BlockSpec((tokens, width), lambda i, where: (0, 3)),
                pl.BlockSpec((tokens, tile), lambda i, where: (0, where[1] * (2 * width // tile) + i)),
            ]
            + ([] if got is None else [blocks]),
            out_specs=blocks,
            scratch_shapes=[pltpu.VMEM((width, tokens), LOW)],
        ),
        compiler_params=pltpu.CompilerParams(vmem_limit_bytes=24 << 20),
        cost_estimate=pl.CostEstimate(
            flops=4 * tokens * width * width, bytes_accessed=8 << 20, transcendentals=0
        ),
        name="lead_grad",
    )(where, far(normed), far(saved), far(grads), *([] if got is None else [got]))


def down_grad_kernel(where_ref, saved_ref, nexts_ref, *refs):
    got_ref, (out_ref, buf_ref, got_buf, sems) = (refs[0] if len(refs) == 5 else None), refs[-4:]
    role, half, spot = where_ref[0], where_ref[1], where_ref[2]
    at = pl.program_id(0)
    unit = saved_ref.shape[1] // 4

    @pl.when(role == 2)
    def _():
        if got_ref is not None:
            bring = pltpu.make_async_copy(got_ref, got_buf, sems.at[1])
            pl.when(at == 0)(bring.start)
        result = matmul_tn(saved_ref[...], nexts_ref[...])
        if got_ref is not None:
            pl.when(at == 0)(bring.wait)

        def put(block, rows, part):
            if got_ref is not None:
                part = part + got_buf[block, rows, :].astype(WIDE)
            buf_ref[block, rows, :] = part.astype(LOW)

        @pl.when(half == 0)
        def _():
            put((at - spot + 4) % 4, slice(None), result)

        @pl.when(half == 1)
        def _():
            rows = pl.ds(pl.multiple_of(at * unit, unit), unit)
            for y in range(4):
                put((y - spot + 4) % 4, rows, result[y * unit : (y + 1) * unit])

        @pl.when(at == pl.num_programs(0) - 1)
        def _():
            copy = pltpu.make_async_copy(buf_ref, out_ref, sems.at[0])
            copy.start()
            copy.wait()


def down_grad(where, saved, nexts, got=None):
    tokens, hidden = saved.shape
    width = nexts.shape[1]
    rows = hidden // 8
    live = lambda where: jnp.where(where[0] == 2, 1, 0)
    small = (8, 128)
    return pl.pallas_call(
        down_grad_kernel,
        out_shape=pltpu.HBM((4, rows, width), LOW),
        grid_spec=pltpu.PrefetchScalarGridSpec(
            num_scalar_prefetch=1,
            grid=(4,),
            in_specs=[
                pl.BlockSpec((tokens, rows), lambda i, where: (0, (where[1] * 4 + i) * live(where))),
                pl.BlockSpec((tokens, width), lambda i, where: (0, 0)),
            ]
            + ([] if got is None else [HBM_SPEC]),
            out_specs=HBM_SPEC,
            scratch_shapes=[
                pltpu.VMEM((4, rows, width), LOW),
                pltpu.VMEM(small if got is None else (4, rows, width), LOW),
                pltpu.SemaphoreType.DMA((2,)),
            ],
        ),
        compiler_params=pltpu.CompilerParams(vmem_limit_bytes=28 << 20),
        cost_estimate=pl.CostEstimate(
            flops=2 * tokens * width * hidden // 2, bytes_accessed=8 << 20, transcendentals=0
        ),
        name="down_grad",
    )(where, far(saved), far(nexts), *([] if got is None else [far(got)]))


def upper_kernel(where_ref, *refs):
    out_ref = refs[4]
    rows = refs[0].shape[0]
    for at, part in enumerate(refs[:4]):
        place = (where_ref[0] - at + 4) % 4
        out_ref[pl.ds(pl.multiple_of(place * rows, rows), rows), :] = part[...]


def upper_half(where, parts):
    rows, width = parts[0].shape
    return pl.pallas_call(
        upper_kernel,
        out_shape=jax.ShapeDtypeStruct((4 * rows, width), LOW),
        in_specs=[SMEM_SPEC] + [VMEM_SPEC] * 4,
        out_specs=VMEM_SPEC,
        compiler_params=pltpu.CompilerParams(vmem_limit_bytes=8 << 20),
        name="upper_half",
    )(where, *parts)


def hold_down_kernel(where_ref, mine_ref, other_ref, own_ref, out_ref, sems):
    rows = mine_ref.shape[0]
    core = where_ref[1]
    spot = lambda at: out_ref.at[pl.ds(pl.multiple_of(at * rows, rows), rows), :]
    copies = [
        pltpu.make_async_copy(mine_ref, spot(core), sems.at[0]),
        pltpu.make_async_copy(other_ref, spot(1 - core), sems.at[1]),
        pltpu.make_async_copy(own_ref, out_ref.at[pl.ds(2 * rows, 2 * rows), :], sems.at[2]),
    ]
    for copy in copies:
        copy.start()
    for copy in copies:
        copy.wait()


def hold_down(where, mine, other, own):
    rows, width = mine.shape
    return pl.pallas_call(
        hold_down_kernel,
        out_shape=pltpu.VMEM((4 * rows, width), LOW),
        in_specs=[SMEM_SPEC] + [VMEM_SPEC] * 2 + [HBM_SPEC],
        out_specs=VMEM_SPEC,
        scratch_shapes=[pltpu.SemaphoreType.DMA((3,))],
        compiler_params=pltpu.CompilerParams(vmem_limit_bytes=8 << 20),
        name="hold_down",
    )(where, mine, other, far(own))


def noise_kernel(spot, plan_ref, ids_ref, *refs):
    candidates, (packed_ref, noise_ref, buf_ref) = refs[:-3], refs[-3:]
    parts = noise_ref.shape[0]
    chosen(plan_ref[spot], candidates, buf_ref)
    packed_ref[:parts] = buf_ref[...]
    noise_ref[...] = buf_ref[...].astype(WIDE)
    ids = ids_ref[...]
    high = jnp.right_shift(ids, 8).astype(WIDE)
    low = jnp.bitwise_and(ids, 255).astype(WIDE)
    at = lax.broadcasted_iota(jnp.int32, (16, ids.shape[1]), 0)
    split = jnp.where(at == 0, high, jnp.where(at == 1, low, 0.0))
    packed_ref[parts:] = split.astype(LOW)


def noise_pack(spot, plan, ids, candidates):
    parts, tokens = candidates[0].shape
    return pl.pallas_call(
        functools.partial(noise_kernel, spot),
        out_shape=[
            jax.ShapeDtypeStruct((parts + 16, tokens), LOW),
            jax.ShapeDtypeStruct((parts, tokens), WIDE),
        ],
        in_specs=[SMEM_SPEC] + [VMEM_SPEC] * (1 + len(candidates)),
        out_specs=[VMEM_SPEC] * 2,
        scratch_shapes=[pltpu.VMEM((parts, tokens), LOW)],
        compiler_params=pltpu.CompilerParams(vmem_limit_bytes=8 << 20),
        name="noise_pack",
    )(plan, ids, *candidates)


def embed_kernel(base_ref, mine_ref, other_ref, out_ref, total_ref):
    step = pl.program_id(0)
    steps = pl.num_programs(0)
    parts = out_ref.shape[0]
    blocks = total_ref.shape[0] // parts

    def add(gathered_ref):
        count, _, tokens = gathered_ref.shape
        term = None
        for at in range(count):
            split = gathered_ref[at, parts : parts + 16].astype(WIDE)
            ids = (split[0:1] * 256.0 + split[1:2]).astype(jnp.int32) - base_ref[0]
            lane = jnp.bitwise_and(ids, 127)
            hits = lax.broadcasted_iota(jnp.int32, (128, tokens), 0) == lane
            hits = jnp.where(hits, 1.0, 0.0).astype(LOW)
            own = jnp.right_shift(ids, 7)
            grads = gathered_ref[at, :parts]
            masked = jnp.concatenate(
                [grads * jnp.where(own == block, 1.0, 0.0).astype(LOW) for block in range(blocks)]
            )
            part = matmul_nt(masked, hits)
            term = part if term is None else term + part

        @pl.when(step == 0)
        def _():
            total_ref[...] = term

        @pl.when(step > 0)
        def _():
            total_ref[...] += term

    pl.when(step < steps // 2)(lambda: add(mine_ref))
    pl.when(step >= steps // 2)(lambda: add(other_ref))

    @pl.when(step == steps - 1)
    def _():
        rows = out_ref.shape[1]
        for block in range(blocks):
            size = min(128, rows - block * 128)
            out_ref[:, block * 128 : block * 128 + size] = total_ref[
                block * parts : (block + 1) * parts, :size
            ]


def embed_sum(base, mine, other, parts, rows):
    count, deep, tokens = mine.shape
    step = 4
    half = count // step
    blocks = -(-rows // 128)
    return pl.pallas_call(
        embed_kernel,
        out_shape=jax.ShapeDtypeStruct((parts, rows), WIDE),
        grid=(2 * half,),
        in_specs=[
            SMEM_SPEC,
            pl.BlockSpec((step, deep, tokens), lambda i: (jnp.minimum(i, half - 1), 0, 0)),
            pl.BlockSpec((step, deep, tokens), lambda i: (jnp.maximum(i - half, 0), 0, 0)),
        ],
        out_specs=pl.BlockSpec((parts, rows), lambda i: (0, 0)),
        scratch_shapes=[pltpu.VMEM((blocks * parts, 128), WIDE)],
        compiler_params=pltpu.CompilerParams(vmem_limit_bytes=32 << 20),
        cost_estimate=pl.CostEstimate(
            flops=tokens * parts, bytes_accessed=1 << 16, transcendentals=0
        ),
        name="embed_sum",
    )(base, mine, other)


def empty(*kinds):
    return pl.pallas_call(
        lambda *refs: None,
        out_shape=[pltpu.HBM(shape, dtype) for shape, dtype in kinds],
        out_specs=[HBM_SPEC] * len(kinds),
        compiler_params=pltpu.CompilerParams(vmem_limit_bytes=1 << 20),
        name="empty",
    )()


ROW_LEN = 128
SEC, GRP, NX, NY = 4, 2, 4, 4
ALL = ("section", "group", "row")
TURNS = (1, 3, 2)


def route(value, target_of):
    number = lambda s, g, x, y: (s * GRP + g) * NX * NY + x * NY + y
    pairs = []
    for at in itertools.product(range(SEC), range(GRP), range(NX), range(NY)):
        target = target_of(*at)
        if target is not None:
            pairs.append((number(*at), number(*target)))
    return lax.ppermute(value, ALL, pairs)


def link(value, source, target):
    return route(value, lambda s, g, x, y: (target, g, x, y) if s == source else None)


def turn(value, by):
    return route(value, lambda s, g, x, y: ((s + by) % SEC, g, x, y))


def swap_cores(value, sections=range(SEC)):
    return route(value, lambda s, g, x, y: (s, 1 - g, x, y) if s in sections else None)


def plane_route(value, by, first, sections=range(SEC)):
    def target_of(s, g, x, y):
        if s not in sections:
            return None
        if (g == 0) == first:
            return (s, g, (x + by) % NX, y)
        return (s, g, x, (y + by) % NY)

    return route(value, target_of)


def after(value, earlier):
    return lax.optimization_barrier((value, earlier))[0]


def row_block(values, block, count):
    size = values.shape[0] // count
    return lax.dynamic_slice_in_dim(values, block * size, size, 0)


def plane_first(mine, sections=range(SEC)):
    return [mine[0]] + [plane_route(mine[by], by, True, sections) for by in TURNS]


def plane_sum(pieces):
    total = pieces[0].astype(WIDE)
    for piece in pieces[1:]:
        total = total + piece.astype(WIDE)
    return total.astype(LOW)


def plane_second(pieces, second, sections=range(SEC)):
    total = plane_sum(pieces)
    return [row_block(total, second, 4)] + [
        plane_route(row_block(total, (second + by) % 4, 4), by, False, sections) for by in TURNS
    ]


def group_exchange(values, first):
    number = lambda s, g, x, y: (s * GRP + g) * NX * NY + x * NY + y
    groups = []
    for s in range(SEC):
        for g in range(GRP):
            along_x = (g == 0) == first
            for at in range(4):
                groups.append(
                    [number(s, g, i, at) if along_x else number(s, g, at, i) for i in range(4)]
                )
    return lax.all_to_all(values, ALL, 0, 0, axis_index_groups=groups, tiled=True)


def section_exchange(values):
    return lax.all_to_all(values, "section", 0, 0, tiled=True)


def plans(micro, vocab_part):
    last = SEC - 1
    steps = micro + 2 * last
    table = np.zeros((SEC, 6 * steps + 2), np.int32)
    for s in range(SEC):
        for way in range(2):
            depth = s if way == 0 else last - s
            for step in range(steps):
                at = step - 2 * depth
                if 0 <= at < micro:
                    sources = ([0] if step < micro else []) + [
                        d + 1 for d in range(last) if 0 <= step - 2 - 2 * d < micro
                    ]
                    spot = 3 * (way * steps + step)
                    table[s, spot : spot + 3] = (1 + s % 2, at, sources.index(depth))
        table[s, 6 * steps :] = (s * vocab_part, s)
    return table


def local(
    token_ids,
    segment_ids,
    noise_input,
    embed_table,
    input_proj,
    norm_gain,
    lead_weight,
    down_weight,
    final_gain,
    readout_proj,
    head_table,
):
    section = lax.axis_index("section")
    core = lax.axis_index("group")
    row = lax.axis_index("row")
    x_at, y_at = row // NY, row % NY
    first_at = jnp.where(core == 0, x_at, y_at)
    micro, _, tokens = token_ids.shape
    width = input_proj.shape[1]
    hidden = lead_weight.shape[2]
    half_rows = down_weight.shape[1]
    emb_part = input_proj.shape[0]
    vocab_part, emb = head_table.shape
    vocab = embed_table.shape[0]
    all_tokens = micro * tokens
    last = SEC - 1
    gain_half = norm_gain.astype(WIDE)
    lead = lead_weight[0]
    own_down = down_weight[0]
    seg_row = segment_ids
    flat_ids = token_ids.reshape(-1)

    plan = plans(micro, vocab_part)
    steps = micro + 2 * last
    table = lax.dynamic_index_in_dim(jnp.asarray(plan), section, 0, False)
    flat_ids = after(flat_ids, table)
    where_start = jnp.stack((first_at, core)).astype(jnp.int32)
    to_first = lambda v: [v] + [link(v, s, 0) for s in range(1, SEC)]
    eighth = row_block(row_block(own_down, core, 2), first_at, 4)
    eighth = jnp.where(section == 1, link(eighth, 0, 1), link(eighth, 2, 3))
    noise = noise_input[:, 0].transpose(2, 0, 1).reshape(emb_part, -1)
    own_embedded = lookup(flat_ids[None], embed_table.T, noise, 3200)
    parts = to_first(jnp.concatenate((own_embedded, input_proj), axis=1))
    embedded = jnp.concatenate([part[:, :all_tokens] for part in parts])
    input_full = jnp.concatenate([part[:, all_tokens:] for part in parts])
    first_in = matmul_tn(embedded, input_full).astype(LOW).reshape(micro, tokens, width)
    eighth = after(eighth, own_embedded)
    eighths = [eighth] + [plane_route(eighth, by, True) for by in (1, 2, 3)]
    upper = upper_half(where_start, [after(part, first_in) for part in eighths])
    held_down = hold_down(where_start, upper, swap_cores(upper), own_down)

    kept = empty(
        ((micro, tokens, width), LOW),
        ((micro, tokens, width), LOW),
        ((micro, tokens, hidden), LOW),
        ((micro, tokens, hidden), WIDE),
    )

    def sources(first, step, hops, order):
        arrived = [hops[step - 2, s] for s in order if (step - 2, s) in hops]
        return ([first[step]] if step < micro else []) + arrived

    outs, hops = [], {}
    for step in range(steps):
        out, *kept = forward_stage(
            3 * step,
            table,
            sources(first_in, step, hops, range(SEC)),
            seg_row,
            gain_half,
            held_lead if step > 0 else lead,
            held_down if step > 1 else None,
            kept,
            step == 0,
        )
        if step == 0:
            held_lead = kept.pop()
        outs.append(out)
        for s in range(last):
            if 0 <= step - 2 * s < micro:
                ready = after(out, hops[step - 1, s]) if (step - 1, s) in hops else out
                hops[step, s] = link(ready, s, s + 1)
        if step == 2:
            readout_own = after(readout_proj.T, out)
            readout_full = jnp.concatenate(
                [link(readout_own, s, last) for s in range(last)] + [readout_own]
            )
    entries, normeds, saved, inner = kept

    final_rows = jnp.concatenate(outs[2 * last :]).astype(WIDE)
    normed_f, factor_f = layer_norm(final_rows)
    gain_f = final_gain.astype(WIDE)
    final_low = (normed_f * gain_f).astype(LOW)
    readout = matmul_nt(final_low, readout_full).astype(LOW)
    sent = [link(readout, last, s) for s in range(last)]
    readout, peak, total = head_stats(6 * steps + 1, table, sent + [readout], head_table, 2000)
    stats = jnp.concatenate((peak, total))
    all_stats = section_exchange(jnp.tile(stats, (SEC, 1))).reshape(SEC, 2, all_tokens)
    peak = jnp.max(all_stats[:, 0], axis=0)
    total = jnp.sum(all_stats[:, 1] * jnp.exp(all_stats[:, 0] - peak), axis=0)
    logsum = (peak + jnp.log(total))[None]
    head_grad, grad_readout = head_grads(
        6 * steps, table, readout, head_table, logsum, flat_ids[None]
    )
    grad_low = grad_readout.astype(LOW)
    for s in range(last):
        grad_readout = grad_readout + link(grad_low, s, last).astype(WIDE)
    grad_readout = grad_readout.astype(LOW)
    head_grad = lax.psum_scatter(head_grad, "row", scatter_dimension=0)
    readout_grad = matmul_tn(final_low, grad_readout)
    grad_final = matmul(grad_readout, readout_full)
    final_gain_grad = jnp.sum(grad_final * normed_f, axis=0)
    last_grads = norm_back(grad_final * gain_f, normed_f, factor_f).astype(LOW)
    last_grads = last_grads.reshape(micro, tokens, width)

    totals = empty(
        ((micro, tokens, width), LOW),
        ((micro, tokens, hidden), LOW),
        ((micro, 8, width), WIDE),
    )
    outs, hops = [], {}
    for step in range(steps):
        out, *totals = backward_stage(
            3 * (steps + step),
            table,
            sources(last_grads, step, hops, range(SEC - 1, -1, -1)),
            seg_row,
            gain_half,
            held_lead,
            held_down,
            entries,
            saved,
            inner,
            totals,
        )
        outs.append(out)
        for s in range(1, SEC):
            if 0 <= step - 2 * (last - s) < micro:
                ready = after(out, hops[step - 1, s]) if (step - 1, s) in hops else out
                hops[step, s] = link(ready, s, s - 1)
    section, core, row = lax.optimization_barrier((section, core, row, out))[:3]
    x_at, y_at = row // NY, row % NY
    first_at, second_at = jnp.where(core == 0, x_at, y_at), jnp.where(core == 0, y_at, x_at)
    is_mlp = section % 2 == 1

    first_grads = jnp.concatenate(outs[2 * last :])
    noise_grad = matmul_nt(input_full, first_grads).astype(LOW)
    pieces = noise_grad.reshape(SEC, emb_part, all_tokens)
    sent = [link(pieces[s], 0, s) for s in range(1, SEC)]

    grad_nexts, grads, gain_grads = totals
    gain_grad = jnp.sum(gain_grads[:, 0], axis=0)
    flat = lambda v: v.reshape(all_tokens, v.shape[-1])
    grads = after(grads, head_grad)
    normed, grad_nexts, grads, saved = flat(normeds), flat(grad_nexts), flat(grads), flat(saved)
    odd = (1, 3)
    role = jnp.where(is_mlp, 2, 1)
    where_other = jnp.stack((role, 1 - core, second_at)).astype(jnp.int32)
    where_mine = jnp.stack((role, core, first_at)).astype(jnp.int32)
    both = lambda mine, other: jnp.where(
        core == 0,
        jnp.concatenate((mine, other), axis=1),
        jnp.concatenate((other, mine), axis=1),
    )
    down_got = swap_cores(down_grad(where_other, saved, grad_nexts), odd)
    lead_got = swap_cores(lead_grad(where_other, normed, saved, grads))
    down_mine = down_grad(where_mine, saved, grad_nexts, down_got)
    down_first = plane_first(down_mine, odd)

    input_grad = matmul(embedded, first_grads).reshape(SEC, 16, 4, width)
    input_grad = input_grad.transpose(1, 0, 2, 3).reshape(16, 16, width)
    readout_grad = readout_grad.reshape(16, 16, width)
    vectors = jnp.concatenate(
        (
            gain_grad.reshape(16, 64),
            final_gain_grad.reshape(SEC, 16, 16).transpose(1, 0, 2).reshape(16, 64),
            jnp.zeros((16, width - 128), WIDE),
        ),
        axis=1,
    )
    small = jnp.concatenate(
        (
            jnp.where(section == 0, input_grad, readout_grad),
            vectors[:, None],
            jnp.zeros((16, 15, width), WIDE),
        ),
        axis=1,
    ).astype(LOW)
    late_ids = after(flat_ids, down_mine)[None]
    packed, noise_wide = noise_pack(6 * steps + 1, table, late_ids, [pieces[0]] + sent)
    half_of = lambda which: lax.dynamic_slice_in_dim(small, which * (width // 2), width // 2, 2)
    small = half_of(core).astype(WIDE) + swap_cores(half_of(1 - core)).astype(WIDE)
    small = small.astype(LOW).reshape(NX, NY, 32, width // 2)
    small = jnp.where(core == 0, small, small.swapaxes(0, 1)).reshape(4, NY * 32, width // 2)
    deep = emb_part + 16

    def exchange(blocks, packed, first):
        rows = blocks.shape[1]
        everywhere = jnp.broadcast_to(packed, (4,) + packed.shape)
        got = group_exchange(jnp.concatenate((blocks, everywhere), axis=1), first)
        return jnp.sum(got[:, :rows].astype(WIDE), axis=0).astype(LOW), got[:, rows:]

    small, packed = exchange(small, packed, True)
    lead_mine = lead_grad(after(where_mine, packed), normed, saved, grads, lead_got)
    lead_first = plane_first(lead_mine)
    packed = after(packed, lead_mine)
    small, packed = exchange(
        small.reshape(4, 32, width // 2), packed.reshape(4 * deep, all_tokens), False
    )
    packed = packed.reshape(16, deep, all_tokens)
    packed_other = swap_cores(packed)
    small = both(small, swap_cores(small))
    embed_grad = embed_sum(
        (row * (vocab // 16)).reshape(1), packed, packed_other, emb_part, vocab // 16
    )
    down_second = plane_second(after(down_first, packed), second_at, odd)
    lead_second = plane_second(after(lead_first, packed), second_at)
    down_part = plane_sum(after(down_second, embed_grad))
    lead_part = plane_sum(after(lead_second, embed_grad))
    noise_out = noise_wide.reshape(emb_part, micro, tokens).transpose(1, 2, 0)
    lead_out = both(lead_part, swap_cores(lead_part)).astype(WIDE)

    def first_target(s, g, x, y):
        if s % 2 == 0:
            return None
        return (s - 1, 0, x, y) if g == 0 else (s, 0, x, y)

    def second_target(s, g, x, y):
        return (s - 1, 1, x, y) if s % 2 == 1 and g == 0 else None

    to_core_0 = route(down_part, first_target)
    to_core_1 = route(down_part, second_target)
    down_out = jnp.where(
        core == 0, to_core_0, jnp.where(is_mlp, down_part, to_core_1)
    ).astype(WIDE)

    small = after(small, (lead_part, down_part))
    gain_out = small[16, :64].astype(WIDE)
    input_rows = small[:16].reshape(SEC, 4, width)
    readout_rows = small[:16].reshape(64, SEC, 64)
    final_rows = small[16, 64:128].reshape(SEC, 16)

    finals = jnp.pad(final_rows, ((0, 0), (0, width - 16)))[:, None]
    mine = jnp.where(
        section == 0, input_rows, readout_rows.transpose(1, 0, 2).reshape(SEC, 4, width)
    )
    shared = section_exchange(
        jnp.concatenate((mine, finals, jnp.zeros((SEC, 3, width), LOW)), axis=1)
    )
    input_out = shared[0, :4]
    readout_out = shared[last, :4].reshape(64, 64)
    final_out = shared[last, 4, :16]

    head_out = pair_sum(head_grad, swap_cores(head_grad), vocab_part // (NX * NY))
    return (
        noise_out[:, None],
        embed_grad.T,
        input_out.astype(WIDE),
        gain_out[None],
        lead_out[None],
        down_out[None],
        final_out.astype(WIDE),
        readout_out.astype(WIDE),
        head_out,
    )


def solution(mesh):
    in_specs = (
        P(None, ("group", "row"), None),
        P(None, ("group", "row"), None),
        P(None, ("group", "row"), None, "section"),
        P(None, "section"),
        P("section", None),
        P("section", None),
        P("section", None, None),
        P("section", None, None),
        P(),
        P(None, "section"),
        P("section", None),
    )
    out_specs = (
        P(None, ("group", "row"), None, "section"),
        P("row", "section"),
        P(("section", "row"), None),
        P("section", "row"),
        P("section", "row", None),
        P("section", "row", None),
        P(("section", "row")),
        P("row", "section"),
        P(("section", "row"), None),
    )
    return jax.shard_map(local, mesh=mesh, in_specs=in_specs, out_specs=out_specs, check_vma=False)
```

```python
import functools
import itertools

import jax
import jax.numpy as jnp
import numpy as np
from jax import lax
from jax.experimental import pallas as pl
from jax.experimental.pallas import tpu as pltpu
from jax.sharding import PartitionSpec as P

HEADS = 16
HEAD_SIZE = 64
LOW = jnp.bfloat16
WIDE = jnp.float32
EPSILON = 1e-05
MASKED = -1000000000.0
CHUNK = 1024
GELU_A = 0.7978845608028654
GELU_B = 0.044715
HBM_SPEC = pl.BlockSpec(memory_space=pltpu.HBM)
VMEM_SPEC = pl.BlockSpec(memory_space=pltpu.VMEM)
SMEM_SPEC = pl.BlockSpec(memory_space=pltpu.SMEM)


def matmul(former, latter):
    return jnp.dot(former, latter, preferred_element_type=WIDE)


def matmul_nt(former, latter):
    return lax.dot_general(
        former, latter, (((1,), (1,)), ((), ())), preferred_element_type=WIDE
    )


def matmul_tn(former, latter):
    return lax.dot_general(
        former, latter, (((0,), (0,)), ((), ())), preferred_element_type=WIDE
    )


def layer_norm(values):
    centre = jnp.mean(values, axis=-1, keepdims=True)
    centred = values - centre
    variance = jnp.mean(centred * centred, axis=-1, keepdims=True)
    factor = lax.rsqrt(variance + EPSILON)
    return (centred * factor, factor)


def norm_back(grad_normed, normed, factor):
    first_mean = jnp.mean(grad_normed, axis=-1, keepdims=True)
    second_mean = jnp.mean(grad_normed * normed, axis=-1, keepdims=True)
    return factor * (grad_normed - first_mean - normed * second_mean)


def gelu(v):
    return 0.5 * v * (1.0 + jnp.tanh(GELU_A * (v + GELU_B * (v * v * v))))


def gelu_slope(v):
    square = v * v
    bend = jnp.tanh(GELU_A * (v + GELU_B * (square * v)))
    return 0.5 * (1.0 + bend) + 0.5 * v * (1.0 - bend * bend) * (
        GELU_A * (1.0 + 3.0 * GELU_B * square)
    )


def head_probs(scores, same):
    scores = jnp.where(same, scores * HEAD_SIZE ** (-0.5), MASKED)
    expo = jnp.exp(scores - jnp.max(scores, axis=-1, keepdims=True))
    return expo * (1.0 / jnp.sum(expo, axis=-1, keepdims=True))


def same_segment(row):
    across = jnp.broadcast_to(row.astype(WIDE), (row.shape[1], row.shape[1]))
    return across.T == across


def lanes(at, size):
    return pl.ds(pl.multiple_of(at, 128), size)


def turn_kernel(spot, live, plan_ref, value_ref, out_ref):
    @pl.when(jnp.bitwise_and(plan_ref[spot], 1) >= live)
    def _():
        out_ref[...] = value_ref[...].T


def turned(spot, plan, value, live):
    rows, columns = value.shape
    if rows > columns:
        tile = rows // 8
        blocks = (pl.BlockSpec((tile, columns), lambda i: (i, 0)), pl.BlockSpec((columns, tile), lambda i: (0, i)))
    else:
        tile = columns // 8
        blocks = (pl.BlockSpec((rows, tile), lambda i: (0, i)), pl.BlockSpec((tile, rows), lambda i: (i, 0)))
    return pl.pallas_call(
        functools.partial(turn_kernel, spot, live),
        out_shape=pltpu.VMEM((columns, rows), LOW),
        grid=(8,),
        in_specs=[SMEM_SPEC, blocks[0]],
        out_specs=blocks[1],
        compiler_params=pltpu.CompilerParams(vmem_limit_bytes=12 << 20),
        cost_estimate=pl.CostEstimate(flops=0, bytes_accessed=1024, transcendentals=0),
        name="turned",
    )(plan, far(value))


def chosen(choice, candidates, buffer):
    for at, candidate in enumerate(candidates):

        @pl.when(choice == at)
        def _():
            buffer[...] = candidate[...]


def forward_kernel(spot, with_down, loads, count, *refs):
    table_ref, candidates, refs = refs[0], refs[1 : 1 + count], refs[1 + count :]
    if not with_down:
        refs = refs[:3] + (None,) + refs[3:]
    source_ref = load_sems = None
    if loads:
        source_ref, load_sems = refs[2], refs[-1]
        refs = refs[:2] + (refs[13],) + refs[3:13] + refs[14:-1]
    forward_body(spot, table_ref, candidates, source_ref, load_sems, *refs)


def forward_body(
    spot,
    table_ref,
    candidates,
    source_ref,
    load_sems,
    seg_row_ref,
    gain_ref,
    lead_ref,
    down_ref,
    entries_in,
    normeds_in,
    saved_in,
    inner_in,
    out_ref,
    entries_ref,
    normeds_ref,
    saved_ref,
    inner_ref,
    normed_buf,
    saved_buf,
    inner_buf,
    result_buf,
    scores_buf,
    probs_buf,
    entry_ref,
    out_sems,
):
    role, slot = table_ref[spot], table_ref[spot + 1]
    tokens, width = entry_ref.shape
    keeps = [
        pltpu.make_async_copy(entry_ref, entries_ref.at[slot], out_sems.at[0]),
        pltpu.make_async_copy(normed_buf, normeds_ref.at[slot], out_sems.at[1]),
        pltpu.make_async_copy(saved_buf, saved_ref.at[slot], out_sems.at[2]),
    ]
    keep_inner = pltpu.make_async_copy(inner_buf, inner_ref.at[slot], out_sems.at[3])

    def load(j):
        at = lanes(j * CHUNK, CHUNK)
        return pltpu.make_async_copy(source_ref.at[:, at], lead_ref.at[:, at], load_sems.at[j])

    def loaded(j):
        if source_ref is not None:
            load(j).wait()

    if source_ref is not None:
        for j in range(lead_ref.shape[1] // CHUNK):
            load(j).start()

        @pl.when(role != 1)
        def _():
            pl.loop(0, lead_ref.shape[1] // CHUNK)(loaded)

    @pl.when(role > 0)
    def _():
        chosen(table_ref[spot + 2], candidates, entry_ref)
        normed, _ = layer_norm(entry_ref[...].astype(WIDE))
        normed_buf[...] = (normed * gain_ref[...]).astype(LOW)
        keeps[0].start()
        keeps[1].start()

    @pl.when(role == 1)
    def _():
        @pl.loop(0, 3 * width // CHUNK, unroll=2)
        def _(j):
            at = lanes(j * CHUNK, CHUNK)
            loaded(j)
            saved_buf[:, at] = matmul(normed_buf[...], lead_ref[:, at]).astype(LOW)

        left = lax.broadcasted_iota(jnp.int32, (tokens, 128), 1) < HEAD_SIZE
        zero = jnp.zeros((tokens, 128), LOW)

        @pl.loop(0, HEADS // 8)
        def _(group):
            for pair in range(4):
                at = group * 512 + pair * 128
                query = saved_buf[:, lanes(at, 128)]
                key = saved_buf[:, lanes(width + at, 128)]
                scores_buf[group * 8 + 2 * pair] = matmul_nt(jnp.where(left, query, zero), key)
                scores_buf[group * 8 + 2 * pair + 1] = matmul_nt(jnp.where(left, zero, query), key)

        @pl.loop(0, HEADS // 4)
        def _(group):
            same = same_segment(seg_row_ref[slot])
            for head in range(4):
                at = group * 4 + head
                probs_buf[at] = head_probs(scores_buf[at], same).astype(LOW)

        @pl.loop(0, HEADS // 8)
        def _(group):
            for pair in range(4):
                at = group * 512 + pair * 128
                value = saved_buf[:, lanes(2 * width + at, 128)]
                mixed = jnp.where(
                    left,
                    matmul(probs_buf[group * 8 + 2 * pair], value),
                    matmul(probs_buf[group * 8 + 2 * pair + 1], value),
                )
                saved_buf[:, lanes(3 * width + at, 128)] = mixed.astype(LOW)

        keeps[2].start()

        @pl.loop(0, width // CHUNK)
        def _(j):
            at = lanes(j * CHUNK, CHUNK)
            loaded(3 * width // CHUNK + j)
            term = matmul(saved_buf[:, 3 * width :], lead_ref[:, lanes(3 * width + j * CHUNK, CHUNK)])
            out_ref[:, at] = (entry_ref[:, at].astype(WIDE) + term).astype(LOW)

    def feed_forward():
        result_buf[...] = entry_ref[...].astype(WIDE)

        @pl.loop(0, lead_ref.shape[1] // CHUNK, unroll=2)
        def _(j):
            at = lanes(j * CHUNK, CHUNK)
            inner = matmul(normed_buf[...], lead_ref[:, at])
            inner_buf[:, at] = inner
            active = gelu(inner).astype(LOW)
            saved_buf[:, at] = active
            result_buf[...] += matmul(active, down_ref[pl.ds(j * CHUNK, CHUNK), :])

        keeps[2].start()
        keep_inner.start()
        out_ref[...] = result_buf[...].astype(LOW)
        keep_inner.wait()

    if down_ref is not None:
        pl.when(role == 2)(feed_forward)

    @pl.when(role > 0)
    def _():
        for keep in keeps:
            keep.wait()


def pinned(value):
    return pltpu.with_memory_space_constraint(value, pltpu.VMEM)


def far(value):
    return pltpu.with_memory_space_constraint(value, pltpu.HBM)


def forward_stage(spot, table, entries, seg_row, gain, lead, down, kept, loads=False):
    tokens, width = entries[0].shape
    hidden = lead.shape[1]
    count = len(entries) + (3 if down is None else 4)
    given = [VMEM_SPEC] * (len(entries) + 2) + [HBM_SPEC if loads else VMEM_SPEC]
    return pl.pallas_call(
        functools.partial(forward_kernel, spot, down is not None, loads, len(entries)),
        out_shape=[jax.ShapeDtypeStruct((tokens, width), LOW)]
        + [jax.ShapeDtypeStruct(k.shape, k.dtype) for k in kept]
        + ([pltpu.VMEM(lead.shape, LOW)] if loads else []),
        in_specs=[SMEM_SPEC] + given + [VMEM_SPEC] * (down is not None) + [HBM_SPEC] * 4,
        out_specs=[VMEM_SPEC] + [HBM_SPEC] * 4 + [VMEM_SPEC] * loads,
        scratch_shapes=[
            pltpu.VMEM((tokens, width), LOW),
            pltpu.VMEM((tokens, hidden), LOW),
            pltpu.VMEM((tokens, hidden), WIDE),
            pltpu.VMEM((tokens, width), WIDE),
            pltpu.VMEM((HEADS, tokens, tokens), WIDE),
            pltpu.VMEM((HEADS, tokens, tokens), LOW),
            pltpu.VMEM((tokens, width), LOW),
            pltpu.SemaphoreType.DMA((4,)),
        ]
        + ([pltpu.SemaphoreType.DMA((hidden // CHUNK,))] if loads else []),
        input_output_aliases={count + 1 + i: 1 + i for i in range(4)},
        compiler_params=pltpu.CompilerParams(vmem_limit_bytes=18 << 20),
        cost_estimate=pl.CostEstimate(
            flops=4 * tokens * width * hidden, bytes_accessed=20 << 20, transcendentals=0
        ),
        name="forward_stage",
    )(
        table,
        *entries,
        seg_row,
        gain,
        (far if loads else pinned)(lead),
        *([pinned(down)] if down is not None else []),
        *map(far, kept),
    )


def backward_kernel(spot, count, *refs):
    backward_body(spot, refs[0], refs[1 : 1 + count], *refs[1 + count :])


def backward_body(
    spot,
    table_ref,
    candidates,
    seg_row_ref,
    gain_ref,
    lead_ref,
    down_ref,
    entries_ref,
    saved_ref,
    inner_ref,
    nexts_in,
    grads_in,
    gains_in,
    out_ref,
    nexts_ref,
    grads_ref,
    gains_ref,
    saved_buf,
    inner_buf,
    grads_buf,
    mixed_buf,
    gain_buf,
    entry_buf,
    normed_buf,
    scores_buf,
    probs_grad_buf,
    probs_buf,
    scores_grad_buf,
    grad_ref,
    in_sems,
    out_sems,
):
    role, slot = table_ref[spot], table_ref[spot + 1]
    tokens, width = grad_ref.shape
    bring_saved = pltpu.make_async_copy(saved_ref.at[slot], saved_buf, in_sems.at[0])
    bring_inner = pltpu.make_async_copy(inner_ref.at[slot], inner_buf, in_sems.at[1])
    bring_entry = pltpu.make_async_copy(entries_ref.at[slot], entry_buf, in_sems.at[2])
    keep_next = pltpu.make_async_copy(grad_ref, nexts_ref.at[slot], out_sems.at[0])
    keep_grads = pltpu.make_async_copy(grads_buf, grads_ref.at[slot], out_sems.at[1])
    keep_gain = pltpu.make_async_copy(gain_buf, gains_ref.at[slot], out_sems.at[2])

    @pl.when(role == 2)
    def _():
        bring_inner.start()

    @pl.when(role == 1)
    def _():
        bring_saved.start()

    @pl.when(role > 0)
    def _():
        bring_entry.start()
        chosen(table_ref[spot + 2], candidates, grad_ref)
        keep_next.start()
        normed_buf[...] = jnp.zeros_like(normed_buf)

    @pl.when(role == 1)
    def _():
        grads_buf[:, 3 * width :] = grad_ref[...]
        mixed_buf[...] = matmul(grad_ref[...], lead_ref[3 * width :, :]).astype(LOW)
        bring_saved.wait()
        left = lax.broadcasted_iota(jnp.int32, (tokens, 128), 1) < HEAD_SIZE
        zero = jnp.zeros((tokens, 128), LOW)
        scale = HEAD_SIZE ** (-0.5)

        @pl.loop(0, HEADS // 8)
        def _(group):
            for pair in range(4):
                at = group * 512 + pair * 128
                query = saved_buf[:, lanes(at, 128)]
                key = saved_buf[:, lanes(width + at, 128)]
                value = saved_buf[:, lanes(2 * width + at, 128)]
                grad = mixed_buf[:, lanes(at, 128)]
                for own in (0, 1):
                    mine = lambda v: jnp.where(left, v, zero) if own == 0 else jnp.where(left, zero, v)
                    scores_buf[group * 8 + 2 * pair + own] = matmul_nt(mine(query), key)
                    probs_grad_buf[group * 8 + 2 * pair + own] = matmul_nt(mine(grad), value)

        @pl.loop(0, HEADS // 4)
        def _(group):
            same = same_segment(seg_row_ref[slot])
            for head in range(4):
                at = group * 4 + head
                probs = head_probs(scores_buf[at], same)
                probs_buf[at] = probs.astype(LOW)
                grad_probs = probs_grad_buf[at]
                scores_grad_buf[at] = (
                    probs * (grad_probs - jnp.sum(probs * grad_probs, axis=-1, keepdims=True))
                ).astype(LOW)

        @pl.loop(0, HEADS // 4)
        def _(group):
            for pair in range(2):
                at = group * 256 + pair * 128
                query = saved_buf[:, lanes(at, 128)]
                key = saved_buf[:, lanes(width + at, 128)]
                grad = mixed_buf[:, lanes(at, 128)]
                parts = []
                for own in (0, 1):
                    probs = probs_buf[group * 4 + 2 * pair + own]
                    grad_low = scores_grad_buf[group * 4 + 2 * pair + own]
                    parts.append(
                        (
                            matmul(grad_low, key) * scale,
                            matmul_tn(grad_low, query) * scale,
                            matmul_tn(probs, grad),
                        )
                    )
                for which in range(3):
                    grads_buf[:, lanes(which * width + at, 128)] = jnp.where(
                        left, parts[0][which], parts[1][which]
                    ).astype(LOW)

        @pl.loop(0, 3 * width // CHUNK, unroll=2)
        def _(j):
            at = lanes(j * CHUNK, CHUNK)
            normed_buf[...] += matmul(grads_buf[:, at], lead_ref[pl.ds(j * CHUNK, CHUNK), :])

    @pl.when(role == 2)
    def _():
        bring_inner.wait()

        @pl.loop(0, lead_ref.shape[0] // CHUNK, unroll=2)
        def _(j):
            at = lanes(j * CHUNK, CHUNK)
            grad_active = matmul(grad_ref[...], down_ref[:, at])
            grads = (gelu_slope(inner_buf[:, at]) * grad_active).astype(LOW)
            grads_buf[:, at] = grads
            normed_buf[...] += matmul(grads, lead_ref[pl.ds(j * CHUNK, CHUNK), :])

    @pl.when(role > 0)
    def _():
        keep_grads.start()
        bring_entry.wait()
        grad_normed = normed_buf[...]
        normed, factor = layer_norm(entry_buf[...].astype(WIDE))
        gain_buf[...] = jnp.broadcast_to(
            jnp.sum(grad_normed * normed, axis=0, keepdims=True), gain_buf.shape
        )
        keep_gain.start()
        out_ref[...] = (
            grad_ref[...].astype(WIDE) + norm_back(grad_normed * gain_ref[...], normed, factor)
        ).astype(LOW)
        keep_next.wait()
        keep_grads.wait()
        keep_gain.wait()


def backward_stage(
    spot, table, nexts, seg_row, gain, lead, down, entries, saved, inner, totals
):
    tokens, width = nexts[0].shape
    count = len(nexts)
    hidden = lead.shape[0]
    return pl.pallas_call(
        functools.partial(backward_kernel, spot, count),
        out_shape=[jax.ShapeDtypeStruct((tokens, width), LOW)]
        + [jax.ShapeDtypeStruct(k.shape, k.dtype) for k in totals],
        in_specs=[SMEM_SPEC] + [VMEM_SPEC] * (count + 4) + [HBM_SPEC] * 6,
        out_specs=[VMEM_SPEC] + [HBM_SPEC] * 3,
        scratch_shapes=[
            pltpu.VMEM((tokens, hidden), LOW),
            pltpu.VMEM((tokens, hidden), WIDE),
            pltpu.VMEM((tokens, hidden), LOW),
            pltpu.VMEM((tokens, width), LOW),
            pltpu.VMEM((8, width), WIDE),
            pltpu.VMEM((tokens, width), LOW),
            pltpu.VMEM((tokens, width), WIDE),
            pltpu.VMEM((HEADS, tokens, tokens), WIDE),
            pltpu.VMEM((HEADS, tokens, tokens), WIDE),
            pltpu.VMEM((HEADS, tokens, tokens), LOW),
            pltpu.VMEM((HEADS, tokens, tokens), LOW),
            pltpu.VMEM((tokens, width), LOW),
            pltpu.SemaphoreType.DMA((3,)),
            pltpu.SemaphoreType.DMA((3,)),
        ],
        input_output_aliases={count + 8 + i: 1 + i for i in range(3)},
        compiler_params=pltpu.CompilerParams(vmem_limit_bytes=18 << 20),
        cost_estimate=pl.CostEstimate(
            flops=4 * tokens * width * hidden, bytes_accessed=20 << 20, transcendentals=0
        ),
        name="backward_stage",
    )(
        table,
        *nexts,
        seg_row,
        gain,
        pinned(lead),
        pinned(down),
        far(entries),
        far(saved),
        far(inner),
        *map(far, totals),
    )


def stats_kernel(spot, plan_ref, *refs):
    candidates, (table_ref, readout_ref, peak_ref, total_ref) = refs[:-4], refs[-4:]
    step = pl.program_id(0)

    @pl.when(step == 0)
    def _():
        chosen(plan_ref[spot], candidates, readout_ref)

    logits = matmul_nt(table_ref[...], readout_ref[...])
    own_peak = jnp.max(logits, axis=0, keepdims=True)
    own_total = lambda peak: jnp.sum(jnp.exp(logits - peak), axis=0, keepdims=True)

    @pl.when(step == 0)
    def _():
        peak_ref[...] = own_peak
        total_ref[...] = own_total(own_peak)

    @pl.when(step > 0)
    def _():
        peak = jnp.maximum(peak_ref[...], own_peak)
        total_ref[...] = total_ref[...] * jnp.exp(peak_ref[...] - peak) + own_total(peak)
        peak_ref[...] = peak


def head_stats(spot, plan, readouts, table, tile):
    tokens, emb = readouts[0].shape
    vocab = table.shape[0]
    whole = pl.BlockSpec((1, tokens), lambda i: (0, 0))
    rows = pl.BlockSpec((tokens, emb), lambda i: (0, 0))
    return pl.pallas_call(
        functools.partial(stats_kernel, spot),
        out_shape=[jax.ShapeDtypeStruct((tokens, emb), LOW)]
        + [jax.ShapeDtypeStruct((1, tokens), WIDE)] * 2,
        grid=(vocab // tile,),
        in_specs=[SMEM_SPEC]
        + [rows] * len(readouts)
        + [pl.BlockSpec((tile, emb), lambda i: (i, 0))],
        out_specs=[rows, whole, whole],
        compiler_params=pltpu.CompilerParams(vmem_limit_bytes=32 << 20),
        cost_estimate=pl.CostEstimate(
            flops=2 * tokens * vocab * emb, bytes_accessed=5 << 20, transcendentals=tokens * vocab
        ),
        name="head_stats",
    )(plan, *readouts, far(table))


def head_kernel(spot, table_base_ref, readout_ref, table_ref, logsum_ref, ids_ref, head_ref, grad_ref):
    tile = table_ref.shape[0]
    logits = matmul_nt(table_ref[...], readout_ref[...])
    ids = ids_ref[...] - (table_base_ref[spot] + pl.program_id(0) * tile)
    hits = lax.broadcasted_iota(jnp.int32, logits.shape, 0) == ids
    probs = jnp.exp(logits - logsum_ref[...])
    grads = jnp.where(hits, probs - 1.0, probs).astype(LOW)
    head = matmul(grads, readout_ref[...])
    unit = tile // 4
    for shard in range(4):
        head_ref[shard, :unit] = head[shard * unit : (shard + 1) * unit].astype(LOW)
    term = matmul_tn(grads, table_ref[...])

    @pl.when(pl.program_id(0) == 0)
    def _():
        grad_ref[...] = term

    @pl.when(pl.program_id(0) > 0)
    def _():
        grad_ref[...] += term


def head_grads(spot, base, readout, table, logsum, ids):
    tokens, emb = readout.shape
    vocab = table.shape[0]
    row = pl.BlockSpec((1, tokens), lambda i: (0, 0))
    whole = pl.BlockSpec((tokens, emb), lambda i: (0, 0))
    part = pl.BlockSpec((vocab // 4, emb), lambda i: (i, 0))
    return pl.pallas_call(
        functools.partial(head_kernel, spot),
        out_shape=[
            pltpu.HBM((16, 512, emb), LOW),
            jax.ShapeDtypeStruct((tokens, emb), WIDE),
        ],
        grid=(4,),
        in_specs=[SMEM_SPEC, whole, part, row, row],
        out_specs=[pl.BlockSpec((4, 512, emb), lambda i: (i, 0, 0)), whole],
        compiler_params=pltpu.CompilerParams(vmem_limit_bytes=32 << 20),
        cost_estimate=pl.CostEstimate(
            flops=6 * tokens * vocab * emb, bytes_accessed=9 << 20, transcendentals=tokens * vocab
        ),
        name="head_grads",
    )(base, readout, far(table), logsum, ids)


def pair_kernel(former_ref, latter_ref, out_ref):
    rows = out_ref.shape[0]
    out_ref[...] = former_ref[:rows].astype(WIDE) + latter_ref[:rows].astype(WIDE)


def pair_sum(former, latter, rows):
    return pl.pallas_call(
        pair_kernel,
        out_shape=jax.ShapeDtypeStruct((rows, former.shape[1]), WIDE),
        in_specs=[VMEM_SPEC] * 2,
        out_specs=VMEM_SPEC,
        compiler_params=pltpu.CompilerParams(vmem_limit_bytes=8 << 20),
        cost_estimate=pl.CostEstimate(flops=0, bytes_accessed=1024, transcendentals=0),
        name="pair_sum",
    )(former, latter)


def lookup_kernel(ids_ref, table_ref, noise_ref, out_ref, total_ref, low_ref):
    step = pl.program_id(0)
    parts, tile = table_ref.shape
    tokens = ids_ref.shape[1]
    blocks = tile // 128

    @pl.when(step == 0)
    def _():
        lane = jnp.bitwise_and(ids_ref[...], 127)
        hits = lax.broadcasted_iota(jnp.int32, (128, tokens), 0) == lane
        low_ref[...] = jnp.where(hits, 1.0, 0.0).astype(LOW)
        total_ref[...] = noise_ref[...].astype(WIDE)

    stacked = jnp.concatenate(
        [table_ref[:, block * 128 : (block + 1) * 128] for block in range(blocks)]
    )
    found = matmul(stacked, low_ref[...])
    own = jnp.right_shift(ids_ref[...], 7) - step * blocks
    total = jnp.zeros_like(total_ref)
    for block in range(blocks):
        total = jnp.where(own == block, found[block * parts : (block + 1) * parts], total)
    total_ref[...] += total

    @pl.when(step == pl.num_programs(0) - 1)
    def _():
        out_ref[...] = total_ref[...].astype(LOW)


def lookup(ids, table, noise, tile):
    parts, vocab = table.shape
    tokens = ids.shape[1]
    whole = pl.BlockSpec((parts, tokens), lambda i: (0, 0))
    return pl.pallas_call(
        lookup_kernel,
        out_shape=jax.ShapeDtypeStruct((parts, tokens), LOW),
        grid=(vocab // tile,),
        in_specs=[
            pl.BlockSpec((1, tokens), lambda i: (0, 0)),
            pl.BlockSpec((parts, tile), lambda i: (0, i)),
            whole,
        ],
        out_specs=whole,
        scratch_shapes=[pltpu.VMEM((parts, tokens), WIDE), pltpu.VMEM((128, tokens), LOW)],
        compiler_params=pltpu.CompilerParams(vmem_limit_bytes=32 << 20),
        cost_estimate=pl.CostEstimate(
            flops=2 * 128 * vocab * tokens, bytes_accessed=4 << 20, transcendentals=0
        ),
        name="lookup",
    )(ids, far(table), noise)


def lead_grad_kernel(where_ref, normed_ref, mixed_ref, grads_ref, *refs):
    got_ref, out_refs, (turned_ref, result_ref) = None, refs[:-2], refs[-2:]
    if len(out_refs) > 1:
        got_ref, out_refs = out_refs[0], out_refs[1:]
    role, half, spot = where_ref[0], where_ref[1], where_ref[2]
    step = pl.program_id(0)
    width = normed_ref.shape[1]
    steps = pl.num_programs(0)
    use_mixed = jnp.logical_and(role == 1, half == 1)

    @pl.when(step == 0)
    def _():
        turned_ref[...] = normed_ref[...].T

    @pl.when(jnp.logical_and(step == steps // 2, use_mixed))
    def _():
        turned_ref[...] = mixed_ref[...].T

    result_ref[...] = matmul(turned_ref[...], grads_ref[...])
    unit = width // 16

    def put(block, rows, part):
        if got_ref is not None:
            part = part + got_ref[block, rows, :].astype(WIDE)
        out_ref = out_refs[0].at[block] if got_ref is None else out_refs[block]
        out_ref[rows, :] = part.astype(LOW)

    @pl.when(half == 0)
    def _():
        for block in range(4):
            x = (spot + block) % 4
            put(block, slice(None), result_ref[pl.ds(pl.multiple_of(x * 4 * unit, 4 * unit), 4 * unit)])

    @pl.when(half == 1)
    def _():
        for block in range(4):
            y = (spot + block) % 4
            for x in range(4):
                rows = pl.ds(pl.multiple_of((4 * x + y) * unit, unit), unit)
                put(block, slice(x * unit, (x + 1) * unit), result_ref[rows])


CHEAP = pl.CostEstimate(flops=0, bytes_accessed=1024, transcendentals=0)


def lead_grad(where, normed, saved, grads, got=None):
    tokens, width = normed.shape
    tile = 512
    whole = pl.BlockSpec((4, width // 4, tile), lambda i, where: (0, 0, i))
    block = pl.BlockSpec((width // 4, tile), lambda i, where: (0, i))
    shape = (width // 4, 2 * width)
    return pl.pallas_call(
        lead_grad_kernel,
        out_shape=[jax.ShapeDtypeStruct((4,) + shape, LOW)]
        if got is None
        else [jax.ShapeDtypeStruct(shape, LOW)] * 4,
        grid_spec=pltpu.PrefetchScalarGridSpec(
            num_scalar_prefetch=1,
            grid=(2 * width // tile,),
            in_specs=[
                pl.BlockSpec((tokens, width), lambda i, where: (0, 0)),
                pl.BlockSpec((tokens, width), lambda i, where: (0, 3)),
                pl.BlockSpec((tokens, tile), lambda i, where: (0, where[1] * (2 * width // tile) + i)),
            ]
            + ([] if got is None else [whole]),
            out_specs=[whole] if got is None else [block] * 4,
            scratch_shapes=[pltpu.VMEM((width, tokens), LOW), pltpu.VMEM((width, tile), WIDE)],
        ),
        compiler_params=pltpu.CompilerParams(vmem_limit_bytes=24 << 20),
        cost_estimate=CHEAP
        if got is None
        else pl.CostEstimate(
            flops=4 * tokens * width * width, bytes_accessed=12 << 20, transcendentals=0
        ),
        name="lead_grad",
    )(where, far(normed), far(saved), far(grads), *([] if got is None else [got]))


def down_grad_kernel(where_ref, saved_ref, nexts_ref, *refs):
    got_ref, out_refs, (buf_ref, got_buf, sems) = None, refs[:-3], refs[-3:]
    if len(out_refs) > 1:
        got_ref, out_refs = out_refs[0], out_refs[1:]
    role, half, spot = where_ref[0], where_ref[1], where_ref[2]
    at = pl.program_id(0)
    unit = saved_ref.shape[1] // 4

    @pl.when(role == 2)
    def _():
        if got_ref is not None:
            bring = pltpu.make_async_copy(got_ref, got_buf, sems.at[4])
            pl.when(at == 0)(bring.start)
        result = matmul_tn(saved_ref[...], nexts_ref[...])
        if got_ref is not None:
            pl.when(at == 0)(bring.wait)

        def put(block, rows, part):
            if got_ref is not None:
                part = part + got_buf[block, rows, :].astype(WIDE)
            buf_ref[block, rows, :] = part.astype(LOW)

        @pl.when(half == 0)
        def _():
            put((at - spot + 4) % 4, slice(None), result)

        @pl.when(half == 1)
        def _():
            rows = pl.ds(pl.multiple_of(at * unit, unit), unit)
            for y in range(4):
                put((y - spot + 4) % 4, rows, result[y * unit : (y + 1) * unit])

        @pl.when(at == pl.num_programs(0) - 1)
        def _():
            copies = [pltpu.make_async_copy(buf_ref, out_refs[0], sems.at[0])]
            if got_ref is not None:
                copies = [
                    pltpu.make_async_copy(buf_ref.at[block], out_ref, sems.at[block])
                    for block, out_ref in enumerate(out_refs)
                ]
            for copy in copies:
                copy.start()
            for copy in copies:
                copy.wait()


def down_grad(where, saved, nexts, got=None):
    tokens, hidden = saved.shape
    width = nexts.shape[1]
    rows = hidden // 8
    live = lambda where: jnp.where(where[0] == 2, 1, 0)
    return pl.pallas_call(
        down_grad_kernel,
        out_shape=[pltpu.HBM((4, rows, width), LOW)]
        if got is None
        else [pltpu.HBM((rows, width), LOW)] * 4,
        grid_spec=pltpu.PrefetchScalarGridSpec(
            num_scalar_prefetch=1,
            grid=(4,),
            in_specs=[
                pl.BlockSpec((tokens, rows), lambda i, where: (0, (where[1] * 4 + i) * live(where))),
                pl.BlockSpec((tokens, width), lambda i, where: (0, 0)),
            ]
            + ([] if got is None else [HBM_SPEC]),
            out_specs=[HBM_SPEC] * (1 if got is None else 4),
            scratch_shapes=[
                pltpu.VMEM((4, rows, width), LOW),
                pltpu.VMEM((4, 16, 128) if got is None else (4, rows, width), LOW),
                pltpu.SemaphoreType.DMA((5,)),
            ],
        ),
        compiler_params=pltpu.CompilerParams(vmem_limit_bytes=28 << 20),
        cost_estimate=CHEAP,
        name="down_grad",
    )(where, far(saved), far(nexts), *([] if got is None else [far(got)]))


def upper_kernel(where_ref, *refs):
    out_ref = refs[4]
    rows = refs[0].shape[0]
    for at, part in enumerate(refs[:4]):
        place = (where_ref[0] - at + 4) % 4
        out_ref[pl.ds(pl.multiple_of(place * rows, rows), rows), :] = part[...]


def upper_half(where, parts):
    rows, width = parts[0].shape
    return pl.pallas_call(
        upper_kernel,
        out_shape=jax.ShapeDtypeStruct((4 * rows, width), LOW),
        in_specs=[SMEM_SPEC] + [VMEM_SPEC] * 4,
        out_specs=VMEM_SPEC,
        compiler_params=pltpu.CompilerParams(vmem_limit_bytes=8 << 20),
        name="upper_half",
    )(where, *parts)


def hold_down_kernel(where_ref, mine_ref, other_ref, own_ref, out_ref, sems):
    rows = mine_ref.shape[0]
    core = where_ref[1]
    spot = lambda at: out_ref.at[pl.ds(pl.multiple_of(at * rows, rows), rows), :]
    copies = [
        pltpu.make_async_copy(mine_ref, spot(core), sems.at[0]),
        pltpu.make_async_copy(other_ref, spot(1 - core), sems.at[1]),
        pltpu.make_async_copy(own_ref, out_ref.at[pl.ds(2 * rows, 2 * rows), :], sems.at[2]),
    ]
    for copy in copies:
        copy.start()
    for copy in copies:
        copy.wait()


def hold_down(where, mine, other, own):
    rows, width = mine.shape
    return pl.pallas_call(
        hold_down_kernel,
        out_shape=pltpu.VMEM((4 * rows, width), LOW),
        in_specs=[SMEM_SPEC] + [VMEM_SPEC] * 2 + [HBM_SPEC],
        out_specs=VMEM_SPEC,
        scratch_shapes=[pltpu.SemaphoreType.DMA((3,))],
        compiler_params=pltpu.CompilerParams(vmem_limit_bytes=8 << 20),
        name="hold_down",
    )(where, mine, other, far(own))


def noise_kernel(spot, plan_ref, ids_ref, *refs):
    candidates, (packed_ref, noise_ref, buf_ref) = refs[:-3], refs[-3:]
    parts = noise_ref.shape[0]
    chosen(plan_ref[spot], candidates, buf_ref)
    packed_ref[:parts] = buf_ref[...]
    noise_ref[...] = buf_ref[...].astype(WIDE)
    ids = ids_ref[...]
    high = jnp.right_shift(ids, 8).astype(WIDE)
    low = jnp.bitwise_and(ids, 255).astype(WIDE)
    at = lax.broadcasted_iota(jnp.int32, (16, ids.shape[1]), 0)
    split = jnp.where(at == 0, high, jnp.where(at == 1, low, 0.0))
    packed_ref[parts:] = split.astype(LOW)


def noise_pack(spot, plan, ids, candidates):
    parts, tokens = candidates[0].shape
    return pl.pallas_call(
        functools.partial(noise_kernel, spot),
        out_shape=[
            jax.ShapeDtypeStruct((parts + 16, tokens), LOW),
            jax.ShapeDtypeStruct((parts, tokens), WIDE),
        ],
        in_specs=[SMEM_SPEC] + [VMEM_SPEC] * (1 + len(candidates)),
        out_specs=[VMEM_SPEC] * 2,
        scratch_shapes=[pltpu.VMEM((parts, tokens), LOW)],
        compiler_params=pltpu.CompilerParams(vmem_limit_bytes=8 << 20),
        cost_estimate=CHEAP,
        name="noise_pack",
    )(plan, ids, *candidates)


def embed_kernel(base_ref, mine_ref, other_ref, out_ref, total_ref):
    step = pl.program_id(0)
    steps = pl.num_programs(0)
    parts = out_ref.shape[0]
    blocks = total_ref.shape[0] // parts

    def add(gathered_ref):
        count, _, tokens = gathered_ref.shape
        term = None
        for at in range(count):
            split = gathered_ref[at, parts : parts + 16].astype(WIDE)
            ids = (split[0:1] * 256.0 + split[1:2]).astype(jnp.int32) - base_ref[0]
            lane = jnp.bitwise_and(ids, 127)
            hits = lax.broadcasted_iota(jnp.int32, (128, tokens), 0) == lane
            hits = jnp.where(hits, 1.0, 0.0).astype(LOW)
            own = jnp.right_shift(ids, 7)
            grads = gathered_ref[at, :parts]
            masked = jnp.concatenate(
                [grads * jnp.where(own == block, 1.0, 0.0).astype(LOW) for block in range(blocks)]
            )
            part = matmul_nt(masked, hits)
            term = part if term is None else term + part

        @pl.when(step == 0)
        def _():
            total_ref[...] = term

        @pl.when(step > 0)
        def _():
            total_ref[...] += term

    pl.when(step < steps // 2)(lambda: add(mine_ref))
    pl.when(step >= steps // 2)(lambda: add(other_ref))

    @pl.when(step == steps - 1)
    def _():
        rows = out_ref.shape[1]
        for block in range(blocks):
            size = min(128, rows - block * 128)
            out_ref[:, block * 128 : block * 128 + size] = total_ref[
                block * parts : (block + 1) * parts, :size
            ]


def embed_sum(base, mine, other, parts, rows):
    count, deep, tokens = mine.shape
    step = 4
    half = count // step
    blocks = -(-rows // 128)
    return pl.pallas_call(
        embed_kernel,
        out_shape=jax.ShapeDtypeStruct((parts, rows), WIDE),
        grid=(2 * half,),
        in_specs=[
            SMEM_SPEC,
            pl.BlockSpec((step, deep, tokens), lambda i: (jnp.minimum(i, half - 1), 0, 0)),
            pl.BlockSpec((step, deep, tokens), lambda i: (jnp.maximum(i - half, 0), 0, 0)),
        ],
        out_specs=pl.BlockSpec((parts, rows), lambda i: (0, 0)),
        scratch_shapes=[pltpu.VMEM((blocks * parts, 128), WIDE)],
        compiler_params=pltpu.CompilerParams(vmem_limit_bytes=32 << 20),
        cost_estimate=CHEAP,
        name="embed_sum",
    )(base, mine, other)


def empty(*kinds):
    return pl.pallas_call(
        lambda *refs: None,
        out_shape=[pltpu.HBM(shape, dtype) for shape, dtype in kinds],
        out_specs=[HBM_SPEC] * len(kinds),
        compiler_params=pltpu.CompilerParams(vmem_limit_bytes=1 << 20),
        name="empty",
    )()


ROW_LEN = 128
SEC, GRP, NX, NY = 4, 2, 4, 4
ALL = ("section", "group", "row")
TURNS = (1, 3, 2)


def route(value, target_of):
    number = lambda s, g, x, y: (s * GRP + g) * NX * NY + x * NY + y
    pairs = []
    for at in itertools.product(range(SEC), range(GRP), range(NX), range(NY)):
        target = target_of(*at)
        if target is not None:
            pairs.append((number(*at), number(*target)))
    return lax.ppermute(value, ALL, pairs)


def link(value, source, target):
    return route(value, lambda s, g, x, y: (target, g, x, y) if s == source else None)


def turn(value, by):
    return route(value, lambda s, g, x, y: ((s + by) % SEC, g, x, y))


def swap_cores(value, sections=range(SEC)):
    return route(value, lambda s, g, x, y: (s, 1 - g, x, y) if s in sections else None)


def plane_route(value, by, first, sections=range(SEC)):
    def target_of(s, g, x, y):
        if s not in sections:
            return None
        if (g == 0) == first:
            return (s, g, (x + by) % NX, y)
        return (s, g, x, (y + by) % NY)

    return route(value, target_of)


def after(value, earlier):
    return lax.optimization_barrier((value, earlier))[0]


def row_block(values, block, count):
    size = values.shape[0] // count
    return lax.dynamic_slice_in_dim(values, block * size, size, 0)


def plane_first(mine, sections=range(SEC)):
    return [mine[0]] + [plane_route(mine[by], by, True, sections) for by in TURNS]


def plane_sum(pieces):
    total = pieces[0].astype(WIDE)
    for piece in pieces[1:]:
        total = total + piece.astype(WIDE)
    return total.astype(LOW)


def plane_second(pieces, second, sections=range(SEC)):
    total = plane_sum(pieces)
    return [row_block(total, second, 4)] + [
        plane_route(row_block(total, (second + by) % 4, 4), by, False, sections) for by in TURNS
    ]


def group_exchange(values, first):
    number = lambda s, g, x, y: (s * GRP + g) * NX * NY + x * NY + y
    groups = []
    for s in range(SEC):
        for g in range(GRP):
            along_x = (g == 0) == first
            for at in range(4):
                groups.append(
                    [number(s, g, i, at) if along_x else number(s, g, at, i) for i in range(4)]
                )
    return lax.all_to_all(values, ALL, 0, 0, axis_index_groups=groups, tiled=True)


def section_exchange(values):
    return lax.all_to_all(values, "section", 0, 0, tiled=True)


def plans(micro, vocab_part):
    last = SEC - 1
    steps = micro + 2 * last
    table = np.zeros((SEC, 6 * steps + 2), np.int32)
    for s in range(SEC):
        for way in range(2):
            depth = s if way == 0 else last - s
            for step in range(steps):
                at = step - 2 * depth
                if 0 <= at < micro:
                    sources = ([0] if step < micro else []) + [
                        d + 1 for d in range(last) if 0 <= step - 2 - 2 * d < micro
                    ]
                    spot = 3 * (way * steps + step)
                    table[s, spot : spot + 3] = (1 + s % 2, at, sources.index(depth))
        table[s, 6 * steps :] = (s * vocab_part, s)
    return table


def local(
    token_ids,
    segment_ids,
    noise_input,
    embed_table,
    input_proj,
    norm_gain,
    lead_weight,
    down_weight,
    final_gain,
    readout_proj,
    head_table,
):
    section = lax.axis_index("section")
    core = lax.axis_index("group")
    row = lax.axis_index("row")
    x_at, y_at = row // NY, row % NY
    first_at = jnp.where(core == 0, x_at, y_at)
    micro, _, tokens = token_ids.shape
    width = input_proj.shape[1]
    hidden = lead_weight.shape[2]
    half_rows = down_weight.shape[1]
    emb_part = input_proj.shape[0]
    vocab_part, emb = head_table.shape
    vocab = embed_table.shape[0]
    all_tokens = micro * tokens
    last = SEC - 1
    gain_half = norm_gain.astype(WIDE)
    lead = lead_weight[0]
    own_down = down_weight[0]
    seg_row = segment_ids
    flat_ids = token_ids.reshape(-1)

    plan = plans(micro, vocab_part)
    steps = micro + 2 * last
    table = lax.dynamic_index_in_dim(jnp.asarray(plan), section, 0, False)
    flat_ids = after(flat_ids, table)
    where_start = jnp.stack((first_at, core)).astype(jnp.int32)
    to_first = lambda v: [v] + [link(v, s, 0) for s in range(1, SEC)]
    eighth = row_block(row_block(own_down, core, 2), first_at, 4)
    eighth = jnp.where(section == 1, link(eighth, 0, 1), link(eighth, 2, 3))
    noise = noise_input[:, 0].transpose(2, 0, 1).reshape(emb_part, -1)
    own_embedded = lookup(flat_ids[None], embed_table.T, noise, 3200)
    parts = to_first(jnp.concatenate((own_embedded, input_proj), axis=1))
    embedded = jnp.concatenate([part[:, :all_tokens] for part in parts])
    input_full = jnp.concatenate([part[:, all_tokens:] for part in parts])
    first_in = matmul_tn(embedded, input_full).astype(LOW).reshape(micro, tokens, width)
    eighth = after(eighth, own_embedded)
    eighths = [eighth] + [plane_route(eighth, by, True) for by in (1, 2, 3)]
    upper = upper_half(where_start, [after(part, first_in) for part in eighths])
    held_down = hold_down(where_start, upper, swap_cores(upper), own_down)

    kept = empty(
        ((micro, tokens, width), LOW),
        ((micro, tokens, width), LOW),
        ((micro, tokens, hidden), LOW),
        ((micro, tokens, hidden), WIDE),
    )

    def sources(first, step, hops, order):
        arrived = [hops[step - 2, s] for s in order if (step - 2, s) in hops]
        return ([first[step]] if step < micro else []) + arrived

    outs, hops = [], {}
    for step in range(steps):
        out, *kept = forward_stage(
            3 * step,
            table,
            sources(first_in, step, hops, range(SEC)),
            seg_row,
            gain_half,
            held_lead if step > 0 else lead,
            held_down if step > 1 else None,
            kept,
            step == 0,
        )
        if step == 0:
            held_lead = kept.pop()
        outs.append(out)
        for s in range(last):
            if 0 <= step - 2 * s < micro:
                ready = after(out, hops[step - 1, s]) if (step - 1, s) in hops else out
                hops[step, s] = link(ready, s, s + 1)
        if step == 2:
            readout_own = after(readout_proj.T, out)
            readout_full = jnp.concatenate(
                [link(readout_own, s, last) for s in range(last)] + [readout_own]
            )
    entries, normeds, saved, inner = kept

    final_rows = jnp.concatenate(outs[2 * last :]).astype(WIDE)
    normed_f, factor_f = layer_norm(final_rows)
    gain_f = final_gain.astype(WIDE)
    final_low = (normed_f * gain_f).astype(LOW)
    readout = matmul_nt(final_low, readout_full).astype(LOW)
    sent = [link(readout, last, s) for s in range(last)]
    readout, peak, total = head_stats(6 * steps + 1, table, sent + [readout], head_table, 2000)
    stats = jnp.concatenate((peak, total))
    all_stats = section_exchange(jnp.tile(stats, (SEC, 1))).reshape(SEC, 2, all_tokens)
    peak = jnp.max(all_stats[:, 0], axis=0)
    total = jnp.sum(all_stats[:, 1] * jnp.exp(all_stats[:, 0] - peak), axis=0)
    logsum = (peak + jnp.log(total))[None]
    head_grad, grad_readout = head_grads(
        6 * steps, table, readout, head_table, logsum, flat_ids[None]
    )
    grad_low = grad_readout.astype(LOW)
    for s in range(last):
        grad_readout = grad_readout + link(grad_low, s, last).astype(WIDE)
    grad_readout = grad_readout.astype(LOW)
    head_grad = lax.psum_scatter(head_grad, "row", scatter_dimension=0)
    readout_grad = matmul_tn(final_low, grad_readout)
    grad_final = matmul(grad_readout, readout_full)
    final_gain_grad = jnp.sum(grad_final * normed_f, axis=0)
    last_grads = norm_back(grad_final * gain_f, normed_f, factor_f).astype(LOW)
    last_grads = last_grads.reshape(micro, tokens, width)

    lead_turned = turned(6 * steps + 1, table, after(lead, grad_low), 0)
    down_turned = turned(6 * steps + 1, table, after(held_down, grad_low), 1)
    totals = empty(
        ((micro, tokens, width), LOW),
        ((micro, tokens, hidden), LOW),
        ((micro, 8, width), WIDE),
    )
    outs, hops = [], {}
    for step in range(steps):
        out, *totals = backward_stage(
            3 * (steps + step),
            table,
            sources(last_grads, step, hops, range(SEC - 1, -1, -1)),
            seg_row,
            gain_half,
            lead_turned,
            down_turned,
            entries,
            saved,
            inner,
            totals,
        )
        outs.append(out)
        for s in range(1, SEC):
            if 0 <= step - 2 * (last - s) < micro:
                ready = after(out, hops[step - 1, s]) if (step - 1, s) in hops else out
                hops[step, s] = link(ready, s, s - 1)
    section, core, row, readout_grad, final_gain_grad = lax.optimization_barrier(
        (section, core, row, readout_grad, final_gain_grad, out)
    )[:5]
    x_at, y_at = row // NY, row % NY
    first_at, second_at = jnp.where(core == 0, x_at, y_at), jnp.where(core == 0, y_at, x_at)
    is_mlp = section % 2 == 1

    first_grads = jnp.concatenate(outs[2 * last :])
    noise_grad = matmul_nt(input_full, first_grads).astype(LOW)
    pieces = noise_grad.reshape(SEC, emb_part, all_tokens)
    sent = [link(pieces[s], 0, s) for s in range(1, SEC)]

    grad_nexts, grads, gain_grads = totals
    gain_grad = jnp.sum(gain_grads[:, 0], axis=0)
    flat = lambda v: v.reshape(all_tokens, v.shape[-1])
    grads = after(grads, head_grad)
    normed, grad_nexts, grads, saved = flat(normeds), flat(grad_nexts), flat(grads), flat(saved)
    odd = (1, 3)
    role = jnp.where(is_mlp, 2, 1)
    where_other = jnp.stack((role, 1 - core, second_at)).astype(jnp.int32)
    where_mine = jnp.stack((role, core, first_at)).astype(jnp.int32)
    both = lambda mine, other: jnp.where(
        core == 0,
        jnp.concatenate((mine, other), axis=1),
        jnp.concatenate((other, mine), axis=1),
    )
    down_got = swap_cores(down_grad(where_other, saved, grad_nexts)[0], odd)
    down_mine = down_grad(where_mine, saved, grad_nexts, down_got)
    down_first = plane_first(down_mine, odd)
    late_ids = after(flat_ids, down_mine)[None]
    packed, noise_wide = noise_pack(6 * steps + 1, table, late_ids, [pieces[0]] + sent)
    where_other = after(where_other, packed)
    lead_got = swap_cores(lead_grad(where_other, normed, saved, grads)[0])

    input_grad = matmul(embedded, first_grads).reshape(SEC, 16, 4, width)
    input_grad = input_grad.transpose(1, 0, 2, 3).reshape(16, 16, width)
    readout_grad = readout_grad.reshape(16, 16, width)
    vectors = jnp.concatenate(
        (
            gain_grad.reshape(16, 64),
            final_gain_grad.reshape(SEC, 16, 16).transpose(1, 0, 2).reshape(16, 64),
            jnp.zeros((16, width - 128), WIDE),
        ),
        axis=1,
    )
    small = jnp.concatenate(
        (
            jnp.where(section == 0, input_grad, readout_grad),
            vectors[:, None],
            jnp.zeros((16, 15, width), WIDE),
        ),
        axis=1,
    ).astype(LOW)
    half_of = lambda which: lax.dynamic_slice_in_dim(small, which * (width // 2), width // 2, 2)
    small = half_of(core).astype(WIDE) + swap_cores(half_of(1 - core)).astype(WIDE)
    small = small.astype(LOW).reshape(NX, NY, 32, width // 2)
    small = jnp.where(core == 0, small, small.swapaxes(0, 1)).reshape(4, NY * 32, width // 2)
    deep = emb_part + 16

    def exchange(blocks, packed, first):
        rows = blocks.shape[1]
        everywhere = jnp.broadcast_to(packed, (4,) + packed.shape)
        got = group_exchange(jnp.concatenate((blocks, everywhere), axis=1), first)
        return jnp.sum(got[:, :rows].astype(WIDE), axis=0).astype(LOW), got[:, rows:]

    small, packed = exchange(small, packed, True)
    lead_mine = lead_grad(after(where_mine, packed), normed, saved, grads, lead_got)
    lead_first = plane_first(lead_mine)
    packed = after(packed, lead_mine)
    small, packed = exchange(
        small.reshape(4, 32, width // 2), packed.reshape(4 * deep, all_tokens), False
    )
    packed = packed.reshape(16, deep, all_tokens)
    packed_other = swap_cores(packed)
    small = both(small, swap_cores(small))
    embed_grad = embed_sum(
        (row * (vocab // 16)).reshape(1), packed, packed_other, emb_part, vocab // 16
    )
    down_second = plane_second(after(down_first, packed), second_at, odd)
    lead_second = plane_second(after(lead_first, packed), second_at)
    down_part = plane_sum(after(down_second, embed_grad))
    lead_part = plane_sum(after(lead_second, embed_grad))
    noise_out = noise_wide.reshape(emb_part, micro, tokens).transpose(1, 2, 0)
    lead_out = both(lead_part, swap_cores(lead_part)).astype(WIDE)

    def first_target(s, g, x, y):
        if s % 2 == 0:
            return None
        return (s - 1, 0, x, y) if g == 0 else (s, 0, x, y)

    def second_target(s, g, x, y):
        return (s - 1, 1, x, y) if s % 2 == 1 and g == 0 else None

    to_core_0 = route(down_part, first_target)
    to_core_1 = route(down_part, second_target)
    down_out = jnp.where(
        core == 0, to_core_0, jnp.where(is_mlp, down_part, to_core_1)
    ).astype(WIDE)

    small = after(small, (lead_part, down_part))
    gain_out = small[16, :64].astype(WIDE)
    input_rows = small[:16].reshape(SEC, 4, width)
    readout_rows = small[:16].reshape(64, SEC, 64)
    final_rows = small[16, 64:128].reshape(SEC, 16)

    finals = jnp.pad(final_rows, ((0, 0), (0, width - 16)))[:, None]
    mine = jnp.where(
        section == 0, input_rows, readout_rows.transpose(1, 0, 2).reshape(SEC, 4, width)
    )
    shared = section_exchange(
        jnp.concatenate((mine, finals, jnp.zeros((SEC, 3, width), LOW)), axis=1)
    )
    input_out = shared[0, :4]
    readout_out = shared[last, :4].reshape(64, 64)
    final_out = shared[last, 4, :16]

    head_out = pair_sum(head_grad, swap_cores(head_grad), vocab_part // (NX * NY))
    return (
        noise_out[:, None],
        embed_grad.T,
        input_out.astype(WIDE),
        gain_out[None],
        lead_out[None],
        down_out[None],
        final_out.astype(WIDE),
        readout_out.astype(WIDE),
        head_out,
    )


def solution(mesh):
    in_specs = (
        P(None, ("group", "row"), None),
        P(None, ("group", "row"), None),
        P(None, ("group", "row"), None, "section"),
        P(None, "section"),
        P("section", None),
        P("section", None),
        P("section", None, None),
        P("section", None, None),
        P(),
        P(None, "section"),
        P("section", None),
    )
    out_specs = (
        P(None, ("group", "row"), None, "section"),
        P("row", "section"),
        P(("section", "row"), None),
        P("section", "row"),
        P("section", "row", None),
        P("section", "row", None),
        P(("section", "row")),
        P("row", "section"),
        P(("section", "row"), None),
    )
    return jax.shard_map(local, mesh=mesh, in_specs=in_specs, out_specs=out_specs, check_vma=False)
```

```python
import functools
import itertools

import jax
import jax.numpy as jnp
import numpy as np
from jax import lax
from jax.experimental import pallas as pl
from jax.experimental.pallas import tpu as pltpu
from jax.sharding import PartitionSpec as P

HEADS = 16
HEAD_SIZE = 64
LOW = jnp.bfloat16
WIDE = jnp.float32
EPSILON = 1e-05
MASKED = -1000000000.0
CHUNK = 1024
GELU_A = 0.7978845608028654
GELU_B = 0.044715
HBM_SPEC = pl.BlockSpec(memory_space=pltpu.HBM)
VMEM_SPEC = pl.BlockSpec(memory_space=pltpu.VMEM)
SMEM_SPEC = pl.BlockSpec(memory_space=pltpu.SMEM)


def matmul(former, latter):
    return jnp.dot(former, latter, preferred_element_type=WIDE)


def matmul_nt(former, latter):
    return lax.dot_general(
        former, latter, (((1,), (1,)), ((), ())), preferred_element_type=WIDE
    )


def matmul_tn(former, latter):
    return lax.dot_general(
        former, latter, (((0,), (0,)), ((), ())), preferred_element_type=WIDE
    )


def layer_norm(values):
    centre = jnp.mean(values, axis=-1, keepdims=True)
    centred = values - centre
    variance = jnp.mean(centred * centred, axis=-1, keepdims=True)
    factor = lax.rsqrt(variance + EPSILON)
    return (centred * factor, factor)


def norm_back(grad_normed, normed, factor):
    first_mean = jnp.mean(grad_normed, axis=-1, keepdims=True)
    second_mean = jnp.mean(grad_normed * normed, axis=-1, keepdims=True)
    return factor * (grad_normed - first_mean - normed * second_mean)


def gelu(v):
    return 0.5 * v * (1.0 + jnp.tanh(GELU_A * (v + GELU_B * (v * v * v))))


def gelu_slope(v):
    square = v * v
    bend = jnp.tanh(GELU_A * (v + GELU_B * (square * v)))
    return 0.5 * (1.0 + bend) + 0.5 * v * (1.0 - bend * bend) * (
        GELU_A * (1.0 + 3.0 * GELU_B * square)
    )


def head_probs(scores, same):
    scores = jnp.where(same, scores * HEAD_SIZE ** (-0.5), MASKED)
    expo = jnp.exp(scores - jnp.max(scores, axis=-1, keepdims=True))
    return expo * (1.0 / jnp.sum(expo, axis=-1, keepdims=True))


def same_segment(row):
    across = jnp.broadcast_to(row.astype(WIDE), (row.shape[1], row.shape[1]))
    return across.T == across


def lanes(at, size):
    return pl.ds(pl.multiple_of(at, 128), size)


def turn_kernel(spot, live, plan_ref, value_ref, out_ref):
    @pl.when(jnp.bitwise_and(plan_ref[spot], 1) >= live)
    def _():
        out_ref[...] = value_ref[...].T


def turned(spot, plan, value, live):
    rows, columns = value.shape
    if rows > columns:
        tile = rows // 8
        blocks = (pl.BlockSpec((tile, columns), lambda i: (i, 0)), pl.BlockSpec((columns, tile), lambda i: (0, i)))
    else:
        tile = columns // 8
        blocks = (pl.BlockSpec((rows, tile), lambda i: (0, i)), pl.BlockSpec((tile, rows), lambda i: (i, 0)))
    return pl.pallas_call(
        functools.partial(turn_kernel, spot, live),
        out_shape=pltpu.VMEM((columns, rows), LOW),
        grid=(8,),
        in_specs=[SMEM_SPEC, blocks[0]],
        out_specs=blocks[1],
        compiler_params=pltpu.CompilerParams(vmem_limit_bytes=12 << 20),
        cost_estimate=pl.CostEstimate(flops=0, bytes_accessed=1024, transcendentals=0),
        name="turned",
    )(plan, far(value))


def chosen(choice, candidates, buffer):
    for at, candidate in enumerate(candidates):

        @pl.when(choice == at)
        def _():
            buffer[...] = candidate[...]


def forward_kernel(spot, with_down, loads, count, *refs):
    table_ref, candidates, refs = refs[0], refs[1 : 1 + count], refs[1 + count :]
    if not with_down:
        refs = refs[:3] + (None,) + refs[3:]
    source_ref = load_sems = None
    if loads:
        source_ref, load_sems = refs[2], refs[-1]
        refs = refs[:2] + (refs[13],) + refs[3:13] + refs[14:-1]
    forward_body(spot, table_ref, candidates, source_ref, load_sems, *refs)


def forward_body(
    spot,
    table_ref,
    candidates,
    source_ref,
    load_sems,
    seg_row_ref,
    gain_ref,
    lead_ref,
    down_ref,
    entries_in,
    normeds_in,
    saved_in,
    inner_in,
    out_ref,
    entries_ref,
    normeds_ref,
    saved_ref,
    inner_ref,
    normed_buf,
    saved_buf,
    inner_buf,
    result_buf,
    scores_buf,
    probs_buf,
    entry_ref,
    out_sems,
):
    role, slot = table_ref[spot], table_ref[spot + 1]
    tokens, width = entry_ref.shape
    keeps = [
        pltpu.make_async_copy(entry_ref, entries_ref.at[slot], out_sems.at[0]),
        pltpu.make_async_copy(normed_buf, normeds_ref.at[slot], out_sems.at[1]),
        pltpu.make_async_copy(saved_buf, saved_ref.at[slot], out_sems.at[2]),
    ]
    keep_inner = pltpu.make_async_copy(inner_buf, inner_ref.at[slot], out_sems.at[3])

    def load(j):
        at = lanes(j * CHUNK, CHUNK)
        return pltpu.make_async_copy(source_ref.at[:, at], lead_ref.at[:, at], load_sems.at[j])

    def loaded(j):
        if source_ref is not None:
            load(j).wait()

    if source_ref is not None:
        for j in range(lead_ref.shape[1] // CHUNK):
            load(j).start()

        @pl.when(role != 1)
        def _():
            pl.loop(0, lead_ref.shape[1] // CHUNK)(loaded)

    @pl.when(role > 0)
    def _():
        chosen(table_ref[spot + 2], candidates, entry_ref)
        normed, _ = layer_norm(entry_ref[...].astype(WIDE))
        normed_buf[...] = (normed * gain_ref[...]).astype(LOW)
        keeps[0].start()
        keeps[1].start()

    @pl.when(role == 1)
    def _():
        @pl.loop(0, 3 * width // CHUNK, unroll=2)
        def _(j):
            at = lanes(j * CHUNK, CHUNK)
            loaded(j)
            saved_buf[:, at] = matmul(normed_buf[...], lead_ref[:, at]).astype(LOW)

        left = lax.broadcasted_iota(jnp.int32, (tokens, 128), 1) < HEAD_SIZE
        zero = jnp.zeros((tokens, 128), LOW)

        @pl.loop(0, HEADS // 8)
        def _(group):
            for pair in range(4):
                at = group * 512 + pair * 128
                query = saved_buf[:, lanes(at, 128)]
                key = saved_buf[:, lanes(width + at, 128)]
                scores_buf[group * 8 + 2 * pair] = matmul_nt(jnp.where(left, query, zero), key)
                scores_buf[group * 8 + 2 * pair + 1] = matmul_nt(jnp.where(left, zero, query), key)

        @pl.loop(0, HEADS // 4)
        def _(group):
            same = same_segment(seg_row_ref[slot])
            for head in range(4):
                at = group * 4 + head
                probs_buf[at] = head_probs(scores_buf[at], same).astype(LOW)

        @pl.loop(0, HEADS // 8)
        def _(group):
            for pair in range(4):
                at = group * 512 + pair * 128
                value = saved_buf[:, lanes(2 * width + at, 128)]
                mixed = jnp.where(
                    left,
                    matmul(probs_buf[group * 8 + 2 * pair], value),
                    matmul(probs_buf[group * 8 + 2 * pair + 1], value),
                )
                saved_buf[:, lanes(3 * width + at, 128)] = mixed.astype(LOW)

        keeps[2].start()

        @pl.loop(0, width // CHUNK)
        def _(j):
            at = lanes(j * CHUNK, CHUNK)
            loaded(3 * width // CHUNK + j)
            term = matmul(saved_buf[:, 3 * width :], lead_ref[:, lanes(3 * width + j * CHUNK, CHUNK)])
            out_ref[:, at] = (entry_ref[:, at].astype(WIDE) + term).astype(LOW)

    def feed_forward():
        result_buf[...] = entry_ref[...].astype(WIDE)

        @pl.loop(0, lead_ref.shape[1] // CHUNK, unroll=2)
        def _(j):
            at = lanes(j * CHUNK, CHUNK)
            inner = matmul(normed_buf[...], lead_ref[:, at])
            inner_buf[:, at] = inner
            active = gelu(inner).astype(LOW)
            saved_buf[:, at] = active
            result_buf[...] += matmul(active, down_ref[pl.ds(j * CHUNK, CHUNK), :])

        keeps[2].start()
        keep_inner.start()
        out_ref[...] = result_buf[...].astype(LOW)
        keep_inner.wait()

    if down_ref is not None:
        pl.when(role == 2)(feed_forward)

    @pl.when(role > 0)
    def _():
        for keep in keeps:
            keep.wait()


def pinned(value):
    return pltpu.with_memory_space_constraint(value, pltpu.VMEM)


def far(value):
    return pltpu.with_memory_space_constraint(value, pltpu.HBM)


def forward_stage(spot, table, entries, seg_row, gain, lead, down, kept, loads=False):
    tokens, width = entries[0].shape
    hidden = lead.shape[1]
    count = len(entries) + (3 if down is None else 4)
    given = [VMEM_SPEC] * (len(entries) + 2) + [HBM_SPEC if loads else VMEM_SPEC]
    return pl.pallas_call(
        functools.partial(forward_kernel, spot, down is not None, loads, len(entries)),
        out_shape=[jax.ShapeDtypeStruct((tokens, width), LOW)]
        + [jax.ShapeDtypeStruct(k.shape, k.dtype) for k in kept]
        + ([pltpu.VMEM(lead.shape, LOW)] if loads else []),
        in_specs=[SMEM_SPEC] + given + [VMEM_SPEC] * (down is not None) + [HBM_SPEC] * 4,
        out_specs=[VMEM_SPEC] + [HBM_SPEC] * 4 + [VMEM_SPEC] * loads,
        scratch_shapes=[
            pltpu.VMEM((tokens, width), LOW),
            pltpu.VMEM((tokens, hidden), LOW),
            pltpu.VMEM((tokens, hidden), WIDE),
            pltpu.VMEM((tokens, width), WIDE),
            pltpu.VMEM((HEADS, tokens, tokens), WIDE),
            pltpu.VMEM((HEADS, tokens, tokens), LOW),
            pltpu.VMEM((tokens, width), LOW),
            pltpu.SemaphoreType.DMA((4,)),
        ]
        + ([pltpu.SemaphoreType.DMA((hidden // CHUNK,))] if loads else []),
        input_output_aliases={count + 1 + i: 1 + i for i in range(4)},
        compiler_params=pltpu.CompilerParams(vmem_limit_bytes=18 << 20),
        cost_estimate=pl.CostEstimate(
            flops=4 * tokens * width * hidden, bytes_accessed=20 << 20, transcendentals=0
        ),
        name="forward_stage",
    )(
        table,
        *entries,
        seg_row,
        gain,
        (far if loads else pinned)(lead),
        *([pinned(down)] if down is not None else []),
        *map(far, kept),
    )


def backward_kernel(spot, count, *refs):
    backward_body(spot, refs[0], refs[1 : 1 + count], *refs[1 + count :])


def backward_body(
    spot,
    table_ref,
    candidates,
    seg_row_ref,
    gain_ref,
    lead_ref,
    down_ref,
    entries_ref,
    saved_ref,
    inner_ref,
    nexts_in,
    grads_in,
    gains_in,
    out_ref,
    nexts_ref,
    grads_ref,
    gains_ref,
    saved_buf,
    inner_buf,
    grads_buf,
    mixed_buf,
    gain_buf,
    entry_buf,
    normed_buf,
    scores_buf,
    probs_grad_buf,
    probs_buf,
    scores_grad_buf,
    grad_ref,
    in_sems,
    out_sems,
):
    role, slot = table_ref[spot], table_ref[spot + 1]
    tokens, width = grad_ref.shape
    bring_saved = pltpu.make_async_copy(saved_ref.at[slot], saved_buf, in_sems.at[0])
    bring_inner = pltpu.make_async_copy(inner_ref.at[slot], inner_buf, in_sems.at[1])
    bring_entry = pltpu.make_async_copy(entries_ref.at[slot], entry_buf, in_sems.at[2])
    keep_next = pltpu.make_async_copy(grad_ref, nexts_ref.at[slot], out_sems.at[0])
    keep_grads = pltpu.make_async_copy(grads_buf, grads_ref.at[slot], out_sems.at[1])
    keep_gain = pltpu.make_async_copy(gain_buf, gains_ref.at[slot], out_sems.at[2])

    @pl.when(role == 2)
    def _():
        bring_inner.start()

    @pl.when(role == 1)
    def _():
        bring_saved.start()

    @pl.when(role > 0)
    def _():
        bring_entry.start()
        chosen(table_ref[spot + 2], candidates, grad_ref)
        keep_next.start()
        normed_buf[...] = jnp.zeros_like(normed_buf)

    @pl.when(role == 1)
    def _():
        grads_buf[:, 3 * width :] = grad_ref[...]
        mixed_buf[...] = matmul(grad_ref[...], lead_ref[3 * width :, :]).astype(LOW)
        bring_saved.wait()
        left = lax.broadcasted_iota(jnp.int32, (tokens, 128), 1) < HEAD_SIZE
        zero = jnp.zeros((tokens, 128), LOW)
        scale = HEAD_SIZE ** (-0.5)

        @pl.loop(0, HEADS // 8)
        def _(group):
            for pair in range(4):
                at = group * 512 + pair * 128
                query = saved_buf[:, lanes(at, 128)]
                key = saved_buf[:, lanes(width + at, 128)]
                value = saved_buf[:, lanes(2 * width + at, 128)]
                grad = mixed_buf[:, lanes(at, 128)]
                for own in (0, 1):
                    mine = lambda v: jnp.where(left, v, zero) if own == 0 else jnp.where(left, zero, v)
                    scores_buf[group * 8 + 2 * pair + own] = matmul_nt(mine(query), key)
                    probs_grad_buf[group * 8 + 2 * pair + own] = matmul_nt(mine(grad), value)

        @pl.loop(0, HEADS // 4)
        def _(group):
            same = same_segment(seg_row_ref[slot])
            for head in range(4):
                at = group * 4 + head
                probs = head_probs(scores_buf[at], same)
                probs_buf[at] = probs.astype(LOW)
                grad_probs = probs_grad_buf[at]
                scores_grad_buf[at] = (
                    probs * (grad_probs - jnp.sum(probs * grad_probs, axis=-1, keepdims=True))
                ).astype(LOW)

        @pl.loop(0, HEADS // 4)
        def _(group):
            for pair in range(2):
                at = group * 256 + pair * 128
                query = saved_buf[:, lanes(at, 128)]
                key = saved_buf[:, lanes(width + at, 128)]
                grad = mixed_buf[:, lanes(at, 128)]
                parts = []
                for own in (0, 1):
                    probs = probs_buf[group * 4 + 2 * pair + own]
                    grad_low = scores_grad_buf[group * 4 + 2 * pair + own]
                    parts.append(
                        (
                            matmul(grad_low, key) * scale,
                            matmul_tn(grad_low, query) * scale,
                            matmul_tn(probs, grad),
                        )
                    )
                for which in range(3):
                    grads_buf[:, lanes(which * width + at, 128)] = jnp.where(
                        left, parts[0][which], parts[1][which]
                    ).astype(LOW)

        @pl.loop(0, 3 * width // CHUNK, unroll=2)
        def _(j):
            at = lanes(j * CHUNK, CHUNK)
            normed_buf[...] += matmul(grads_buf[:, at], lead_ref[pl.ds(j * CHUNK, CHUNK), :])

    @pl.when(role == 2)
    def _():
        bring_inner.wait()

        @pl.loop(0, lead_ref.shape[0] // CHUNK, unroll=2)
        def _(j):
            at = lanes(j * CHUNK, CHUNK)
            grad_active = matmul(grad_ref[...], down_ref[:, at])
            grads = (gelu_slope(inner_buf[:, at]) * grad_active).astype(LOW)
            grads_buf[:, at] = grads
            normed_buf[...] += matmul(grads, lead_ref[pl.ds(j * CHUNK, CHUNK), :])

    @pl.when(role > 0)
    def _():
        keep_grads.start()
        bring_entry.wait()
        grad_normed = normed_buf[...]
        normed, factor = layer_norm(entry_buf[...].astype(WIDE))
        gain_buf[...] = jnp.broadcast_to(
            jnp.sum(grad_normed * normed, axis=0, keepdims=True), gain_buf.shape
        )
        keep_gain.start()
        out_ref[...] = (
            grad_ref[...].astype(WIDE) + norm_back(grad_normed * gain_ref[...], normed, factor)
        ).astype(LOW)
        keep_next.wait()
        keep_grads.wait()
        keep_gain.wait()


def backward_stage(
    spot, table, nexts, seg_row, gain, lead, down, entries, saved, inner, totals
):
    tokens, width = nexts[0].shape
    count = len(nexts)
    hidden = lead.shape[0]
    return pl.pallas_call(
        functools.partial(backward_kernel, spot, count),
        out_shape=[jax.ShapeDtypeStruct((tokens, width), LOW)]
        + [jax.ShapeDtypeStruct(k.shape, k.dtype) for k in totals],
        in_specs=[SMEM_SPEC] + [VMEM_SPEC] * (count + 4) + [HBM_SPEC] * 6,
        out_specs=[VMEM_SPEC] + [HBM_SPEC] * 3,
        scratch_shapes=[
            pltpu.VMEM((tokens, hidden), LOW),
            pltpu.VMEM((tokens, hidden), WIDE),
            pltpu.VMEM((tokens, hidden), LOW),
            pltpu.VMEM((tokens, width), LOW),
            pltpu.VMEM((8, width), WIDE),
            pltpu.VMEM((tokens, width), LOW),
            pltpu.VMEM((tokens, width), WIDE),
            pltpu.VMEM((HEADS, tokens, tokens), WIDE),
            pltpu.VMEM((HEADS, tokens, tokens), WIDE),
            pltpu.VMEM((HEADS, tokens, tokens), LOW),
            pltpu.VMEM((HEADS, tokens, tokens), LOW),
            pltpu.VMEM((tokens, width), LOW),
            pltpu.SemaphoreType.DMA((3,)),
            pltpu.SemaphoreType.DMA((3,)),
        ],
        input_output_aliases={count + 8 + i: 1 + i for i in range(3)},
        compiler_params=pltpu.CompilerParams(vmem_limit_bytes=18 << 20),
        cost_estimate=pl.CostEstimate(
            flops=4 * tokens * width * hidden, bytes_accessed=20 << 20, transcendentals=0
        ),
        name="backward_stage",
    )(
        table,
        *nexts,
        seg_row,
        gain,
        pinned(lead),
        pinned(down),
        far(entries),
        far(saved),
        far(inner),
        *map(far, totals),
    )


def stats_kernel(spot, plan_ref, *refs):
    candidates, (table_ref, readout_ref, peak_ref, total_ref) = refs[:-4], refs[-4:]
    step = pl.program_id(0)

    @pl.when(step == 0)
    def _():
        chosen(plan_ref[spot], candidates, readout_ref)

    logits = matmul_nt(table_ref[...], readout_ref[...])
    own_peak = jnp.max(logits, axis=0, keepdims=True)
    own_total = lambda peak: jnp.sum(jnp.exp(logits - peak), axis=0, keepdims=True)

    @pl.when(step == 0)
    def _():
        peak_ref[...] = own_peak
        total_ref[...] = own_total(own_peak)

    @pl.when(step > 0)
    def _():
        peak = jnp.maximum(peak_ref[...], own_peak)
        total_ref[...] = total_ref[...] * jnp.exp(peak_ref[...] - peak) + own_total(peak)
        peak_ref[...] = peak


def head_stats(spot, plan, readouts, table, tile):
    tokens, emb = readouts[0].shape
    vocab = table.shape[0]
    whole = pl.BlockSpec((1, tokens), lambda i: (0, 0))
    rows = pl.BlockSpec((tokens, emb), lambda i: (0, 0))
    return pl.pallas_call(
        functools.partial(stats_kernel, spot),
        out_shape=[jax.ShapeDtypeStruct((tokens, emb), LOW)]
        + [jax.ShapeDtypeStruct((1, tokens), WIDE)] * 2,
        grid=(vocab // tile,),
        in_specs=[SMEM_SPEC]
        + [rows] * len(readouts)
        + [pl.BlockSpec((tile, emb), lambda i: (i, 0))],
        out_specs=[rows, whole, whole],
        compiler_params=pltpu.CompilerParams(vmem_limit_bytes=32 << 20),
        cost_estimate=pl.CostEstimate(
            flops=2 * tokens * vocab * emb, bytes_accessed=5 << 20, transcendentals=tokens * vocab
        ),
        name="head_stats",
    )(plan, *readouts, far(table))


def head_kernel(spot, table_base_ref, readout_ref, table_ref, logsum_ref, ids_ref, head_ref, grad_ref):
    tile = table_ref.shape[0]
    logits = matmul_nt(table_ref[...], readout_ref[...])
    ids = ids_ref[...] - (table_base_ref[spot] + pl.program_id(0) * tile)
    hits = lax.broadcasted_iota(jnp.int32, logits.shape, 0) == ids
    probs = jnp.exp(logits - logsum_ref[...])
    grads = jnp.where(hits, probs - 1.0, probs).astype(LOW)
    head = matmul(grads, readout_ref[...])
    unit = tile // 4
    for shard in range(4):
        head_ref[shard, :unit] = head[shard * unit : (shard + 1) * unit].astype(LOW)
    term = matmul_tn(grads, table_ref[...])

    @pl.when(pl.program_id(0) == 0)
    def _():
        grad_ref[...] = term

    @pl.when(pl.program_id(0) > 0)
    def _():
        grad_ref[...] += term


def head_grads(spot, base, readout, table, logsum, ids):
    tokens, emb = readout.shape
    vocab = table.shape[0]
    row = pl.BlockSpec((1, tokens), lambda i: (0, 0))
    whole = pl.BlockSpec((tokens, emb), lambda i: (0, 0))
    part = pl.BlockSpec((vocab // 4, emb), lambda i: (i, 0))
    return pl.pallas_call(
        functools.partial(head_kernel, spot),
        out_shape=[
            pltpu.HBM((16, 512, emb), LOW),
            jax.ShapeDtypeStruct((tokens, emb), WIDE),
        ],
        grid=(4,),
        in_specs=[SMEM_SPEC, whole, part, row, row],
        out_specs=[pl.BlockSpec((4, 512, emb), lambda i: (i, 0, 0)), whole],
        compiler_params=pltpu.CompilerParams(vmem_limit_bytes=32 << 20),
        cost_estimate=pl.CostEstimate(
            flops=6 * tokens * vocab * emb, bytes_accessed=9 << 20, transcendentals=tokens * vocab
        ),
        name="head_grads",
    )(base, readout, far(table), logsum, ids)


def pair_kernel(former_ref, latter_ref, out_ref):
    rows = out_ref.shape[0]
    out_ref[...] = former_ref[:rows].astype(WIDE) + latter_ref[:rows].astype(WIDE)


def pair_sum(former, latter, rows):
    return pl.pallas_call(
        pair_kernel,
        out_shape=jax.ShapeDtypeStruct((rows, former.shape[1]), WIDE),
        in_specs=[VMEM_SPEC] * 2,
        out_specs=VMEM_SPEC,
        compiler_params=pltpu.CompilerParams(vmem_limit_bytes=8 << 20),
        cost_estimate=pl.CostEstimate(flops=0, bytes_accessed=1024, transcendentals=0),
        name="pair_sum",
    )(former, latter)


def lookup_kernel(ids_ref, table_ref, noise_ref, out_ref, total_ref, low_ref):
    step = pl.program_id(0)
    parts, tile = table_ref.shape
    tokens = ids_ref.shape[1]
    blocks = tile // 128

    @pl.when(step == 0)
    def _():
        lane = jnp.bitwise_and(ids_ref[...], 127)
        hits = lax.broadcasted_iota(jnp.int32, (128, tokens), 0) == lane
        low_ref[...] = jnp.where(hits, 1.0, 0.0).astype(LOW)
        total_ref[...] = noise_ref[...].astype(WIDE)

    stacked = jnp.concatenate(
        [table_ref[:, block * 128 : (block + 1) * 128] for block in range(blocks)]
    )
    found = matmul(stacked, low_ref[...])
    own = jnp.right_shift(ids_ref[...], 7) - step * blocks
    total = jnp.zeros_like(total_ref)
    for block in range(blocks):
        total = jnp.where(own == block, found[block * parts : (block + 1) * parts], total)
    total_ref[...] += total

    @pl.when(step == pl.num_programs(0) - 1)
    def _():
        out_ref[...] = total_ref[...].astype(LOW)


def lookup(ids, table, noise, tile):
    parts, vocab = table.shape
    tokens = ids.shape[1]
    whole = pl.BlockSpec((parts, tokens), lambda i: (0, 0))
    return pl.pallas_call(
        lookup_kernel,
        out_shape=jax.ShapeDtypeStruct((parts, tokens), LOW),
        grid=(vocab // tile,),
        in_specs=[
            pl.BlockSpec((1, tokens), lambda i: (0, 0)),
            pl.BlockSpec((parts, tile), lambda i: (0, i)),
            whole,
        ],
        out_specs=whole,
        scratch_shapes=[pltpu.VMEM((parts, tokens), WIDE), pltpu.VMEM((128, tokens), LOW)],
        compiler_params=pltpu.CompilerParams(vmem_limit_bytes=32 << 20),
        cost_estimate=pl.CostEstimate(
            flops=2 * 128 * vocab * tokens, bytes_accessed=4 << 20, transcendentals=0
        ),
        name="lookup",
    )(ids, far(table), noise)


def lead_grad_kernel(where_ref, normed_ref, mixed_ref, grads_ref, *refs):
    got_ref, out_refs, (turned_ref, result_ref) = None, refs[:-2], refs[-2:]
    if len(out_refs) > 1:
        got_ref, out_refs = out_refs[0], out_refs[1:]
    role, half, spot = where_ref[0], where_ref[1], where_ref[2]
    step = pl.program_id(0)
    width = normed_ref.shape[1]
    steps = pl.num_programs(0)
    use_mixed = jnp.logical_and(role == 1, half == 1)

    @pl.when(step == 0)
    def _():
        turned_ref[...] = normed_ref[...].T

    @pl.when(jnp.logical_and(step == steps // 2, use_mixed))
    def _():
        turned_ref[...] = mixed_ref[...].T

    result_ref[...] = matmul(turned_ref[...], grads_ref[...])
    unit = width // 16

    def put(block, rows, part):
        if got_ref is not None:
            part = part + got_ref[block, rows, :].astype(WIDE)
        out_ref = out_refs[0].at[block] if got_ref is None else out_refs[block]
        out_ref[rows, :] = part.astype(LOW)

    @pl.when(half == 0)
    def _():
        for block in range(4):
            x = (spot + block) % 4
            put(block, slice(None), result_ref[pl.ds(pl.multiple_of(x * 4 * unit, 4 * unit), 4 * unit)])

    @pl.when(half == 1)
    def _():
        for block in range(4):
            y = (spot + block) % 4
            for x in range(4):
                rows = pl.ds(pl.multiple_of((4 * x + y) * unit, unit), unit)
                put(block, slice(x * unit, (x + 1) * unit), result_ref[rows])


CHEAP = pl.CostEstimate(flops=0, bytes_accessed=1024, transcendentals=0)


def lead_grad(where, normed, saved, grads, got=None):
    tokens, width = normed.shape
    tile = 512
    whole = pl.BlockSpec((4, width // 4, tile), lambda i, where: (0, 0, i))
    block = pl.BlockSpec((width // 4, tile), lambda i, where: (0, i))
    shape = (width // 4, 2 * width)
    return pl.pallas_call(
        lead_grad_kernel,
        out_shape=[jax.ShapeDtypeStruct((4,) + shape, LOW)]
        if got is None
        else [jax.ShapeDtypeStruct(shape, LOW)] * 4,
        grid_spec=pltpu.PrefetchScalarGridSpec(
            num_scalar_prefetch=1,
            grid=(2 * width // tile,),
            in_specs=[
                pl.BlockSpec((tokens, width), lambda i, where: (0, 0)),
                pl.BlockSpec((tokens, width), lambda i, where: (0, 3)),
                pl.BlockSpec((tokens, tile), lambda i, where: (0, where[1] * (2 * width // tile) + i)),
            ]
            + ([] if got is None else [whole]),
            out_specs=[whole] if got is None else [block] * 4,
            scratch_shapes=[pltpu.VMEM((width, tokens), LOW), pltpu.VMEM((width, tile), WIDE)],
        ),
        compiler_params=pltpu.CompilerParams(vmem_limit_bytes=24 << 20),
        cost_estimate=CHEAP
        if got is None
        else pl.CostEstimate(
            flops=4 * tokens * width * width, bytes_accessed=12 << 20, transcendentals=0
        ),
        name="lead_grad",
    )(where, far(normed), far(saved), far(grads), *([] if got is None else [got]))


def down_grad_kernel(where_ref, saved_ref, nexts_ref, *refs):
    got_ref, out_refs, (buf_ref, got_buf, sems) = None, refs[:-3], refs[-3:]
    if len(out_refs) > 1:
        got_ref, out_refs = out_refs[0], out_refs[1:]
    role, half, spot = where_ref[0], where_ref[1], where_ref[2]
    at = pl.program_id(0)
    unit = saved_ref.shape[1] // 4

    @pl.when(role == 2)
    def _():
        if got_ref is not None:
            bring = pltpu.make_async_copy(got_ref, got_buf, sems.at[4])
            pl.when(at == 0)(bring.start)
        result = matmul_tn(saved_ref[...], nexts_ref[...])
        if got_ref is not None:
            pl.when(at == 0)(bring.wait)

        def put(block, rows, part):
            if got_ref is not None:
                part = part + got_buf[block, rows, :].astype(WIDE)
            buf_ref[block, rows, :] = part.astype(LOW)

        @pl.when(half == 0)
        def _():
            put((at - spot + 4) % 4, slice(None), result)

        @pl.when(half == 1)
        def _():
            rows = pl.ds(pl.multiple_of(at * unit, unit), unit)
            for y in range(4):
                put((y - spot + 4) % 4, rows, result[y * unit : (y + 1) * unit])

        @pl.when(at == pl.num_programs(0) - 1)
        def _():
            copies = [pltpu.make_async_copy(buf_ref, out_refs[0], sems.at[0])]
            if got_ref is not None:
                copies = [
                    pltpu.make_async_copy(buf_ref.at[block], out_ref, sems.at[block])
                    for block, out_ref in enumerate(out_refs)
                ]
            for copy in copies:
                copy.start()
            for copy in copies:
                copy.wait()


def down_grad(where, saved, nexts, got=None):
    tokens, hidden = saved.shape
    width = nexts.shape[1]
    rows = hidden // 8
    live = lambda where: jnp.where(where[0] == 2, 1, 0)
    return pl.pallas_call(
        down_grad_kernel,
        out_shape=[pltpu.HBM((4, rows, width), LOW)]
        if got is None
        else [pltpu.HBM((rows, width), LOW)] * 4,
        grid_spec=pltpu.PrefetchScalarGridSpec(
            num_scalar_prefetch=1,
            grid=(4,),
            in_specs=[
                pl.BlockSpec((tokens, rows), lambda i, where: (0, (where[1] * 4 + i) * live(where))),
                pl.BlockSpec((tokens, width), lambda i, where: (0, 0)),
            ]
            + ([] if got is None else [HBM_SPEC]),
            out_specs=[HBM_SPEC] * (1 if got is None else 4),
            scratch_shapes=[
                pltpu.VMEM((4, rows, width), LOW),
                pltpu.VMEM((4, 16, 128) if got is None else (4, rows, width), LOW),
                pltpu.SemaphoreType.DMA((5,)),
            ],
        ),
        compiler_params=pltpu.CompilerParams(vmem_limit_bytes=28 << 20),
        cost_estimate=CHEAP,
        name="down_grad",
    )(where, far(saved), far(nexts), *([] if got is None else [far(got)]))


def upper_kernel(where_ref, *refs):
    out_ref = refs[4]
    rows = refs[0].shape[0]
    for at, part in enumerate(refs[:4]):
        place = (where_ref[0] - at + 4) % 4
        out_ref[pl.ds(pl.multiple_of(place * rows, rows), rows), :] = part[...]


def upper_half(where, parts):
    rows, width = parts[0].shape
    return pl.pallas_call(
        upper_kernel,
        out_shape=jax.ShapeDtypeStruct((4 * rows, width), LOW),
        in_specs=[SMEM_SPEC] + [VMEM_SPEC] * 4,
        out_specs=VMEM_SPEC,
        compiler_params=pltpu.CompilerParams(vmem_limit_bytes=8 << 20),
        name="upper_half",
    )(where, *parts)


def hold_down_kernel(where_ref, mine_ref, other_ref, own_ref, out_ref, sems):
    rows = mine_ref.shape[0]
    core = where_ref[1]
    spot = lambda at: out_ref.at[pl.ds(pl.multiple_of(at * rows, rows), rows), :]
    copies = [
        pltpu.make_async_copy(mine_ref, spot(core), sems.at[0]),
        pltpu.make_async_copy(other_ref, spot(1 - core), sems.at[1]),
        pltpu.make_async_copy(own_ref, out_ref.at[pl.ds(2 * rows, 2 * rows), :], sems.at[2]),
    ]
    for copy in copies:
        copy.start()
    for copy in copies:
        copy.wait()


def hold_down(where, mine, other, own):
    rows, width = mine.shape
    return pl.pallas_call(
        hold_down_kernel,
        out_shape=pltpu.VMEM((4 * rows, width), LOW),
        in_specs=[SMEM_SPEC] + [VMEM_SPEC] * 2 + [HBM_SPEC],
        out_specs=VMEM_SPEC,
        scratch_shapes=[pltpu.SemaphoreType.DMA((3,))],
        compiler_params=pltpu.CompilerParams(vmem_limit_bytes=8 << 20),
        name="hold_down",
    )(where, mine, other, far(own))


def noise_kernel(spot, plan_ref, ids_ref, *refs):
    candidates, (packed_ref, noise_ref, buf_ref) = refs[:-3], refs[-3:]
    parts = noise_ref.shape[0]
    chosen(plan_ref[spot], candidates, buf_ref)
    packed_ref[:parts] = buf_ref[...]
    noise_ref[...] = buf_ref[...].astype(WIDE)
    ids = ids_ref[...]
    high = jnp.right_shift(ids, 8).astype(WIDE)
    low = jnp.bitwise_and(ids, 255).astype(WIDE)
    at = lax.broadcasted_iota(jnp.int32, (16, ids.shape[1]), 0)
    split = jnp.where(at == 0, high, jnp.where(at == 1, low, 0.0))
    packed_ref[parts:] = split.astype(LOW)


def noise_pack(spot, plan, ids, candidates):
    parts, tokens = candidates[0].shape
    return pl.pallas_call(
        functools.partial(noise_kernel, spot),
        out_shape=[
            jax.ShapeDtypeStruct((parts + 16, tokens), LOW),
            jax.ShapeDtypeStruct((parts, tokens), WIDE),
        ],
        in_specs=[SMEM_SPEC] + [VMEM_SPEC] * (1 + len(candidates)),
        out_specs=[VMEM_SPEC] * 2,
        scratch_shapes=[pltpu.VMEM((parts, tokens), LOW)],
        compiler_params=pltpu.CompilerParams(vmem_limit_bytes=8 << 20),
        cost_estimate=CHEAP,
        name="noise_pack",
    )(plan, ids, *candidates)


def embed_kernel(base_ref, mine_ref, other_ref, out_ref, total_ref):
    step = pl.program_id(0)
    steps = pl.num_programs(0)
    parts = out_ref.shape[0]
    blocks = total_ref.shape[0] // parts

    def add(gathered_ref):
        count, _, tokens = gathered_ref.shape
        term = None
        for at in range(count):
            split = gathered_ref[at, parts : parts + 16].astype(WIDE)
            ids = (split[0:1] * 256.0 + split[1:2]).astype(jnp.int32) - base_ref[0]
            lane = jnp.bitwise_and(ids, 127)
            hits = lax.broadcasted_iota(jnp.int32, (128, tokens), 0) == lane
            hits = jnp.where(hits, 1.0, 0.0).astype(LOW)
            own = jnp.right_shift(ids, 7)
            grads = gathered_ref[at, :parts]
            masked = jnp.concatenate(
                [grads * jnp.where(own == block, 1.0, 0.0).astype(LOW) for block in range(blocks)]
            )
            part = matmul_nt(masked, hits)
            term = part if term is None else term + part

        @pl.when(step == 0)
        def _():
            total_ref[...] = term

        @pl.when(step > 0)
        def _():
            total_ref[...] += term

    pl.when(step < steps // 2)(lambda: add(mine_ref))
    pl.when(step >= steps // 2)(lambda: add(other_ref))

    @pl.when(step == steps - 1)
    def _():
        rows = out_ref.shape[1]
        for block in range(blocks):
            size = min(128, rows - block * 128)
            out_ref[:, block * 128 : block * 128 + size] = total_ref[
                block * parts : (block + 1) * parts, :size
            ]


def embed_sum(base, mine, other, parts, rows):
    count, deep, tokens = mine.shape
    step = 4
    half = count // step
    blocks = -(-rows // 128)
    return pl.pallas_call(
        embed_kernel,
        out_shape=jax.ShapeDtypeStruct((parts, rows), WIDE),
        grid=(2 * half,),
        in_specs=[
            SMEM_SPEC,
            pl.BlockSpec((step, deep, tokens), lambda i: (jnp.minimum(i, half - 1), 0, 0)),
            pl.BlockSpec((step, deep, tokens), lambda i: (jnp.maximum(i - half, 0), 0, 0)),
        ],
        out_specs=pl.BlockSpec((parts, rows), lambda i: (0, 0)),
        scratch_shapes=[pltpu.VMEM((blocks * parts, 128), WIDE)],
        compiler_params=pltpu.CompilerParams(vmem_limit_bytes=32 << 20),
        cost_estimate=CHEAP,
        name="embed_sum",
    )(base, mine, other)


def empty(*kinds):
    return pl.pallas_call(
        lambda *refs: None,
        out_shape=[pltpu.HBM(shape, dtype) for shape, dtype in kinds],
        out_specs=[HBM_SPEC] * len(kinds),
        compiler_params=pltpu.CompilerParams(vmem_limit_bytes=1 << 20),
        name="empty",
    )()


ROW_LEN = 128
SEC, GRP, NX, NY = 4, 2, 4, 4
ALL = ("section", "group", "row")
TURNS = (1, 3, 2)


def route(value, target_of):
    number = lambda s, g, x, y: (s * GRP + g) * NX * NY + x * NY + y
    pairs = []
    for at in itertools.product(range(SEC), range(GRP), range(NX), range(NY)):
        target = target_of(*at)
        if target is not None:
            pairs.append((number(*at), number(*target)))
    return lax.ppermute(value, ALL, pairs)


def link(value, source, target):
    return route(value, lambda s, g, x, y: (target, g, x, y) if s == source else None)


def turn(value, by):
    return route(value, lambda s, g, x, y: ((s + by) % SEC, g, x, y))


def swap_cores(value, sections=range(SEC)):
    return route(value, lambda s, g, x, y: (s, 1 - g, x, y) if s in sections else None)


def plane_route(value, by, first, sections=range(SEC)):
    def target_of(s, g, x, y):
        if s not in sections:
            return None
        if (g == 0) == first:
            return (s, g, (x + by) % NX, y)
        return (s, g, x, (y + by) % NY)

    return route(value, target_of)


def after(value, earlier):
    return lax.optimization_barrier((value, earlier))[0]


def row_block(values, block, count):
    size = values.shape[0] // count
    return lax.dynamic_slice_in_dim(values, block * size, size, 0)


def plane_first(mine, sections=range(SEC)):
    return [mine[0]] + [plane_route(mine[by], by, True, sections) for by in TURNS]


def plane_sum(pieces):
    total = pieces[0].astype(WIDE)
    for piece in pieces[1:]:
        total = total + piece.astype(WIDE)
    return total.astype(LOW)


def plane_second(pieces, second, sections=range(SEC)):
    total = plane_sum(pieces)
    return [row_block(total, second, 4)] + [
        plane_route(row_block(total, (second + by) % 4, 4), by, False, sections) for by in TURNS
    ]


def group_exchange(values, first):
    number = lambda s, g, x, y: (s * GRP + g) * NX * NY + x * NY + y
    groups = []
    for s in range(SEC):
        for g in range(GRP):
            along_x = (g == 0) == first
            for at in range(4):
                groups.append(
                    [number(s, g, i, at) if along_x else number(s, g, at, i) for i in range(4)]
                )
    return lax.all_to_all(values, ALL, 0, 0, axis_index_groups=groups, tiled=True)


def section_exchange(values):
    return lax.all_to_all(values, "section", 0, 0, tiled=True)


def plans(micro, vocab_part):
    last = SEC - 1
    steps = micro + 2 * last
    table = np.zeros((SEC, 6 * steps + 2), np.int32)
    for s in range(SEC):
        for way in range(2):
            depth = s if way == 0 else last - s
            for step in range(steps):
                at = step - 2 * depth
                if 0 <= at < micro:
                    sources = ([0] if step < micro else []) + [
                        d + 1 for d in range(last) if 0 <= step - 2 - 2 * d < micro
                    ]
                    spot = 3 * (way * steps + step)
                    table[s, spot : spot + 3] = (1 + s % 2, at, sources.index(depth))
        table[s, 6 * steps :] = (s * vocab_part, s)
    return table


def local(
    token_ids,
    segment_ids,
    noise_input,
    embed_table,
    input_proj,
    norm_gain,
    lead_weight,
    down_weight,
    final_gain,
    readout_proj,
    head_table,
):
    section = lax.axis_index("section")
    core = lax.axis_index("group")
    row = lax.axis_index("row")
    x_at, y_at = row // NY, row % NY
    first_at = jnp.where(core == 0, x_at, y_at)
    micro, _, tokens = token_ids.shape
    width = input_proj.shape[1]
    hidden = lead_weight.shape[2]
    half_rows = down_weight.shape[1]
    emb_part = input_proj.shape[0]
    vocab_part, emb = head_table.shape
    vocab = embed_table.shape[0]
    all_tokens = micro * tokens
    last = SEC - 1
    gain_half = norm_gain.astype(WIDE)
    lead = lead_weight[0]
    own_down = down_weight[0]
    seg_row = segment_ids
    flat_ids = token_ids.reshape(-1)

    plan = plans(micro, vocab_part)
    steps = micro + 2 * last
    table = lax.dynamic_index_in_dim(jnp.asarray(plan), section, 0, False)
    flat_ids = after(flat_ids, table)
    where_start = jnp.stack((first_at, core)).astype(jnp.int32)
    to_first = lambda v: [v] + [link(v, s, 0) for s in range(1, SEC)]
    eighth = row_block(row_block(own_down, core, 2), first_at, 4)
    eighth = jnp.where(section == 1, link(eighth, 0, 1), link(eighth, 2, 3))
    noise = noise_input[:, 0].transpose(2, 0, 1).reshape(emb_part, -1)
    own_embedded = lookup(flat_ids[None], embed_table.T, noise, 3200)
    parts = to_first(jnp.concatenate((own_embedded, input_proj), axis=1))
    embedded = jnp.concatenate([part[:, :all_tokens] for part in parts])
    input_full = jnp.concatenate([part[:, all_tokens:] for part in parts])
    first_in = matmul_tn(embedded, input_full).astype(LOW).reshape(micro, tokens, width)
    eighth = after(eighth, own_embedded)
    eighths = [eighth] + [plane_route(eighth, by, True) for by in (1, 2, 3)]
    upper = upper_half(where_start, [after(part, first_in) for part in eighths])
    held_down = hold_down(where_start, upper, swap_cores(upper), own_down)

    kept = empty(
        ((micro, tokens, width), LOW),
        ((micro, tokens, width), LOW),
        ((micro, tokens, hidden), LOW),
        ((micro, tokens, hidden), WIDE),
    )

    def sources(first, step, hops, order):
        arrived = [hops[step - 2, s] for s in order if (step - 2, s) in hops]
        return ([first[step]] if step < micro else []) + arrived

    outs, hops = [], {}
    for step in range(steps):
        out, *kept = forward_stage(
            3 * step,
            table,
            sources(first_in, step, hops, range(SEC)),
            seg_row,
            gain_half,
            held_lead if step > 0 else lead,
            held_down if step > 1 else None,
            kept,
            step == 0,
        )
        if step == 0:
            held_lead = kept.pop()
        outs.append(out)
        for s in range(last):
            if 0 <= step - 2 * s < micro:
                ready = after(out, hops[step - 1, s]) if (step - 1, s) in hops else out
                hops[step, s] = link(ready, s, s + 1)
        if step == 2:
            readout_own = after(readout_proj.T, out)
            readout_full = jnp.concatenate(
                [link(readout_own, s, last) for s in range(last)] + [readout_own]
            )
    entries, normeds, saved, inner = kept

    final_rows = jnp.concatenate(outs[2 * last :]).astype(WIDE)
    normed_f, factor_f = layer_norm(final_rows)
    gain_f = final_gain.astype(WIDE)
    final_low = (normed_f * gain_f).astype(LOW)
    readout = matmul_nt(final_low, readout_full).astype(LOW)
    sent = [link(readout, last, s) for s in range(last)]
    readout, peak, total = head_stats(6 * steps + 1, table, sent + [readout], head_table, 2000)
    stats = jnp.concatenate((peak, total))
    all_stats = section_exchange(jnp.tile(stats, (SEC, 1))).reshape(SEC, 2, all_tokens)
    peak = jnp.max(all_stats[:, 0], axis=0)
    total = jnp.sum(all_stats[:, 1] * jnp.exp(all_stats[:, 0] - peak), axis=0)
    logsum = (peak + jnp.log(total))[None]
    head_grad, grad_readout = head_grads(
        6 * steps, table, readout, head_table, logsum, flat_ids[None]
    )
    grad_low = grad_readout.astype(LOW)
    for s in range(last):
        grad_readout = grad_readout + link(grad_low, s, last).astype(WIDE)
    grad_readout = grad_readout.astype(LOW)
    head_grad = lax.psum_scatter(head_grad, "row", scatter_dimension=0)
    readout_grad = matmul_tn(final_low, grad_readout)
    grad_final = matmul(grad_readout, readout_full)
    final_gain_grad = jnp.sum(grad_final * normed_f, axis=0)
    last_grads = norm_back(grad_final * gain_f, normed_f, factor_f).astype(LOW)
    last_grads = last_grads.reshape(micro, tokens, width)

    lead_turned = turned(6 * steps + 1, table, after(lead, grad_low), 0)
    down_turned = turned(6 * steps + 1, table, after(held_down, grad_low), 1)
    totals = empty(
        ((micro, tokens, width), LOW),
        ((micro, tokens, hidden), LOW),
        ((micro, 8, width), WIDE),
    )
    outs, hops = [], {}
    for step in range(steps):
        out, *totals = backward_stage(
            3 * (steps + step),
            table,
            sources(last_grads, step, hops, range(SEC - 1, -1, -1)),
            seg_row,
            gain_half,
            lead_turned,
            down_turned,
            entries,
            saved,
            inner,
            totals,
        )
        outs.append(out)
        for s in range(1, SEC):
            if 0 <= step - 2 * (last - s) < micro:
                ready = after(out, hops[step - 1, s]) if (step - 1, s) in hops else out
                hops[step, s] = link(ready, s, s - 1)
    section, core, row, readout_grad, final_gain_grad = lax.optimization_barrier(
        (section, core, row, readout_grad, final_gain_grad, out)
    )[:5]
    x_at, y_at = row // NY, row % NY
    first_at, second_at = jnp.where(core == 0, x_at, y_at), jnp.where(core == 0, y_at, x_at)
    is_mlp = section % 2 == 1

    first_grads = jnp.concatenate(outs[2 * last :])
    noise_grad = matmul_nt(input_full, first_grads).astype(LOW)
    pieces = noise_grad.reshape(SEC, emb_part, all_tokens)
    sent = [link(pieces[s], 0, s) for s in range(1, SEC)]

    grad_nexts, grads, gain_grads = totals
    gain_grad = jnp.sum(gain_grads[:, 0], axis=0)
    flat = lambda v: v.reshape(all_tokens, v.shape[-1])
    grads = after(grads, head_grad)
    normed, grad_nexts, grads, saved = flat(normeds), flat(grad_nexts), flat(grads), flat(saved)
    odd = (1, 3)
    role = jnp.where(is_mlp, 2, 1)
    where_other = jnp.stack((role, 1 - core, second_at)).astype(jnp.int32)
    where_mine = jnp.stack((role, core, first_at)).astype(jnp.int32)
    both = lambda mine, other: jnp.where(
        core == 0,
        jnp.concatenate((mine, other), axis=1),
        jnp.concatenate((other, mine), axis=1),
    )
    down_got = swap_cores(down_grad(where_other, saved, grad_nexts)[0], odd)
    down_mine = down_grad(where_mine, saved, grad_nexts, down_got)
    down_first = plane_first(down_mine, odd)
    late_ids = after(flat_ids, down_mine)[None]
    packed, noise_wide = noise_pack(6 * steps + 1, table, late_ids, [pieces[0]] + sent)
    where_other = after(where_other, packed)
    lead_got = swap_cores(lead_grad(where_other, normed, saved, grads)[0])

    input_grad = matmul(embedded, first_grads).reshape(SEC, 16, 4, width)
    input_grad = input_grad.transpose(1, 0, 2, 3).reshape(16, 16, width)
    readout_grad = readout_grad.reshape(16, 16, width)
    vectors = jnp.concatenate(
        (
            gain_grad.reshape(16, 64),
            final_gain_grad.reshape(SEC, 16, 16).transpose(1, 0, 2).reshape(16, 64),
            jnp.zeros((16, width - 128), WIDE),
        ),
        axis=1,
    )
    small = jnp.concatenate(
        (
            jnp.where(section == 0, input_grad, readout_grad),
            vectors[:, None],
            jnp.zeros((16, 15, width), WIDE),
        ),
        axis=1,
    ).astype(LOW)
    half_of = lambda which: lax.dynamic_slice_in_dim(small, which * (width // 2), width // 2, 2)
    small = half_of(core).astype(WIDE) + swap_cores(half_of(1 - core)).astype(WIDE)
    small = small.astype(LOW).reshape(NX, NY, 32, width // 2)
    small = jnp.where(core == 0, small, small.swapaxes(0, 1)).reshape(4, NY * 32, width // 2)
    deep = emb_part + 16

    def exchange(blocks, packed, first):
        rows = blocks.shape[1]
        everywhere = jnp.broadcast_to(packed, (4,) + packed.shape)
        got = group_exchange(jnp.concatenate((blocks, everywhere), axis=1), first)
        return jnp.sum(got[:, :rows].astype(WIDE), axis=0).astype(LOW), got[:, rows:]

    small, packed = exchange(after(small, down_first), packed, True)
    small, packed = exchange(
        small.reshape(4, 32, width // 2), packed.reshape(4 * deep, all_tokens), False
    )
    packed = packed.reshape(16, deep, all_tokens)
    down_second = plane_second(after(down_first, packed), second_at, odd)
    lead_mine = lead_grad(after(where_mine, packed), normed, saved, grads, lead_got)
    lead_first = plane_first(lead_mine)
    packed_other = swap_cores(packed)
    small = both(small, swap_cores(small))
    embed_grad = embed_sum(
        (row * (vocab // 16)).reshape(1), packed, packed_other, emb_part, vocab // 16
    )
    gain_out = small[16, :64].astype(WIDE)
    input_rows = small[:16].reshape(SEC, 4, width)
    readout_rows = small[:16].reshape(64, SEC, 64)
    final_rows = small[16, 64:128].reshape(SEC, 16)

    finals = jnp.pad(final_rows, ((0, 0), (0, width - 16)))[:, None]
    mine = jnp.where(
        section == 0, input_rows, readout_rows.transpose(1, 0, 2).reshape(SEC, 4, width)
    )
    shared = section_exchange(
        jnp.concatenate((mine, finals, jnp.zeros((SEC, 3, width), LOW)), axis=1)
    )
    input_out = shared[0, :4]
    readout_out = shared[last, :4].reshape(64, 64)
    final_out = shared[last, 4, :16]

    ready = (embed_grad, shared)
    lead_second = plane_second(after(lead_first, ready), second_at)
    down_part = plane_sum(after(down_second, ready))
    lead_part = plane_sum(lead_second)
    noise_out = noise_wide.reshape(emb_part, micro, tokens).transpose(1, 2, 0)
    lead_out = both(lead_part, swap_cores(lead_part)).astype(WIDE)

    def first_target(s, g, x, y):
        if s % 2 == 0:
            return None
        return (s - 1, 0, x, y) if g == 0 else (s, 0, x, y)

    def second_target(s, g, x, y):
        return (s - 1, 1, x, y) if s % 2 == 1 and g == 0 else None

    to_core_0 = route(down_part, first_target)
    to_core_1 = route(down_part, second_target)
    down_out = jnp.where(
        core == 0, to_core_0, jnp.where(is_mlp, down_part, to_core_1)
    ).astype(WIDE)

    head_out = pair_sum(head_grad, swap_cores(head_grad), vocab_part // (NX * NY))
    return (
        noise_out[:, None],
        embed_grad.T,
        input_out.astype(WIDE),
        gain_out[None],
        lead_out[None],
        down_out[None],
        final_out.astype(WIDE),
        readout_out.astype(WIDE),
        head_out,
    )


def solution(mesh):
    in_specs = (
        P(None, ("group", "row"), None),
        P(None, ("group", "row"), None),
        P(None, ("group", "row"), None, "section"),
        P(None, "section"),
        P("section", None),
        P("section", None),
        P("section", None, None),
        P("section", None, None),
        P(),
        P(None, "section"),
        P("section", None),
    )
    out_specs = (
        P(None, ("group", "row"), None, "section"),
        P("row", "section"),
        P(("section", "row"), None),
        P("section", "row"),
        P("section", "row", None),
        P("section", "row", None),
        P(("section", "row")),
        P("row", "section"),
        P(("section", "row"), None),
    )
    return jax.shard_map(local, mesh=mesh, in_specs=in_specs, out_specs=out_specs, check_vma=False)
```

```python
import functools
import itertools

import jax
import jax.numpy as jnp
import numpy as np
from jax import lax
from jax.experimental import pallas as pl
from jax.experimental.pallas import tpu as pltpu
from jax.sharding import PartitionSpec as P

HEADS = 16
HEAD_SIZE = 64
LOW = jnp.bfloat16
WIDE = jnp.float32
EPSILON = 1e-05
MASKED = -1000000000.0
CHUNK = 1024
GELU_A = 0.7978845608028654
GELU_B = 0.044715
HBM_SPEC = pl.BlockSpec(memory_space=pltpu.HBM)
VMEM_SPEC = pl.BlockSpec(memory_space=pltpu.VMEM)
SMEM_SPEC = pl.BlockSpec(memory_space=pltpu.SMEM)


def matmul(former, latter):
    return jnp.dot(former, latter, preferred_element_type=WIDE)


def matmul_nt(former, latter):
    return lax.dot_general(
        former, latter, (((1,), (1,)), ((), ())), preferred_element_type=WIDE
    )


def matmul_tn(former, latter):
    return lax.dot_general(
        former, latter, (((0,), (0,)), ((), ())), preferred_element_type=WIDE
    )


def layer_norm(values):
    centre = jnp.mean(values, axis=-1, keepdims=True)
    centred = values - centre
    variance = jnp.mean(centred * centred, axis=-1, keepdims=True)
    factor = lax.rsqrt(variance + EPSILON)
    return (centred * factor, factor)


def norm_back(grad_normed, normed, factor):
    first_mean = jnp.mean(grad_normed, axis=-1, keepdims=True)
    second_mean = jnp.mean(grad_normed * normed, axis=-1, keepdims=True)
    return factor * (grad_normed - first_mean - normed * second_mean)


def gelu(v):
    return 0.5 * v * (1.0 + jnp.tanh(GELU_A * (v + GELU_B * (v * v * v))))


def gelu_slope(v):
    square = v * v
    bend = jnp.tanh(GELU_A * (v + GELU_B * (square * v)))
    return 0.5 * (1.0 + bend) + 0.5 * v * (1.0 - bend * bend) * (
        GELU_A * (1.0 + 3.0 * GELU_B * square)
    )


def head_probs(scores, same):
    scores = jnp.where(same, scores * HEAD_SIZE ** (-0.5), MASKED)
    expo = jnp.exp(scores - jnp.max(scores, axis=-1, keepdims=True))
    return expo * (1.0 / jnp.sum(expo, axis=-1, keepdims=True))


def same_segment(row):
    across = jnp.broadcast_to(row.astype(WIDE), (row.shape[1], row.shape[1]))
    return across.T == across


def lanes(at, size):
    return pl.ds(pl.multiple_of(at, 128), size)


def turn_kernel(spot, live, plan_ref, value_ref, out_ref):
    @pl.when(jnp.bitwise_and(plan_ref[spot], 1) >= live)
    def _():
        out_ref[...] = value_ref[...].T


def turned(spot, plan, value, live):
    rows, columns = value.shape
    if rows > columns:
        tile = rows // 8
        blocks = (pl.BlockSpec((tile, columns), lambda i: (i, 0)), pl.BlockSpec((columns, tile), lambda i: (0, i)))
    else:
        tile = columns // 8
        blocks = (pl.BlockSpec((rows, tile), lambda i: (0, i)), pl.BlockSpec((tile, rows), lambda i: (i, 0)))
    return pl.pallas_call(
        functools.partial(turn_kernel, spot, live),
        out_shape=pltpu.VMEM((columns, rows), LOW),
        grid=(8,),
        in_specs=[SMEM_SPEC, blocks[0]],
        out_specs=blocks[1],
        compiler_params=pltpu.CompilerParams(vmem_limit_bytes=12 << 20),
        cost_estimate=pl.CostEstimate(flops=0, bytes_accessed=1024, transcendentals=0),
        name="turned",
    )(plan, far(value))


def chosen(choice, candidates, buffer):
    for at, candidate in enumerate(candidates):

        @pl.when(choice == at)
        def _():
            buffer[...] = candidate[...]


def forward_kernel(spot, with_down, loads, count, *refs):
    table_ref, candidates, refs = refs[0], refs[1 : 1 + count], refs[1 + count :]
    if not with_down:
        refs = refs[:3] + (None,) + refs[3:]
    source_ref = load_sems = None
    if loads:
        source_ref, load_sems = refs[2], refs[-1]
        refs = refs[:2] + (refs[13],) + refs[3:13] + refs[14:-1]
    forward_body(spot, table_ref, candidates, source_ref, load_sems, *refs)


def forward_body(
    spot,
    table_ref,
    candidates,
    source_ref,
    load_sems,
    seg_row_ref,
    gain_ref,
    lead_ref,
    down_ref,
    entries_in,
    normeds_in,
    saved_in,
    inner_in,
    out_ref,
    entries_ref,
    normeds_ref,
    saved_ref,
    inner_ref,
    normed_buf,
    saved_buf,
    inner_buf,
    result_buf,
    scores_buf,
    probs_buf,
    entry_ref,
    out_sems,
):
    role, slot = table_ref[spot], table_ref[spot + 1]
    tokens, width = entry_ref.shape
    keeps = [
        pltpu.make_async_copy(entry_ref, entries_ref.at[slot], out_sems.at[0]),
        pltpu.make_async_copy(normed_buf, normeds_ref.at[slot], out_sems.at[1]),
        pltpu.make_async_copy(saved_buf, saved_ref.at[slot], out_sems.at[2]),
    ]
    keep_inner = pltpu.make_async_copy(inner_buf, inner_ref.at[slot], out_sems.at[3])

    def load(j):
        at = lanes(j * CHUNK, CHUNK)
        return pltpu.make_async_copy(source_ref.at[:, at], lead_ref.at[:, at], load_sems.at[j])

    def loaded(j):
        if source_ref is not None:
            load(j).wait()

    if source_ref is not None:
        for j in range(lead_ref.shape[1] // CHUNK):
            load(j).start()

        @pl.when(role != 1)
        def _():
            pl.loop(0, lead_ref.shape[1] // CHUNK)(loaded)

    @pl.when(role > 0)
    def _():
        chosen(table_ref[spot + 2], candidates, entry_ref)
        normed, _ = layer_norm(entry_ref[...].astype(WIDE))
        normed_buf[...] = (normed * gain_ref[...]).astype(LOW)
        keeps[0].start()
        keeps[1].start()

    @pl.when(role == 1)
    def _():
        @pl.loop(0, 3 * width // CHUNK, unroll=2)
        def _(j):
            at = lanes(j * CHUNK, CHUNK)
            loaded(j)
            saved_buf[:, at] = matmul(normed_buf[...], lead_ref[:, at]).astype(LOW)

        left = lax.broadcasted_iota(jnp.int32, (tokens, 128), 1) < HEAD_SIZE
        zero = jnp.zeros((tokens, 128), LOW)

        @pl.loop(0, HEADS // 8)
        def _(group):
            for pair in range(4):
                at = group * 512 + pair * 128
                query = saved_buf[:, lanes(at, 128)]
                key = saved_buf[:, lanes(width + at, 128)]
                scores_buf[group * 8 + 2 * pair] = matmul_nt(jnp.where(left, query, zero), key)
                scores_buf[group * 8 + 2 * pair + 1] = matmul_nt(jnp.where(left, zero, query), key)

        @pl.loop(0, HEADS // 4)
        def _(group):
            same = same_segment(seg_row_ref[slot])
            for head in range(4):
                at = group * 4 + head
                probs_buf[at] = head_probs(scores_buf[at], same).astype(LOW)

        @pl.loop(0, HEADS // 8)
        def _(group):
            for pair in range(4):
                at = group * 512 + pair * 128
                value = saved_buf[:, lanes(2 * width + at, 128)]
                mixed = jnp.where(
                    left,
                    matmul(probs_buf[group * 8 + 2 * pair], value),
                    matmul(probs_buf[group * 8 + 2 * pair + 1], value),
                )
                saved_buf[:, lanes(3 * width + at, 128)] = mixed.astype(LOW)

        keeps[2].start()

        @pl.loop(0, width // CHUNK)
        def _(j):
            at = lanes(j * CHUNK, CHUNK)
            loaded(3 * width // CHUNK + j)
            term = matmul(saved_buf[:, 3 * width :], lead_ref[:, lanes(3 * width + j * CHUNK, CHUNK)])
            out_ref[:, at] = (entry_ref[:, at].astype(WIDE) + term).astype(LOW)

    def feed_forward():
        result_buf[...] = entry_ref[...].astype(WIDE)

        @pl.loop(0, lead_ref.shape[1] // CHUNK, unroll=2)
        def _(j):
            at = lanes(j * CHUNK, CHUNK)
            inner = matmul(normed_buf[...], lead_ref[:, at])
            inner_buf[:, at] = inner
            active = gelu(inner).astype(LOW)
            saved_buf[:, at] = active
            result_buf[...] += matmul(active, down_ref[pl.ds(j * CHUNK, CHUNK), :])

        keeps[2].start()
        keep_inner.start()
        out_ref[...] = result_buf[...].astype(LOW)
        keep_inner.wait()

    if down_ref is not None:
        pl.when(role == 2)(feed_forward)

    @pl.when(role > 0)
    def _():
        for keep in keeps:
            keep.wait()


def pinned(value):
    return pltpu.with_memory_space_constraint(value, pltpu.VMEM)


def far(value):
    return pltpu.with_memory_space_constraint(value, pltpu.HBM)


def forward_stage(spot, table, entries, seg_row, gain, lead, down, kept, loads=False):
    tokens, width = entries[0].shape
    hidden = lead.shape[1]
    count = len(entries) + (3 if down is None else 4)
    given = [VMEM_SPEC] * (len(entries) + 2) + [HBM_SPEC if loads else VMEM_SPEC]
    return pl.pallas_call(
        functools.partial(forward_kernel, spot, down is not None, loads, len(entries)),
        out_shape=[jax.ShapeDtypeStruct((tokens, width), LOW)]
        + [jax.ShapeDtypeStruct(k.shape, k.dtype) for k in kept]
        + ([pltpu.VMEM(lead.shape, LOW)] if loads else []),
        in_specs=[SMEM_SPEC] + given + [VMEM_SPEC] * (down is not None) + [HBM_SPEC] * 4,
        out_specs=[VMEM_SPEC] + [HBM_SPEC] * 4 + [VMEM_SPEC] * loads,
        scratch_shapes=[
            pltpu.VMEM((tokens, width), LOW),
            pltpu.VMEM((tokens, hidden), LOW),
            pltpu.VMEM((tokens, hidden), WIDE),
            pltpu.VMEM((tokens, width), WIDE),
            pltpu.VMEM((HEADS, tokens, tokens), WIDE),
            pltpu.VMEM((HEADS, tokens, tokens), LOW),
            pltpu.VMEM((tokens, width), LOW),
            pltpu.SemaphoreType.DMA((4,)),
        ]
        + ([pltpu.SemaphoreType.DMA((hidden // CHUNK,))] if loads else []),
        input_output_aliases={count + 1 + i: 1 + i for i in range(4)},
        compiler_params=pltpu.CompilerParams(vmem_limit_bytes=18 << 20),
        cost_estimate=pl.CostEstimate(
            flops=4 * tokens * width * hidden, bytes_accessed=20 << 20, transcendentals=0
        ),
        name="forward_stage",
    )(
        table,
        *entries,
        seg_row,
        gain,
        (far if loads else pinned)(lead),
        *([pinned(down)] if down is not None else []),
        *map(far, kept),
    )


def backward_kernel(spot, count, *refs):
    backward_body(spot, refs[0], refs[1 : 1 + count], *refs[1 + count :])


def backward_body(
    spot,
    table_ref,
    candidates,
    seg_row_ref,
    gain_ref,
    lead_ref,
    down_ref,
    entries_ref,
    saved_ref,
    inner_ref,
    nexts_in,
    grads_in,
    gains_in,
    out_ref,
    nexts_ref,
    grads_ref,
    gains_ref,
    saved_buf,
    inner_buf,
    grads_buf,
    mixed_buf,
    gain_buf,
    entry_buf,
    normed_buf,
    scores_buf,
    probs_grad_buf,
    probs_buf,
    scores_grad_buf,
    grad_ref,
    in_sems,
    out_sems,
):
    role, slot = table_ref[spot], table_ref[spot + 1]
    tokens, width = grad_ref.shape
    bring_saved = pltpu.make_async_copy(saved_ref.at[slot], saved_buf, in_sems.at[0])
    bring_inner = pltpu.make_async_copy(inner_ref.at[slot], inner_buf, in_sems.at[1])
    bring_entry = pltpu.make_async_copy(entries_ref.at[slot], entry_buf, in_sems.at[2])
    keep_next = pltpu.make_async_copy(grad_ref, nexts_ref.at[slot], out_sems.at[0])
    keep_grads = pltpu.make_async_copy(grads_buf, grads_ref.at[slot], out_sems.at[1])
    keep_gain = pltpu.make_async_copy(gain_buf, gains_ref.at[slot], out_sems.at[2])

    @pl.when(role == 2)
    def _():
        bring_inner.start()

    @pl.when(role == 1)
    def _():
        bring_saved.start()

    @pl.when(role > 0)
    def _():
        bring_entry.start()
        chosen(table_ref[spot + 2], candidates, grad_ref)
        keep_next.start()
        normed_buf[...] = jnp.zeros_like(normed_buf)

    @pl.when(role == 1)
    def _():
        grads_buf[:, 3 * width :] = grad_ref[...]
        mixed_buf[...] = matmul(grad_ref[...], lead_ref[3 * width :, :]).astype(LOW)
        bring_saved.wait()
        left = lax.broadcasted_iota(jnp.int32, (tokens, 128), 1) < HEAD_SIZE
        zero = jnp.zeros((tokens, 128), LOW)
        scale = HEAD_SIZE ** (-0.5)

        @pl.loop(0, HEADS // 8)
        def _(group):
            for pair in range(4):
                at = group * 512 + pair * 128
                query = saved_buf[:, lanes(at, 128)]
                key = saved_buf[:, lanes(width + at, 128)]
                value = saved_buf[:, lanes(2 * width + at, 128)]
                grad = mixed_buf[:, lanes(at, 128)]
                for own in (0, 1):
                    mine = lambda v: jnp.where(left, v, zero) if own == 0 else jnp.where(left, zero, v)
                    scores_buf[group * 8 + 2 * pair + own] = matmul_nt(mine(query), key)
                    probs_grad_buf[group * 8 + 2 * pair + own] = matmul_nt(mine(grad), value)

        @pl.loop(0, HEADS // 4)
        def _(group):
            same = same_segment(seg_row_ref[slot])
            for head in range(4):
                at = group * 4 + head
                probs = head_probs(scores_buf[at], same)
                probs_buf[at] = probs.astype(LOW)
                grad_probs = probs_grad_buf[at]
                scores_grad_buf[at] = (
                    probs * (grad_probs - jnp.sum(probs * grad_probs, axis=-1, keepdims=True))
                ).astype(LOW)

        @pl.loop(0, HEADS // 4)
        def _(group):
            for pair in range(2):
                at = group * 256 + pair * 128
                query = saved_buf[:, lanes(at, 128)]
                key = saved_buf[:, lanes(width + at, 128)]
                grad = mixed_buf[:, lanes(at, 128)]
                parts = []
                for own in (0, 1):
                    probs = probs_buf[group * 4 + 2 * pair + own]
                    grad_low = scores_grad_buf[group * 4 + 2 * pair + own]
                    parts.append(
                        (
                            matmul(grad_low, key) * scale,
                            matmul_tn(grad_low, query) * scale,
                            matmul_tn(probs, grad),
                        )
                    )
                for which in range(3):
                    grads_buf[:, lanes(which * width + at, 128)] = jnp.where(
                        left, parts[0][which], parts[1][which]
                    ).astype(LOW)

        @pl.loop(0, 3 * width // CHUNK, unroll=2)
        def _(j):
            at = lanes(j * CHUNK, CHUNK)
            normed_buf[...] += matmul(grads_buf[:, at], lead_ref[pl.ds(j * CHUNK, CHUNK), :])

    @pl.when(role == 2)
    def _():
        bring_inner.wait()

        @pl.loop(0, lead_ref.shape[0] // CHUNK, unroll=2)
        def _(j):
            at = lanes(j * CHUNK, CHUNK)
            grad_active = matmul(grad_ref[...], down_ref[:, at])
            grads = (gelu_slope(inner_buf[:, at]) * grad_active).astype(LOW)
            grads_buf[:, at] = grads
            normed_buf[...] += matmul(grads, lead_ref[pl.ds(j * CHUNK, CHUNK), :])

    @pl.when(role > 0)
    def _():
        keep_grads.start()
        bring_entry.wait()
        grad_normed = normed_buf[...]
        normed, factor = layer_norm(entry_buf[...].astype(WIDE))
        gain_buf[...] = jnp.broadcast_to(
            jnp.sum(grad_normed * normed, axis=0, keepdims=True), gain_buf.shape
        )
        keep_gain.start()
        out_ref[...] = (
            grad_ref[...].astype(WIDE) + norm_back(grad_normed * gain_ref[...], normed, factor)
        ).astype(LOW)
        keep_next.wait()
        keep_grads.wait()
        keep_gain.wait()


def backward_stage(
    spot, table, nexts, seg_row, gain, lead, down, entries, saved, inner, totals
):
    tokens, width = nexts[0].shape
    count = len(nexts)
    hidden = lead.shape[0]
    return pl.pallas_call(
        functools.partial(backward_kernel, spot, count),
        out_shape=[jax.ShapeDtypeStruct((tokens, width), LOW)]
        + [jax.ShapeDtypeStruct(k.shape, k.dtype) for k in totals],
        in_specs=[SMEM_SPEC] + [VMEM_SPEC] * (count + 4) + [HBM_SPEC] * 6,
        out_specs=[VMEM_SPEC] + [HBM_SPEC] * 3,
        scratch_shapes=[
            pltpu.VMEM((tokens, hidden), LOW),
            pltpu.VMEM((tokens, hidden), WIDE),
            pltpu.VMEM((tokens, hidden), LOW),
            pltpu.VMEM((tokens, width), LOW),
            pltpu.VMEM((8, width), WIDE),
            pltpu.VMEM((tokens, width), LOW),
            pltpu.VMEM((tokens, width), WIDE),
            pltpu.VMEM((HEADS, tokens, tokens), WIDE),
            pltpu.VMEM((HEADS, tokens, tokens), WIDE),
            pltpu.VMEM((HEADS, tokens, tokens), LOW),
            pltpu.VMEM((HEADS, tokens, tokens), LOW),
            pltpu.VMEM((tokens, width), LOW),
            pltpu.SemaphoreType.DMA((3,)),
            pltpu.SemaphoreType.DMA((3,)),
        ],
        input_output_aliases={count + 8 + i: 1 + i for i in range(3)},
        compiler_params=pltpu.CompilerParams(vmem_limit_bytes=18 << 20),
        cost_estimate=pl.CostEstimate(
            flops=4 * tokens * width * hidden, bytes_accessed=20 << 20, transcendentals=0
        ),
        name="backward_stage",
    )(
        table,
        *nexts,
        seg_row,
        gain,
        pinned(lead),
        pinned(down),
        far(entries),
        far(saved),
        far(inner),
        *map(far, totals),
    )


def stats_kernel(spot, plan_ref, *refs):
    candidates, (table_ref, readout_ref, peak_ref, total_ref) = refs[:-4], refs[-4:]
    step = pl.program_id(0)

    @pl.when(step == 0)
    def _():
        chosen(plan_ref[spot], candidates, readout_ref)

    logits = matmul_nt(table_ref[...], readout_ref[...])
    own_peak = jnp.max(logits, axis=0, keepdims=True)
    own_total = lambda peak: jnp.sum(jnp.exp(logits - peak), axis=0, keepdims=True)

    @pl.when(step == 0)
    def _():
        peak_ref[...] = own_peak
        total_ref[...] = own_total(own_peak)

    @pl.when(step > 0)
    def _():
        peak = jnp.maximum(peak_ref[...], own_peak)
        total_ref[...] = total_ref[...] * jnp.exp(peak_ref[...] - peak) + own_total(peak)
        peak_ref[...] = peak


def head_stats(spot, plan, readouts, table, tile):
    tokens, emb = readouts[0].shape
    vocab = table.shape[0]
    whole = pl.BlockSpec((1, tokens), lambda i: (0, 0))
    rows = pl.BlockSpec((tokens, emb), lambda i: (0, 0))
    return pl.pallas_call(
        functools.partial(stats_kernel, spot),
        out_shape=[jax.ShapeDtypeStruct((tokens, emb), LOW)]
        + [jax.ShapeDtypeStruct((1, tokens), WIDE)] * 2,
        grid=(vocab // tile,),
        in_specs=[SMEM_SPEC]
        + [rows] * len(readouts)
        + [pl.BlockSpec((tile, emb), lambda i: (i, 0))],
        out_specs=[rows, whole, whole],
        compiler_params=pltpu.CompilerParams(vmem_limit_bytes=32 << 20),
        cost_estimate=pl.CostEstimate(
            flops=2 * tokens * vocab * emb, bytes_accessed=5 << 20, transcendentals=tokens * vocab
        ),
        name="head_stats",
    )(plan, *readouts, far(table))


def head_kernel(spot, table_base_ref, readout_ref, table_ref, logsum_ref, ids_ref, head_ref, grad_ref):
    tile = table_ref.shape[0]
    logits = matmul_nt(table_ref[...], readout_ref[...])
    ids = ids_ref[...] - (table_base_ref[spot] + pl.program_id(0) * tile)
    hits = lax.broadcasted_iota(jnp.int32, logits.shape, 0) == ids
    probs = jnp.exp(logits - logsum_ref[...])
    grads = jnp.where(hits, probs - 1.0, probs).astype(LOW)
    head = matmul(grads, readout_ref[...])
    unit = tile // 4
    for shard in range(4):
        head_ref[shard, :unit] = head[shard * unit : (shard + 1) * unit].astype(LOW)
    term = matmul_tn(grads, table_ref[...])

    @pl.when(pl.program_id(0) == 0)
    def _():
        grad_ref[...] = term

    @pl.when(pl.program_id(0) > 0)
    def _():
        grad_ref[...] += term


def head_grads(spot, base, readout, table, logsum, ids):
    tokens, emb = readout.shape
    vocab = table.shape[0]
    row = pl.BlockSpec((1, tokens), lambda i: (0, 0))
    whole = pl.BlockSpec((tokens, emb), lambda i: (0, 0))
    part = pl.BlockSpec((vocab // 4, emb), lambda i: (i, 0))
    return pl.pallas_call(
        functools.partial(head_kernel, spot),
        out_shape=[
            pltpu.HBM((16, 512, emb), LOW),
            jax.ShapeDtypeStruct((tokens, emb), WIDE),
        ],
        grid=(4,),
        in_specs=[SMEM_SPEC, whole, part, row, row],
        out_specs=[pl.BlockSpec((4, 512, emb), lambda i: (i, 0, 0)), whole],
        compiler_params=pltpu.CompilerParams(vmem_limit_bytes=32 << 20),
        cost_estimate=pl.CostEstimate(
            flops=6 * tokens * vocab * emb, bytes_accessed=9 << 20, transcendentals=tokens * vocab
        ),
        name="head_grads",
    )(base, readout, far(table), logsum, ids)


def pair_kernel(former_ref, latter_ref, out_ref):
    rows = out_ref.shape[0]
    out_ref[...] = former_ref[:rows].astype(WIDE) + latter_ref[:rows].astype(WIDE)


def pair_sum(former, latter, rows):
    return pl.pallas_call(
        pair_kernel,
        out_shape=jax.ShapeDtypeStruct((rows, former.shape[1]), WIDE),
        in_specs=[VMEM_SPEC] * 2,
        out_specs=VMEM_SPEC,
        compiler_params=pltpu.CompilerParams(vmem_limit_bytes=8 << 20),
        cost_estimate=pl.CostEstimate(flops=0, bytes_accessed=1024, transcendentals=0),
        name="pair_sum",
    )(former, latter)


def lookup_kernel(ids_ref, table_ref, noise_ref, out_ref, total_ref, low_ref):
    step = pl.program_id(0)
    parts, tile = table_ref.shape
    tokens = ids_ref.shape[1]
    blocks = tile // 128

    @pl.when(step == 0)
    def _():
        lane = jnp.bitwise_and(ids_ref[...], 127)
        hits = lax.broadcasted_iota(jnp.int32, (128, tokens), 0) == lane
        low_ref[...] = jnp.where(hits, 1.0, 0.0).astype(LOW)
        total_ref[...] = noise_ref[...].astype(WIDE)

    stacked = jnp.concatenate(
        [table_ref[:, block * 128 : (block + 1) * 128] for block in range(blocks)]
    )
    found = matmul(stacked, low_ref[...])
    own = jnp.right_shift(ids_ref[...], 7) - step * blocks
    total = jnp.zeros_like(total_ref)
    for block in range(blocks):
        total = jnp.where(own == block, found[block * parts : (block + 1) * parts], total)
    total_ref[...] += total

    @pl.when(step == pl.num_programs(0) - 1)
    def _():
        out_ref[...] = total_ref[...].astype(LOW)


def lookup(ids, table, noise, tile):
    parts, vocab = table.shape
    tokens = ids.shape[1]
    whole = pl.BlockSpec((parts, tokens), lambda i: (0, 0))
    return pl.pallas_call(
        lookup_kernel,
        out_shape=jax.ShapeDtypeStruct((parts, tokens), LOW),
        grid=(vocab // tile,),
        in_specs=[
            pl.BlockSpec((1, tokens), lambda i: (0, 0)),
            pl.BlockSpec((parts, tile), lambda i: (0, i)),
            whole,
        ],
        out_specs=whole,
        scratch_shapes=[pltpu.VMEM((parts, tokens), WIDE), pltpu.VMEM((128, tokens), LOW)],
        compiler_params=pltpu.CompilerParams(vmem_limit_bytes=32 << 20),
        cost_estimate=pl.CostEstimate(
            flops=2 * 128 * vocab * tokens, bytes_accessed=4 << 20, transcendentals=0
        ),
        name="lookup",
    )(ids, far(table), noise)


def lead_grad_kernel(where_ref, normed_ref, mixed_ref, grads_ref, *refs):
    got_ref, out_refs, (turned_ref, result_ref) = None, refs[:-2], refs[-2:]
    if len(out_refs) > 1:
        got_ref, out_refs = out_refs[0], out_refs[1:]
    role, half, spot = where_ref[0], where_ref[1], where_ref[2]
    step = pl.program_id(0)
    width = normed_ref.shape[1]
    steps = pl.num_programs(0)
    use_mixed = jnp.logical_and(role == 1, half == 1)

    @pl.when(step == 0)
    def _():
        turned_ref[...] = normed_ref[...].T

    @pl.when(jnp.logical_and(step == steps // 2, use_mixed))
    def _():
        turned_ref[...] = mixed_ref[...].T

    result_ref[...] = matmul(turned_ref[...], grads_ref[...])
    unit = width // 16

    def put(block, rows, part):
        if got_ref is not None:
            part = part + got_ref[block, rows, :].astype(WIDE)
        out_ref = out_refs[0].at[block] if got_ref is None else out_refs[block]
        out_ref[rows, :] = part.astype(LOW)

    @pl.when(half == 0)
    def _():
        for block in range(4):
            x = (spot + block) % 4
            put(block, slice(None), result_ref[pl.ds(pl.multiple_of(x * 4 * unit, 4 * unit), 4 * unit)])

    @pl.when(half == 1)
    def _():
        for block in range(4):
            y = (spot + block) % 4
            for x in range(4):
                rows = pl.ds(pl.multiple_of((4 * x + y) * unit, unit), unit)
                put(block, slice(x * unit, (x + 1) * unit), result_ref[rows])


CHEAP = pl.CostEstimate(flops=0, bytes_accessed=1024, transcendentals=0)


def lead_grad(where, normed, saved, grads, got=None):
    tokens, width = normed.shape
    tile = 1024
    whole = pl.BlockSpec((4, width // 4, tile), lambda i, where: (0, 0, i))
    block = pl.BlockSpec((width // 4, tile), lambda i, where: (0, i))
    shape = (width // 4, 2 * width)
    return pl.pallas_call(
        lead_grad_kernel,
        out_shape=[jax.ShapeDtypeStruct((4,) + shape, LOW)]
        if got is None
        else [jax.ShapeDtypeStruct(shape, LOW)] * 4,
        grid_spec=pltpu.PrefetchScalarGridSpec(
            num_scalar_prefetch=1,
            grid=(2 * width // tile,),
            in_specs=[
                pl.BlockSpec((tokens, width), lambda i, where: (0, 0)),
                pl.BlockSpec((tokens, width), lambda i, where: (0, 3)),
                pl.BlockSpec((tokens, tile), lambda i, where: (0, where[1] * (2 * width // tile) + i)),
            ]
            + ([] if got is None else [whole]),
            out_specs=[whole] if got is None else [block] * 4,
            scratch_shapes=[pltpu.VMEM((width, tokens), LOW), pltpu.VMEM((width, tile), WIDE)],
        ),
        compiler_params=pltpu.CompilerParams(vmem_limit_bytes=24 << 20),
        cost_estimate=CHEAP
        if got is None
        else pl.CostEstimate(
            flops=4 * tokens * width * width, bytes_accessed=12 << 20, transcendentals=0
        ),
        name="lead_grad",
    )(where, normed, saved, grads, *([] if got is None else [got]))


def down_grad_kernel(where_ref, saved_ref, nexts_ref, *refs):
    got_ref, out_refs, (buf_ref, got_buf, sems) = None, refs[:-3], refs[-3:]
    if len(out_refs) > 1:
        got_ref, out_refs = out_refs[0], out_refs[1:]
    role, half, spot = where_ref[0], where_ref[1], where_ref[2]
    at = pl.program_id(0)
    unit = saved_ref.shape[1] // 4

    @pl.when(role == 2)
    def _():
        if got_ref is not None:
            bring = pltpu.make_async_copy(got_ref, got_buf, sems.at[4])
            pl.when(at == 0)(bring.start)
        result = matmul_tn(saved_ref[...], nexts_ref[...])
        if got_ref is not None:
            pl.when(at == 0)(bring.wait)

        def put(block, rows, part):
            if got_ref is not None:
                part = part + got_buf[block, rows, :].astype(WIDE)
            buf_ref[block, rows, :] = part.astype(LOW)

        @pl.when(half == 0)
        def _():
            put((at - spot + 4) % 4, slice(None), result)

        @pl.when(half == 1)
        def _():
            rows = pl.ds(pl.multiple_of(at * unit, unit), unit)
            for y in range(4):
                put((y - spot + 4) % 4, rows, result[y * unit : (y + 1) * unit])

        @pl.when(at == pl.num_programs(0) - 1)
        def _():
            copies = [pltpu.make_async_copy(buf_ref, out_refs[0], sems.at[0])]
            if got_ref is not None:
                copies = [
                    pltpu.make_async_copy(buf_ref.at[block], out_ref, sems.at[block])
                    for block, out_ref in enumerate(out_refs)
                ]
            for copy in copies:
                copy.start()
            for copy in copies:
                copy.wait()


def down_grad(where, saved, nexts, got=None):
    tokens, hidden = saved.shape
    width = nexts.shape[1]
    rows = hidden // 8
    live = lambda where: jnp.where(where[0] == 2, 1, 0)
    return pl.pallas_call(
        down_grad_kernel,
        out_shape=[pltpu.HBM((4, rows, width), LOW)]
        if got is None
        else [pltpu.HBM((rows, width), LOW)] * 4,
        grid_spec=pltpu.PrefetchScalarGridSpec(
            num_scalar_prefetch=1,
            grid=(4,),
            in_specs=[
                pl.BlockSpec((tokens, rows), lambda i, where: (0, (where[1] * 4 + i) * live(where))),
                pl.BlockSpec((tokens, width), lambda i, where: (0, 0)),
            ]
            + ([] if got is None else [HBM_SPEC]),
            out_specs=[HBM_SPEC] * (1 if got is None else 4),
            scratch_shapes=[
                pltpu.VMEM((4, rows, width), LOW),
                pltpu.VMEM((4, 16, 128) if got is None else (4, rows, width), LOW),
                pltpu.SemaphoreType.DMA((5,)),
            ],
        ),
        compiler_params=pltpu.CompilerParams(vmem_limit_bytes=28 << 20),
        cost_estimate=CHEAP,
        name="down_grad",
    )(where, saved, nexts, *([] if got is None else [far(got)]))


def upper_kernel(where_ref, *refs):
    out_ref = refs[4]
    rows = refs[0].shape[0]
    for at, part in enumerate(refs[:4]):
        place = (where_ref[0] - at + 4) % 4
        out_ref[pl.ds(pl.multiple_of(place * rows, rows), rows), :] = part[...]


def upper_half(where, parts):
    rows, width = parts[0].shape
    return pl.pallas_call(
        upper_kernel,
        out_shape=jax.ShapeDtypeStruct((4 * rows, width), LOW),
        in_specs=[SMEM_SPEC] + [VMEM_SPEC] * 4,
        out_specs=VMEM_SPEC,
        compiler_params=pltpu.CompilerParams(vmem_limit_bytes=8 << 20),
        name="upper_half",
    )(where, *parts)


def hold_down_kernel(where_ref, mine_ref, other_ref, own_ref, out_ref, sems):
    rows = mine_ref.shape[0]
    core = where_ref[1]
    spot = lambda at: out_ref.at[pl.ds(pl.multiple_of(at * rows, rows), rows), :]
    copies = [
        pltpu.make_async_copy(mine_ref, spot(core), sems.at[0]),
        pltpu.make_async_copy(other_ref, spot(1 - core), sems.at[1]),
        pltpu.make_async_copy(own_ref, out_ref.at[pl.ds(2 * rows, 2 * rows), :], sems.at[2]),
    ]
    for copy in copies:
        copy.start()
    for copy in copies:
        copy.wait()


def hold_down(where, mine, other, own):
    rows, width = mine.shape
    return pl.pallas_call(
        hold_down_kernel,
        out_shape=pltpu.VMEM((4 * rows, width), LOW),
        in_specs=[SMEM_SPEC] + [VMEM_SPEC] * 2 + [HBM_SPEC],
        out_specs=VMEM_SPEC,
        scratch_shapes=[pltpu.SemaphoreType.DMA((3,))],
        compiler_params=pltpu.CompilerParams(vmem_limit_bytes=8 << 20),
        name="hold_down",
    )(where, mine, other, far(own))


def noise_kernel(spot, plan_ref, ids_ref, *refs):
    candidates, (packed_ref, noise_ref, buf_ref) = refs[:-3], refs[-3:]
    parts = noise_ref.shape[0]
    chosen(plan_ref[spot], candidates, buf_ref)
    packed_ref[:parts] = buf_ref[...]
    noise_ref[...] = buf_ref[...].astype(WIDE)
    ids = ids_ref[...]
    high = jnp.right_shift(ids, 8).astype(WIDE)
    low = jnp.bitwise_and(ids, 255).astype(WIDE)
    at = lax.broadcasted_iota(jnp.int32, (16, ids.shape[1]), 0)
    split = jnp.where(at == 0, high, jnp.where(at == 1, low, 0.0))
    packed_ref[parts:] = split.astype(LOW)


def noise_pack(spot, plan, ids, candidates):
    parts, tokens = candidates[0].shape
    return pl.pallas_call(
        functools.partial(noise_kernel, spot),
        out_shape=[
            jax.ShapeDtypeStruct((parts + 16, tokens), LOW),
            jax.ShapeDtypeStruct((parts, tokens), WIDE),
        ],
        in_specs=[SMEM_SPEC] + [VMEM_SPEC] * (1 + len(candidates)),
        out_specs=[VMEM_SPEC] * 2,
        scratch_shapes=[pltpu.VMEM((parts, tokens), LOW)],
        compiler_params=pltpu.CompilerParams(vmem_limit_bytes=8 << 20),
        cost_estimate=CHEAP,
        name="noise_pack",
    )(plan, ids, *candidates)


def embed_kernel(base_ref, mine_ref, other_ref, out_ref, total_ref):
    step = pl.program_id(0)
    steps = pl.num_programs(0)
    parts = out_ref.shape[0]
    blocks = total_ref.shape[0] // parts

    def add(gathered_ref):
        count, _, tokens = gathered_ref.shape
        term = None
        for at in range(count):
            split = gathered_ref[at, parts : parts + 16].astype(WIDE)
            ids = (split[0:1] * 256.0 + split[1:2]).astype(jnp.int32) - base_ref[0]
            lane = jnp.bitwise_and(ids, 127)
            hits = lax.broadcasted_iota(jnp.int32, (128, tokens), 0) == lane
            hits = jnp.where(hits, 1.0, 0.0).astype(LOW)
            own = jnp.right_shift(ids, 7)
            grads = gathered_ref[at, :parts]
            masked = jnp.concatenate(
                [grads * jnp.where(own == block, 1.0, 0.0).astype(LOW) for block in range(blocks)]
            )
            part = matmul_nt(masked, hits)
            term = part if term is None else term + part

        @pl.when(step == 0)
        def _():
            total_ref[...] = term

        @pl.when(step > 0)
        def _():
            total_ref[...] += term

    pl.when(step < steps // 2)(lambda: add(mine_ref))
    pl.when(step >= steps // 2)(lambda: add(other_ref))

    @pl.when(step == steps - 1)
    def _():
        rows = out_ref.shape[1]
        for block in range(blocks):
            size = min(128, rows - block * 128)
            out_ref[:, block * 128 : block * 128 + size] = total_ref[
                block * parts : (block + 1) * parts, :size
            ]


def embed_sum(base, mine, other, parts, rows):
    count, deep, tokens = mine.shape
    step = 4
    half = count // step
    blocks = -(-rows // 128)
    return pl.pallas_call(
        embed_kernel,
        out_shape=jax.ShapeDtypeStruct((parts, rows), WIDE),
        grid=(2 * half,),
        in_specs=[
            SMEM_SPEC,
            pl.BlockSpec((step, deep, tokens), lambda i: (jnp.minimum(i, half - 1), 0, 0)),
            pl.BlockSpec((step, deep, tokens), lambda i: (jnp.maximum(i - half, 0), 0, 0)),
        ],
        out_specs=pl.BlockSpec((parts, rows), lambda i: (0, 0)),
        scratch_shapes=[pltpu.VMEM((blocks * parts, 128), WIDE)],
        compiler_params=pltpu.CompilerParams(vmem_limit_bytes=32 << 20),
        cost_estimate=CHEAP,
        name="embed_sum",
    )(base, mine, other)


def empty(*kinds):
    return pl.pallas_call(
        lambda *refs: None,
        out_shape=[pltpu.HBM(shape, dtype) for shape, dtype in kinds],
        out_specs=[HBM_SPEC] * len(kinds),
        compiler_params=pltpu.CompilerParams(vmem_limit_bytes=1 << 20),
        name="empty",
    )()


ROW_LEN = 128
SEC, GRP, NX, NY = 4, 2, 4, 4
ALL = ("section", "group", "row")
TURNS = (1, 3, 2)


def route(value, target_of):
    number = lambda s, g, x, y: (s * GRP + g) * NX * NY + x * NY + y
    pairs = []
    for at in itertools.product(range(SEC), range(GRP), range(NX), range(NY)):
        target = target_of(*at)
        if target is not None:
            pairs.append((number(*at), number(*target)))
    return lax.ppermute(value, ALL, pairs)


def link(value, source, target):
    return route(value, lambda s, g, x, y: (target, g, x, y) if s == source else None)


def turn(value, by):
    return route(value, lambda s, g, x, y: ((s + by) % SEC, g, x, y))


def swap_cores(value, sections=range(SEC)):
    return route(value, lambda s, g, x, y: (s, 1 - g, x, y) if s in sections else None)


def plane_route(value, by, first, sections=range(SEC)):
    def target_of(s, g, x, y):
        if s not in sections:
            return None
        if (g == 0) == first:
            return (s, g, (x + by) % NX, y)
        return (s, g, x, (y + by) % NY)

    return route(value, target_of)


def after(value, earlier):
    return lax.optimization_barrier((value, earlier))[0]


def row_block(values, block, count):
    size = values.shape[0] // count
    return lax.dynamic_slice_in_dim(values, block * size, size, 0)


def plane_first(mine, sections=range(SEC)):
    return [mine[0]] + [plane_route(mine[by], by, True, sections) for by in TURNS]


def plane_sum(pieces):
    total = pieces[0].astype(WIDE)
    for piece in pieces[1:]:
        total = total + piece.astype(WIDE)
    return total.astype(LOW)


def plane_second(pieces, second, sections=range(SEC)):
    total = plane_sum(pieces)
    return [row_block(total, second, 4)] + [
        plane_route(row_block(total, (second + by) % 4, 4), by, False, sections) for by in TURNS
    ]


def group_exchange(values, first):
    number = lambda s, g, x, y: (s * GRP + g) * NX * NY + x * NY + y
    groups = []
    for s in range(SEC):
        for g in range(GRP):
            along_x = (g == 0) == first
            for at in range(4):
                groups.append(
                    [number(s, g, i, at) if along_x else number(s, g, at, i) for i in range(4)]
                )
    return lax.all_to_all(values, ALL, 0, 0, axis_index_groups=groups, tiled=True)


def section_exchange(values):
    return lax.all_to_all(values, "section", 0, 0, tiled=True)


def plans(micro, vocab_part):
    last = SEC - 1
    steps = micro + 2 * last
    table = np.zeros((SEC, 6 * steps + 2), np.int32)
    for s in range(SEC):
        for way in range(2):
            depth = s if way == 0 else last - s
            for step in range(steps):
                at = step - 2 * depth
                if 0 <= at < micro:
                    sources = ([0] if step < micro else []) + [
                        d + 1 for d in range(last) if 0 <= step - 2 - 2 * d < micro
                    ]
                    spot = 3 * (way * steps + step)
                    table[s, spot : spot + 3] = (1 + s % 2, at, sources.index(depth))
        table[s, 6 * steps :] = (s * vocab_part, s)
    return table


def local(
    token_ids,
    segment_ids,
    noise_input,
    embed_table,
    input_proj,
    norm_gain,
    lead_weight,
    down_weight,
    final_gain,
    readout_proj,
    head_table,
):
    section = lax.axis_index("section")
    core = lax.axis_index("group")
    row = lax.axis_index("row")
    x_at, y_at = row // NY, row % NY
    first_at = jnp.where(core == 0, x_at, y_at)
    micro, _, tokens = token_ids.shape
    width = input_proj.shape[1]
    hidden = lead_weight.shape[2]
    half_rows = down_weight.shape[1]
    emb_part = input_proj.shape[0]
    vocab_part, emb = head_table.shape
    vocab = embed_table.shape[0]
    all_tokens = micro * tokens
    last = SEC - 1
    gain_half = norm_gain.astype(WIDE)
    lead = lead_weight[0]
    own_down = down_weight[0]
    seg_row = segment_ids
    flat_ids = token_ids.reshape(-1)

    plan = plans(micro, vocab_part)
    steps = micro + 2 * last
    table = lax.dynamic_index_in_dim(jnp.asarray(plan), section, 0, False)
    flat_ids = after(flat_ids, table)
    where_start = jnp.stack((first_at, core)).astype(jnp.int32)
    to_first = lambda v: [v] + [link(v, s, 0) for s in range(1, SEC)]
    eighth = row_block(row_block(own_down, core, 2), first_at, 4)
    eighth = jnp.where(section == 1, link(eighth, 0, 1), link(eighth, 2, 3))
    noise = noise_input[:, 0].transpose(2, 0, 1).reshape(emb_part, -1)
    own_embedded = lookup(flat_ids[None], embed_table.T, noise, 3200)
    parts = to_first(jnp.concatenate((own_embedded, input_proj), axis=1))
    embedded = jnp.concatenate([part[:, :all_tokens] for part in parts])
    input_full = jnp.concatenate([part[:, all_tokens:] for part in parts])
    first_in = matmul_tn(embedded, input_full).astype(LOW).reshape(micro, tokens, width)
    eighth = after(eighth, first_in)
    eighths = [eighth] + [plane_route(eighth, by, True) for by in (1, 2, 3)]
    upper = upper_half(where_start, [after(part, first_in) for part in eighths])
    held_down = hold_down(where_start, upper, swap_cores(upper), own_down)

    kept = empty(
        ((micro, tokens, width), LOW),
        ((micro, tokens, width), LOW),
        ((micro, tokens, hidden), LOW),
        ((micro, tokens, hidden), WIDE),
    )

    def sources(first, step, hops, order):
        arrived = [hops[step - 2, s] for s in order if (step - 2, s) in hops]
        return ([first[step]] if step < micro else []) + arrived

    outs, hops = [], {}
    for step in range(steps):
        out, *kept = forward_stage(
            3 * step,
            table,
            sources(first_in, step, hops, range(SEC)),
            seg_row,
            gain_half,
            held_lead if step > 0 else lead,
            held_down if step > 1 else None,
            kept,
            step == 0,
        )
        if step == 0:
            held_lead = kept.pop()
        outs.append(out)
        for s in range(last):
            if 0 <= step - 2 * s < micro:
                ready = after(out, hops[step - 1, s]) if (step - 1, s) in hops else out
                hops[step, s] = link(ready, s, s + 1)
        if step == 2:
            readout_own = after(readout_proj.T, out)
            readout_full = jnp.concatenate(
                [link(readout_own, s, last) for s in range(last)] + [readout_own]
            )
    entries, normeds, saved, inner = kept

    final_rows = jnp.concatenate(outs[2 * last :]).astype(WIDE)
    normed_f, factor_f = layer_norm(final_rows)
    gain_f = final_gain.astype(WIDE)
    final_low = (normed_f * gain_f).astype(LOW)
    readout = matmul_nt(final_low, readout_full).astype(LOW)
    sent = [link(readout, last, s) for s in range(last)]
    readout, peak, total = head_stats(6 * steps + 1, table, sent + [readout], head_table, 2000)
    stats = jnp.concatenate((peak, total))
    all_stats = section_exchange(jnp.tile(stats, (SEC, 1))).reshape(SEC, 2, all_tokens)
    peak = jnp.max(all_stats[:, 0], axis=0)
    total = jnp.sum(all_stats[:, 1] * jnp.exp(all_stats[:, 0] - peak), axis=0)
    logsum = (peak + jnp.log(total))[None]
    head_grad, grad_readout = head_grads(
        6 * steps, table, readout, head_table, logsum, flat_ids[None]
    )
    grad_low = grad_readout.astype(LOW)
    for s in range(last):
        grad_readout = grad_readout + link(grad_low, s, last).astype(WIDE)
    grad_readout = grad_readout.astype(LOW)
    head_grad = lax.psum_scatter(head_grad, "row", scatter_dimension=0)
    readout_grad = matmul_tn(final_low, grad_readout)
    grad_final = matmul(grad_readout, readout_full)
    final_gain_grad = jnp.sum(grad_final * normed_f, axis=0)
    last_grads = norm_back(grad_final * gain_f, normed_f, factor_f).astype(LOW)
    last_grads = last_grads.reshape(micro, tokens, width)

    lead_turned = turned(6 * steps + 1, table, after(lead, grad_low), 0)
    down_turned = turned(6 * steps + 1, table, after(held_down, grad_low), 1)
    totals = empty(
        ((micro, tokens, width), LOW),
        ((micro, tokens, hidden), LOW),
        ((micro, 8, width), WIDE),
    )
    outs, hops = [], {}
    for step in range(steps):
        out, *totals = backward_stage(
            3 * (steps + step),
            table,
            sources(last_grads, step, hops, range(SEC - 1, -1, -1)),
            seg_row,
            gain_half,
            lead_turned,
            down_turned,
            entries,
            saved,
            inner,
            totals,
        )
        outs.append(out)
        for s in range(1, SEC):
            if 0 <= step - 2 * (last - s) < micro:
                ready = after(out, hops[step - 1, s]) if (step - 1, s) in hops else out
                hops[step, s] = link(ready, s, s - 1)
    section, core, row, readout_grad, final_gain_grad = lax.optimization_barrier(
        (section, core, row, readout_grad, final_gain_grad, out)
    )[:5]
    x_at, y_at = row // NY, row % NY
    first_at, second_at = jnp.where(core == 0, x_at, y_at), jnp.where(core == 0, y_at, x_at)
    is_mlp = section % 2 == 1

    first_grads = jnp.concatenate(outs[2 * last :])
    noise_grad = matmul_nt(input_full, first_grads).astype(LOW)
    pieces = noise_grad.reshape(SEC, emb_part, all_tokens)
    sent = [link(pieces[s], 0, s) for s in range(1, SEC)]

    grad_nexts, grads, gain_grads = totals
    gain_grad = jnp.sum(gain_grads[:, 0], axis=0)
    flat = lambda v: v.reshape(all_tokens, v.shape[-1])
    grads = after(grads, head_grad)
    normed, grad_nexts, grads, saved = flat(normeds), flat(grad_nexts), flat(grads), flat(saved)
    odd = (1, 3)
    role = jnp.where(is_mlp, 2, 1)
    where_other = jnp.stack((role, 1 - core, second_at)).astype(jnp.int32)
    where_mine = jnp.stack((role, core, first_at)).astype(jnp.int32)
    both = lambda mine, other: jnp.where(
        core == 0,
        jnp.concatenate((mine, other), axis=1),
        jnp.concatenate((other, mine), axis=1),
    )
    down_got = swap_cores(down_grad(where_other, saved, grad_nexts)[0], odd)
    lead_other = lead_grad(where_other, normed, saved, grads)[0]
    lead_got = swap_cores(lead_other)
    down_mine = down_grad(after(where_mine, lead_other), saved, grad_nexts, down_got)
    down_first = plane_first(down_mine, odd)
    late_ids = after(flat_ids, down_mine)[None]
    packed, noise_wide = noise_pack(6 * steps + 1, table, late_ids, [pieces[0]] + sent)

    input_grad = matmul(embedded, first_grads).reshape(SEC, 16, 4, width)
    input_grad = input_grad.transpose(1, 0, 2, 3).reshape(16, 16, width)
    readout_grad = readout_grad.reshape(16, 16, width)
    vectors = jnp.concatenate(
        (
            gain_grad.reshape(16, 64),
            final_gain_grad.reshape(SEC, 16, 16).transpose(1, 0, 2).reshape(16, 64),
            jnp.zeros((16, width - 128), WIDE),
        ),
        axis=1,
    )
    small = jnp.concatenate(
        (
            jnp.where(section == 0, input_grad, readout_grad),
            vectors[:, None],
            jnp.zeros((16, 15, width), WIDE),
        ),
        axis=1,
    ).astype(LOW)
    half_of = lambda which: lax.dynamic_slice_in_dim(small, which * (width // 2), width // 2, 2)
    small = half_of(core).astype(WIDE) + swap_cores(half_of(1 - core)).astype(WIDE)
    small = small.astype(LOW).reshape(NX, NY, 32, width // 2)
    small = jnp.where(core == 0, small, small.swapaxes(0, 1)).reshape(4, NY * 32, width // 2)
    deep = emb_part + 16

    def exchange(blocks, packed, first):
        rows = blocks.shape[1]
        everywhere = jnp.broadcast_to(packed, (4,) + packed.shape)
        got = group_exchange(jnp.concatenate((blocks, everywhere), axis=1), first)
        return jnp.sum(got[:, :rows].astype(WIDE), axis=0).astype(LOW), got[:, rows:]

    small, packed = exchange(after(small, down_first), packed, True)
    small, packed = exchange(
        small.reshape(4, 32, width // 2), packed.reshape(4 * deep, all_tokens), False
    )
    packed = packed.reshape(16, deep, all_tokens)
    down_second = plane_second(after(down_first, packed), second_at, odd)
    lead_mine = lead_grad(after(where_mine, packed), normed, saved, grads, lead_got)
    lead_first = plane_first(lead_mine)
    packed_other = swap_cores(packed)
    small = both(small, swap_cores(small))
    embed_grad = embed_sum(
        (row * (vocab // 16)).reshape(1), packed, packed_other, emb_part, vocab // 16
    )
    gain_out = small[16, :64].astype(WIDE)
    input_rows = small[:16].reshape(SEC, 4, width)
    readout_rows = small[:16].reshape(64, SEC, 64)
    final_rows = small[16, 64:128].reshape(SEC, 16)

    finals = jnp.pad(final_rows, ((0, 0), (0, width - 16)))[:, None]
    mine = jnp.where(
        section == 0, input_rows, readout_rows.transpose(1, 0, 2).reshape(SEC, 4, width)
    )
    shared = section_exchange(
        jnp.concatenate((mine, finals, jnp.zeros((SEC, 3, width), LOW)), axis=1)
    )
    input_out = shared[0, :4]
    readout_out = shared[last, :4].reshape(64, 64)
    final_out = shared[last, 4, :16]

    ready = (embed_grad, shared)
    lead_second = plane_second(after(lead_first, ready), second_at)
    down_part = plane_sum(after(down_second, ready))
    lead_part = plane_sum(lead_second)
    noise_out = noise_wide.reshape(emb_part, micro, tokens).transpose(1, 2, 0)
    lead_out = both(lead_part, swap_cores(lead_part)).astype(WIDE)

    def first_target(s, g, x, y):
        if s % 2 == 0:
            return None
        return (s - 1, 0, x, y) if g == 0 else (s, 0, x, y)

    def second_target(s, g, x, y):
        return (s - 1, 1, x, y) if s % 2 == 1 and g == 0 else None

    to_core_0 = route(down_part, first_target)
    to_core_1 = route(down_part, second_target)
    down_out = jnp.where(
        core == 0, to_core_0, jnp.where(is_mlp, down_part, to_core_1)
    ).astype(WIDE)

    head_out = pair_sum(head_grad, swap_cores(head_grad), vocab_part // (NX * NY))
    return (
        noise_out[:, None],
        embed_grad.T,
        input_out.astype(WIDE),
        gain_out[None],
        lead_out[None],
        down_out[None],
        final_out.astype(WIDE),
        readout_out.astype(WIDE),
        head_out,
    )


def solution(mesh):
    in_specs = (
        P(None, ("group", "row"), None),
        P(None, ("group", "row"), None),
        P(None, ("group", "row"), None, "section"),
        P(None, "section"),
        P("section", None),
        P("section", None),
        P("section", None, None),
        P("section", None, None),
        P(),
        P(None, "section"),
        P("section", None),
    )
    out_specs = (
        P(None, ("group", "row"), None, "section"),
        P("row", "section"),
        P(("section", "row"), None),
        P("section", "row"),
        P("section", "row", None),
        P("section", "row", None),
        P(("section", "row")),
        P("row", "section"),
        P(("section", "row"), None),
    )
    return jax.shard_map(local, mesh=mesh, in_specs=in_specs, out_specs=out_specs, check_vma=False)
```

```python
import functools
import itertools

import jax
import jax.numpy as jnp
import numpy as np
from jax import lax
from jax.experimental import pallas as pl
from jax.experimental.pallas import tpu as pltpu
from jax.sharding import PartitionSpec as P

HEADS = 16
HEAD_SIZE = 64
LOW = jnp.bfloat16
WIDE = jnp.float32
EPSILON = 1e-05
MASKED = -1000000000.0
CHUNK = 1024
GELU_A = 0.7978845608028654
GELU_B = 0.044715
HBM_SPEC = pl.BlockSpec(memory_space=pltpu.HBM)
VMEM_SPEC = pl.BlockSpec(memory_space=pltpu.VMEM)
SMEM_SPEC = pl.BlockSpec(memory_space=pltpu.SMEM)


def matmul(former, latter):
    return jnp.dot(former, latter, preferred_element_type=WIDE)


def matmul_nt(former, latter):
    return lax.dot_general(
        former, latter, (((1,), (1,)), ((), ())), preferred_element_type=WIDE
    )


def matmul_tn(former, latter):
    return lax.dot_general(
        former, latter, (((0,), (0,)), ((), ())), preferred_element_type=WIDE
    )


def layer_norm(values):
    centre = jnp.mean(values, axis=-1, keepdims=True)
    centred = values - centre
    variance = jnp.mean(centred * centred, axis=-1, keepdims=True)
    factor = lax.rsqrt(variance + EPSILON)
    return (centred * factor, factor)


def norm_back(grad_normed, normed, factor):
    first_mean = jnp.mean(grad_normed, axis=-1, keepdims=True)
    second_mean = jnp.mean(grad_normed * normed, axis=-1, keepdims=True)
    return factor * (grad_normed - first_mean - normed * second_mean)


def gelu(v):
    return 0.5 * v * (1.0 + jnp.tanh(GELU_A * (v + GELU_B * (v * v * v))))


def gelu_slope(v):
    square = v * v
    bend = jnp.tanh(GELU_A * (v + GELU_B * (square * v)))
    return 0.5 * (1.0 + bend) + 0.5 * v * (1.0 - bend * bend) * (
        GELU_A * (1.0 + 3.0 * GELU_B * square)
    )


def head_probs(scores, same):
    scores = jnp.where(same, scores * HEAD_SIZE ** (-0.5), MASKED)
    expo = jnp.exp(scores - jnp.max(scores, axis=-1, keepdims=True))
    return expo * (1.0 / jnp.sum(expo, axis=-1, keepdims=True))


def same_segment(row):
    across = jnp.broadcast_to(row.astype(WIDE), (row.shape[1], row.shape[1]))
    return across.T == across


def lanes(at, size):
    return pl.ds(pl.multiple_of(at, 128), size)


def turn_kernel(spot, live, plan_ref, value_ref, out_ref):
    @pl.when(jnp.bitwise_and(plan_ref[spot], 1) >= live)
    def _():
        out_ref[...] = value_ref[...].T


def turned(spot, plan, value, live):
    rows, columns = value.shape
    if rows > columns:
        tile = rows // 8
        blocks = (pl.BlockSpec((tile, columns), lambda i: (i, 0)), pl.BlockSpec((columns, tile), lambda i: (0, i)))
    else:
        tile = columns // 8
        blocks = (pl.BlockSpec((rows, tile), lambda i: (0, i)), pl.BlockSpec((tile, rows), lambda i: (i, 0)))
    return pl.pallas_call(
        functools.partial(turn_kernel, spot, live),
        out_shape=pltpu.VMEM((columns, rows), LOW),
        grid=(8,),
        in_specs=[SMEM_SPEC, blocks[0]],
        out_specs=blocks[1],
        compiler_params=pltpu.CompilerParams(vmem_limit_bytes=12 << 20),
        cost_estimate=pl.CostEstimate(flops=0, bytes_accessed=1024, transcendentals=0),
        name="turned",
    )(plan, far(value))


def chosen(choice, candidates, buffer):
    for at, candidate in enumerate(candidates):

        @pl.when(choice == at)
        def _():
            buffer[...] = candidate[...]


def forward_kernel(spot, with_down, loads, count, *refs):
    table_ref, candidates, refs = refs[0], refs[1 : 1 + count], refs[1 + count :]
    if not with_down:
        refs = refs[:3] + (None,) + refs[3:]
    source_ref = load_sems = None
    if loads:
        source_ref, load_sems = refs[2], refs[-1]
        refs = refs[:2] + (refs[13],) + refs[3:13] + refs[14:-1]
    forward_body(spot, table_ref, candidates, source_ref, load_sems, *refs)


def forward_body(
    spot,
    table_ref,
    candidates,
    source_ref,
    load_sems,
    seg_row_ref,
    gain_ref,
    lead_ref,
    down_ref,
    entries_in,
    normeds_in,
    saved_in,
    inner_in,
    out_ref,
    entries_ref,
    normeds_ref,
    saved_ref,
    inner_ref,
    normed_buf,
    saved_buf,
    inner_buf,
    result_buf,
    scores_buf,
    probs_buf,
    entry_ref,
    out_sems,
):
    role, slot = table_ref[spot], table_ref[spot + 1]
    tokens, width = entry_ref.shape
    keeps = [
        pltpu.make_async_copy(entry_ref, entries_ref.at[slot], out_sems.at[0]),
        pltpu.make_async_copy(normed_buf, normeds_ref.at[slot], out_sems.at[1]),
        pltpu.make_async_copy(saved_buf, saved_ref.at[slot], out_sems.at[2]),
    ]
    keep_inner = pltpu.make_async_copy(inner_buf, inner_ref.at[slot], out_sems.at[3])

    def load(j):
        at = lanes(j * CHUNK, CHUNK)
        return pltpu.make_async_copy(source_ref.at[:, at], lead_ref.at[:, at], load_sems.at[j])

    def loaded(j):
        if source_ref is not None:
            load(j).wait()

    if source_ref is not None:
        for j in range(lead_ref.shape[1] // CHUNK):
            load(j).start()

        @pl.when(role != 1)
        def _():
            pl.loop(0, lead_ref.shape[1] // CHUNK)(loaded)

    @pl.when(role > 0)
    def _():
        chosen(table_ref[spot + 2], candidates, entry_ref)
        normed, _ = layer_norm(entry_ref[...].astype(WIDE))
        normed_buf[...] = (normed * gain_ref[...]).astype(LOW)
        keeps[0].start()
        keeps[1].start()

    @pl.when(role == 1)
    def _():
        @pl.loop(0, 3 * width // CHUNK, unroll=2)
        def _(j):
            at = lanes(j * CHUNK, CHUNK)
            loaded(j)
            saved_buf[:, at] = matmul(normed_buf[...], lead_ref[:, at]).astype(LOW)

        left = lax.broadcasted_iota(jnp.int32, (tokens, 128), 1) < HEAD_SIZE
        zero = jnp.zeros((tokens, 128), LOW)

        @pl.loop(0, HEADS // 8)
        def _(group):
            for pair in range(4):
                at = group * 512 + pair * 128
                query = saved_buf[:, lanes(at, 128)]
                key = saved_buf[:, lanes(width + at, 128)]
                scores_buf[group * 8 + 2 * pair] = matmul_nt(jnp.where(left, query, zero), key)
                scores_buf[group * 8 + 2 * pair + 1] = matmul_nt(jnp.where(left, zero, query), key)

        @pl.loop(0, HEADS // 4)
        def _(group):
            same = same_segment(seg_row_ref[slot])
            for head in range(4):
                at = group * 4 + head
                probs_buf[at] = head_probs(scores_buf[at], same).astype(LOW)

        @pl.loop(0, HEADS // 8)
        def _(group):
            for pair in range(4):
                at = group * 512 + pair * 128
                value = saved_buf[:, lanes(2 * width + at, 128)]
                mixed = jnp.where(
                    left,
                    matmul(probs_buf[group * 8 + 2 * pair], value),
                    matmul(probs_buf[group * 8 + 2 * pair + 1], value),
                )
                saved_buf[:, lanes(3 * width + at, 128)] = mixed.astype(LOW)

        keeps[2].start()

        @pl.loop(0, width // CHUNK)
        def _(j):
            at = lanes(j * CHUNK, CHUNK)
            loaded(3 * width // CHUNK + j)
            term = matmul(saved_buf[:, 3 * width :], lead_ref[:, lanes(3 * width + j * CHUNK, CHUNK)])
            out_ref[:, at] = (entry_ref[:, at].astype(WIDE) + term).astype(LOW)

    def feed_forward():
        result_buf[...] = entry_ref[...].astype(WIDE)

        @pl.loop(0, lead_ref.shape[1] // CHUNK, unroll=2)
        def _(j):
            at = lanes(j * CHUNK, CHUNK)
            inner = matmul(normed_buf[...], lead_ref[:, at])
            inner_buf[:, at] = inner
            active = gelu(inner).astype(LOW)
            saved_buf[:, at] = active
            result_buf[...] += matmul(active, down_ref[pl.ds(j * CHUNK, CHUNK), :])

        keeps[2].start()
        keep_inner.start()
        out_ref[...] = result_buf[...].astype(LOW)
        keep_inner.wait()

    if down_ref is not None:
        pl.when(role == 2)(feed_forward)

    @pl.when(role > 0)
    def _():
        for keep in keeps:
            keep.wait()


def pinned(value):
    return pltpu.with_memory_space_constraint(value, pltpu.VMEM)


def far(value):
    return pltpu.with_memory_space_constraint(value, pltpu.HBM)


def forward_stage(spot, table, entries, seg_row, gain, lead, down, kept, loads=False):
    tokens, width = entries[0].shape
    hidden = lead.shape[1]
    count = len(entries) + (3 if down is None else 4)
    given = [VMEM_SPEC] * (len(entries) + 2) + [HBM_SPEC if loads else VMEM_SPEC]
    return pl.pallas_call(
        functools.partial(forward_kernel, spot, down is not None, loads, len(entries)),
        out_shape=[jax.ShapeDtypeStruct((tokens, width), LOW)]
        + [jax.ShapeDtypeStruct(k.shape, k.dtype) for k in kept]
        + ([pltpu.VMEM(lead.shape, LOW)] if loads else []),
        in_specs=[SMEM_SPEC] + given + [VMEM_SPEC] * (down is not None) + [HBM_SPEC] * 4,
        out_specs=[VMEM_SPEC] + [HBM_SPEC] * 4 + [VMEM_SPEC] * loads,
        scratch_shapes=[
            pltpu.VMEM((tokens, width), LOW),
            pltpu.VMEM((tokens, hidden), LOW),
            pltpu.VMEM((tokens, hidden), WIDE),
            pltpu.VMEM((tokens, width), WIDE),
            pltpu.VMEM((HEADS, tokens, tokens), WIDE),
            pltpu.VMEM((HEADS, tokens, tokens), LOW),
            pltpu.VMEM((tokens, width), LOW),
            pltpu.SemaphoreType.DMA((4,)),
        ]
        + ([pltpu.SemaphoreType.DMA((hidden // CHUNK,))] if loads else []),
        input_output_aliases={count + 1 + i: 1 + i for i in range(4)},
        compiler_params=pltpu.CompilerParams(vmem_limit_bytes=18 << 20),
        cost_estimate=pl.CostEstimate(
            flops=4 * tokens * width * hidden, bytes_accessed=20 << 20, transcendentals=0
        ),
        name="forward_stage",
    )(
        table,
        *entries,
        seg_row,
        gain,
        (far if loads else pinned)(lead),
        *([pinned(down)] if down is not None else []),
        *map(far, kept),
    )


def backward_kernel(spot, count, *refs):
    backward_body(spot, refs[0], refs[1 : 1 + count], *refs[1 + count :])


def backward_body(
    spot,
    table_ref,
    candidates,
    seg_row_ref,
    gain_ref,
    lead_ref,
    down_ref,
    entries_ref,
    saved_ref,
    inner_ref,
    nexts_in,
    grads_in,
    gains_in,
    out_ref,
    nexts_ref,
    grads_ref,
    gains_ref,
    saved_buf,
    inner_buf,
    grads_buf,
    mixed_buf,
    gain_buf,
    entry_buf,
    normed_buf,
    scores_buf,
    probs_grad_buf,
    probs_buf,
    scores_grad_buf,
    grad_ref,
    in_sems,
    out_sems,
):
    role, slot = table_ref[spot], table_ref[spot + 1]
    tokens, width = grad_ref.shape
    bring_saved = pltpu.make_async_copy(saved_ref.at[slot], saved_buf, in_sems.at[0])
    bring_inner = pltpu.make_async_copy(inner_ref.at[slot], inner_buf, in_sems.at[1])
    bring_entry = pltpu.make_async_copy(entries_ref.at[slot], entry_buf, in_sems.at[2])
    keep_next = pltpu.make_async_copy(grad_ref, nexts_ref.at[slot], out_sems.at[0])
    keep_grads = pltpu.make_async_copy(grads_buf, grads_ref.at[slot], out_sems.at[1])
    keep_gain = pltpu.make_async_copy(gain_buf, gains_ref.at[slot], out_sems.at[2])

    @pl.when(role == 2)
    def _():
        bring_inner.start()

    @pl.when(role == 1)
    def _():
        bring_saved.start()

    @pl.when(role > 0)
    def _():
        bring_entry.start()
        chosen(table_ref[spot + 2], candidates, grad_ref)
        keep_next.start()
        normed_buf[...] = jnp.zeros_like(normed_buf)

    @pl.when(role == 1)
    def _():
        grads_buf[:, 3 * width :] = grad_ref[...]
        mixed_buf[...] = matmul(grad_ref[...], lead_ref[3 * width :, :]).astype(LOW)
        bring_saved.wait()
        left = lax.broadcasted_iota(jnp.int32, (tokens, 128), 1) < HEAD_SIZE
        zero = jnp.zeros((tokens, 128), LOW)
        scale = HEAD_SIZE ** (-0.5)

        @pl.loop(0, HEADS // 8)
        def _(group):
            for pair in range(4):
                at = group * 512 + pair * 128
                query = saved_buf[:, lanes(at, 128)]
                key = saved_buf[:, lanes(width + at, 128)]
                value = saved_buf[:, lanes(2 * width + at, 128)]
                grad = mixed_buf[:, lanes(at, 128)]
                for own in (0, 1):
                    mine = lambda v: jnp.where(left, v, zero) if own == 0 else jnp.where(left, zero, v)
                    scores_buf[group * 8 + 2 * pair + own] = matmul_nt(mine(query), key)
                    probs_grad_buf[group * 8 + 2 * pair + own] = matmul_nt(mine(grad), value)

        @pl.loop(0, HEADS // 4)
        def _(group):
            same = same_segment(seg_row_ref[slot])
            for head in range(4):
                at = group * 4 + head
                probs = head_probs(scores_buf[at], same)
                probs_buf[at] = probs.astype(LOW)
                grad_probs = probs_grad_buf[at]
                scores_grad_buf[at] = (
                    probs * (grad_probs - jnp.sum(probs * grad_probs, axis=-1, keepdims=True))
                ).astype(LOW)

        @pl.loop(0, HEADS // 4)
        def _(group):
            for pair in range(2):
                at = group * 256 + pair * 128
                query = saved_buf[:, lanes(at, 128)]
                key = saved_buf[:, lanes(width + at, 128)]
                grad = mixed_buf[:, lanes(at, 128)]
                parts = []
                for own in (0, 1):
                    probs = probs_buf[group * 4 + 2 * pair + own]
                    grad_low = scores_grad_buf[group * 4 + 2 * pair + own]
                    parts.append(
                        (
                            matmul(grad_low, key) * scale,
                            matmul_tn(grad_low, query) * scale,
                            matmul_tn(probs, grad),
                        )
                    )
                for which in range(3):
                    grads_buf[:, lanes(which * width + at, 128)] = jnp.where(
                        left, parts[0][which], parts[1][which]
                    ).astype(LOW)

        @pl.loop(0, 3 * width // CHUNK, unroll=2)
        def _(j):
            at = lanes(j * CHUNK, CHUNK)
            normed_buf[...] += matmul(grads_buf[:, at], lead_ref[pl.ds(j * CHUNK, CHUNK), :])

    @pl.when(role == 2)
    def _():
        bring_inner.wait()

        @pl.loop(0, lead_ref.shape[0] // CHUNK, unroll=2)
        def _(j):
            at = lanes(j * CHUNK, CHUNK)
            grad_active = matmul(grad_ref[...], down_ref[:, at])
            grads = (gelu_slope(inner_buf[:, at]) * grad_active).astype(LOW)
            grads_buf[:, at] = grads
            normed_buf[...] += matmul(grads, lead_ref[pl.ds(j * CHUNK, CHUNK), :])

    @pl.when(role > 0)
    def _():
        keep_grads.start()
        bring_entry.wait()
        grad_normed = normed_buf[...]
        normed, factor = layer_norm(entry_buf[...].astype(WIDE))
        gain_buf[...] = jnp.broadcast_to(
            jnp.sum(grad_normed * normed, axis=0, keepdims=True), gain_buf.shape
        )
        keep_gain.start()
        out_ref[...] = (
            grad_ref[...].astype(WIDE) + norm_back(grad_normed * gain_ref[...], normed, factor)
        ).astype(LOW)
        keep_next.wait()
        keep_grads.wait()
        keep_gain.wait()


def backward_stage(
    spot, table, nexts, seg_row, gain, lead, down, entries, saved, inner, totals
):
    tokens, width = nexts[0].shape
    count = len(nexts)
    hidden = lead.shape[0]
    return pl.pallas_call(
        functools.partial(backward_kernel, spot, count),
        out_shape=[jax.ShapeDtypeStruct((tokens, width), LOW)]
        + [jax.ShapeDtypeStruct(k.shape, k.dtype) for k in totals],
        in_specs=[SMEM_SPEC] + [VMEM_SPEC] * (count + 4) + [HBM_SPEC] * 6,
        out_specs=[VMEM_SPEC] + [HBM_SPEC] * 3,
        scratch_shapes=[
            pltpu.VMEM((tokens, hidden), LOW),
            pltpu.VMEM((tokens, hidden), WIDE),
            pltpu.VMEM((tokens, hidden), LOW),
            pltpu.VMEM((tokens, width), LOW),
            pltpu.VMEM((8, width), WIDE),
            pltpu.VMEM((tokens, width), LOW),
            pltpu.VMEM((tokens, width), WIDE),
            pltpu.VMEM((HEADS, tokens, tokens), WIDE),
            pltpu.VMEM((HEADS, tokens, tokens), WIDE),
            pltpu.VMEM((HEADS, tokens, tokens), LOW),
            pltpu.VMEM((HEADS, tokens, tokens), LOW),
            pltpu.VMEM((tokens, width), LOW),
            pltpu.SemaphoreType.DMA((3,)),
            pltpu.SemaphoreType.DMA((3,)),
        ],
        input_output_aliases={count + 8 + i: 1 + i for i in range(3)},
        compiler_params=pltpu.CompilerParams(vmem_limit_bytes=18 << 20),
        cost_estimate=pl.CostEstimate(
            flops=4 * tokens * width * hidden, bytes_accessed=20 << 20, transcendentals=0
        ),
        name="backward_stage",
    )(
        table,
        *nexts,
        seg_row,
        gain,
        pinned(lead),
        pinned(down),
        far(entries),
        far(saved),
        far(inner),
        *map(far, totals),
    )


def stats_kernel(spot, plan_ref, *refs):
    candidates, (table_ref, readout_ref, peak_ref, total_ref) = refs[:-4], refs[-4:]
    step = pl.program_id(0)

    @pl.when(step == 0)
    def _():
        chosen(plan_ref[spot], candidates, readout_ref)

    logits = matmul_nt(table_ref[...], readout_ref[...])
    own_peak = jnp.max(logits, axis=0, keepdims=True)
    own_total = lambda peak: jnp.sum(jnp.exp(logits - peak), axis=0, keepdims=True)

    @pl.when(step == 0)
    def _():
        peak_ref[...] = own_peak
        total_ref[...] = own_total(own_peak)

    @pl.when(step > 0)
    def _():
        peak = jnp.maximum(peak_ref[...], own_peak)
        total_ref[...] = total_ref[...] * jnp.exp(peak_ref[...] - peak) + own_total(peak)
        peak_ref[...] = peak


def head_stats(spot, plan, readouts, table, tile):
    tokens, emb = readouts[0].shape
    vocab = table.shape[0]
    whole = pl.BlockSpec((1, tokens), lambda i: (0, 0))
    rows = pl.BlockSpec((tokens, emb), lambda i: (0, 0))
    return pl.pallas_call(
        functools.partial(stats_kernel, spot),
        out_shape=[jax.ShapeDtypeStruct((tokens, emb), LOW)]
        + [jax.ShapeDtypeStruct((1, tokens), WIDE)] * 2,
        grid=(vocab // tile,),
        in_specs=[SMEM_SPEC]
        + [rows] * len(readouts)
        + [pl.BlockSpec((tile, emb), lambda i: (i, 0))],
        out_specs=[rows, whole, whole],
        compiler_params=pltpu.CompilerParams(vmem_limit_bytes=32 << 20),
        cost_estimate=pl.CostEstimate(
            flops=2 * tokens * vocab * emb, bytes_accessed=5 << 20, transcendentals=tokens * vocab
        ),
        name="head_stats",
    )(plan, *readouts, far(table))


def head_kernel(spot, table_base_ref, readout_ref, table_ref, logsum_ref, ids_ref, head_ref, grad_ref):
    tile = table_ref.shape[0]
    logits = matmul_nt(table_ref[...], readout_ref[...])
    ids = ids_ref[...] - (table_base_ref[spot] + pl.program_id(0) * tile)
    hits = lax.broadcasted_iota(jnp.int32, logits.shape, 0) == ids
    probs = jnp.exp(logits - logsum_ref[...])
    grads = jnp.where(hits, probs - 1.0, probs).astype(LOW)
    head = matmul(grads, readout_ref[...])
    unit = tile // 4
    for shard in range(4):
        head_ref[shard, :unit] = head[shard * unit : (shard + 1) * unit].astype(LOW)
    term = matmul_tn(grads, table_ref[...])

    @pl.when(pl.program_id(0) == 0)
    def _():
        grad_ref[...] = term

    @pl.when(pl.program_id(0) > 0)
    def _():
        grad_ref[...] += term


def head_grads(spot, base, readout, table, logsum, ids):
    tokens, emb = readout.shape
    vocab = table.shape[0]
    row = pl.BlockSpec((1, tokens), lambda i: (0, 0))
    whole = pl.BlockSpec((tokens, emb), lambda i: (0, 0))
    part = pl.BlockSpec((vocab // 4, emb), lambda i: (i, 0))
    return pl.pallas_call(
        functools.partial(head_kernel, spot),
        out_shape=[
            pltpu.HBM((16, 512, emb), LOW),
            jax.ShapeDtypeStruct((tokens, emb), WIDE),
        ],
        grid=(4,),
        in_specs=[SMEM_SPEC, whole, part, row, row],
        out_specs=[pl.BlockSpec((4, 512, emb), lambda i: (i, 0, 0)), whole],
        compiler_params=pltpu.CompilerParams(vmem_limit_bytes=32 << 20),
        cost_estimate=pl.CostEstimate(
            flops=6 * tokens * vocab * emb, bytes_accessed=9 << 20, transcendentals=tokens * vocab
        ),
        name="head_grads",
    )(base, readout, far(table), logsum, ids)


def pair_kernel(former_ref, latter_ref, out_ref):
    rows = out_ref.shape[0]
    out_ref[...] = former_ref[:rows].astype(WIDE) + latter_ref[:rows].astype(WIDE)


def pair_sum(former, latter, rows):
    return pl.pallas_call(
        pair_kernel,
        out_shape=jax.ShapeDtypeStruct((rows, former.shape[1]), WIDE),
        in_specs=[VMEM_SPEC] * 2,
        out_specs=VMEM_SPEC,
        compiler_params=pltpu.CompilerParams(vmem_limit_bytes=8 << 20),
        cost_estimate=pl.CostEstimate(flops=0, bytes_accessed=1024, transcendentals=0),
        name="pair_sum",
    )(former, latter)


def lookup_kernel(ids_ref, table_ref, noise_ref, out_ref, total_ref, low_ref):
    step = pl.program_id(0)
    parts, tile = table_ref.shape
    tokens = ids_ref.shape[1]
    blocks = tile // 128

    @pl.when(step == 0)
    def _():
        lane = jnp.bitwise_and(ids_ref[...], 127)
        hits = lax.broadcasted_iota(jnp.int32, (128, tokens), 0) == lane
        low_ref[...] = jnp.where(hits, 1.0, 0.0).astype(LOW)
        total_ref[...] = noise_ref[...].astype(WIDE)

    stacked = jnp.concatenate(
        [table_ref[:, block * 128 : (block + 1) * 128] for block in range(blocks)]
    )
    found = matmul(stacked, low_ref[...])
    own = jnp.right_shift(ids_ref[...], 7) - step * blocks
    total = jnp.zeros_like(total_ref)
    for block in range(blocks):
        total = jnp.where(own == block, found[block * parts : (block + 1) * parts], total)
    total_ref[...] += total

    @pl.when(step == pl.num_programs(0) - 1)
    def _():
        out_ref[...] = total_ref[...].astype(LOW)


def lookup(ids, table, noise, tile):
    parts, vocab = table.shape
    tokens = ids.shape[1]
    whole = pl.BlockSpec((parts, tokens), lambda i: (0, 0))
    return pl.pallas_call(
        lookup_kernel,
        out_shape=jax.ShapeDtypeStruct((parts, tokens), LOW),
        grid=(vocab // tile,),
        in_specs=[
            pl.BlockSpec((1, tokens), lambda i: (0, 0)),
            pl.BlockSpec((parts, tile), lambda i: (0, i)),
            whole,
        ],
        out_specs=whole,
        scratch_shapes=[pltpu.VMEM((parts, tokens), WIDE), pltpu.VMEM((128, tokens), LOW)],
        compiler_params=pltpu.CompilerParams(vmem_limit_bytes=32 << 20),
        cost_estimate=pl.CostEstimate(
            flops=2 * 128 * vocab * tokens, bytes_accessed=4 << 20, transcendentals=0
        ),
        name="lookup",
    )(ids, far(table), noise)


def lead_grad_kernel(where_ref, normed_ref, mixed_ref, grads_ref, *refs):
    got_ref, out_refs, (turned_ref, result_ref) = None, refs[:-2], refs[-2:]
    if len(out_refs) > 1:
        got_ref, out_refs = out_refs[0], out_refs[1:]
    role, half, spot = where_ref[0], where_ref[1], where_ref[2]
    step = pl.program_id(0)
    width = normed_ref.shape[1]
    steps = pl.num_programs(0)
    use_mixed = jnp.logical_and(role == 1, half == 1)

    @pl.when(step == 0)
    def _():
        turned_ref[...] = normed_ref[...].T

    @pl.when(jnp.logical_and(step == steps // 2, use_mixed))
    def _():
        turned_ref[...] = mixed_ref[...].T

    result_ref[...] = matmul(turned_ref[...], grads_ref[...])
    unit = width // 16

    def put(block, rows, part):
        if got_ref is not None:
            part = part + got_ref[block, rows, :].astype(WIDE)
        out_ref = out_refs[0].at[block] if got_ref is None else out_refs[block]
        out_ref[rows, :] = part.astype(LOW)

    @pl.when(half == 0)
    def _():
        for block in range(4):
            x = (spot + block) % 4
            put(block, slice(None), result_ref[pl.ds(pl.multiple_of(x * 4 * unit, 4 * unit), 4 * unit)])

    @pl.when(half == 1)
    def _():
        for block in range(4):
            y = (spot + block) % 4
            for x in range(4):
                rows = pl.ds(pl.multiple_of((4 * x + y) * unit, unit), unit)
                put(block, slice(x * unit, (x + 1) * unit), result_ref[rows])


CHEAP = pl.CostEstimate(flops=0, bytes_accessed=1024, transcendentals=0)


def lead_grad(where, normed, saved, grads, got=None):
    tokens, width = normed.shape
    tile = 1024
    whole = pl.BlockSpec((4, width // 4, tile), lambda i, where: (0, 0, i))
    block = pl.BlockSpec((width // 4, tile), lambda i, where: (0, i))
    shape = (width // 4, 2 * width)
    return pl.pallas_call(
        lead_grad_kernel,
        out_shape=[jax.ShapeDtypeStruct((4,) + shape, LOW)]
        if got is None
        else [jax.ShapeDtypeStruct(shape, LOW)] * 4,
        grid_spec=pltpu.PrefetchScalarGridSpec(
            num_scalar_prefetch=1,
            grid=(2 * width // tile,),
            in_specs=[
                pl.BlockSpec((tokens, width), lambda i, where: (0, 0)),
                pl.BlockSpec((tokens, width), lambda i, where: (0, 3)),
                pl.BlockSpec((tokens, tile), lambda i, where: (0, where[1] * (2 * width // tile) + i)),
            ]
            + ([] if got is None else [whole]),
            out_specs=[whole] if got is None else [block] * 4,
            scratch_shapes=[pltpu.VMEM((width, tokens), LOW), pltpu.VMEM((width, tile), WIDE)],
        ),
        compiler_params=pltpu.CompilerParams(vmem_limit_bytes=24 << 20),
        cost_estimate=CHEAP
        if got is None
        else pl.CostEstimate(
            flops=4 * tokens * width * width, bytes_accessed=12 << 20, transcendentals=0
        ),
        name="lead_grad",
    )(where, far(normed), far(saved), far(grads), *([] if got is None else [got]))


def down_grad_kernel(where_ref, saved_ref, nexts_ref, *refs):
    got_ref, out_refs, (buf_ref, got_buf, sems) = None, refs[:-3], refs[-3:]
    if len(out_refs) > 1:
        got_ref, out_refs = out_refs[0], out_refs[1:]
    role, half, spot = where_ref[0], where_ref[1], where_ref[2]
    at = pl.program_id(0)
    unit = saved_ref.shape[1] // 4

    @pl.when(role == 2)
    def _():
        if got_ref is not None:
            bring = pltpu.make_async_copy(got_ref, got_buf, sems.at[4])
            pl.when(at == 0)(bring.start)
        result = matmul_tn(saved_ref[...], nexts_ref[...])
        if got_ref is not None:
            pl.when(at == 0)(bring.wait)

        def put(block, rows, part):
            if got_ref is not None:
                part = part + got_buf[block, rows, :].astype(WIDE)
            buf_ref[block, rows, :] = part.astype(LOW)

        @pl.when(half == 0)
        def _():
            put((at - spot + 4) % 4, slice(None), result)

        @pl.when(half == 1)
        def _():
            rows = pl.ds(pl.multiple_of(at * unit, unit), unit)
            for y in range(4):
                put((y - spot + 4) % 4, rows, result[y * unit : (y + 1) * unit])

        @pl.when(at == pl.num_programs(0) - 1)
        def _():
            copies = [pltpu.make_async_copy(buf_ref, out_refs[0], sems.at[0])]
            if got_ref is not None:
                copies = [
                    pltpu.make_async_copy(buf_ref.at[block], out_ref, sems.at[block])
                    for block, out_ref in enumerate(out_refs)
                ]
            for copy in copies:
                copy.start()
            for copy in copies:
                copy.wait()


def down_grad(where, saved, nexts, got=None):
    tokens, hidden = saved.shape
    width = nexts.shape[1]
    rows = hidden // 8
    live = lambda where: jnp.where(where[0] == 2, 1, 0)
    return pl.pallas_call(
        down_grad_kernel,
        out_shape=[pltpu.HBM((4, rows, width), LOW)]
        if got is None
        else [pltpu.HBM((rows, width), LOW)] * 4,
        grid_spec=pltpu.PrefetchScalarGridSpec(
            num_scalar_prefetch=1,
            grid=(4,),
            in_specs=[
                pl.BlockSpec((tokens, rows), lambda i, where: (0, (where[1] * 4 + i) * live(where))),
                pl.BlockSpec((tokens, width), lambda i, where: (0, 0)),
            ]
            + ([] if got is None else [HBM_SPEC]),
            out_specs=[HBM_SPEC] * (1 if got is None else 4),
            scratch_shapes=[
                pltpu.VMEM((4, rows, width), LOW),
                pltpu.VMEM((4, 16, 128) if got is None else (4, rows, width), LOW),
                pltpu.SemaphoreType.DMA((5,)),
            ],
        ),
        compiler_params=pltpu.CompilerParams(vmem_limit_bytes=28 << 20),
        cost_estimate=CHEAP,
        name="down_grad",
    )(where, far(saved), far(nexts), *([] if got is None else [far(got)]))


def upper_kernel(where_ref, *refs):
    out_ref = refs[4]
    rows = refs[0].shape[0]
    for at, part in enumerate(refs[:4]):
        place = (where_ref[0] - at + 4) % 4
        out_ref[pl.ds(pl.multiple_of(place * rows, rows), rows), :] = part[...]


def upper_half(where, parts):
    rows, width = parts[0].shape
    return pl.pallas_call(
        upper_kernel,
        out_shape=jax.ShapeDtypeStruct((4 * rows, width), LOW),
        in_specs=[SMEM_SPEC] + [VMEM_SPEC] * 4,
        out_specs=VMEM_SPEC,
        compiler_params=pltpu.CompilerParams(vmem_limit_bytes=8 << 20),
        name="upper_half",
    )(where, *parts)


def hold_down_kernel(where_ref, mine_ref, other_ref, own_ref, out_ref, sems):
    rows = mine_ref.shape[0]
    core = where_ref[1]
    spot = lambda at: out_ref.at[pl.ds(pl.multiple_of(at * rows, rows), rows), :]
    copies = [
        pltpu.make_async_copy(mine_ref, spot(core), sems.at[0]),
        pltpu.make_async_copy(other_ref, spot(1 - core), sems.at[1]),
        pltpu.make_async_copy(own_ref, out_ref.at[pl.ds(2 * rows, 2 * rows), :], sems.at[2]),
    ]
    for copy in copies:
        copy.start()
    for copy in copies:
        copy.wait()


def hold_down(where, mine, other, own):
    rows, width = mine.shape
    return pl.pallas_call(
        hold_down_kernel,
        out_shape=pltpu.VMEM((4 * rows, width), LOW),
        in_specs=[SMEM_SPEC] + [VMEM_SPEC] * 2 + [HBM_SPEC],
        out_specs=VMEM_SPEC,
        scratch_shapes=[pltpu.SemaphoreType.DMA((3,))],
        compiler_params=pltpu.CompilerParams(vmem_limit_bytes=8 << 20),
        name="hold_down",
    )(where, mine, other, far(own))


def noise_kernel(spot, plan_ref, ids_ref, *refs):
    candidates, (packed_ref, noise_ref, buf_ref) = refs[:-3], refs[-3:]
    parts = noise_ref.shape[0]
    chosen(plan_ref[spot], candidates, buf_ref)
    packed_ref[:parts] = buf_ref[...]
    noise_ref[...] = buf_ref[...].astype(WIDE)
    ids = ids_ref[...]
    high = jnp.right_shift(ids, 8).astype(WIDE)
    low = jnp.bitwise_and(ids, 255).astype(WIDE)
    at = lax.broadcasted_iota(jnp.int32, (16, ids.shape[1]), 0)
    split = jnp.where(at == 0, high, jnp.where(at == 1, low, 0.0))
    packed_ref[parts:] = split.astype(LOW)


def noise_pack(spot, plan, ids, candidates):
    parts, tokens = candidates[0].shape
    return pl.pallas_call(
        functools.partial(noise_kernel, spot),
        out_shape=[
            jax.ShapeDtypeStruct((parts + 16, tokens), LOW),
            jax.ShapeDtypeStruct((parts, tokens), WIDE),
        ],
        in_specs=[SMEM_SPEC] + [VMEM_SPEC] * (1 + len(candidates)),
        out_specs=[VMEM_SPEC] * 2,
        scratch_shapes=[pltpu.VMEM((parts, tokens), LOW)],
        compiler_params=pltpu.CompilerParams(vmem_limit_bytes=8 << 20),
        cost_estimate=CHEAP,
        name="noise_pack",
    )(plan, ids, *candidates)


def embed_kernel(base_ref, mine_ref, other_ref, out_ref, total_ref):
    step = pl.program_id(0)
    steps = pl.num_programs(0)
    parts = out_ref.shape[0]
    blocks = total_ref.shape[0] // parts

    def add(gathered_ref):
        count, _, tokens = gathered_ref.shape
        term = None
        for at in range(count):
            split = gathered_ref[at, parts : parts + 16].astype(WIDE)
            ids = (split[0:1] * 256.0 + split[1:2]).astype(jnp.int32) - base_ref[0]
            lane = jnp.bitwise_and(ids, 127)
            hits = lax.broadcasted_iota(jnp.int32, (128, tokens), 0) == lane
            hits = jnp.where(hits, 1.0, 0.0).astype(LOW)
            own = jnp.right_shift(ids, 7)
            grads = gathered_ref[at, :parts]
            masked = jnp.concatenate(
                [grads * jnp.where(own == block, 1.0, 0.0).astype(LOW) for block in range(blocks)]
            )
            part = matmul_nt(masked, hits)
            term = part if term is None else term + part

        @pl.when(step == 0)
        def _():
            total_ref[...] = term

        @pl.when(step > 0)
        def _():
            total_ref[...] += term

    pl.when(step < steps // 2)(lambda: add(mine_ref))
    pl.when(step >= steps // 2)(lambda: add(other_ref))

    @pl.when(step == steps - 1)
    def _():
        rows = out_ref.shape[1]
        for block in range(blocks):
            size = min(128, rows - block * 128)
            out_ref[:, block * 128 : block * 128 + size] = total_ref[
                block * parts : (block + 1) * parts, :size
            ]


def embed_sum(base, mine, other, parts, rows):
    count, deep, tokens = mine.shape
    step = 4
    half = count // step
    blocks = -(-rows // 128)
    return pl.pallas_call(
        embed_kernel,
        out_shape=jax.ShapeDtypeStruct((parts, rows), WIDE),
        grid=(2 * half,),
        in_specs=[
            SMEM_SPEC,
            pl.BlockSpec((step, deep, tokens), lambda i: (jnp.minimum(i, half - 1), 0, 0)),
            pl.BlockSpec((step, deep, tokens), lambda i: (jnp.maximum(i - half, 0), 0, 0)),
        ],
        out_specs=pl.BlockSpec((parts, rows), lambda i: (0, 0)),
        scratch_shapes=[pltpu.VMEM((blocks * parts, 128), WIDE)],
        compiler_params=pltpu.CompilerParams(vmem_limit_bytes=32 << 20),
        cost_estimate=CHEAP,
        name="embed_sum",
    )(base, mine, other)


def empty(*kinds):
    return pl.pallas_call(
        lambda *refs: None,
        out_shape=[pltpu.HBM(shape, dtype) for shape, dtype in kinds],
        out_specs=[HBM_SPEC] * len(kinds),
        compiler_params=pltpu.CompilerParams(vmem_limit_bytes=1 << 20),
        name="empty",
    )()


ROW_LEN = 128
SEC, GRP, NX, NY = 4, 2, 4, 4
ALL = ("section", "group", "row")
TURNS = (1, 3, 2)


def route(value, target_of):
    number = lambda s, g, x, y: (s * GRP + g) * NX * NY + x * NY + y
    pairs = []
    for at in itertools.product(range(SEC), range(GRP), range(NX), range(NY)):
        target = target_of(*at)
        if target is not None:
            pairs.append((number(*at), number(*target)))
    return lax.ppermute(value, ALL, pairs)


def link(value, source, target):
    return route(value, lambda s, g, x, y: (target, g, x, y) if s == source else None)


def turn(value, by):
    return route(value, lambda s, g, x, y: ((s + by) % SEC, g, x, y))


def swap_cores(value, sections=range(SEC)):
    return route(value, lambda s, g, x, y: (s, 1 - g, x, y) if s in sections else None)


def plane_route(value, by, first, sections=range(SEC)):
    def target_of(s, g, x, y):
        if s not in sections:
            return None
        if (g == 0) == first:
            return (s, g, (x + by) % NX, y)
        return (s, g, x, (y + by) % NY)

    return route(value, target_of)


def after(value, earlier):
    return lax.optimization_barrier((value, earlier))[0]


def row_block(values, block, count):
    size = values.shape[0] // count
    return lax.dynamic_slice_in_dim(values, block * size, size, 0)


def plane_first(mine, sections=range(SEC)):
    return [mine[0]] + [plane_route(mine[by], by, True, sections) for by in TURNS]


def plane_sum(pieces):
    total = pieces[0].astype(WIDE)
    for piece in pieces[1:]:
        total = total + piece.astype(WIDE)
    return total.astype(LOW)


def plane_second(pieces, second, sections=range(SEC)):
    total = plane_sum(pieces)
    return [row_block(total, second, 4)] + [
        plane_route(row_block(total, (second + by) % 4, 4), by, False, sections) for by in TURNS
    ]


def group_exchange(values, first):
    number = lambda s, g, x, y: (s * GRP + g) * NX * NY + x * NY + y
    groups = []
    for s in range(SEC):
        for g in range(GRP):
            along_x = (g == 0) == first
            for at in range(4):
                groups.append(
                    [number(s, g, i, at) if along_x else number(s, g, at, i) for i in range(4)]
                )
    return lax.all_to_all(values, ALL, 0, 0, axis_index_groups=groups, tiled=True)


def section_exchange(values):
    return lax.all_to_all(values, "section", 0, 0, tiled=True)


def plans(micro, vocab_part):
    last = SEC - 1
    steps = micro + 2 * last
    table = np.zeros((SEC, 6 * steps + 2), np.int32)
    for s in range(SEC):
        for way in range(2):
            depth = s if way == 0 else last - s
            for step in range(steps):
                at = step - 2 * depth
                if 0 <= at < micro:
                    sources = ([0] if step < micro else []) + [
                        d + 1 for d in range(last) if 0 <= step - 2 - 2 * d < micro
                    ]
                    spot = 3 * (way * steps + step)
                    table[s, spot : spot + 3] = (1 + s % 2, at, sources.index(depth))
        table[s, 6 * steps :] = (s * vocab_part, s)
    return table


def local(
    token_ids,
    segment_ids,
    noise_input,
    embed_table,
    input_proj,
    norm_gain,
    lead_weight,
    down_weight,
    final_gain,
    readout_proj,
    head_table,
):
    section = lax.axis_index("section")
    core = lax.axis_index("group")
    row = lax.axis_index("row")
    x_at, y_at = row // NY, row % NY
    first_at = jnp.where(core == 0, x_at, y_at)
    micro, _, tokens = token_ids.shape
    width = input_proj.shape[1]
    hidden = lead_weight.shape[2]
    half_rows = down_weight.shape[1]
    emb_part = input_proj.shape[0]
    vocab_part, emb = head_table.shape
    vocab = embed_table.shape[0]
    all_tokens = micro * tokens
    last = SEC - 1
    gain_half = norm_gain.astype(WIDE)
    lead = lead_weight[0]
    own_down = down_weight[0]
    seg_row = segment_ids
    flat_ids = token_ids.reshape(-1)

    plan = plans(micro, vocab_part)
    steps = micro + 2 * last
    table = lax.dynamic_index_in_dim(jnp.asarray(plan), section, 0, False)
    flat_ids = after(flat_ids, table)
    where_start = jnp.stack((first_at, core)).astype(jnp.int32)
    to_first = lambda v: [v] + [link(v, s, 0) for s in range(1, SEC)]
    eighth = row_block(row_block(own_down, core, 2), first_at, 4)
    eighth = jnp.where(section == 1, link(eighth, 0, 1), link(eighth, 2, 3))
    noise = noise_input[:, 0].transpose(2, 0, 1).reshape(emb_part, -1)
    own_embedded = lookup(flat_ids[None], embed_table.T, noise, 3200)
    parts = to_first(jnp.concatenate((own_embedded, input_proj), axis=1))
    embedded = jnp.concatenate([part[:, :all_tokens] for part in parts])
    input_full = jnp.concatenate([part[:, all_tokens:] for part in parts])
    first_in = matmul_tn(embedded, input_full).astype(LOW).reshape(micro, tokens, width)
    odd = (1, 3)
    eighth = after(eighth, own_embedded)
    eighths = [eighth] + [plane_route(eighth, by, True, odd) for by in (1, 2, 3)]
    upper = upper_half(where_start, [after(part, first_in) for part in eighths])
    held_down = hold_down(where_start, upper, swap_cores(upper, odd), own_down)

    kept = empty(
        ((micro, tokens, width), LOW),
        ((micro, tokens, width), LOW),
        ((micro, tokens, hidden), LOW),
        ((micro, tokens, hidden), WIDE),
    )

    def sources(first, step, hops, order):
        arrived = [hops[step - 2, s] for s in order if (step - 2, s) in hops]
        return ([first[step]] if step < micro else []) + arrived

    outs, hops = [], {}
    for step in range(steps):
        out, *kept = forward_stage(
            3 * step,
            table,
            sources(first_in, step, hops, range(SEC)),
            seg_row,
            gain_half,
            held_lead if step > 0 else lead,
            held_down if step > 1 else None,
            kept,
            step == 0,
        )
        if step == 0:
            held_lead = kept.pop()
        outs.append(out)
        for s in range(last):
            if 0 <= step - 2 * s < micro:
                ready = after(out, hops[step - 1, s]) if (step - 1, s) in hops else out
                hops[step, s] = link(ready, s, s + 1)
        if step == 2:
            readout_own = after(readout_proj.T, out)
            readout_full = jnp.concatenate(
                [link(readout_own, s, last) for s in range(last)] + [readout_own]
            )
    entries, normeds, saved, inner = kept

    final_rows = jnp.concatenate(outs[2 * last :]).astype(WIDE)
    normed_f, factor_f = layer_norm(final_rows)
    gain_f = final_gain.astype(WIDE)
    final_low = (normed_f * gain_f).astype(LOW)
    readout = matmul_nt(final_low, readout_full).astype(LOW)
    sent = [link(readout, last, s) for s in range(last)]
    readout, peak, total = head_stats(6 * steps + 1, table, sent + [readout], head_table, 2000)
    stats = jnp.concatenate((peak, total))
    all_stats = section_exchange(jnp.tile(stats, (SEC, 1))).reshape(SEC, 2, all_tokens)
    peak = jnp.max(all_stats[:, 0], axis=0)
    total = jnp.sum(all_stats[:, 1] * jnp.exp(all_stats[:, 0] - peak), axis=0)
    logsum = (peak + jnp.log(total))[None]
    head_grad, grad_readout = head_grads(
        6 * steps, table, readout, head_table, logsum, flat_ids[None]
    )
    grad_low = grad_readout.astype(LOW)
    for s in range(last):
        grad_readout = grad_readout + link(grad_low, s, last).astype(WIDE)
    grad_readout = grad_readout.astype(LOW)
    head_grad = lax.psum_scatter(head_grad, "row", scatter_dimension=0)
    readout_grad = matmul_tn(final_low, grad_readout)
    grad_final = matmul(grad_readout, readout_full)
    final_gain_grad = jnp.sum(grad_final * normed_f, axis=0)
    last_grads = norm_back(grad_final * gain_f, normed_f, factor_f).astype(LOW)
    last_grads = last_grads.reshape(micro, tokens, width)

    lead_turned = turned(6 * steps + 1, table, after(lead, grad_low), 0)
    down_turned = turned(6 * steps + 1, table, after(held_down, grad_low), 1)
    totals = empty(
        ((micro, tokens, width), LOW),
        ((micro, tokens, hidden), LOW),
        ((micro, 8, width), WIDE),
    )
    outs, hops = [], {}
    for step in range(steps):
        out, *totals = backward_stage(
            3 * (steps + step),
            table,
            sources(last_grads, step, hops, range(SEC - 1, -1, -1)),
            seg_row,
            gain_half,
            lead_turned,
            down_turned,
            entries,
            saved,
            inner,
            totals,
        )
        outs.append(out)
        for s in range(1, SEC):
            if 0 <= step - 2 * (last - s) < micro:
                ready = after(out, hops[step - 1, s]) if (step - 1, s) in hops else out
                hops[step, s] = link(ready, s, s - 1)
    section, core, row, readout_grad, final_gain_grad = lax.optimization_barrier(
        (section, core, row, readout_grad, final_gain_grad, out)
    )[:5]
    x_at, y_at = row // NY, row % NY
    first_at, second_at = jnp.where(core == 0, x_at, y_at), jnp.where(core == 0, y_at, x_at)
    is_mlp = section % 2 == 1

    first_grads = jnp.concatenate(outs[2 * last :])
    noise_grad = matmul_nt(input_full, first_grads).astype(LOW)
    pieces = noise_grad.reshape(SEC, emb_part, all_tokens)
    sent = [link(pieces[s], 0, s) for s in range(1, SEC)]

    grad_nexts, grads, gain_grads = totals
    gain_grad = jnp.sum(gain_grads[:, 0], axis=0)
    flat = lambda v: v.reshape(all_tokens, v.shape[-1])
    grads = after(grads, head_grad)
    normed, grad_nexts, grads, saved = flat(normeds), flat(grad_nexts), flat(grads), flat(saved)
    role = jnp.where(is_mlp, 2, 1)
    where_other = jnp.stack((role, 1 - core, second_at)).astype(jnp.int32)
    where_mine = jnp.stack((role, core, first_at)).astype(jnp.int32)
    both = lambda mine, other: jnp.where(
        core == 0,
        jnp.concatenate((mine, other), axis=1),
        jnp.concatenate((other, mine), axis=1),
    )
    down_got = swap_cores(down_grad(where_other, saved, grad_nexts)[0], odd)
    lead_other = lead_grad(where_other, normed, saved, grads)[0]
    lead_got = swap_cores(lead_other)
    down_mine = down_grad(after(where_mine, lead_other), saved, grad_nexts, down_got)
    down_first = plane_first(down_mine, odd)
    late_ids = after(flat_ids, down_mine)[None]
    packed, noise_wide = noise_pack(6 * steps + 1, table, late_ids, [pieces[0]] + sent)

    input_grad = matmul(embedded, first_grads).reshape(SEC, 16, 4, width)
    input_grad = input_grad.transpose(1, 0, 2, 3).reshape(16, 16, width)
    readout_grad = readout_grad.reshape(16, 16, width)
    vectors = jnp.concatenate(
        (
            gain_grad.reshape(16, 64),
            final_gain_grad.reshape(SEC, 16, 16).transpose(1, 0, 2).reshape(16, 64),
            jnp.zeros((16, width - 128), WIDE),
        ),
        axis=1,
    )
    small = jnp.concatenate(
        (
            jnp.where(section == 0, input_grad, readout_grad),
            vectors[:, None],
            jnp.zeros((16, 15, width), WIDE),
        ),
        axis=1,
    ).astype(LOW)
    half_of = lambda which: lax.dynamic_slice_in_dim(small, which * (width // 2), width // 2, 2)
    small = half_of(core).astype(WIDE) + swap_cores(half_of(1 - core)).astype(WIDE)
    small = small.astype(LOW).reshape(NX, NY, 32, width // 2)
    small = jnp.where(core == 0, small, small.swapaxes(0, 1)).reshape(4, NY * 32, width // 2)
    deep = emb_part + 16

    def exchange(blocks, packed, first):
        rows = blocks.shape[1]
        everywhere = jnp.broadcast_to(packed, (4,) + packed.shape)
        got = group_exchange(jnp.concatenate((blocks, everywhere), axis=1), first)
        return jnp.sum(got[:, :rows].astype(WIDE), axis=0).astype(LOW), got[:, rows:]

    lead_mine = lead_grad(where_mine, normed, saved, grads, lead_got)
    lead_first = plane_first(lead_mine)
    packed = after(packed, lead_mine)
    down_first = after(down_first, lead_mine)
    small, packed = exchange(after(small, down_first), packed, True)
    small, packed = exchange(
        small.reshape(4, 32, width // 2), packed.reshape(4 * deep, all_tokens), False
    )
    packed = packed.reshape(16, deep, all_tokens)
    down_second = plane_second(after(down_first, packed), second_at, odd)
    lead_second = plane_second(after(lead_first, packed), second_at)
    packed_other = swap_cores(packed)
    small = both(small, swap_cores(small))
    embed_grad = embed_sum(
        (row * (vocab // 16)).reshape(1), packed, packed_other, emb_part, vocab // 16
    )
    down_part = plane_sum(after(down_second, embed_grad))
    lead_part = plane_sum(after(lead_second, embed_grad))
    noise_out = noise_wide.reshape(emb_part, micro, tokens).transpose(1, 2, 0)
    lead_out = both(lead_part, swap_cores(lead_part)).astype(WIDE)

    def first_target(s, g, x, y):
        if s % 2 == 0:
            return None
        return (s - 1, 0, x, y) if g == 0 else (s, 0, x, y)

    def second_target(s, g, x, y):
        return (s - 1, 1, x, y) if s % 2 == 1 and g == 0 else None

    to_core_0 = route(down_part, first_target)
    to_core_1 = route(down_part, second_target)
    down_out = jnp.where(
        core == 0, to_core_0, jnp.where(is_mlp, down_part, to_core_1)
    ).astype(WIDE)

    small = after(small, (lead_part, down_part))
    gain_out = small[16, :64].astype(WIDE)
    input_rows = small[:16].reshape(SEC, 4, width)
    readout_rows = small[:16].reshape(64, SEC, 64)
    final_rows = small[16, 64:128].reshape(SEC, 16)

    finals = jnp.pad(final_rows, ((0, 0), (0, width - 16)))[:, None]
    mine = jnp.where(
        section == 0, input_rows, readout_rows.transpose(1, 0, 2).reshape(SEC, 4, width)
    )
    shared = section_exchange(
        jnp.concatenate((mine, finals, jnp.zeros((SEC, 3, width), LOW)), axis=1)
    )
    input_out = shared[0, :4]
    readout_out = shared[last, :4].reshape(64, 64)
    final_out = shared[last, 4, :16]

    head_out = pair_sum(head_grad, swap_cores(head_grad), vocab_part // (NX * NY))
    return (
        noise_out[:, None],
        embed_grad.T,
        input_out.astype(WIDE),
        gain_out[None],
        lead_out[None],
        down_out[None],
        final_out.astype(WIDE),
        readout_out.astype(WIDE),
        head_out,
    )


def solution(mesh):
    in_specs = (
        P(None, ("group", "row"), None),
        P(None, ("group", "row"), None),
        P(None, ("group", "row"), None, "section"),
        P(None, "section"),
        P("section", None),
        P("section", None),
        P("section", None, None),
        P("section", None, None),
        P(),
        P(None, "section"),
        P("section", None),
    )
    out_specs = (
        P(None, ("group", "row"), None, "section"),
        P("row", "section"),
        P(("section", "row"), None),
        P("section", "row"),
        P("section", "row", None),
        P("section", "row", None),
        P(("section", "row")),
        P("row", "section"),
        P(("section", "row"), None),
    )
    return jax.shard_map(local, mesh=mesh, in_specs=in_specs, out_specs=out_specs, check_vma=False)
```

```python
import functools
import itertools

import jax
import jax.numpy as jnp
import numpy as np
from jax import lax
from jax.experimental import pallas as pl
from jax.experimental.pallas import tpu as pltpu
from jax.sharding import PartitionSpec as P

HEADS = 16
HEAD_SIZE = 64
LOW = jnp.bfloat16
WIDE = jnp.float32
EPSILON = 1e-05
MASKED = -1000000000.0
CHUNK = 1024
GELU_A = 0.7978845608028654
GELU_B = 0.044715
HBM_SPEC = pl.BlockSpec(memory_space=pltpu.HBM)
VMEM_SPEC = pl.BlockSpec(memory_space=pltpu.VMEM)
SMEM_SPEC = pl.BlockSpec(memory_space=pltpu.SMEM)


def matmul(former, latter):
    return jnp.dot(former, latter, preferred_element_type=WIDE)


def matmul_nt(former, latter):
    return lax.dot_general(
        former, latter, (((1,), (1,)), ((), ())), preferred_element_type=WIDE
    )


def matmul_tn(former, latter):
    return lax.dot_general(
        former, latter, (((0,), (0,)), ((), ())), preferred_element_type=WIDE
    )


def layer_norm(values):
    centre = jnp.mean(values, axis=-1, keepdims=True)
    centred = values - centre
    variance = jnp.mean(centred * centred, axis=-1, keepdims=True)
    factor = lax.rsqrt(variance + EPSILON)
    return (centred * factor, factor)


def norm_back(grad_normed, normed, factor):
    first_mean = jnp.mean(grad_normed, axis=-1, keepdims=True)
    second_mean = jnp.mean(grad_normed * normed, axis=-1, keepdims=True)
    return factor * (grad_normed - first_mean - normed * second_mean)


def gelu(v):
    return 0.5 * v * (1.0 + jnp.tanh(GELU_A * (v + GELU_B * (v * v * v))))


def gelu_slope(v):
    square = v * v
    bend = jnp.tanh(GELU_A * (v + GELU_B * (square * v)))
    return 0.5 * (1.0 + bend) + 0.5 * v * (1.0 - bend * bend) * (
        GELU_A * (1.0 + 3.0 * GELU_B * square)
    )


def head_probs(scores, same):
    scores = jnp.where(same, scores * HEAD_SIZE ** (-0.5), MASKED)
    expo = jnp.exp(scores - jnp.max(scores, axis=-1, keepdims=True))
    return expo * (1.0 / jnp.sum(expo, axis=-1, keepdims=True))


def same_segment(row):
    across = jnp.broadcast_to(row.astype(WIDE), (row.shape[1], row.shape[1]))
    return across.T == across


def lanes(at, size):
    return pl.ds(pl.multiple_of(at, 128), size)


def turn_kernel(spot, live, plan_ref, value_ref, out_ref):
    @pl.when(jnp.bitwise_and(plan_ref[spot], 1) >= live)
    def _():
        out_ref[...] = value_ref[...].T


def turned(spot, plan, value, live):
    rows, columns = value.shape
    if rows > columns:
        tile = rows // 8
        blocks = (pl.BlockSpec((tile, columns), lambda i: (i, 0)), pl.BlockSpec((columns, tile), lambda i: (0, i)))
    else:
        tile = columns // 8
        blocks = (pl.BlockSpec((rows, tile), lambda i: (0, i)), pl.BlockSpec((tile, rows), lambda i: (i, 0)))
    return pl.pallas_call(
        functools.partial(turn_kernel, spot, live),
        out_shape=pltpu.VMEM((columns, rows), LOW),
        grid=(8,),
        in_specs=[SMEM_SPEC, blocks[0]],
        out_specs=blocks[1],
        compiler_params=pltpu.CompilerParams(vmem_limit_bytes=12 << 20),
        cost_estimate=pl.CostEstimate(flops=0, bytes_accessed=1024, transcendentals=0),
        name="turned",
    )(plan, far(value))


def chosen(choice, candidates, buffer):
    for at, candidate in enumerate(candidates):

        @pl.when(choice == at)
        def _():
            buffer[...] = candidate[...]


def forward_kernel(spot, with_down, loads, count, *refs):
    table_ref, candidates, refs = refs[0], refs[1 : 1 + count], refs[1 + count :]
    if not with_down:
        refs = refs[:3] + (None,) + refs[3:]
    source_ref = load_sems = None
    if loads:
        source_ref, load_sems = refs[2], refs[-1]
        refs = refs[:2] + (refs[13],) + refs[3:13] + refs[14:-1]
    forward_body(spot, table_ref, candidates, source_ref, load_sems, *refs)


def forward_body(
    spot,
    table_ref,
    candidates,
    source_ref,
    load_sems,
    seg_row_ref,
    gain_ref,
    lead_ref,
    down_ref,
    entries_in,
    normeds_in,
    saved_in,
    inner_in,
    out_ref,
    entries_ref,
    normeds_ref,
    saved_ref,
    inner_ref,
    normed_buf,
    saved_buf,
    inner_buf,
    result_buf,
    scores_buf,
    probs_buf,
    entry_ref,
    out_sems,
):
    role, slot = table_ref[spot], table_ref[spot + 1]
    tokens, width = entry_ref.shape
    keeps = [
        pltpu.make_async_copy(entry_ref, entries_ref.at[slot], out_sems.at[0]),
        pltpu.make_async_copy(normed_buf, normeds_ref.at[slot], out_sems.at[1]),
        pltpu.make_async_copy(saved_buf, saved_ref.at[slot], out_sems.at[2]),
    ]
    keep_inner = pltpu.make_async_copy(inner_buf, inner_ref.at[slot], out_sems.at[3])

    def load(j):
        at = lanes(j * CHUNK, CHUNK)
        return pltpu.make_async_copy(source_ref.at[:, at], lead_ref.at[:, at], load_sems.at[j])

    def loaded(j):
        if source_ref is not None:
            load(j).wait()

    if source_ref is not None:
        for j in range(lead_ref.shape[1] // CHUNK):
            load(j).start()

        @pl.when(role != 1)
        def _():
            pl.loop(0, lead_ref.shape[1] // CHUNK)(loaded)

    @pl.when(role > 0)
    def _():
        chosen(table_ref[spot + 2], candidates, entry_ref)
        normed, _ = layer_norm(entry_ref[...].astype(WIDE))
        normed_buf[...] = (normed * gain_ref[...]).astype(LOW)
        keeps[0].start()
        keeps[1].start()

    @pl.when(role == 1)
    def _():
        @pl.loop(0, 3 * width // CHUNK, unroll=2)
        def _(j):
            at = lanes(j * CHUNK, CHUNK)
            loaded(j)
            saved_buf[:, at] = matmul(normed_buf[...], lead_ref[:, at]).astype(LOW)

        left = lax.broadcasted_iota(jnp.int32, (tokens, 128), 1) < HEAD_SIZE
        zero = jnp.zeros((tokens, 128), LOW)

        @pl.loop(0, HEADS // 8)
        def _(group):
            for pair in range(4):
                at = group * 512 + pair * 128
                query = saved_buf[:, lanes(at, 128)]
                key = saved_buf[:, lanes(width + at, 128)]
                scores_buf[group * 8 + 2 * pair] = matmul_nt(jnp.where(left, query, zero), key)
                scores_buf[group * 8 + 2 * pair + 1] = matmul_nt(jnp.where(left, zero, query), key)

        @pl.loop(0, HEADS // 4)
        def _(group):
            same = same_segment(seg_row_ref[slot])
            for head in range(4):
                at = group * 4 + head
                probs_buf[at] = head_probs(scores_buf[at], same).astype(LOW)

        @pl.loop(0, HEADS // 8)
        def _(group):
            for pair in range(4):
                at = group * 512 + pair * 128
                value = saved_buf[:, lanes(2 * width + at, 128)]
                mixed = jnp.where(
                    left,
                    matmul(probs_buf[group * 8 + 2 * pair], value),
                    matmul(probs_buf[group * 8 + 2 * pair + 1], value),
                )
                saved_buf[:, lanes(3 * width + at, 128)] = mixed.astype(LOW)

        keeps[2].start()

        @pl.loop(0, width // CHUNK)
        def _(j):
            at = lanes(j * CHUNK, CHUNK)
            loaded(3 * width // CHUNK + j)
            term = matmul(saved_buf[:, 3 * width :], lead_ref[:, lanes(3 * width + j * CHUNK, CHUNK)])
            out_ref[:, at] = (entry_ref[:, at].astype(WIDE) + term).astype(LOW)

    def feed_forward():
        result_buf[...] = entry_ref[...].astype(WIDE)

        @pl.loop(0, lead_ref.shape[1] // CHUNK, unroll=2)
        def _(j):
            at = lanes(j * CHUNK, CHUNK)
            inner = matmul(normed_buf[...], lead_ref[:, at])
            inner_buf[:, at] = inner
            active = gelu(inner).astype(LOW)
            saved_buf[:, at] = active
            result_buf[...] += matmul(active, down_ref[pl.ds(j * CHUNK, CHUNK), :])

        keeps[2].start()
        keep_inner.start()
        out_ref[...] = result_buf[...].astype(LOW)
        keep_inner.wait()

    if down_ref is not None:
        pl.when(role == 2)(feed_forward)

    @pl.when(role > 0)
    def _():
        for keep in keeps:
            keep.wait()


def pinned(value):
    return pltpu.with_memory_space_constraint(value, pltpu.VMEM)


def far(value):
    return pltpu.with_memory_space_constraint(value, pltpu.HBM)


def forward_stage(spot, table, entries, seg_row, gain, lead, down, kept, loads=False):
    tokens, width = entries[0].shape
    hidden = lead.shape[1]
    count = len(entries) + (3 if down is None else 4)
    given = [VMEM_SPEC] * (len(entries) + 2) + [HBM_SPEC if loads else VMEM_SPEC]
    return pl.pallas_call(
        functools.partial(forward_kernel, spot, down is not None, loads, len(entries)),
        out_shape=[jax.ShapeDtypeStruct((tokens, width), LOW)]
        + [jax.ShapeDtypeStruct(k.shape, k.dtype) for k in kept]
        + ([pltpu.VMEM(lead.shape, LOW)] if loads else []),
        in_specs=[SMEM_SPEC] + given + [VMEM_SPEC] * (down is not None) + [HBM_SPEC] * 4,
        out_specs=[VMEM_SPEC] + [HBM_SPEC] * 4 + [VMEM_SPEC] * loads,
        scratch_shapes=[
            pltpu.VMEM((tokens, width), LOW),
            pltpu.VMEM((tokens, hidden), LOW),
            pltpu.VMEM((tokens, hidden), WIDE),
            pltpu.VMEM((tokens, width), WIDE),
            pltpu.VMEM((HEADS, tokens, tokens), WIDE),
            pltpu.VMEM((HEADS, tokens, tokens), LOW),
            pltpu.VMEM((tokens, width), LOW),
            pltpu.SemaphoreType.DMA((4,)),
        ]
        + ([pltpu.SemaphoreType.DMA((hidden // CHUNK,))] if loads else []),
        input_output_aliases={count + 1 + i: 1 + i for i in range(4)},
        compiler_params=pltpu.CompilerParams(vmem_limit_bytes=18 << 20),
        cost_estimate=pl.CostEstimate(
            flops=4 * tokens * width * hidden, bytes_accessed=20 << 20, transcendentals=0
        ),
        name="forward_stage",
    )(
        table,
        *entries,
        seg_row,
        gain,
        (far if loads else pinned)(lead),
        *([pinned(down)] if down is not None else []),
        *map(far, kept),
    )


def backward_kernel(spot, count, *refs):
    backward_body(spot, refs[0], refs[1 : 1 + count], *refs[1 + count :])


def backward_body(
    spot,
    table_ref,
    candidates,
    seg_row_ref,
    gain_ref,
    lead_ref,
    down_ref,
    entries_ref,
    saved_ref,
    inner_ref,
    nexts_in,
    grads_in,
    gains_in,
    out_ref,
    nexts_ref,
    grads_ref,
    gains_ref,
    saved_buf,
    inner_buf,
    grads_buf,
    mixed_buf,
    gain_buf,
    entry_buf,
    normed_buf,
    scores_buf,
    probs_grad_buf,
    probs_buf,
    scores_grad_buf,
    grad_ref,
    in_sems,
    out_sems,
):
    role, slot = table_ref[spot], table_ref[spot + 1]
    tokens, width = grad_ref.shape
    bring_saved = pltpu.make_async_copy(saved_ref.at[slot], saved_buf, in_sems.at[0])
    bring_inner = pltpu.make_async_copy(inner_ref.at[slot], inner_buf, in_sems.at[1])
    bring_entry = pltpu.make_async_copy(entries_ref.at[slot], entry_buf, in_sems.at[2])
    keep_next = pltpu.make_async_copy(grad_ref, nexts_ref.at[slot], out_sems.at[0])
    keep_grads = pltpu.make_async_copy(grads_buf, grads_ref.at[slot], out_sems.at[1])
    keep_gain = pltpu.make_async_copy(gain_buf, gains_ref.at[slot], out_sems.at[2])

    @pl.when(role == 2)
    def _():
        bring_inner.start()

    @pl.when(role == 1)
    def _():
        bring_saved.start()

    @pl.when(role > 0)
    def _():
        bring_entry.start()
        chosen(table_ref[spot + 2], candidates, grad_ref)
        keep_next.start()
        normed_buf[...] = jnp.zeros_like(normed_buf)

    @pl.when(role == 1)
    def _():
        grads_buf[:, 3 * width :] = grad_ref[...]
        mixed_buf[...] = matmul(grad_ref[...], lead_ref[3 * width :, :]).astype(LOW)
        bring_saved.wait()
        left = lax.broadcasted_iota(jnp.int32, (tokens, 128), 1) < HEAD_SIZE
        zero = jnp.zeros((tokens, 128), LOW)
        scale = HEAD_SIZE ** (-0.5)

        @pl.loop(0, HEADS // 8)
        def _(group):
            for pair in range(4):
                at = group * 512 + pair * 128
                query = saved_buf[:, lanes(at, 128)]
                key = saved_buf[:, lanes(width + at, 128)]
                value = saved_buf[:, lanes(2 * width + at, 128)]
                grad = mixed_buf[:, lanes(at, 128)]
                for own in (0, 1):
                    mine = lambda v: jnp.where(left, v, zero) if own == 0 else jnp.where(left, zero, v)
                    scores_buf[group * 8 + 2 * pair + own] = matmul_nt(mine(query), key)
                    probs_grad_buf[group * 8 + 2 * pair + own] = matmul_nt(mine(grad), value)

        @pl.loop(0, HEADS // 4)
        def _(group):
            same = same_segment(seg_row_ref[slot])
            for head in range(4):
                at = group * 4 + head
                probs = head_probs(scores_buf[at], same)
                probs_buf[at] = probs.astype(LOW)
                grad_probs = probs_grad_buf[at]
                scores_grad_buf[at] = (
                    probs * (grad_probs - jnp.sum(probs * grad_probs, axis=-1, keepdims=True))
                ).astype(LOW)

        @pl.loop(0, HEADS // 4)
        def _(group):
            for pair in range(2):
                at = group * 256 + pair * 128
                query = saved_buf[:, lanes(at, 128)]
                key = saved_buf[:, lanes(width + at, 128)]
                grad = mixed_buf[:, lanes(at, 128)]
                parts = []
                for own in (0, 1):
                    probs = probs_buf[group * 4 + 2 * pair + own]
                    grad_low = scores_grad_buf[group * 4 + 2 * pair + own]
                    parts.append(
                        (
                            matmul(grad_low, key) * scale,
                            matmul_tn(grad_low, query) * scale,
                            matmul_tn(probs, grad),
                        )
                    )
                for which in range(3):
                    grads_buf[:, lanes(which * width + at, 128)] = jnp.where(
                        left, parts[0][which], parts[1][which]
                    ).astype(LOW)

        @pl.loop(0, 3 * width // CHUNK, unroll=2)
        def _(j):
            at = lanes(j * CHUNK, CHUNK)
            normed_buf[...] += matmul(grads_buf[:, at], lead_ref[pl.ds(j * CHUNK, CHUNK), :])

    @pl.when(role == 2)
    def _():
        bring_inner.wait()

        @pl.loop(0, lead_ref.shape[0] // CHUNK, unroll=2)
        def _(j):
            at = lanes(j * CHUNK, CHUNK)
            grad_active = matmul(grad_ref[...], down_ref[:, at])
            grads = (gelu_slope(inner_buf[:, at]) * grad_active).astype(LOW)
            grads_buf[:, at] = grads
            normed_buf[...] += matmul(grads, lead_ref[pl.ds(j * CHUNK, CHUNK), :])

    @pl.when(role > 0)
    def _():
        keep_grads.start()
        bring_entry.wait()
        grad_normed = normed_buf[...]
        normed, factor = layer_norm(entry_buf[...].astype(WIDE))
        gain_buf[...] = jnp.broadcast_to(
            jnp.sum(grad_normed * normed, axis=0, keepdims=True), gain_buf.shape
        )
        keep_gain.start()
        out_ref[...] = (
            grad_ref[...].astype(WIDE) + norm_back(grad_normed * gain_ref[...], normed, factor)
        ).astype(LOW)
        keep_next.wait()
        keep_grads.wait()
        keep_gain.wait()


def backward_stage(
    spot, table, nexts, seg_row, gain, lead, down, entries, saved, inner, totals
):
    tokens, width = nexts[0].shape
    count = len(nexts)
    hidden = lead.shape[0]
    return pl.pallas_call(
        functools.partial(backward_kernel, spot, count),
        out_shape=[jax.ShapeDtypeStruct((tokens, width), LOW)]
        + [jax.ShapeDtypeStruct(k.shape, k.dtype) for k in totals],
        in_specs=[SMEM_SPEC] + [VMEM_SPEC] * (count + 4) + [HBM_SPEC] * 6,
        out_specs=[VMEM_SPEC] + [HBM_SPEC] * 3,
        scratch_shapes=[
            pltpu.VMEM((tokens, hidden), LOW),
            pltpu.VMEM((tokens, hidden), WIDE),
            pltpu.VMEM((tokens, hidden), LOW),
            pltpu.VMEM((tokens, width), LOW),
            pltpu.VMEM((8, width), WIDE),
            pltpu.VMEM((tokens, width), LOW),
            pltpu.VMEM((tokens, width), WIDE),
            pltpu.VMEM((HEADS, tokens, tokens), WIDE),
            pltpu.VMEM((HEADS, tokens, tokens), WIDE),
            pltpu.VMEM((HEADS, tokens, tokens), LOW),
            pltpu.VMEM((HEADS, tokens, tokens), LOW),
            pltpu.VMEM((tokens, width), LOW),
            pltpu.SemaphoreType.DMA((3,)),
            pltpu.SemaphoreType.DMA((3,)),
        ],
        input_output_aliases={count + 8 + i: 1 + i for i in range(3)},
        compiler_params=pltpu.CompilerParams(vmem_limit_bytes=18 << 20),
        cost_estimate=pl.CostEstimate(
            flops=4 * tokens * width * hidden, bytes_accessed=20 << 20, transcendentals=0
        ),
        name="backward_stage",
    )(
        table,
        *nexts,
        seg_row,
        gain,
        pinned(lead),
        pinned(down),
        far(entries),
        far(saved),
        far(inner),
        *map(far, totals),
    )


def stats_kernel(spot, plan_ref, *refs):
    candidates, (table_ref, readout_ref, peak_ref, total_ref) = refs[:-4], refs[-4:]
    step = pl.program_id(0)

    @pl.when(step == 0)
    def _():
        chosen(plan_ref[spot], candidates, readout_ref)

    logits = matmul_nt(table_ref[...], readout_ref[...])
    own_peak = jnp.max(logits, axis=0, keepdims=True)
    own_total = lambda peak: jnp.sum(jnp.exp(logits - peak), axis=0, keepdims=True)

    @pl.when(step == 0)
    def _():
        peak_ref[...] = own_peak
        total_ref[...] = own_total(own_peak)

    @pl.when(step > 0)
    def _():
        peak = jnp.maximum(peak_ref[...], own_peak)
        total_ref[...] = total_ref[...] * jnp.exp(peak_ref[...] - peak) + own_total(peak)
        peak_ref[...] = peak


def head_stats(spot, plan, readouts, table, tile):
    tokens, emb = readouts[0].shape
    vocab = table.shape[0]
    whole = pl.BlockSpec((1, tokens), lambda i: (0, 0))
    rows = pl.BlockSpec((tokens, emb), lambda i: (0, 0))
    return pl.pallas_call(
        functools.partial(stats_kernel, spot),
        out_shape=[jax.ShapeDtypeStruct((tokens, emb), LOW)]
        + [jax.ShapeDtypeStruct((1, tokens), WIDE)] * 2,
        grid=(vocab // tile,),
        in_specs=[SMEM_SPEC]
        + [rows] * len(readouts)
        + [pl.BlockSpec((tile, emb), lambda i: (i, 0))],
        out_specs=[rows, whole, whole],
        compiler_params=pltpu.CompilerParams(vmem_limit_bytes=32 << 20),
        cost_estimate=pl.CostEstimate(
            flops=2 * tokens * vocab * emb, bytes_accessed=5 << 20, transcendentals=tokens * vocab
        ),
        name="head_stats",
    )(plan, *readouts, far(table))


def head_kernel(spot, table_base_ref, readout_ref, table_ref, logsum_ref, ids_ref, head_ref, grad_ref):
    tile = table_ref.shape[0]
    logits = matmul_nt(table_ref[...], readout_ref[...])
    ids = ids_ref[...] - (table_base_ref[spot] + pl.program_id(0) * tile)
    hits = lax.broadcasted_iota(jnp.int32, logits.shape, 0) == ids
    probs = jnp.exp(logits - logsum_ref[...])
    grads = jnp.where(hits, probs - 1.0, probs).astype(LOW)
    head = matmul(grads, readout_ref[...])
    unit = tile // 4
    for shard in range(4):
        head_ref[shard, :unit] = head[shard * unit : (shard + 1) * unit].astype(LOW)
    term = matmul_tn(grads, table_ref[...])

    @pl.when(pl.program_id(0) == 0)
    def _():
        grad_ref[...] = term

    @pl.when(pl.program_id(0) > 0)
    def _():
        grad_ref[...] += term


def head_grads(spot, base, readout, table, logsum, ids):
    tokens, emb = readout.shape
    vocab = table.shape[0]
    row = pl.BlockSpec((1, tokens), lambda i: (0, 0))
    whole = pl.BlockSpec((tokens, emb), lambda i: (0, 0))
    part = pl.BlockSpec((vocab // 4, emb), lambda i: (i, 0))
    return pl.pallas_call(
        functools.partial(head_kernel, spot),
        out_shape=[
            pltpu.HBM((16, 512, emb), LOW),
            jax.ShapeDtypeStruct((tokens, emb), WIDE),
        ],
        grid=(4,),
        in_specs=[SMEM_SPEC, whole, part, row, row],
        out_specs=[pl.BlockSpec((4, 512, emb), lambda i: (i, 0, 0)), whole],
        compiler_params=pltpu.CompilerParams(vmem_limit_bytes=32 << 20),
        cost_estimate=pl.CostEstimate(
            flops=6 * tokens * vocab * emb, bytes_accessed=9 << 20, transcendentals=tokens * vocab
        ),
        name="head_grads",
    )(base, readout, far(table), logsum, ids)


def pair_kernel(former_ref, latter_ref, out_ref):
    rows = out_ref.shape[0]
    out_ref[...] = former_ref[:rows].astype(WIDE) + latter_ref[:rows].astype(WIDE)


def pair_sum(former, latter, rows):
    return pl.pallas_call(
        pair_kernel,
        out_shape=jax.ShapeDtypeStruct((rows, former.shape[1]), WIDE),
        in_specs=[VMEM_SPEC] * 2,
        out_specs=VMEM_SPEC,
        compiler_params=pltpu.CompilerParams(vmem_limit_bytes=8 << 20),
        cost_estimate=pl.CostEstimate(flops=0, bytes_accessed=1024, transcendentals=0),
        name="pair_sum",
    )(former, latter)


def lookup_kernel(ids_ref, table_ref, noise_ref, out_ref, total_ref, low_ref):
    step = pl.program_id(0)
    parts, tile = table_ref.shape
    tokens = ids_ref.shape[1]
    blocks = tile // 128

    @pl.when(step == 0)
    def _():
        lane = jnp.bitwise_and(ids_ref[...], 127)
        hits = lax.broadcasted_iota(jnp.int32, (128, tokens), 0) == lane
        low_ref[...] = jnp.where(hits, 1.0, 0.0).astype(LOW)
        total_ref[...] = noise_ref[...].astype(WIDE)

    stacked = jnp.concatenate(
        [table_ref[:, block * 128 : (block + 1) * 128] for block in range(blocks)]
    )
    found = matmul(stacked, low_ref[...])
    own = jnp.right_shift(ids_ref[...], 7) - step * blocks
    total = jnp.zeros_like(total_ref)
    for block in range(blocks):
        total = jnp.where(own == block, found[block * parts : (block + 1) * parts], total)
    total_ref[...] += total

    @pl.when(step == pl.num_programs(0) - 1)
    def _():
        out_ref[...] = total_ref[...].astype(LOW)


def lookup(ids, table, noise, tile):
    parts, vocab = table.shape
    tokens = ids.shape[1]
    whole = pl.BlockSpec((parts, tokens), lambda i: (0, 0))
    return pl.pallas_call(
        lookup_kernel,
        out_shape=jax.ShapeDtypeStruct((parts, tokens), LOW),
        grid=(vocab // tile,),
        in_specs=[
            pl.BlockSpec((1, tokens), lambda i: (0, 0)),
            pl.BlockSpec((parts, tile), lambda i: (0, i)),
            whole,
        ],
        out_specs=whole,
        scratch_shapes=[pltpu.VMEM((parts, tokens), WIDE), pltpu.VMEM((128, tokens), LOW)],
        compiler_params=pltpu.CompilerParams(vmem_limit_bytes=32 << 20),
        cost_estimate=pl.CostEstimate(
            flops=2 * 128 * vocab * tokens, bytes_accessed=4 << 20, transcendentals=0
        ),
        name="lookup",
    )(ids, far(table), noise)


def lead_grad_kernel(where_ref, normed_ref, mixed_ref, grads_ref, *refs):
    got_ref, out_refs, (turned_ref, result_ref) = None, refs[:-2], refs[-2:]
    if len(out_refs) > 1:
        got_ref, out_refs = out_refs[0], out_refs[1:]
    role, half, spot = where_ref[0], where_ref[1], where_ref[2]
    step = pl.program_id(0)
    width = normed_ref.shape[1]
    steps = pl.num_programs(0)
    use_mixed = jnp.logical_and(role == 1, half == 1)

    @pl.when(step == 0)
    def _():
        turned_ref[...] = normed_ref[...].T

    @pl.when(jnp.logical_and(step == steps // 2, use_mixed))
    def _():
        turned_ref[...] = mixed_ref[...].T

    result_ref[...] = matmul(turned_ref[...], grads_ref[...])
    unit = width // 16

    def put(block, rows, part):
        if got_ref is not None:
            part = part + got_ref[block, rows, :].astype(WIDE)
        out_ref = out_refs[0].at[block] if got_ref is None else out_refs[block]
        out_ref[rows, :] = part.astype(LOW)

    @pl.when(half == 0)
    def _():
        for block in range(4):
            x = (spot + block) % 4
            put(block, slice(None), result_ref[pl.ds(pl.multiple_of(x * 4 * unit, 4 * unit), 4 * unit)])

    @pl.when(half == 1)
    def _():
        for block in range(4):
            y = (spot + block) % 4
            for x in range(4):
                rows = pl.ds(pl.multiple_of((4 * x + y) * unit, unit), unit)
                put(block, slice(x * unit, (x + 1) * unit), result_ref[rows])


CHEAP = pl.CostEstimate(flops=0, bytes_accessed=1024, transcendentals=0)


def lead_grad(where, normed, saved, grads, got=None):
    tokens, width = normed.shape
    tile = 1024
    whole = pl.BlockSpec((4, width // 4, tile), lambda i, where: (0, 0, i))
    block = pl.BlockSpec((width // 4, tile), lambda i, where: (0, i))
    shape = (width // 4, 2 * width)
    return pl.pallas_call(
        lead_grad_kernel,
        out_shape=[jax.ShapeDtypeStruct((4,) + shape, LOW)]
        if got is None
        else [jax.ShapeDtypeStruct(shape, LOW)] * 4,
        grid_spec=pltpu.PrefetchScalarGridSpec(
            num_scalar_prefetch=1,
            grid=(2 * width // tile,),
            in_specs=[
                pl.BlockSpec((tokens, width), lambda i, where: (0, 0)),
                pl.BlockSpec((tokens, width), lambda i, where: (0, 3)),
                pl.BlockSpec((tokens, tile), lambda i, where: (0, where[1] * (2 * width // tile) + i)),
            ]
            + ([] if got is None else [whole]),
            out_specs=[whole] if got is None else [block] * 4,
            scratch_shapes=[pltpu.VMEM((width, tokens), LOW), pltpu.VMEM((width, tile), WIDE)],
        ),
        compiler_params=pltpu.CompilerParams(vmem_limit_bytes=24 << 20),
        cost_estimate=CHEAP
        if got is None
        else pl.CostEstimate(
            flops=4 * tokens * width * width, bytes_accessed=12 << 20, transcendentals=0
        ),
        name="lead_grad",
    )(where, far(normed), far(saved), far(grads), *([] if got is None else [got]))


def down_grad_kernel(where_ref, saved_ref, nexts_ref, *refs):
    got_ref, out_refs, (buf_ref, got_buf, sems) = None, refs[:-3], refs[-3:]
    if len(out_refs) > 1:
        got_ref, out_refs = out_refs[0], out_refs[1:]
    role, half, spot = where_ref[0], where_ref[1], where_ref[2]
    at = pl.program_id(0)
    unit = saved_ref.shape[1] // 4

    @pl.when(role == 2)
    def _():
        if got_ref is not None:
            bring = pltpu.make_async_copy(got_ref, got_buf, sems.at[4])
            pl.when(at == 0)(bring.start)
        result = matmul_tn(saved_ref[...], nexts_ref[...])
        if got_ref is not None:
            pl.when(at == 0)(bring.wait)

        def put(block, rows, part):
            if got_ref is not None:
                part = part + got_buf[block, rows, :].astype(WIDE)
            buf_ref[block, rows, :] = part.astype(LOW)

        @pl.when(half == 0)
        def _():
            put((at - spot + 4) % 4, slice(None), result)

        @pl.when(half == 1)
        def _():
            rows = pl.ds(pl.multiple_of(at * unit, unit), unit)
            for y in range(4):
                put((y - spot + 4) % 4, rows, result[y * unit : (y + 1) * unit])

        @pl.when(at == pl.num_programs(0) - 1)
        def _():
            copies = [pltpu.make_async_copy(buf_ref, out_refs[0], sems.at[0])]
            if got_ref is not None:
                copies = [
                    pltpu.make_async_copy(buf_ref.at[block], out_ref, sems.at[block])
                    for block, out_ref in enumerate(out_refs)
                ]
            for copy in copies:
                copy.start()
            for copy in copies:
                copy.wait()


def down_grad(where, saved, nexts, got=None):
    tokens, hidden = saved.shape
    width = nexts.shape[1]
    rows = hidden // 8
    live = lambda where: jnp.where(where[0] == 2, 1, 0)
    return pl.pallas_call(
        down_grad_kernel,
        out_shape=[pltpu.HBM((4, rows, width), LOW)]
        if got is None
        else [pltpu.HBM((rows, width), LOW)] * 4,
        grid_spec=pltpu.PrefetchScalarGridSpec(
            num_scalar_prefetch=1,
            grid=(4,),
            in_specs=[
                pl.BlockSpec((tokens, rows), lambda i, where: (0, (where[1] * 4 + i) * live(where))),
                pl.BlockSpec((tokens, width), lambda i, where: (0, 0)),
            ]
            + ([] if got is None else [HBM_SPEC]),
            out_specs=[HBM_SPEC] * (1 if got is None else 4),
            scratch_shapes=[
                pltpu.VMEM((4, rows, width), LOW),
                pltpu.VMEM((4, 16, 128) if got is None else (4, rows, width), LOW),
                pltpu.SemaphoreType.DMA((5,)),
            ],
        ),
        compiler_params=pltpu.CompilerParams(vmem_limit_bytes=28 << 20),
        cost_estimate=CHEAP,
        name="down_grad",
    )(where, far(saved), far(nexts), *([] if got is None else [far(got)]))


def upper_kernel(where_ref, *refs):
    out_ref = refs[4]
    rows = refs[0].shape[0]
    for at, part in enumerate(refs[:4]):
        place = (where_ref[0] - at + 4) % 4
        out_ref[pl.ds(pl.multiple_of(place * rows, rows), rows), :] = part[...]


def upper_half(where, parts):
    rows, width = parts[0].shape
    return pl.pallas_call(
        upper_kernel,
        out_shape=jax.ShapeDtypeStruct((4 * rows, width), LOW),
        in_specs=[SMEM_SPEC] + [VMEM_SPEC] * 4,
        out_specs=VMEM_SPEC,
        compiler_params=pltpu.CompilerParams(vmem_limit_bytes=8 << 20),
        name="upper_half",
    )(where, *parts)


def hold_down_kernel(where_ref, mine_ref, other_ref, own_ref, out_ref, sems):
    rows = mine_ref.shape[0]
    core = where_ref[1]
    spot = lambda at: out_ref.at[pl.ds(pl.multiple_of(at * rows, rows), rows), :]
    copies = [
        pltpu.make_async_copy(mine_ref, spot(core), sems.at[0]),
        pltpu.make_async_copy(other_ref, spot(1 - core), sems.at[1]),
        pltpu.make_async_copy(own_ref, out_ref.at[pl.ds(2 * rows, 2 * rows), :], sems.at[2]),
    ]
    for copy in copies:
        copy.start()
    for copy in copies:
        copy.wait()


def hold_down(where, mine, other, own):
    rows, width = mine.shape
    return pl.pallas_call(
        hold_down_kernel,
        out_shape=pltpu.VMEM((4 * rows, width), LOW),
        in_specs=[SMEM_SPEC] + [VMEM_SPEC] * 2 + [HBM_SPEC],
        out_specs=VMEM_SPEC,
        scratch_shapes=[pltpu.SemaphoreType.DMA((3,))],
        compiler_params=pltpu.CompilerParams(vmem_limit_bytes=8 << 20),
        name="hold_down",
    )(where, mine, other, far(own))


def noise_kernel(spot, plan_ref, ids_ref, *refs):
    candidates, (packed_ref, noise_ref, buf_ref) = refs[:-3], refs[-3:]
    parts = noise_ref.shape[0]
    chosen(plan_ref[spot], candidates, buf_ref)
    packed_ref[:parts] = buf_ref[...]
    noise_ref[...] = buf_ref[...].astype(WIDE)
    ids = ids_ref[...]
    high = jnp.right_shift(ids, 8).astype(WIDE)
    low = jnp.bitwise_and(ids, 255).astype(WIDE)
    at = lax.broadcasted_iota(jnp.int32, (16, ids.shape[1]), 0)
    split = jnp.where(at == 0, high, jnp.where(at == 1, low, 0.0))
    packed_ref[parts:] = split.astype(LOW)


def noise_pack(spot, plan, ids, candidates):
    parts, tokens = candidates[0].shape
    return pl.pallas_call(
        functools.partial(noise_kernel, spot),
        out_shape=[
            jax.ShapeDtypeStruct((parts + 16, tokens), LOW),
            jax.ShapeDtypeStruct((parts, tokens), WIDE),
        ],
        in_specs=[SMEM_SPEC] + [VMEM_SPEC] * (1 + len(candidates)),
        out_specs=[VMEM_SPEC] * 2,
        scratch_shapes=[pltpu.VMEM((parts, tokens), LOW)],
        compiler_params=pltpu.CompilerParams(vmem_limit_bytes=8 << 20),
        cost_estimate=CHEAP,
        name="noise_pack",
    )(plan, ids, *candidates)


def embed_kernel(base_ref, mine_ref, other_ref, out_ref, total_ref):
    step = pl.program_id(0)
    steps = pl.num_programs(0)
    parts = out_ref.shape[0]
    blocks = total_ref.shape[0] // parts

    def add(gathered_ref):
        count, _, tokens = gathered_ref.shape
        term = None
        for at in range(count):
            split = gathered_ref[at, parts : parts + 16].astype(WIDE)
            ids = (split[0:1] * 256.0 + split[1:2]).astype(jnp.int32) - base_ref[0]
            lane = jnp.bitwise_and(ids, 127)
            hits = lax.broadcasted_iota(jnp.int32, (128, tokens), 0) == lane
            hits = jnp.where(hits, 1.0, 0.0).astype(LOW)
            own = jnp.right_shift(ids, 7)
            grads = gathered_ref[at, :parts]
            masked = jnp.concatenate(
                [grads * jnp.where(own == block, 1.0, 0.0).astype(LOW) for block in range(blocks)]
            )
            part = matmul_nt(masked, hits)
            term = part if term is None else term + part

        @pl.when(step == 0)
        def _():
            total_ref[...] = term

        @pl.when(step > 0)
        def _():
            total_ref[...] += term

    pl.when(step < steps // 2)(lambda: add(mine_ref))
    pl.when(step >= steps // 2)(lambda: add(other_ref))

    @pl.when(step == steps - 1)
    def _():
        rows = out_ref.shape[1]
        for block in range(blocks):
            size = min(128, rows - block * 128)
            out_ref[:, block * 128 : block * 128 + size] = total_ref[
                block * parts : (block + 1) * parts, :size
            ]


def embed_sum(base, mine, other, parts, rows):
    count, deep, tokens = mine.shape
    step = 4
    half = count // step
    blocks = -(-rows // 128)
    return pl.pallas_call(
        embed_kernel,
        out_shape=jax.ShapeDtypeStruct((parts, rows), WIDE),
        grid=(2 * half,),
        in_specs=[
            SMEM_SPEC,
            pl.BlockSpec((step, deep, tokens), lambda i: (jnp.minimum(i, half - 1), 0, 0)),
            pl.BlockSpec((step, deep, tokens), lambda i: (jnp.maximum(i - half, 0), 0, 0)),
        ],
        out_specs=pl.BlockSpec((parts, rows), lambda i: (0, 0)),
        scratch_shapes=[pltpu.VMEM((blocks * parts, 128), WIDE)],
        compiler_params=pltpu.CompilerParams(vmem_limit_bytes=32 << 20),
        cost_estimate=CHEAP,
        name="embed_sum",
    )(base, mine, other)


def empty(*kinds):
    return pl.pallas_call(
        lambda *refs: None,
        out_shape=[pltpu.HBM(shape, dtype) for shape, dtype in kinds],
        out_specs=[HBM_SPEC] * len(kinds),
        compiler_params=pltpu.CompilerParams(vmem_limit_bytes=1 << 20),
        name="empty",
    )()


ROW_LEN = 128
SEC, GRP, NX, NY = 4, 2, 4, 4
ALL = ("section", "group", "row")
TURNS = (1, 3, 2)


def route(value, target_of):
    number = lambda s, g, x, y: (s * GRP + g) * NX * NY + x * NY + y
    pairs = []
    for at in itertools.product(range(SEC), range(GRP), range(NX), range(NY)):
        target = target_of(*at)
        if target is not None:
            pairs.append((number(*at), number(*target)))
    return lax.ppermute(value, ALL, pairs)


def link(value, source, target):
    return route(value, lambda s, g, x, y: (target, g, x, y) if s == source else None)


def turn(value, by):
    return route(value, lambda s, g, x, y: ((s + by) % SEC, g, x, y))


def swap_cores(value, sections=range(SEC)):
    return route(value, lambda s, g, x, y: (s, 1 - g, x, y) if s in sections else None)


def plane_route(value, by, first, sections=range(SEC)):
    def target_of(s, g, x, y):
        if s not in sections:
            return None
        if (g == 0) == first:
            return (s, g, (x + by) % NX, y)
        return (s, g, x, (y + by) % NY)

    return route(value, target_of)


def after(value, earlier):
    return lax.optimization_barrier((value, earlier))[0]


def row_block(values, block, count):
    size = values.shape[0] // count
    return lax.dynamic_slice_in_dim(values, block * size, size, 0)


def plane_first(mine, sections=range(SEC)):
    return [mine[0]] + [plane_route(mine[by], by, True, sections) for by in TURNS]


def plane_sum(pieces):
    total = pieces[0].astype(WIDE)
    for piece in pieces[1:]:
        total = total + piece.astype(WIDE)
    return total.astype(LOW)


def plane_second(pieces, second, sections=range(SEC)):
    total = plane_sum(pieces)
    return [row_block(total, second, 4)] + [
        plane_route(row_block(total, (second + by) % 4, 4), by, False, sections) for by in TURNS
    ]


def group_exchange(values, first):
    number = lambda s, g, x, y: (s * GRP + g) * NX * NY + x * NY + y
    groups = []
    for s in range(SEC):
        for g in range(GRP):
            along_x = (g == 0) == first
            for at in range(4):
                groups.append(
                    [number(s, g, i, at) if along_x else number(s, g, at, i) for i in range(4)]
                )
    return lax.all_to_all(values, ALL, 0, 0, axis_index_groups=groups, tiled=True)


def section_exchange(values):
    return lax.all_to_all(values, "section", 0, 0, tiled=True)


def plans(micro, vocab_part):
    last = SEC - 1
    steps = micro + 2 * last
    table = np.zeros((SEC, 6 * steps + 2), np.int32)
    for s in range(SEC):
        for way in range(2):
            depth = s if way == 0 else last - s
            for step in range(steps):
                at = step - 2 * depth
                if 0 <= at < micro:
                    sources = ([0] if step < micro else []) + [
                        d + 1 for d in range(last) if 0 <= step - 2 - 2 * d < micro
                    ]
                    spot = 3 * (way * steps + step)
                    table[s, spot : spot + 3] = (1 + s % 2, at, sources.index(depth))
        table[s, 6 * steps :] = (s * vocab_part, s)
    return table


def local(
    token_ids,
    segment_ids,
    noise_input,
    embed_table,
    input_proj,
    norm_gain,
    lead_weight,
    down_weight,
    final_gain,
    readout_proj,
    head_table,
):
    section = lax.axis_index("section")
    core = lax.axis_index("group")
    row = lax.axis_index("row")
    x_at, y_at = row // NY, row % NY
    first_at = jnp.where(core == 0, x_at, y_at)
    micro, _, tokens = token_ids.shape
    width = input_proj.shape[1]
    hidden = lead_weight.shape[2]
    half_rows = down_weight.shape[1]
    emb_part = input_proj.shape[0]
    vocab_part, emb = head_table.shape
    vocab = embed_table.shape[0]
    all_tokens = micro * tokens
    last = SEC - 1
    gain_half = norm_gain.astype(WIDE)
    lead = lead_weight[0]
    own_down = down_weight[0]
    seg_row = segment_ids
    flat_ids = token_ids.reshape(-1)

    plan = plans(micro, vocab_part)
    steps = micro + 2 * last
    table = lax.dynamic_index_in_dim(jnp.asarray(plan), section, 0, False)
    flat_ids = after(flat_ids, table)
    where_start = jnp.stack((first_at, core)).astype(jnp.int32)
    to_first = lambda v: [v] + [link(v, s, 0) for s in range(1, SEC)]
    eighth = row_block(row_block(own_down, core, 2), first_at, 4)
    eighth = jnp.where(section == 1, link(eighth, 0, 1), link(eighth, 2, 3))
    noise = noise_input[:, 0].transpose(2, 0, 1).reshape(emb_part, -1)
    own_embedded = lookup(flat_ids[None], embed_table.T, noise, 3200)
    parts = to_first(jnp.concatenate((own_embedded, input_proj), axis=1))
    embedded = jnp.concatenate([part[:, :all_tokens] for part in parts])
    input_full = jnp.concatenate([part[:, all_tokens:] for part in parts])
    first_in = matmul_tn(embedded, input_full).astype(LOW).reshape(micro, tokens, width)
    odd = (1, 3)
    eighth = after(eighth, first_in)
    eighths = [eighth] + [plane_route(eighth, by, True, odd) for by in (1, 2, 3)]
    upper = upper_half(where_start, [after(part, first_in) for part in eighths])
    held_down = hold_down(where_start, upper, swap_cores(upper, odd), own_down)

    kept = empty(
        ((micro, tokens, width), LOW),
        ((micro, tokens, width), LOW),
        ((micro, tokens, hidden), LOW),
        ((micro, tokens, hidden), WIDE),
    )

    def sources(first, step, hops, order):
        arrived = [hops[step - 2, s] for s in order if (step - 2, s) in hops]
        return ([first[step]] if step < micro else []) + arrived

    outs, hops = [], {}
    for step in range(steps):
        out, *kept = forward_stage(
            3 * step,
            table,
            sources(first_in, step, hops, range(SEC)),
            seg_row,
            gain_half,
            held_lead if step > 0 else lead,
            held_down if step > 1 else None,
            kept,
            step == 0,
        )
        if step == 0:
            held_lead = kept.pop()
        outs.append(out)
        for s in range(last):
            if 0 <= step - 2 * s < micro:
                ready = after(out, hops[step - 1, s]) if (step - 1, s) in hops else out
                hops[step, s] = link(ready, s, s + 1)
        if step == 2:
            readout_own = after(readout_proj.T, out)
            readout_full = jnp.concatenate(
                [link(readout_own, s, last) for s in range(last)] + [readout_own]
            )
    entries, normeds, saved, inner = kept

    final_rows = jnp.concatenate(outs[2 * last :]).astype(WIDE)
    normed_f, factor_f = layer_norm(final_rows)
    gain_f = final_gain.astype(WIDE)
    final_low = (normed_f * gain_f).astype(LOW)
    readout = matmul_nt(final_low, readout_full).astype(LOW)
    sent = [link(readout, last, s) for s in range(last)]
    readout, peak, total = head_stats(6 * steps + 1, table, sent + [readout], head_table, 2000)
    stats = jnp.concatenate((peak, total))
    all_stats = section_exchange(jnp.tile(stats, (SEC, 1))).reshape(SEC, 2, all_tokens)
    peak = jnp.max(all_stats[:, 0], axis=0)
    total = jnp.sum(all_stats[:, 1] * jnp.exp(all_stats[:, 0] - peak), axis=0)
    logsum = (peak + jnp.log(total))[None]
    head_grad, grad_readout = head_grads(
        6 * steps, table, readout, head_table, logsum, flat_ids[None]
    )
    grad_low = grad_readout.astype(LOW)
    for s in range(last):
        grad_readout = grad_readout + link(grad_low, s, last).astype(WIDE)
    grad_readout = grad_readout.astype(LOW)
    head_grad = lax.psum_scatter(head_grad, "row", scatter_dimension=0)
    readout_grad = matmul_tn(final_low, grad_readout)
    grad_final = matmul(grad_readout, readout_full)
    final_gain_grad = jnp.sum(grad_final * normed_f, axis=0)
    last_grads = norm_back(grad_final * gain_f, normed_f, factor_f).astype(LOW)
    last_grads = last_grads.reshape(micro, tokens, width)

    lead_turned = turned(6 * steps + 1, table, after(lead, grad_low), 0)
    down_turned = turned(6 * steps + 1, table, after(held_down, grad_low), 1)
    totals = empty(
        ((micro, tokens, width), LOW),
        ((micro, tokens, hidden), LOW),
        ((micro, 8, width), WIDE),
    )
    outs, hops = [], {}
    for step in range(steps):
        out, *totals = backward_stage(
            3 * (steps + step),
            table,
            sources(last_grads, step, hops, range(SEC - 1, -1, -1)),
            seg_row,
            gain_half,
            lead_turned,
            down_turned,
            entries,
            saved,
            inner,
            totals,
        )
        outs.append(out)
        for s in range(1, SEC):
            if 0 <= step - 2 * (last - s) < micro:
                ready = after(out, hops[step - 1, s]) if (step - 1, s) in hops else out
                hops[step, s] = link(ready, s, s - 1)
    section, core, row, readout_grad, final_gain_grad = lax.optimization_barrier(
        (section, core, row, readout_grad, final_gain_grad, out)
    )[:5]
    x_at, y_at = row // NY, row % NY
    first_at, second_at = jnp.where(core == 0, x_at, y_at), jnp.where(core == 0, y_at, x_at)
    is_mlp = section % 2 == 1

    first_grads = jnp.concatenate(outs[2 * last :])
    noise_grad = matmul_nt(input_full, first_grads).astype(LOW)
    pieces = noise_grad.reshape(SEC, emb_part, all_tokens)
    sent = [link(pieces[s], 0, s) for s in range(1, SEC)]

    grad_nexts, grads, gain_grads = totals
    flat = lambda v: v.reshape(all_tokens, v.shape[-1])
    grads = after(grads, head_grad)
    normed, grad_nexts, grads, saved = flat(normeds), flat(grad_nexts), flat(grads), flat(saved)
    role = jnp.where(is_mlp, 2, 1)
    where_other = jnp.stack((role, 1 - core, second_at)).astype(jnp.int32)
    where_mine = jnp.stack((role, core, first_at)).astype(jnp.int32)
    both = lambda mine, other: jnp.where(
        core == 0,
        jnp.concatenate((mine, other), axis=1),
        jnp.concatenate((other, mine), axis=1),
    )
    down_got = swap_cores(down_grad(where_other, saved, grad_nexts)[0], odd)
    lead_other = lead_grad(where_other, normed, saved, grads)[0]
    lead_got = swap_cores(lead_other)
    down_mine = down_grad(after(where_mine, lead_other), saved, grad_nexts, down_got)
    down_first = plane_first(down_mine, odd)
    late_ids = after(flat_ids, down_mine)[None]
    packed, noise_wide = noise_pack(6 * steps + 1, table, late_ids, [pieces[0]] + sent)

    lead_mine = lead_grad(after(where_mine, packed), normed, saved, grads, lead_got)
    lead_first = plane_first(lead_mine)
    first_grads, gain_grads, readout_grad, final_gain_grad = after(
        (first_grads, gain_grads, readout_grad, final_gain_grad), lead_mine
    )
    gain_grad = jnp.sum(gain_grads[:, 0], axis=0)
    input_grad = matmul(embedded, first_grads).reshape(SEC, 16, 4, width)
    input_grad = input_grad.transpose(1, 0, 2, 3).reshape(16, 16, width)
    readout_grad = readout_grad.reshape(16, 16, width)
    vectors = jnp.concatenate(
        (
            gain_grad.reshape(16, 64),
            final_gain_grad.reshape(SEC, 16, 16).transpose(1, 0, 2).reshape(16, 64),
            jnp.zeros((16, width - 128), WIDE),
        ),
        axis=1,
    )
    small = jnp.concatenate(
        (
            jnp.where(section == 0, input_grad, readout_grad),
            vectors[:, None],
            jnp.zeros((16, 15, width), WIDE),
        ),
        axis=1,
    ).astype(LOW)
    half_of = lambda which: lax.dynamic_slice_in_dim(small, which * (width // 2), width // 2, 2)
    small = half_of(core).astype(WIDE) + swap_cores(half_of(1 - core)).astype(WIDE)
    small = small.astype(LOW).reshape(NX, NY, 32, width // 2)
    small = jnp.where(core == 0, small, small.swapaxes(0, 1)).reshape(4, NY * 32, width // 2)
    deep = emb_part + 16

    def exchange(blocks, packed, first):
        rows = blocks.shape[1]
        everywhere = jnp.broadcast_to(packed, (4,) + packed.shape)
        got = group_exchange(jnp.concatenate((blocks, everywhere), axis=1), first)
        return jnp.sum(got[:, :rows].astype(WIDE), axis=0).astype(LOW), got[:, rows:]

    packed = after(packed, lead_mine)
    down_first = after(down_first, lead_mine)
    small, packed = exchange(after(small, down_first), packed, True)
    small, packed = exchange(
        small.reshape(4, 32, width // 2), packed.reshape(4 * deep, all_tokens), False
    )
    packed = packed.reshape(16, deep, all_tokens)
    down_second = plane_second(after(down_first, packed), second_at, odd)
    lead_second = plane_second(after(lead_first, packed), second_at)
    packed_other = swap_cores(packed)
    small = both(small, swap_cores(small))
    embed_grad = embed_sum(
        (row * (vocab // 16)).reshape(1), packed, packed_other, emb_part, vocab // 16
    )
    down_part = plane_sum(after(down_second, embed_grad))
    lead_part = plane_sum(after(lead_second, embed_grad))
    noise_out = noise_wide.reshape(emb_part, micro, tokens).transpose(1, 2, 0)
    lead_out = both(lead_part, swap_cores(lead_part)).astype(WIDE)

    def first_target(s, g, x, y):
        if s % 2 == 0:
            return None
        return (s - 1, 0, x, y) if g == 0 else (s, 0, x, y)

    def second_target(s, g, x, y):
        return (s - 1, 1, x, y) if s % 2 == 1 and g == 0 else None

    to_core_0 = route(down_part, first_target)
    to_core_1 = route(down_part, second_target)
    down_out = jnp.where(
        core == 0, to_core_0, jnp.where(is_mlp, down_part, to_core_1)
    ).astype(WIDE)

    small = after(small, (lead_part, down_part))
    gain_out = small[16, :64].astype(WIDE)
    input_rows = small[:16].reshape(SEC, 4, width)
    readout_rows = small[:16].reshape(64, SEC, 64)
    final_rows = small[16, 64:128].reshape(SEC, 16)

    finals = jnp.pad(final_rows, ((0, 0), (0, width - 16)))[:, None]
    mine = jnp.where(
        section == 0, input_rows, readout_rows.transpose(1, 0, 2).reshape(SEC, 4, width)
    )
    shared = section_exchange(
        jnp.concatenate((mine, finals, jnp.zeros((SEC, 3, width), LOW)), axis=1)
    )
    input_out = shared[0, :4]
    readout_out = shared[last, :4].reshape(64, 64)
    final_out = shared[last, 4, :16]

    head_out = pair_sum(head_grad, swap_cores(head_grad), vocab_part // (NX * NY))
    return (
        noise_out[:, None],
        embed_grad.T,
        input_out.astype(WIDE),
        gain_out[None],
        lead_out[None],
        down_out[None],
        final_out.astype(WIDE),
        readout_out.astype(WIDE),
        head_out,
    )


def solution(mesh):
    in_specs = (
        P(None, ("group", "row"), None),
        P(None, ("group", "row"), None),
        P(None, ("group", "row"), None, "section"),
        P(None, "section"),
        P("section", None),
        P("section", None),
        P("section", None, None),
        P("section", None, None),
        P(),
        P(None, "section"),
        P("section", None),
    )
    out_specs = (
        P(None, ("group", "row"), None, "section"),
        P("row", "section"),
        P(("section", "row"), None),
        P("section", "row"),
        P("section", "row", None),
        P("section", "row", None),
        P(("section", "row")),
        P("row", "section"),
        P(("section", "row"), None),
    )
    return jax.shard_map(local, mesh=mesh, in_specs=in_specs, out_specs=out_specs, check_vma=False)
```

```python
import functools
import itertools

import jax
import jax.numpy as jnp
import numpy as np
from jax import lax
from jax.experimental import pallas as pl
from jax.experimental.pallas import tpu as pltpu
from jax.sharding import PartitionSpec as P

HEADS = 16
HEAD_SIZE = 64
LOW = jnp.bfloat16
WIDE = jnp.float32
EPSILON = 1e-05
MASKED = -1000000000.0
CHUNK = 1024
GELU_A = 0.7978845608028654
GELU_B = 0.044715
HBM_SPEC = pl.BlockSpec(memory_space=pltpu.HBM)
VMEM_SPEC = pl.BlockSpec(memory_space=pltpu.VMEM)
SMEM_SPEC = pl.BlockSpec(memory_space=pltpu.SMEM)


def matmul(former, latter):
    return jnp.dot(former, latter, preferred_element_type=WIDE)


def matmul_nt(former, latter):
    return lax.dot_general(
        former, latter, (((1,), (1,)), ((), ())), preferred_element_type=WIDE
    )


def matmul_tn(former, latter):
    return lax.dot_general(
        former, latter, (((0,), (0,)), ((), ())), preferred_element_type=WIDE
    )


def layer_norm(values):
    centre = jnp.mean(values, axis=-1, keepdims=True)
    centred = values - centre
    variance = jnp.mean(centred * centred, axis=-1, keepdims=True)
    factor = lax.rsqrt(variance + EPSILON)
    return (centred * factor, factor)


def norm_back(grad_normed, normed, factor):
    first_mean = jnp.mean(grad_normed, axis=-1, keepdims=True)
    second_mean = jnp.mean(grad_normed * normed, axis=-1, keepdims=True)
    return factor * (grad_normed - first_mean - normed * second_mean)


def gelu(v):
    return 0.5 * v * (1.0 + jnp.tanh(GELU_A * (v + GELU_B * (v * v * v))))


def gelu_slope(v):
    square = v * v
    bend = jnp.tanh(GELU_A * (v + GELU_B * (square * v)))
    return 0.5 * (1.0 + bend) + 0.5 * v * (1.0 - bend * bend) * (
        GELU_A * (1.0 + 3.0 * GELU_B * square)
    )


def head_probs(scores, same):
    scores = jnp.where(same, scores * HEAD_SIZE ** (-0.5), MASKED)
    expo = jnp.exp(scores - jnp.max(scores, axis=-1, keepdims=True))
    return expo * (1.0 / jnp.sum(expo, axis=-1, keepdims=True))


def same_segment(row):
    across = jnp.broadcast_to(row.astype(WIDE), (row.shape[1], row.shape[1]))
    return across.T == across


def lanes(at, size):
    return pl.ds(pl.multiple_of(at, 128), size)


def turn_kernel(spot, live, plan_ref, value_ref, out_ref):
    @pl.when(jnp.bitwise_and(plan_ref[spot], 1) >= live)
    def _():
        out_ref[...] = value_ref[...].T


def turned(spot, plan, value, live):
    rows, columns = value.shape
    if rows > columns:
        tile = rows // 8
        blocks = (pl.BlockSpec((tile, columns), lambda i: (i, 0)), pl.BlockSpec((columns, tile), lambda i: (0, i)))
    else:
        tile = columns // 8
        blocks = (pl.BlockSpec((rows, tile), lambda i: (0, i)), pl.BlockSpec((tile, rows), lambda i: (i, 0)))
    return pl.pallas_call(
        functools.partial(turn_kernel, spot, live),
        out_shape=pltpu.VMEM((columns, rows), LOW),
        grid=(8,),
        in_specs=[SMEM_SPEC, blocks[0]],
        out_specs=blocks[1],
        compiler_params=pltpu.CompilerParams(vmem_limit_bytes=12 << 20),
        cost_estimate=pl.CostEstimate(flops=0, bytes_accessed=1024, transcendentals=0),
        name="turned",
    )(plan, far(value))


def chosen(choice, candidates, buffer):
    for at, candidate in enumerate(candidates):

        @pl.when(choice == at)
        def _():
            buffer[...] = candidate[...]


def forward_kernel(spot, with_down, loads, count, *refs):
    table_ref, candidates, refs = refs[0], refs[1 : 1 + count], refs[1 + count :]
    if not with_down:
        refs = refs[:3] + (None,) + refs[3:]
    source_ref = load_sems = None
    if loads:
        source_ref, load_sems = refs[2], refs[-1]
        refs = refs[:2] + (refs[13],) + refs[3:13] + refs[14:-1]
    forward_body(spot, table_ref, candidates, source_ref, load_sems, *refs)


def forward_body(
    spot,
    table_ref,
    candidates,
    source_ref,
    load_sems,
    seg_row_ref,
    gain_ref,
    lead_ref,
    down_ref,
    entries_in,
    normeds_in,
    saved_in,
    inner_in,
    out_ref,
    entries_ref,
    normeds_ref,
    saved_ref,
    inner_ref,
    normed_buf,
    saved_buf,
    inner_buf,
    result_buf,
    scores_buf,
    probs_buf,
    entry_ref,
    out_sems,
):
    role, slot = table_ref[spot], table_ref[spot + 1]
    tokens, width = entry_ref.shape
    keeps = [
        pltpu.make_async_copy(entry_ref, entries_ref.at[slot], out_sems.at[0]),
        pltpu.make_async_copy(normed_buf, normeds_ref.at[slot], out_sems.at[1]),
        pltpu.make_async_copy(saved_buf, saved_ref.at[slot], out_sems.at[2]),
    ]
    keep_inner = pltpu.make_async_copy(inner_buf, inner_ref.at[slot], out_sems.at[3])

    def load(j):
        at = lanes(j * CHUNK, CHUNK)
        return pltpu.make_async_copy(source_ref.at[:, at], lead_ref.at[:, at], load_sems.at[j])

    def loaded(j):
        if source_ref is not None:
            load(j).wait()

    if source_ref is not None:
        for j in range(lead_ref.shape[1] // CHUNK):
            load(j).start()

        @pl.when(role != 1)
        def _():
            pl.loop(0, lead_ref.shape[1] // CHUNK)(loaded)

    @pl.when(role > 0)
    def _():
        chosen(table_ref[spot + 2], candidates, entry_ref)
        normed, _ = layer_norm(entry_ref[...].astype(WIDE))
        normed_buf[...] = (normed * gain_ref[...]).astype(LOW)
        keeps[0].start()
        keeps[1].start()

    @pl.when(role == 1)
    def _():
        @pl.loop(0, 3 * width // CHUNK, unroll=2)
        def _(j):
            at = lanes(j * CHUNK, CHUNK)
            loaded(j)
            saved_buf[:, at] = matmul(normed_buf[...], lead_ref[:, at]).astype(LOW)

        left = lax.broadcasted_iota(jnp.int32, (tokens, 128), 1) < HEAD_SIZE
        zero = jnp.zeros((tokens, 128), LOW)

        @pl.loop(0, HEADS // 8)
        def _(group):
            for pair in range(4):
                at = group * 512 + pair * 128
                query = saved_buf[:, lanes(at, 128)]
                key = saved_buf[:, lanes(width + at, 128)]
                scores_buf[group * 8 + 2 * pair] = matmul_nt(jnp.where(left, query, zero), key)
                scores_buf[group * 8 + 2 * pair + 1] = matmul_nt(jnp.where(left, zero, query), key)

        @pl.loop(0, HEADS // 4)
        def _(group):
            same = same_segment(seg_row_ref[slot])
            for head in range(4):
                at = group * 4 + head
                probs_buf[at] = head_probs(scores_buf[at], same).astype(LOW)

        @pl.loop(0, HEADS // 8)
        def _(group):
            for pair in range(4):
                at = group * 512 + pair * 128
                value = saved_buf[:, lanes(2 * width + at, 128)]
                mixed = jnp.where(
                    left,
                    matmul(probs_buf[group * 8 + 2 * pair], value),
                    matmul(probs_buf[group * 8 + 2 * pair + 1], value),
                )
                saved_buf[:, lanes(3 * width + at, 128)] = mixed.astype(LOW)

        keeps[2].start()

        @pl.loop(0, width // CHUNK)
        def _(j):
            at = lanes(j * CHUNK, CHUNK)
            loaded(3 * width // CHUNK + j)
            term = matmul(saved_buf[:, 3 * width :], lead_ref[:, lanes(3 * width + j * CHUNK, CHUNK)])
            out_ref[:, at] = (entry_ref[:, at].astype(WIDE) + term).astype(LOW)

    def feed_forward():
        result_buf[...] = entry_ref[...].astype(WIDE)

        @pl.loop(0, lead_ref.shape[1] // CHUNK, unroll=2)
        def _(j):
            at = lanes(j * CHUNK, CHUNK)
            inner = matmul(normed_buf[...], lead_ref[:, at])
            inner_buf[:, at] = inner
            active = gelu(inner).astype(LOW)
            saved_buf[:, at] = active
            result_buf[...] += matmul(active, down_ref[pl.ds(j * CHUNK, CHUNK), :])

        keeps[2].start()
        keep_inner.start()
        out_ref[...] = result_buf[...].astype(LOW)
        keep_inner.wait()

    if down_ref is not None:
        pl.when(role == 2)(feed_forward)

    @pl.when(role > 0)
    def _():
        for keep in keeps:
            keep.wait()


def pinned(value):
    return pltpu.with_memory_space_constraint(value, pltpu.VMEM)


def far(value):
    return pltpu.with_memory_space_constraint(value, pltpu.HBM)


def forward_stage(spot, table, entries, seg_row, gain, lead, down, kept, loads=False):
    tokens, width = entries[0].shape
    hidden = lead.shape[1]
    count = len(entries) + (3 if down is None else 4)
    given = [VMEM_SPEC] * (len(entries) + 2) + [HBM_SPEC if loads else VMEM_SPEC]
    return pl.pallas_call(
        functools.partial(forward_kernel, spot, down is not None, loads, len(entries)),
        out_shape=[jax.ShapeDtypeStruct((tokens, width), LOW)]
        + [jax.ShapeDtypeStruct(k.shape, k.dtype) for k in kept]
        + ([pltpu.VMEM(lead.shape, LOW)] if loads else []),
        in_specs=[SMEM_SPEC] + given + [VMEM_SPEC] * (down is not None) + [HBM_SPEC] * 4,
        out_specs=[VMEM_SPEC] + [HBM_SPEC] * 4 + [VMEM_SPEC] * loads,
        scratch_shapes=[
            pltpu.VMEM((tokens, width), LOW),
            pltpu.VMEM((tokens, hidden), LOW),
            pltpu.VMEM((tokens, hidden), WIDE),
            pltpu.VMEM((tokens, width), WIDE),
            pltpu.VMEM((HEADS, tokens, tokens), WIDE),
            pltpu.VMEM((HEADS, tokens, tokens), LOW),
            pltpu.VMEM((tokens, width), LOW),
            pltpu.SemaphoreType.DMA((4,)),
        ]
        + ([pltpu.SemaphoreType.DMA((hidden // CHUNK,))] if loads else []),
        input_output_aliases={count + 1 + i: 1 + i for i in range(4)},
        compiler_params=pltpu.CompilerParams(vmem_limit_bytes=18 << 20),
        cost_estimate=pl.CostEstimate(
            flops=4 * tokens * width * hidden, bytes_accessed=20 << 20, transcendentals=0
        ),
        name="forward_stage",
    )(
        table,
        *entries,
        seg_row,
        gain,
        (far if loads else pinned)(lead),
        *([pinned(down)] if down is not None else []),
        *map(far, kept),
    )


def backward_kernel(spot, count, *refs):
    backward_body(spot, refs[0], refs[1 : 1 + count], *refs[1 + count :])


def backward_body(
    spot,
    table_ref,
    candidates,
    seg_row_ref,
    gain_ref,
    lead_ref,
    down_ref,
    entries_ref,
    saved_ref,
    inner_ref,
    nexts_in,
    grads_in,
    gains_in,
    out_ref,
    nexts_ref,
    grads_ref,
    gains_ref,
    saved_buf,
    inner_buf,
    grads_buf,
    mixed_buf,
    gain_buf,
    entry_buf,
    normed_buf,
    scores_buf,
    probs_grad_buf,
    probs_buf,
    scores_grad_buf,
    grad_ref,
    in_sems,
    out_sems,
):
    role, slot = table_ref[spot], table_ref[spot + 1]
    tokens, width = grad_ref.shape
    bring_saved = pltpu.make_async_copy(saved_ref.at[slot], saved_buf, in_sems.at[0])
    bring_inner = pltpu.make_async_copy(inner_ref.at[slot], inner_buf, in_sems.at[1])
    bring_entry = pltpu.make_async_copy(entries_ref.at[slot], entry_buf, in_sems.at[2])
    keep_next = pltpu.make_async_copy(grad_ref, nexts_ref.at[slot], out_sems.at[0])
    keep_grads = pltpu.make_async_copy(grads_buf, grads_ref.at[slot], out_sems.at[1])
    keep_gain = pltpu.make_async_copy(gain_buf, gains_ref.at[slot], out_sems.at[2])

    @pl.when(role == 2)
    def _():
        bring_inner.start()

    @pl.when(role == 1)
    def _():
        bring_saved.start()

    @pl.when(role > 0)
    def _():
        bring_entry.start()
        chosen(table_ref[spot + 2], candidates, grad_ref)
        keep_next.start()
        normed_buf[...] = jnp.zeros_like(normed_buf)

    @pl.when(role == 1)
    def _():
        grads_buf[:, 3 * width :] = grad_ref[...]
        mixed_buf[...] = matmul(grad_ref[...], lead_ref[3 * width :, :]).astype(LOW)
        bring_saved.wait()
        left = lax.broadcasted_iota(jnp.int32, (tokens, 128), 1) < HEAD_SIZE
        zero = jnp.zeros((tokens, 128), LOW)
        scale = HEAD_SIZE ** (-0.5)

        @pl.loop(0, HEADS // 8)
        def _(group):
            for pair in range(4):
                at = group * 512 + pair * 128
                query = saved_buf[:, lanes(at, 128)]
                key = saved_buf[:, lanes(width + at, 128)]
                value = saved_buf[:, lanes(2 * width + at, 128)]
                grad = mixed_buf[:, lanes(at, 128)]
                for own in (0, 1):
                    mine = lambda v: jnp.where(left, v, zero) if own == 0 else jnp.where(left, zero, v)
                    scores_buf[group * 8 + 2 * pair + own] = matmul_nt(mine(query), key)
                    probs_grad_buf[group * 8 + 2 * pair + own] = matmul_nt(mine(grad), value)

        @pl.loop(0, HEADS // 4)
        def _(group):
            same = same_segment(seg_row_ref[slot])
            for head in range(4):
                at = group * 4 + head
                probs = head_probs(scores_buf[at], same)
                probs_buf[at] = probs.astype(LOW)
                grad_probs = probs_grad_buf[at]
                scores_grad_buf[at] = (
                    probs * (grad_probs - jnp.sum(probs * grad_probs, axis=-1, keepdims=True))
                ).astype(LOW)

        @pl.loop(0, HEADS // 4)
        def _(group):
            for pair in range(2):
                at = group * 256 + pair * 128
                query = saved_buf[:, lanes(at, 128)]
                key = saved_buf[:, lanes(width + at, 128)]
                grad = mixed_buf[:, lanes(at, 128)]
                parts = []
                for own in (0, 1):
                    probs = probs_buf[group * 4 + 2 * pair + own]
                    grad_low = scores_grad_buf[group * 4 + 2 * pair + own]
                    parts.append(
                        (
                            matmul(grad_low, key) * scale,
                            matmul_tn(grad_low, query) * scale,
                            matmul_tn(probs, grad),
                        )
                    )
                for which in range(3):
                    grads_buf[:, lanes(which * width + at, 128)] = jnp.where(
                        left, parts[0][which], parts[1][which]
                    ).astype(LOW)

        @pl.loop(0, 3 * width // CHUNK, unroll=2)
        def _(j):
            at = lanes(j * CHUNK, CHUNK)
            normed_buf[...] += matmul(grads_buf[:, at], lead_ref[pl.ds(j * CHUNK, CHUNK), :])

    @pl.when(role == 2)
    def _():
        bring_inner.wait()

        @pl.loop(0, lead_ref.shape[0] // CHUNK, unroll=2)
        def _(j):
            at = lanes(j * CHUNK, CHUNK)
            grad_active = matmul(grad_ref[...], down_ref[:, at])
            grads = (gelu_slope(inner_buf[:, at]) * grad_active).astype(LOW)
            grads_buf[:, at] = grads
            normed_buf[...] += matmul(grads, lead_ref[pl.ds(j * CHUNK, CHUNK), :])

    @pl.when(role > 0)
    def _():
        keep_grads.start()
        bring_entry.wait()
        grad_normed = normed_buf[...]
        normed, factor = layer_norm(entry_buf[...].astype(WIDE))
        gain_buf[...] = jnp.broadcast_to(
            jnp.sum(grad_normed * normed, axis=0, keepdims=True), gain_buf.shape
        )
        keep_gain.start()
        out_ref[...] = (
            grad_ref[...].astype(WIDE) + norm_back(grad_normed * gain_ref[...], normed, factor)
        ).astype(LOW)
        keep_next.wait()
        keep_grads.wait()
        keep_gain.wait()


def backward_stage(
    spot, table, nexts, seg_row, gain, lead, down, entries, saved, inner, totals
):
    tokens, width = nexts[0].shape
    count = len(nexts)
    hidden = lead.shape[0]
    return pl.pallas_call(
        functools.partial(backward_kernel, spot, count),
        out_shape=[jax.ShapeDtypeStruct((tokens, width), LOW)]
        + [jax.ShapeDtypeStruct(k.shape, k.dtype) for k in totals],
        in_specs=[SMEM_SPEC] + [VMEM_SPEC] * (count + 4) + [HBM_SPEC] * 6,
        out_specs=[VMEM_SPEC] + [HBM_SPEC] * 3,
        scratch_shapes=[
            pltpu.VMEM((tokens, hidden), LOW),
            pltpu.VMEM((tokens, hidden), WIDE),
            pltpu.VMEM((tokens, hidden), LOW),
            pltpu.VMEM((tokens, width), LOW),
            pltpu.VMEM((8, width), WIDE),
            pltpu.VMEM((tokens, width), LOW),
            pltpu.VMEM((tokens, width), WIDE),
            pltpu.VMEM((HEADS, tokens, tokens), WIDE),
            pltpu.VMEM((HEADS, tokens, tokens), WIDE),
            pltpu.VMEM((HEADS, tokens, tokens), LOW),
            pltpu.VMEM((HEADS, tokens, tokens), LOW),
            pltpu.VMEM((tokens, width), LOW),
            pltpu.SemaphoreType.DMA((3,)),
            pltpu.SemaphoreType.DMA((3,)),
        ],
        input_output_aliases={count + 8 + i: 1 + i for i in range(3)},
        compiler_params=pltpu.CompilerParams(vmem_limit_bytes=18 << 20),
        cost_estimate=pl.CostEstimate(
            flops=4 * tokens * width * hidden, bytes_accessed=20 << 20, transcendentals=0
        ),
        name="backward_stage",
    )(
        table,
        *nexts,
        seg_row,
        gain,
        pinned(lead),
        pinned(down),
        far(entries),
        far(saved),
        far(inner),
        *map(far, totals),
    )


def stats_kernel(spot, plan_ref, *refs):
    candidates, (table_ref, readout_ref, peak_ref, total_ref) = refs[:-4], refs[-4:]
    step = pl.program_id(0)

    @pl.when(step == 0)
    def _():
        chosen(plan_ref[spot], candidates, readout_ref)

    logits = matmul_nt(table_ref[...], readout_ref[...])
    own_peak = jnp.max(logits, axis=0, keepdims=True)
    own_total = lambda peak: jnp.sum(jnp.exp(logits - peak), axis=0, keepdims=True)

    @pl.when(step == 0)
    def _():
        peak_ref[...] = own_peak
        total_ref[...] = own_total(own_peak)

    @pl.when(step > 0)
    def _():
        peak = jnp.maximum(peak_ref[...], own_peak)
        total_ref[...] = total_ref[...] * jnp.exp(peak_ref[...] - peak) + own_total(peak)
        peak_ref[...] = peak


def head_stats(spot, plan, readouts, table, tile):
    tokens, emb = readouts[0].shape
    vocab = table.shape[0]
    whole = pl.BlockSpec((1, tokens), lambda i: (0, 0))
    rows = pl.BlockSpec((tokens, emb), lambda i: (0, 0))
    return pl.pallas_call(
        functools.partial(stats_kernel, spot),
        out_shape=[jax.ShapeDtypeStruct((tokens, emb), LOW)]
        + [jax.ShapeDtypeStruct((1, tokens), WIDE)] * 2,
        grid=(vocab // tile,),
        in_specs=[SMEM_SPEC]
        + [rows] * len(readouts)
        + [pl.BlockSpec((tile, emb), lambda i: (i, 0))],
        out_specs=[rows, whole, whole],
        compiler_params=pltpu.CompilerParams(vmem_limit_bytes=32 << 20),
        cost_estimate=pl.CostEstimate(
            flops=2 * tokens * vocab * emb, bytes_accessed=5 << 20, transcendentals=tokens * vocab
        ),
        name="head_stats",
    )(plan, *readouts, far(table))


def head_kernel(spot, table_base_ref, readout_ref, table_ref, logsum_ref, ids_ref, head_ref, grad_ref):
    tile = table_ref.shape[0]
    logits = matmul_nt(table_ref[...], readout_ref[...])
    ids = ids_ref[...] - (table_base_ref[spot] + pl.program_id(0) * tile)
    hits = lax.broadcasted_iota(jnp.int32, logits.shape, 0) == ids
    probs = jnp.exp(logits - logsum_ref[...])
    grads = jnp.where(hits, probs - 1.0, probs).astype(LOW)
    head = matmul(grads, readout_ref[...])
    unit = tile // 4
    for shard in range(4):
        head_ref[shard, :unit] = head[shard * unit : (shard + 1) * unit].astype(LOW)
    term = matmul_tn(grads, table_ref[...])

    @pl.when(pl.program_id(0) == 0)
    def _():
        grad_ref[...] = term

    @pl.when(pl.program_id(0) > 0)
    def _():
        grad_ref[...] += term


def head_grads(spot, base, readout, table, logsum, ids):
    tokens, emb = readout.shape
    vocab = table.shape[0]
    row = pl.BlockSpec((1, tokens), lambda i: (0, 0))
    whole = pl.BlockSpec((tokens, emb), lambda i: (0, 0))
    part = pl.BlockSpec((vocab // 4, emb), lambda i: (i, 0))
    return pl.pallas_call(
        functools.partial(head_kernel, spot),
        out_shape=[
            pltpu.HBM((16, 512, emb), LOW),
            jax.ShapeDtypeStruct((tokens, emb), WIDE),
        ],
        grid=(4,),
        in_specs=[SMEM_SPEC, whole, part, row, row],
        out_specs=[pl.BlockSpec((4, 512, emb), lambda i: (i, 0, 0)), whole],
        compiler_params=pltpu.CompilerParams(vmem_limit_bytes=32 << 20),
        cost_estimate=pl.CostEstimate(
            flops=6 * tokens * vocab * emb, bytes_accessed=9 << 20, transcendentals=tokens * vocab
        ),
        name="head_grads",
    )(base, readout, far(table), logsum, ids)


def pair_kernel(former_ref, latter_ref, out_ref):
    rows = out_ref.shape[0]
    out_ref[...] = former_ref[:rows].astype(WIDE) + latter_ref[:rows].astype(WIDE)


def pair_sum(former, latter, rows):
    return pl.pallas_call(
        pair_kernel,
        out_shape=jax.ShapeDtypeStruct((rows, former.shape[1]), WIDE),
        in_specs=[VMEM_SPEC] * 2,
        out_specs=VMEM_SPEC,
        compiler_params=pltpu.CompilerParams(vmem_limit_bytes=8 << 20),
        cost_estimate=pl.CostEstimate(flops=0, bytes_accessed=1024, transcendentals=0),
        name="pair_sum",
    )(former, latter)


def lookup_kernel(ids_ref, table_ref, noise_ref, out_ref, total_ref, low_ref):
    step = pl.program_id(0)
    parts, tile = table_ref.shape
    tokens = ids_ref.shape[1]
    blocks = tile // 128

    @pl.when(step == 0)
    def _():
        lane = jnp.bitwise_and(ids_ref[...], 127)
        hits = lax.broadcasted_iota(jnp.int32, (128, tokens), 0) == lane
        low_ref[...] = jnp.where(hits, 1.0, 0.0).astype(LOW)
        total_ref[...] = noise_ref[...].astype(WIDE)

    stacked = jnp.concatenate(
        [table_ref[:, block * 128 : (block + 1) * 128] for block in range(blocks)]
    )
    found = matmul(stacked, low_ref[...])
    own = jnp.right_shift(ids_ref[...], 7) - step * blocks
    total = jnp.zeros_like(total_ref)
    for block in range(blocks):
        total = jnp.where(own == block, found[block * parts : (block + 1) * parts], total)
    total_ref[...] += total

    @pl.when(step == pl.num_programs(0) - 1)
    def _():
        out_ref[...] = total_ref[...].astype(LOW)


def lookup(ids, table, noise, tile):
    parts, vocab = table.shape
    tokens = ids.shape[1]
    whole = pl.BlockSpec((parts, tokens), lambda i: (0, 0))
    return pl.pallas_call(
        lookup_kernel,
        out_shape=jax.ShapeDtypeStruct((parts, tokens), LOW),
        grid=(vocab // tile,),
        in_specs=[
            pl.BlockSpec((1, tokens), lambda i: (0, 0)),
            pl.BlockSpec((parts, tile), lambda i: (0, i)),
            whole,
        ],
        out_specs=whole,
        scratch_shapes=[pltpu.VMEM((parts, tokens), WIDE), pltpu.VMEM((128, tokens), LOW)],
        compiler_params=pltpu.CompilerParams(vmem_limit_bytes=32 << 20),
        cost_estimate=pl.CostEstimate(
            flops=2 * 128 * vocab * tokens, bytes_accessed=4 << 20, transcendentals=0
        ),
        name="lookup",
    )(ids, far(table), noise)


def lead_grad_kernel(where_ref, normed_ref, mixed_ref, grads_ref, *refs):
    got_ref, out_refs, (turned_ref, result_ref) = None, refs[:-2], refs[-2:]
    if len(out_refs) > 1:
        got_ref, out_refs = out_refs[0], out_refs[1:]
    role, half, spot = where_ref[0], where_ref[1], where_ref[2]
    step = pl.program_id(0)
    width = normed_ref.shape[1]
    steps = pl.num_programs(0)
    use_mixed = jnp.logical_and(role == 1, half == 1)

    @pl.when(step == 0)
    def _():
        turned_ref[...] = normed_ref[...].T

    @pl.when(jnp.logical_and(step == steps // 2, use_mixed))
    def _():
        turned_ref[...] = mixed_ref[...].T

    result_ref[...] = matmul(turned_ref[...], grads_ref[...])
    unit = width // 16

    def put(block, rows, part):
        if got_ref is not None:
            part = part + got_ref[block, rows, :].astype(WIDE)
        out_ref = out_refs[0].at[block] if got_ref is None else out_refs[block]
        out_ref[rows, :] = part.astype(LOW)

    @pl.when(half == 0)
    def _():
        for block in range(4):
            x = (spot + block) % 4
            put(block, slice(None), result_ref[pl.ds(pl.multiple_of(x * 4 * unit, 4 * unit), 4 * unit)])

    @pl.when(half == 1)
    def _():
        for block in range(4):
            y = (spot + block) % 4
            for x in range(4):
                rows = pl.ds(pl.multiple_of((4 * x + y) * unit, unit), unit)
                put(block, slice(x * unit, (x + 1) * unit), result_ref[rows])


CHEAP = pl.CostEstimate(flops=0, bytes_accessed=1024, transcendentals=0)


def lead_grad(where, normed, saved, grads, got=None):
    tokens, width = normed.shape
    tile = 1024
    whole = pl.BlockSpec((4, width // 4, tile), lambda i, where: (0, 0, i))
    block = pl.BlockSpec((width // 4, tile), lambda i, where: (0, i))
    shape = (width // 4, 2 * width)
    return pl.pallas_call(
        lead_grad_kernel,
        out_shape=[jax.ShapeDtypeStruct((4,) + shape, LOW)]
        if got is None
        else [jax.ShapeDtypeStruct(shape, LOW)] * 4,
        grid_spec=pltpu.PrefetchScalarGridSpec(
            num_scalar_prefetch=1,
            grid=(2 * width // tile,),
            in_specs=[
                pl.BlockSpec((tokens, width), lambda i, where: (0, 0)),
                pl.BlockSpec((tokens, width), lambda i, where: (0, 3)),
                pl.BlockSpec((tokens, tile), lambda i, where: (0, where[1] * (2 * width // tile) + i)),
            ]
            + ([] if got is None else [whole]),
            out_specs=[whole] if got is None else [block] * 4,
            scratch_shapes=[pltpu.VMEM((width, tokens), LOW), pltpu.VMEM((width, tile), WIDE)],
        ),
        compiler_params=pltpu.CompilerParams(vmem_limit_bytes=24 << 20),
        cost_estimate=CHEAP
        if got is None
        else pl.CostEstimate(
            flops=4 * tokens * width * width, bytes_accessed=12 << 20, transcendentals=0
        ),
        name="lead_grad",
    )(where, far(normed), far(saved), far(grads), *([] if got is None else [got]))


def down_grad_kernel(where_ref, saved_ref, nexts_ref, *refs):
    got_ref, out_refs, (buf_ref, got_buf, sems) = None, refs[:-3], refs[-3:]
    if len(out_refs) > 1:
        got_ref, out_refs = out_refs[0], out_refs[1:]
    role, half, spot = where_ref[0], where_ref[1], where_ref[2]
    at = pl.program_id(0)
    unit = saved_ref.shape[1] // 4

    @pl.when(role == 2)
    def _():
        if got_ref is not None:
            bring = pltpu.make_async_copy(got_ref, got_buf, sems.at[4])
            pl.when(at == 0)(bring.start)
        result = matmul_tn(saved_ref[...], nexts_ref[...])
        if got_ref is not None:
            pl.when(at == 0)(bring.wait)

        def put(block, rows, part):
            if got_ref is not None:
                part = part + got_buf[block, rows, :].astype(WIDE)
            buf_ref[block, rows, :] = part.astype(LOW)

        @pl.when(half == 0)
        def _():
            put((at - spot + 4) % 4, slice(None), result)

        @pl.when(half == 1)
        def _():
            rows = pl.ds(pl.multiple_of(at * unit, unit), unit)
            for y in range(4):
                put((y - spot + 4) % 4, rows, result[y * unit : (y + 1) * unit])

        @pl.when(at == pl.num_programs(0) - 1)
        def _():
            copies = [pltpu.make_async_copy(buf_ref, out_refs[0], sems.at[0])]
            if got_ref is not None:
                copies = [
                    pltpu.make_async_copy(buf_ref.at[block], out_ref, sems.at[block])
                    for block, out_ref in enumerate(out_refs)
                ]
            for copy in copies:
                copy.start()
            for copy in copies:
                copy.wait()


def down_grad(where, saved, nexts, got=None):
    tokens, hidden = saved.shape
    width = nexts.shape[1]
    rows = hidden // 8
    live = lambda where: jnp.where(where[0] == 2, 1, 0)
    return pl.pallas_call(
        down_grad_kernel,
        out_shape=[pltpu.HBM((4, rows, width), LOW)]
        if got is None
        else [pltpu.HBM((rows, width), LOW)] * 4,
        grid_spec=pltpu.PrefetchScalarGridSpec(
            num_scalar_prefetch=1,
            grid=(4,),
            in_specs=[
                pl.BlockSpec((tokens, rows), lambda i, where: (0, (where[1] * 4 + i) * live(where))),
                pl.BlockSpec((tokens, width), lambda i, where: (0, 0)),
            ]
            + ([] if got is None else [HBM_SPEC]),
            out_specs=[HBM_SPEC] * (1 if got is None else 4),
            scratch_shapes=[
                pltpu.VMEM((4, rows, width), LOW),
                pltpu.VMEM((4, 16, 128) if got is None else (4, rows, width), LOW),
                pltpu.SemaphoreType.DMA((5,)),
            ],
        ),
        compiler_params=pltpu.CompilerParams(vmem_limit_bytes=28 << 20),
        cost_estimate=CHEAP,
        name="down_grad",
    )(where, far(saved), far(nexts), *([] if got is None else [far(got)]))


def upper_kernel(where_ref, *refs):
    out_ref = refs[4]
    rows = refs[0].shape[0]
    for at, part in enumerate(refs[:4]):
        place = (where_ref[0] - at + 4) % 4
        out_ref[pl.ds(pl.multiple_of(place * rows, rows), rows), :] = part[...]


def upper_half(where, parts):
    rows, width = parts[0].shape
    return pl.pallas_call(
        upper_kernel,
        out_shape=jax.ShapeDtypeStruct((4 * rows, width), LOW),
        in_specs=[SMEM_SPEC] + [VMEM_SPEC] * 4,
        out_specs=VMEM_SPEC,
        compiler_params=pltpu.CompilerParams(vmem_limit_bytes=8 << 20),
        name="upper_half",
    )(where, *parts)


def hold_down_kernel(where_ref, mine_ref, other_ref, own_ref, out_ref, sems):
    rows = mine_ref.shape[0]
    core = where_ref[1]
    spot = lambda at: out_ref.at[pl.ds(pl.multiple_of(at * rows, rows), rows), :]
    copies = [
        pltpu.make_async_copy(mine_ref, spot(core), sems.at[0]),
        pltpu.make_async_copy(other_ref, spot(1 - core), sems.at[1]),
        pltpu.make_async_copy(own_ref, out_ref.at[pl.ds(2 * rows, 2 * rows), :], sems.at[2]),
    ]
    for copy in copies:
        copy.start()
    for copy in copies:
        copy.wait()


def hold_down(where, mine, other, own):
    rows, width = mine.shape
    return pl.pallas_call(
        hold_down_kernel,
        out_shape=pltpu.VMEM((4 * rows, width), LOW),
        in_specs=[SMEM_SPEC] + [VMEM_SPEC] * 2 + [HBM_SPEC],
        out_specs=VMEM_SPEC,
        scratch_shapes=[pltpu.SemaphoreType.DMA((3,))],
        compiler_params=pltpu.CompilerParams(vmem_limit_bytes=8 << 20),
        name="hold_down",
    )(where, mine, other, far(own))


def noise_kernel(spot, plan_ref, ids_ref, *refs):
    candidates, (packed_ref, noise_ref, buf_ref) = refs[:-3], refs[-3:]
    parts = noise_ref.shape[0]
    chosen(plan_ref[spot], candidates, buf_ref)
    packed_ref[:parts] = buf_ref[...]
    noise_ref[...] = buf_ref[...].astype(WIDE)
    ids = ids_ref[...]
    high = jnp.right_shift(ids, 8).astype(WIDE)
    low = jnp.bitwise_and(ids, 255).astype(WIDE)
    at = lax.broadcasted_iota(jnp.int32, (16, ids.shape[1]), 0)
    split = jnp.where(at == 0, high, jnp.where(at == 1, low, 0.0))
    packed_ref[parts:] = split.astype(LOW)


def noise_pack(spot, plan, ids, candidates):
    parts, tokens = candidates[0].shape
    return pl.pallas_call(
        functools.partial(noise_kernel, spot),
        out_shape=[
            jax.ShapeDtypeStruct((parts + 16, tokens), LOW),
            jax.ShapeDtypeStruct((parts, tokens), WIDE),
        ],
        in_specs=[SMEM_SPEC] + [VMEM_SPEC] * (1 + len(candidates)),
        out_specs=[VMEM_SPEC] * 2,
        scratch_shapes=[pltpu.VMEM((parts, tokens), LOW)],
        compiler_params=pltpu.CompilerParams(vmem_limit_bytes=8 << 20),
        cost_estimate=CHEAP,
        name="noise_pack",
    )(plan, ids, *candidates)


def embed_kernel(base_ref, mine_ref, other_ref, out_ref, total_ref):
    step = pl.program_id(0)
    steps = pl.num_programs(0)
    parts = out_ref.shape[0]
    blocks = total_ref.shape[0] // parts

    def add(gathered_ref):
        count, _, tokens = gathered_ref.shape
        term = None
        for at in range(count):
            split = gathered_ref[at, parts : parts + 16].astype(WIDE)
            ids = (split[0:1] * 256.0 + split[1:2]).astype(jnp.int32) - base_ref[0]
            lane = jnp.bitwise_and(ids, 127)
            hits = lax.broadcasted_iota(jnp.int32, (128, tokens), 0) == lane
            hits = jnp.where(hits, 1.0, 0.0).astype(LOW)
            own = jnp.right_shift(ids, 7)
            grads = gathered_ref[at, :parts]
            masked = jnp.concatenate(
                [grads * jnp.where(own == block, 1.0, 0.0).astype(LOW) for block in range(blocks)]
            )
            part = matmul_nt(masked, hits)
            term = part if term is None else term + part

        @pl.when(step == 0)
        def _():
            total_ref[...] = term

        @pl.when(step > 0)
        def _():
            total_ref[...] += term

    pl.when(step < steps // 2)(lambda: add(mine_ref))
    pl.when(step >= steps // 2)(lambda: add(other_ref))

    @pl.when(step == steps - 1)
    def _():
        rows = out_ref.shape[1]
        for block in range(blocks):
            size = min(128, rows - block * 128)
            out_ref[:, block * 128 : block * 128 + size] = total_ref[
                block * parts : (block + 1) * parts, :size
            ]


def embed_sum(base, mine, other, parts, rows):
    count, deep, tokens = mine.shape
    step = 4
    half = count // step
    blocks = -(-rows // 128)
    return pl.pallas_call(
        embed_kernel,
        out_shape=jax.ShapeDtypeStruct((parts, rows), WIDE),
        grid=(2 * half,),
        in_specs=[
            SMEM_SPEC,
            pl.BlockSpec((step, deep, tokens), lambda i: (jnp.minimum(i, half - 1), 0, 0)),
            pl.BlockSpec((step, deep, tokens), lambda i: (jnp.maximum(i - half, 0), 0, 0)),
        ],
        out_specs=pl.BlockSpec((parts, rows), lambda i: (0, 0)),
        scratch_shapes=[pltpu.VMEM((blocks * parts, 128), WIDE)],
        compiler_params=pltpu.CompilerParams(vmem_limit_bytes=32 << 20),
        cost_estimate=CHEAP,
        name="embed_sum",
    )(base, mine, other)


def empty(*kinds):
    return pl.pallas_call(
        lambda *refs: None,
        out_shape=[pltpu.HBM(shape, dtype) for shape, dtype in kinds],
        out_specs=[HBM_SPEC] * len(kinds),
        compiler_params=pltpu.CompilerParams(vmem_limit_bytes=1 << 20),
        name="empty",
    )()


ROW_LEN = 128
SEC, GRP, NX, NY = 4, 2, 4, 4
ALL = ("section", "group", "row")
TURNS = (1, 3, 2)


def route(value, target_of):
    number = lambda s, g, x, y: (s * GRP + g) * NX * NY + x * NY + y
    pairs = []
    for at in itertools.product(range(SEC), range(GRP), range(NX), range(NY)):
        target = target_of(*at)
        if target is not None:
            pairs.append((number(*at), number(*target)))
    return lax.ppermute(value, ALL, pairs)


def link(value, source, target):
    return route(value, lambda s, g, x, y: (target, g, x, y) if s == source else None)


def turn(value, by):
    return route(value, lambda s, g, x, y: ((s + by) % SEC, g, x, y))


def swap_cores(value, sections=range(SEC)):
    return route(value, lambda s, g, x, y: (s, 1 - g, x, y) if s in sections else None)


def plane_route(value, by, first, sections=range(SEC)):
    def target_of(s, g, x, y):
        if s not in sections:
            return None
        if (g == 0) == first:
            return (s, g, (x + by) % NX, y)
        return (s, g, x, (y + by) % NY)

    return route(value, target_of)


def after(value, earlier):
    return lax.optimization_barrier((value, earlier))[0]


def row_block(values, block, count):
    size = values.shape[0] // count
    return lax.dynamic_slice_in_dim(values, block * size, size, 0)


def plane_first(mine, sections=range(SEC)):
    return [mine[0]] + [plane_route(mine[by], by, True, sections) for by in TURNS]


def plane_sum(pieces):
    total = pieces[0].astype(WIDE)
    for piece in pieces[1:]:
        total = total + piece.astype(WIDE)
    return total.astype(LOW)


def plane_second(pieces, second, sections=range(SEC)):
    total = plane_sum(pieces)
    return [row_block(total, second, 4)] + [
        plane_route(row_block(total, (second + by) % 4, 4), by, False, sections) for by in TURNS
    ]


def group_exchange(values, first):
    number = lambda s, g, x, y: (s * GRP + g) * NX * NY + x * NY + y
    groups = []
    for s in range(SEC):
        for g in range(GRP):
            along_x = (g == 0) == first
            for at in range(4):
                groups.append(
                    [number(s, g, i, at) if along_x else number(s, g, at, i) for i in range(4)]
                )
    return lax.all_to_all(values, ALL, 0, 0, axis_index_groups=groups, tiled=True)


def section_exchange(values):
    return lax.all_to_all(values, "section", 0, 0, tiled=True)


def plans(micro, vocab_part):
    last = SEC - 1
    steps = micro + 2 * last
    table = np.zeros((SEC, 6 * steps + 2), np.int32)
    for s in range(SEC):
        for way in range(2):
            depth = s if way == 0 else last - s
            for step in range(steps):
                at = step - 2 * depth
                if 0 <= at < micro:
                    sources = ([0] if step < micro else []) + [
                        d + 1 for d in range(last) if 0 <= step - 2 - 2 * d < micro
                    ]
                    spot = 3 * (way * steps + step)
                    table[s, spot : spot + 3] = (1 + s % 2, at, sources.index(depth))
        table[s, 6 * steps :] = (s * vocab_part, s)
    return table


def local(
    token_ids,
    segment_ids,
    noise_input,
    embed_table,
    input_proj,
    norm_gain,
    lead_weight,
    down_weight,
    final_gain,
    readout_proj,
    head_table,
):
    section = lax.axis_index("section")
    core = lax.axis_index("group")
    row = lax.axis_index("row")
    x_at, y_at = row // NY, row % NY
    first_at = jnp.where(core == 0, x_at, y_at)
    micro, _, tokens = token_ids.shape
    width = input_proj.shape[1]
    hidden = lead_weight.shape[2]
    half_rows = down_weight.shape[1]
    emb_part = input_proj.shape[0]
    vocab_part, emb = head_table.shape
    vocab = embed_table.shape[0]
    all_tokens = micro * tokens
    last = SEC - 1
    gain_half = norm_gain.astype(WIDE)
    lead = lead_weight[0]
    own_down = down_weight[0]
    seg_row = segment_ids
    flat_ids = token_ids.reshape(-1)

    plan = plans(micro, vocab_part)
    steps = micro + 2 * last
    table = lax.dynamic_index_in_dim(jnp.asarray(plan), section, 0, False)
    flat_ids = after(flat_ids, table)
    where_start = jnp.stack((first_at, core)).astype(jnp.int32)
    to_first = lambda v: [v] + [link(v, s, 0) for s in range(1, SEC)]
    eighth = row_block(row_block(own_down, core, 2), first_at, 4)
    eighth = jnp.where(section == 1, link(eighth, 0, 1), link(eighth, 2, 3))
    noise = noise_input[:, 0].transpose(2, 0, 1).reshape(emb_part, -1)
    own_embedded = lookup(flat_ids[None], embed_table.T, noise, 3200)
    parts = to_first(jnp.concatenate((own_embedded, input_proj), axis=1))
    embedded = jnp.concatenate([part[:, :all_tokens] for part in parts])
    input_full = jnp.concatenate([part[:, all_tokens:] for part in parts])
    first_in = matmul_tn(embedded, input_full).astype(LOW).reshape(micro, tokens, width)
    odd = (1, 3)
    eighth = after(eighth, first_in)
    eighths = [eighth] + [plane_route(eighth, by, True, odd) for by in (1, 2, 3)]

    kept = empty(
        ((micro, tokens, width), LOW),
        ((micro, tokens, width), LOW),
        ((micro, tokens, hidden), LOW),
        ((micro, tokens, hidden), WIDE),
    )

    def sources(first, step, hops, order):
        arrived = [hops[step - 2, s] for s in order if (step - 2, s) in hops]
        return ([first[step]] if step < micro else []) + arrived

    outs, hops = [], {}
    for step in range(steps):
        out, *kept = forward_stage(
            3 * step,
            table,
            sources(first_in, step, hops, range(SEC)),
            seg_row,
            gain_half,
            held_lead if step > 0 else lead,
            held_down if step > 1 else None,
            kept,
            step == 0,
        )
        if step == 0:
            held_lead = kept.pop()
            upper = upper_half(where_start, [after(part, out) for part in eighths])
            held_down = hold_down(where_start, upper, swap_cores(upper, odd), own_down)
        outs.append(out)
        for s in range(last):
            if 0 <= step - 2 * s < micro:
                ready = after(out, hops[step - 1, s]) if (step - 1, s) in hops else out
                hops[step, s] = link(ready, s, s + 1)
        if step == 2:
            readout_own = after(readout_proj.T, out)
            readout_full = jnp.concatenate(
                [link(readout_own, s, last) for s in range(last)] + [readout_own]
            )
    entries, normeds, saved, inner = kept

    final_rows = jnp.concatenate(outs[2 * last :]).astype(WIDE)
    normed_f, factor_f = layer_norm(final_rows)
    gain_f = final_gain.astype(WIDE)
    final_low = (normed_f * gain_f).astype(LOW)
    readout = matmul_nt(final_low, readout_full).astype(LOW)
    sent = [link(readout, last, s) for s in range(last)]
    readout, peak, total = head_stats(6 * steps + 1, table, sent + [readout], head_table, 2000)
    stats = jnp.concatenate((peak, total))
    all_stats = section_exchange(jnp.tile(stats, (SEC, 1))).reshape(SEC, 2, all_tokens)
    peak = jnp.max(all_stats[:, 0], axis=0)
    total = jnp.sum(all_stats[:, 1] * jnp.exp(all_stats[:, 0] - peak), axis=0)
    logsum = (peak + jnp.log(total))[None]
    head_grad, grad_readout = head_grads(
        6 * steps, table, readout, head_table, logsum, flat_ids[None]
    )
    grad_low = grad_readout.astype(LOW)
    for s in range(last):
        grad_readout = grad_readout + link(grad_low, s, last).astype(WIDE)
    grad_readout = grad_readout.astype(LOW)
    head_grad = lax.psum_scatter(head_grad, "row", scatter_dimension=0)
    readout_grad = matmul_tn(final_low, grad_readout)
    grad_final = matmul(grad_readout, readout_full)
    final_gain_grad = jnp.sum(grad_final * normed_f, axis=0)
    last_grads = norm_back(grad_final * gain_f, normed_f, factor_f).astype(LOW)
    last_grads = last_grads.reshape(micro, tokens, width)

    lead_turned = turned(6 * steps + 1, table, after(lead, grad_low), 0)
    down_turned = turned(6 * steps + 1, table, after(held_down, grad_low), 1)
    totals = empty(
        ((micro, tokens, width), LOW),
        ((micro, tokens, hidden), LOW),
        ((micro, 8, width), WIDE),
    )
    outs, hops = [], {}
    for step in range(steps):
        out, *totals = backward_stage(
            3 * (steps + step),
            table,
            sources(last_grads, step, hops, range(SEC - 1, -1, -1)),
            seg_row,
            gain_half,
            lead_turned,
            down_turned,
            entries,
            saved,
            inner,
            totals,
        )
        outs.append(out)
        for s in range(1, SEC):
            if 0 <= step - 2 * (last - s) < micro:
                ready = after(out, hops[step - 1, s]) if (step - 1, s) in hops else out
                hops[step, s] = link(ready, s, s - 1)
    section, core, row, readout_grad, final_gain_grad = lax.optimization_barrier(
        (section, core, row, readout_grad, final_gain_grad, out)
    )[:5]
    x_at, y_at = row // NY, row % NY
    first_at, second_at = jnp.where(core == 0, x_at, y_at), jnp.where(core == 0, y_at, x_at)
    is_mlp = section % 2 == 1

    first_grads = jnp.concatenate(outs[2 * last :])
    noise_grad = matmul_nt(input_full, first_grads).astype(LOW)
    pieces = noise_grad.reshape(SEC, emb_part, all_tokens)
    sent = [link(pieces[s], 0, s) for s in range(1, SEC)]

    grad_nexts, grads, gain_grads = totals
    flat = lambda v: v.reshape(all_tokens, v.shape[-1])
    grads = after(grads, head_grad)
    normed, grad_nexts, grads, saved = flat(normeds), flat(grad_nexts), flat(grads), flat(saved)
    role = jnp.where(is_mlp, 2, 1)
    where_other = jnp.stack((role, 1 - core, second_at)).astype(jnp.int32)
    where_mine = jnp.stack((role, core, first_at)).astype(jnp.int32)
    both = lambda mine, other: jnp.where(
        core == 0,
        jnp.concatenate((mine, other), axis=1),
        jnp.concatenate((other, mine), axis=1),
    )
    down_got = swap_cores(down_grad(where_other, saved, grad_nexts)[0], odd)
    lead_other = lead_grad(where_other, normed, saved, grads)[0]
    lead_got = swap_cores(lead_other)
    down_mine = down_grad(after(where_mine, lead_other), saved, grad_nexts, down_got)
    down_first = plane_first(down_mine, odd)
    late_ids = after(flat_ids, down_mine)[None]
    packed, noise_wide = noise_pack(6 * steps + 1, table, late_ids, [pieces[0]] + sent)

    lead_mine = lead_grad(after(where_mine, packed), normed, saved, grads, lead_got)
    lead_first = plane_first(lead_mine)
    first_grads, gain_grads, readout_grad, final_gain_grad = after(
        (first_grads, gain_grads, readout_grad, final_gain_grad), lead_mine
    )
    gain_grad = jnp.sum(gain_grads[:, 0], axis=0)
    input_grad = matmul(embedded, first_grads).reshape(SEC, 16, 4, width)
    input_grad = input_grad.transpose(1, 0, 2, 3).reshape(16, 16, width)
    readout_grad = readout_grad.reshape(16, 16, width)
    vectors = jnp.concatenate(
        (
            gain_grad.reshape(16, 64),
            final_gain_grad.reshape(SEC, 16, 16).transpose(1, 0, 2).reshape(16, 64),
            jnp.zeros((16, width - 128), WIDE),
        ),
        axis=1,
    )
    small = jnp.concatenate(
        (
            jnp.where(section == 0, input_grad, readout_grad),
            vectors[:, None],
            jnp.zeros((16, 15, width), WIDE),
        ),
        axis=1,
    ).astype(LOW)
    half_of = lambda which: lax.dynamic_slice_in_dim(small, which * (width // 2), width // 2, 2)
    small = half_of(core).astype(WIDE) + swap_cores(half_of(1 - core)).astype(WIDE)
    small = small.astype(LOW).reshape(NX, NY, 32, width // 2)
    small = jnp.where(core == 0, small, small.swapaxes(0, 1)).reshape(4, NY * 32, width // 2)
    deep = emb_part + 16

    def exchange(blocks, packed, first):
        rows = blocks.shape[1]
        everywhere = jnp.broadcast_to(packed, (4,) + packed.shape)
        got = group_exchange(jnp.concatenate((blocks, everywhere), axis=1), first)
        return jnp.sum(got[:, :rows].astype(WIDE), axis=0).astype(LOW), got[:, rows:]

    packed = after(packed, lead_mine)
    down_first = after(down_first, lead_mine)
    small, packed = exchange(after(small, down_first), packed, True)
    small, packed = exchange(
        small.reshape(4, 32, width // 2), packed.reshape(4 * deep, all_tokens), False
    )
    packed = packed.reshape(16, deep, all_tokens)
    down_second = plane_second(after(down_first, packed), second_at, odd)
    lead_second = plane_second(after(lead_first, packed), second_at)
    packed_other = swap_cores(packed)
    small = both(small, swap_cores(small))
    embed_grad = embed_sum(
        (row * (vocab // 16)).reshape(1), packed, packed_other, emb_part, vocab // 16
    )
    down_part = plane_sum(after(down_second, embed_grad))
    lead_part = plane_sum(after(lead_second, embed_grad))
    noise_out = noise_wide.reshape(emb_part, micro, tokens).transpose(1, 2, 0)
    lead_out = both(lead_part, swap_cores(lead_part)).astype(WIDE)

    def first_target(s, g, x, y):
        if s % 2 == 0:
            return None
        return (s - 1, 0, x, y) if g == 0 else (s, 0, x, y)

    def second_target(s, g, x, y):
        return (s - 1, 1, x, y) if s % 2 == 1 and g == 0 else None

    to_core_0 = route(down_part, first_target)
    to_core_1 = route(down_part, second_target)
    down_out = jnp.where(
        core == 0, to_core_0, jnp.where(is_mlp, down_part, to_core_1)
    ).astype(WIDE)

    small = after(small, (lead_part, down_part))
    gain_out = small[16, :64].astype(WIDE)
    input_rows = small[:16].reshape(SEC, 4, width)
    readout_rows = small[:16].reshape(64, SEC, 64)
    final_rows = small[16, 64:128].reshape(SEC, 16)

    finals = jnp.pad(final_rows, ((0, 0), (0, width - 16)))[:, None]
    mine = jnp.where(
        section == 0, input_rows, readout_rows.transpose(1, 0, 2).reshape(SEC, 4, width)
    )
    shared = section_exchange(
        jnp.concatenate((mine, finals, jnp.zeros((SEC, 3, width), LOW)), axis=1)
    )
    input_out = shared[0, :4]
    readout_out = shared[last, :4].reshape(64, 64)
    final_out = shared[last, 4, :16]

    head_out = pair_sum(head_grad, swap_cores(head_grad), vocab_part // (NX * NY))
    return (
        noise_out[:, None],
        embed_grad.T,
        input_out.astype(WIDE),
        gain_out[None],
        lead_out[None],
        down_out[None],
        final_out.astype(WIDE),
        readout_out.astype(WIDE),
        head_out,
    )


def solution(mesh):
    in_specs = (
        P(None, ("group", "row"), None),
        P(None, ("group", "row"), None),
        P(None, ("group", "row"), None, "section"),
        P(None, "section"),
        P("section", None),
        P("section", None),
        P("section", None, None),
        P("section", None, None),
        P(),
        P(None, "section"),
        P("section", None),
    )
    out_specs = (
        P(None, ("group", "row"), None, "section"),
        P("row", "section"),
        P(("section", "row"), None),
        P("section", "row"),
        P("section", "row", None),
        P("section", "row", None),
        P(("section", "row")),
        P("row", "section"),
        P(("section", "row"), None),
    )
    return jax.shard_map(local, mesh=mesh, in_specs=in_specs, out_specs=out_specs, check_vma=False)
```

```python
import functools
import itertools

import jax
import jax.numpy as jnp
import numpy as np
from jax import lax
from jax.experimental import pallas as pl
from jax.experimental.pallas import tpu as pltpu
from jax.sharding import PartitionSpec as P

HEADS = 16
HEAD_SIZE = 64
LOW = jnp.bfloat16
WIDE = jnp.float32
EPSILON = 1e-05
MASKED = -1000000000.0
CHUNK = 1024
GELU_A = 0.7978845608028654
GELU_B = 0.044715
HBM_SPEC = pl.BlockSpec(memory_space=pltpu.HBM)
VMEM_SPEC = pl.BlockSpec(memory_space=pltpu.VMEM)
SMEM_SPEC = pl.BlockSpec(memory_space=pltpu.SMEM)


def matmul(former, latter):
    return jnp.dot(former, latter, preferred_element_type=WIDE)


def matmul_nt(former, latter):
    return lax.dot_general(
        former, latter, (((1,), (1,)), ((), ())), preferred_element_type=WIDE
    )


def matmul_tn(former, latter):
    return lax.dot_general(
        former, latter, (((0,), (0,)), ((), ())), preferred_element_type=WIDE
    )


def layer_norm(values):
    centre = jnp.mean(values, axis=-1, keepdims=True)
    centred = values - centre
    variance = jnp.mean(centred * centred, axis=-1, keepdims=True)
    factor = lax.rsqrt(variance + EPSILON)
    return (centred * factor, factor)


def norm_back(grad_normed, normed, factor):
    first_mean = jnp.mean(grad_normed, axis=-1, keepdims=True)
    second_mean = jnp.mean(grad_normed * normed, axis=-1, keepdims=True)
    return factor * (grad_normed - first_mean - normed * second_mean)


def gelu(v):
    return 0.5 * v * (1.0 + jnp.tanh(GELU_A * (v + GELU_B * (v * v * v))))


def gelu_slope(v):
    square = v * v
    bend = jnp.tanh(GELU_A * (v + GELU_B * (square * v)))
    return 0.5 * (1.0 + bend) + 0.5 * v * (1.0 - bend * bend) * (
        GELU_A * (1.0 + 3.0 * GELU_B * square)
    )


def head_probs(scores, same):
    scores = jnp.where(same, scores * HEAD_SIZE ** (-0.5), MASKED)
    expo = jnp.exp(scores - jnp.max(scores, axis=-1, keepdims=True))
    return expo * (1.0 / jnp.sum(expo, axis=-1, keepdims=True))


def same_segment(row):
    across = jnp.broadcast_to(row.astype(WIDE), (row.shape[1], row.shape[1]))
    return across.T == across


def lanes(at, size):
    return pl.ds(pl.multiple_of(at, 128), size)


def turn_kernel(spot, live, plan_ref, value_ref, out_ref):
    @pl.when(jnp.bitwise_and(plan_ref[spot], 1) >= live)
    def _():
        out_ref[...] = value_ref[...].T


def turned(spot, plan, value, live):
    rows, columns = value.shape
    if rows > columns:
        tile = rows // 8
        blocks = (pl.BlockSpec((tile, columns), lambda i: (i, 0)), pl.BlockSpec((columns, tile), lambda i: (0, i)))
    else:
        tile = columns // 8
        blocks = (pl.BlockSpec((rows, tile), lambda i: (0, i)), pl.BlockSpec((tile, rows), lambda i: (i, 0)))
    return pl.pallas_call(
        functools.partial(turn_kernel, spot, live),
        out_shape=pltpu.VMEM((columns, rows), LOW),
        grid=(8,),
        in_specs=[SMEM_SPEC, blocks[0]],
        out_specs=blocks[1],
        compiler_params=pltpu.CompilerParams(vmem_limit_bytes=12 << 20),
        cost_estimate=pl.CostEstimate(flops=0, bytes_accessed=1024, transcendentals=0),
        name="turned",
    )(plan, far(value))


def chosen(choice, candidates, buffer):
    for at, candidate in enumerate(candidates):

        @pl.when(choice == at)
        def _():
            buffer[...] = candidate[...]


def forward_kernel(spot, with_down, loads, count, *refs):
    table_ref, candidates, refs = refs[0], refs[1 : 1 + count], refs[1 + count :]
    if not with_down:
        refs = refs[:3] + (None,) + refs[3:]
    source_ref = load_sems = None
    if loads:
        source_ref, load_sems = refs[2], refs[-1]
        refs = refs[:2] + (refs[13],) + refs[3:13] + refs[14:-1]
    forward_body(spot, table_ref, candidates, source_ref, load_sems, *refs)


def forward_body(
    spot,
    table_ref,
    candidates,
    source_ref,
    load_sems,
    seg_row_ref,
    gain_ref,
    lead_ref,
    down_ref,
    entries_in,
    normeds_in,
    saved_in,
    inner_in,
    out_ref,
    entries_ref,
    normeds_ref,
    saved_ref,
    inner_ref,
    normed_buf,
    saved_buf,
    inner_buf,
    result_buf,
    scores_buf,
    probs_buf,
    entry_ref,
    out_sems,
):
    role, slot = table_ref[spot], table_ref[spot + 1]
    tokens, width = entry_ref.shape
    keeps = [
        pltpu.make_async_copy(entry_ref, entries_ref.at[slot], out_sems.at[0]),
        pltpu.make_async_copy(normed_buf, normeds_ref.at[slot], out_sems.at[1]),
        pltpu.make_async_copy(saved_buf, saved_ref.at[slot], out_sems.at[2]),
    ]
    keep_inner = pltpu.make_async_copy(inner_buf, inner_ref.at[slot], out_sems.at[3])

    def load(j):
        at = lanes(j * CHUNK, CHUNK)
        return pltpu.make_async_copy(source_ref.at[:, at], lead_ref.at[:, at], load_sems.at[j])

    def loaded(j):
        if source_ref is not None:
            load(j).wait()

    if source_ref is not None:
        for j in range(lead_ref.shape[1] // CHUNK):
            load(j).start()

        @pl.when(role != 1)
        def _():
            pl.loop(0, lead_ref.shape[1] // CHUNK)(loaded)

    @pl.when(role > 0)
    def _():
        chosen(table_ref[spot + 2], candidates, entry_ref)
        normed, _ = layer_norm(entry_ref[...].astype(WIDE))
        normed_buf[...] = (normed * gain_ref[...]).astype(LOW)
        keeps[0].start()
        keeps[1].start()

    @pl.when(role == 1)
    def _():
        @pl.loop(0, 3 * width // CHUNK, unroll=3)
        def _(j):
            at = lanes(j * CHUNK, CHUNK)
            loaded(j)
            saved_buf[:, at] = matmul(normed_buf[...], lead_ref[:, at]).astype(LOW)

        left = lax.broadcasted_iota(jnp.int32, (tokens, 128), 1) < HEAD_SIZE
        zero = jnp.zeros((tokens, 128), LOW)

        @pl.loop(0, HEADS // 8, unroll=2)
        def _(group):
            for pair in range(4):
                at = group * 512 + pair * 128
                query = saved_buf[:, lanes(at, 128)]
                key = saved_buf[:, lanes(width + at, 128)]
                scores_buf[group * 8 + 2 * pair] = matmul_nt(jnp.where(left, query, zero), key)
                scores_buf[group * 8 + 2 * pair + 1] = matmul_nt(jnp.where(left, zero, query), key)

        @pl.loop(0, HEADS // 4, unroll=2)
        def _(group):
            same = same_segment(seg_row_ref[slot])
            for head in range(4):
                at = group * 4 + head
                probs_buf[at] = head_probs(scores_buf[at], same).astype(LOW)

        @pl.loop(0, HEADS // 8, unroll=2)
        def _(group):
            for pair in range(4):
                at = group * 512 + pair * 128
                value = saved_buf[:, lanes(2 * width + at, 128)]
                mixed = jnp.where(
                    left,
                    matmul(probs_buf[group * 8 + 2 * pair], value),
                    matmul(probs_buf[group * 8 + 2 * pair + 1], value),
                )
                saved_buf[:, lanes(3 * width + at, 128)] = mixed.astype(LOW)

        keeps[2].start()

        @pl.loop(0, width // CHUNK)
        def _(j):
            at = lanes(j * CHUNK, CHUNK)
            loaded(3 * width // CHUNK + j)
            term = matmul(saved_buf[:, 3 * width :], lead_ref[:, lanes(3 * width + j * CHUNK, CHUNK)])
            out_ref[:, at] = (entry_ref[:, at].astype(WIDE) + term).astype(LOW)

    def feed_forward():
        result_buf[...] = entry_ref[...].astype(WIDE)

        @pl.loop(0, lead_ref.shape[1] // CHUNK, unroll=4)
        def _(j):
            at = lanes(j * CHUNK, CHUNK)
            inner = matmul(normed_buf[...], lead_ref[:, at])
            inner_buf[:, at] = inner
            active = gelu(inner).astype(LOW)
            saved_buf[:, at] = active
            result_buf[...] += matmul(active, down_ref[pl.ds(j * CHUNK, CHUNK), :])

        keeps[2].start()
        keep_inner.start()
        out_ref[...] = result_buf[...].astype(LOW)
        keep_inner.wait()

    if down_ref is not None:
        pl.when(role == 2)(feed_forward)

    @pl.when(role > 0)
    def _():
        for keep in keeps:
            keep.wait()


def pinned(value):
    return pltpu.with_memory_space_constraint(value, pltpu.VMEM)


def far(value):
    return pltpu.with_memory_space_constraint(value, pltpu.HBM)


def forward_stage(spot, table, entries, seg_row, gain, lead, down, kept, loads=False):
    tokens, width = entries[0].shape
    hidden = lead.shape[1]
    count = len(entries) + (3 if down is None else 4)
    given = [VMEM_SPEC] * (len(entries) + 2) + [HBM_SPEC if loads else VMEM_SPEC]
    return pl.pallas_call(
        functools.partial(forward_kernel, spot, down is not None, loads, len(entries)),
        out_shape=[jax.ShapeDtypeStruct((tokens, width), LOW)]
        + [jax.ShapeDtypeStruct(k.shape, k.dtype) for k in kept]
        + ([pltpu.VMEM(lead.shape, LOW)] if loads else []),
        in_specs=[SMEM_SPEC] + given + [VMEM_SPEC] * (down is not None) + [HBM_SPEC] * 4,
        out_specs=[VMEM_SPEC] + [HBM_SPEC] * 4 + [VMEM_SPEC] * loads,
        scratch_shapes=[
            pltpu.VMEM((tokens, width), LOW),
            pltpu.VMEM((tokens, hidden), LOW),
            pltpu.VMEM((tokens, hidden), WIDE),
            pltpu.VMEM((tokens, width), WIDE),
            pltpu.VMEM((HEADS, tokens, tokens), WIDE),
            pltpu.VMEM((HEADS, tokens, tokens), LOW),
            pltpu.VMEM((tokens, width), LOW),
            pltpu.SemaphoreType.DMA((4,)),
        ]
        + ([pltpu.SemaphoreType.DMA((hidden // CHUNK,))] if loads else []),
        input_output_aliases={count + 1 + i: 1 + i for i in range(4)},
        compiler_params=pltpu.CompilerParams(vmem_limit_bytes=18 << 20),
        cost_estimate=pl.CostEstimate(
            flops=4 * tokens * width * hidden, bytes_accessed=20 << 20, transcendentals=0
        ),
        name="forward_stage",
    )(
        table,
        *entries,
        seg_row,
        gain,
        (far if loads else pinned)(lead),
        *([pinned(down)] if down is not None else []),
        *map(far, kept),
    )


def backward_kernel(spot, count, *refs):
    backward_body(spot, refs[0], refs[1 : 1 + count], *refs[1 + count :])


def backward_body(
    spot,
    table_ref,
    candidates,
    seg_row_ref,
    gain_ref,
    lead_ref,
    down_ref,
    entries_ref,
    saved_ref,
    inner_ref,
    nexts_in,
    grads_in,
    gains_in,
    out_ref,
    nexts_ref,
    grads_ref,
    gains_ref,
    saved_buf,
    inner_buf,
    grads_buf,
    mixed_buf,
    gain_buf,
    entry_buf,
    normed_buf,
    scores_buf,
    probs_grad_buf,
    probs_buf,
    scores_grad_buf,
    grad_ref,
    in_sems,
    out_sems,
):
    role, slot = table_ref[spot], table_ref[spot + 1]
    tokens, width = grad_ref.shape
    bring_saved = pltpu.make_async_copy(saved_ref.at[slot], saved_buf, in_sems.at[0])
    bring_inner = pltpu.make_async_copy(inner_ref.at[slot], inner_buf, in_sems.at[1])
    bring_entry = pltpu.make_async_copy(entries_ref.at[slot], entry_buf, in_sems.at[2])
    keep_next = pltpu.make_async_copy(grad_ref, nexts_ref.at[slot], out_sems.at[0])
    keep_grads = pltpu.make_async_copy(grads_buf, grads_ref.at[slot], out_sems.at[1])
    keep_gain = pltpu.make_async_copy(gain_buf, gains_ref.at[slot], out_sems.at[2])

    @pl.when(role == 2)
    def _():
        bring_inner.start()

    @pl.when(role == 1)
    def _():
        bring_saved.start()

    @pl.when(role > 0)
    def _():
        bring_entry.start()
        chosen(table_ref[spot + 2], candidates, grad_ref)
        keep_next.start()
        normed_buf[...] = jnp.zeros_like(normed_buf)

    @pl.when(role == 1)
    def _():
        grads_buf[:, 3 * width :] = grad_ref[...]
        mixed_buf[...] = matmul(grad_ref[...], lead_ref[3 * width :, :]).astype(LOW)
        bring_saved.wait()
        left = lax.broadcasted_iota(jnp.int32, (tokens, 128), 1) < HEAD_SIZE
        zero = jnp.zeros((tokens, 128), LOW)
        scale = HEAD_SIZE ** (-0.5)

        @pl.loop(0, HEADS // 8, unroll=2)
        def _(group):
            for pair in range(4):
                at = group * 512 + pair * 128
                query = saved_buf[:, lanes(at, 128)]
                key = saved_buf[:, lanes(width + at, 128)]
                value = saved_buf[:, lanes(2 * width + at, 128)]
                grad = mixed_buf[:, lanes(at, 128)]
                for own in (0, 1):
                    mine = lambda v: jnp.where(left, v, zero) if own == 0 else jnp.where(left, zero, v)
                    scores_buf[group * 8 + 2 * pair + own] = matmul_nt(mine(query), key)
                    probs_grad_buf[group * 8 + 2 * pair + own] = matmul_nt(mine(grad), value)

        @pl.loop(0, HEADS // 4, unroll=2)
        def _(group):
            same = same_segment(seg_row_ref[slot])
            for head in range(4):
                at = group * 4 + head
                probs = head_probs(scores_buf[at], same)
                probs_buf[at] = probs.astype(LOW)
                grad_probs = probs_grad_buf[at]
                scores_grad_buf[at] = (
                    probs * (grad_probs - jnp.sum(probs * grad_probs, axis=-1, keepdims=True))
                ).astype(LOW)

        @pl.loop(0, HEADS // 4, unroll=2)
        def _(group):
            for pair in range(2):
                at = group * 256 + pair * 128
                query = saved_buf[:, lanes(at, 128)]
                key = saved_buf[:, lanes(width + at, 128)]
                grad = mixed_buf[:, lanes(at, 128)]
                parts = []
                for own in (0, 1):
                    probs = probs_buf[group * 4 + 2 * pair + own]
                    grad_low = scores_grad_buf[group * 4 + 2 * pair + own]
                    parts.append(
                        (
                            matmul(grad_low, key) * scale,
                            matmul_tn(grad_low, query) * scale,
                            matmul_tn(probs, grad),
                        )
                    )
                for which in range(3):
                    grads_buf[:, lanes(which * width + at, 128)] = jnp.where(
                        left, parts[0][which], parts[1][which]
                    ).astype(LOW)

        @pl.loop(0, 3 * width // CHUNK, unroll=3)
        def _(j):
            at = lanes(j * CHUNK, CHUNK)
            normed_buf[...] += matmul(grads_buf[:, at], lead_ref[pl.ds(j * CHUNK, CHUNK), :])

    @pl.when(role == 2)
    def _():
        bring_inner.wait()

        @pl.loop(0, lead_ref.shape[0] // CHUNK, unroll=4)
        def _(j):
            at = lanes(j * CHUNK, CHUNK)
            grad_active = matmul(grad_ref[...], down_ref[:, at])
            grads = (gelu_slope(inner_buf[:, at]) * grad_active).astype(LOW)
            grads_buf[:, at] = grads
            normed_buf[...] += matmul(grads, lead_ref[pl.ds(j * CHUNK, CHUNK), :])

    @pl.when(role > 0)
    def _():
        keep_grads.start()
        bring_entry.wait()
        grad_normed = normed_buf[...]
        normed, factor = layer_norm(entry_buf[...].astype(WIDE))
        gain_buf[...] = jnp.broadcast_to(
            jnp.sum(grad_normed * normed, axis=0, keepdims=True), gain_buf.shape
        )
        keep_gain.start()
        out_ref[...] = (
            grad_ref[...].astype(WIDE) + norm_back(grad_normed * gain_ref[...], normed, factor)
        ).astype(LOW)
        keep_next.wait()
        keep_grads.wait()
        keep_gain.wait()


def backward_stage(
    spot, table, nexts, seg_row, gain, lead, down, entries, saved, inner, totals
):
    tokens, width = nexts[0].shape
    count = len(nexts)
    hidden = lead.shape[0]
    return pl.pallas_call(
        functools.partial(backward_kernel, spot, count),
        out_shape=[jax.ShapeDtypeStruct((tokens, width), LOW)]
        + [jax.ShapeDtypeStruct(k.shape, k.dtype) for k in totals],
        in_specs=[SMEM_SPEC] + [VMEM_SPEC] * (count + 4) + [HBM_SPEC] * 6,
        out_specs=[VMEM_SPEC] + [HBM_SPEC] * 3,
        scratch_shapes=[
            pltpu.VMEM((tokens, hidden), LOW),
            pltpu.VMEM((tokens, hidden), WIDE),
            pltpu.VMEM((tokens, hidden), LOW),
            pltpu.VMEM((tokens, width), LOW),
            pltpu.VMEM((8, width), WIDE),
            pltpu.VMEM((tokens, width), LOW),
            pltpu.VMEM((tokens, width), WIDE),
            pltpu.VMEM((HEADS, tokens, tokens), WIDE),
            pltpu.VMEM((HEADS, tokens, tokens), WIDE),
            pltpu.VMEM((HEADS, tokens, tokens), LOW),
            pltpu.VMEM((HEADS, tokens, tokens), LOW),
            pltpu.VMEM((tokens, width), LOW),
            pltpu.SemaphoreType.DMA((3,)),
            pltpu.SemaphoreType.DMA((3,)),
        ],
        input_output_aliases={count + 8 + i: 1 + i for i in range(3)},
        compiler_params=pltpu.CompilerParams(vmem_limit_bytes=18 << 20),
        cost_estimate=pl.CostEstimate(
            flops=4 * tokens * width * hidden, bytes_accessed=20 << 20, transcendentals=0
        ),
        name="backward_stage",
    )(
        table,
        *nexts,
        seg_row,
        gain,
        pinned(lead),
        pinned(down),
        far(entries),
        far(saved),
        far(inner),
        *map(far, totals),
    )


def stats_kernel(spot, plan_ref, *refs):
    candidates, (table_ref, readout_ref, peak_ref, total_ref) = refs[:-4], refs[-4:]
    step = pl.program_id(0)

    @pl.when(step == 0)
    def _():
        chosen(plan_ref[spot], candidates, readout_ref)

    logits = matmul_nt(table_ref[...], readout_ref[...])
    own_peak = jnp.max(logits, axis=0, keepdims=True)
    own_total = lambda peak: jnp.sum(jnp.exp(logits - peak), axis=0, keepdims=True)

    @pl.when(step == 0)
    def _():
        peak_ref[...] = own_peak
        total_ref[...] = own_total(own_peak)

    @pl.when(step > 0)
    def _():
        peak = jnp.maximum(peak_ref[...], own_peak)
        total_ref[...] = total_ref[...] * jnp.exp(peak_ref[...] - peak) + own_total(peak)
        peak_ref[...] = peak


def head_stats(spot, plan, readouts, table, tile):
    tokens, emb = readouts[0].shape
    vocab = table.shape[0]
    whole = pl.BlockSpec((1, tokens), lambda i: (0, 0))
    rows = pl.BlockSpec((tokens, emb), lambda i: (0, 0))
    return pl.pallas_call(
        functools.partial(stats_kernel, spot),
        out_shape=[jax.ShapeDtypeStruct((tokens, emb), LOW)]
        + [jax.ShapeDtypeStruct((1, tokens), WIDE)] * 2,
        grid=(vocab // tile,),
        in_specs=[SMEM_SPEC]
        + [rows] * len(readouts)
        + [pl.BlockSpec((tile, emb), lambda i: (i, 0))],
        out_specs=[rows, whole, whole],
        compiler_params=pltpu.CompilerParams(vmem_limit_bytes=32 << 20),
        cost_estimate=pl.CostEstimate(
            flops=2 * tokens * vocab * emb, bytes_accessed=5 << 20, transcendentals=tokens * vocab
        ),
        name="head_stats",
    )(plan, *readouts, far(table))


def head_kernel(spot, table_base_ref, readout_ref, table_ref, logsum_ref, ids_ref, head_ref, grad_ref):
    tile = table_ref.shape[0]
    logits = matmul_nt(table_ref[...], readout_ref[...])
    ids = ids_ref[...] - (table_base_ref[spot] + pl.program_id(0) * tile)
    hits = lax.broadcasted_iota(jnp.int32, logits.shape, 0) == ids
    probs = jnp.exp(logits - logsum_ref[...])
    grads = jnp.where(hits, probs - 1.0, probs).astype(LOW)
    head = matmul(grads, readout_ref[...])
    unit = tile // 4
    for shard in range(4):
        head_ref[shard, :unit] = head[shard * unit : (shard + 1) * unit].astype(LOW)
    term = matmul_tn(grads, table_ref[...])

    @pl.when(pl.program_id(0) == 0)
    def _():
        grad_ref[...] = term

    @pl.when(pl.program_id(0) > 0)
    def _():
        grad_ref[...] += term


def head_grads(spot, base, readout, table, logsum, ids):
    tokens, emb = readout.shape
    vocab = table.shape[0]
    row = pl.BlockSpec((1, tokens), lambda i: (0, 0))
    whole = pl.BlockSpec((tokens, emb), lambda i: (0, 0))
    part = pl.BlockSpec((vocab // 4, emb), lambda i: (i, 0))
    return pl.pallas_call(
        functools.partial(head_kernel, spot),
        out_shape=[
            pltpu.HBM((16, 512, emb), LOW),
            jax.ShapeDtypeStruct((tokens, emb), WIDE),
        ],
        grid=(4,),
        in_specs=[SMEM_SPEC, whole, part, row, row],
        out_specs=[pl.BlockSpec((4, 512, emb), lambda i: (i, 0, 0)), whole],
        compiler_params=pltpu.CompilerParams(vmem_limit_bytes=32 << 20),
        cost_estimate=pl.CostEstimate(
            flops=6 * tokens * vocab * emb, bytes_accessed=9 << 20, transcendentals=tokens * vocab
        ),
        name="head_grads",
    )(base, readout, far(table), logsum, ids)


def pair_kernel(former_ref, latter_ref, out_ref):
    rows = out_ref.shape[0]
    out_ref[...] = former_ref[:rows].astype(WIDE) + latter_ref[:rows].astype(WIDE)


def pair_sum(former, latter, rows):
    return pl.pallas_call(
        pair_kernel,
        out_shape=jax.ShapeDtypeStruct((rows, former.shape[1]), WIDE),
        in_specs=[VMEM_SPEC] * 2,
        out_specs=VMEM_SPEC,
        compiler_params=pltpu.CompilerParams(vmem_limit_bytes=8 << 20),
        cost_estimate=pl.CostEstimate(flops=0, bytes_accessed=1024, transcendentals=0),
        name="pair_sum",
    )(former, latter)


def lookup_kernel(ids_ref, table_ref, noise_ref, out_ref, total_ref, low_ref):
    step = pl.program_id(0)
    parts, tile = table_ref.shape
    tokens = ids_ref.shape[1]
    blocks = tile // 128

    @pl.when(step == 0)
    def _():
        lane = jnp.bitwise_and(ids_ref[...], 127)
        hits = lax.broadcasted_iota(jnp.int32, (128, tokens), 0) == lane
        low_ref[...] = jnp.where(hits, 1.0, 0.0).astype(LOW)
        total_ref[...] = noise_ref[...].astype(WIDE)

    stacked = jnp.concatenate(
        [table_ref[:, block * 128 : (block + 1) * 128] for block in range(blocks)]
    )
    found = matmul(stacked, low_ref[...])
    own = jnp.right_shift(ids_ref[...], 7) - step * blocks
    total = jnp.zeros_like(total_ref)
    for block in range(blocks):
        total = jnp.where(own == block, found[block * parts : (block + 1) * parts], total)
    total_ref[...] += total

    @pl.when(step == pl.num_programs(0) - 1)
    def _():
        out_ref[...] = total_ref[...].astype(LOW)


def lookup(ids, table, noise, tile):
    parts, vocab = table.shape
    tokens = ids.shape[1]
    whole = pl.BlockSpec((parts, tokens), lambda i: (0, 0))
    return pl.pallas_call(
        lookup_kernel,
        out_shape=jax.ShapeDtypeStruct((parts, tokens), LOW),
        grid=(vocab // tile,),
        in_specs=[
            pl.BlockSpec((1, tokens), lambda i: (0, 0)),
            pl.BlockSpec((parts, tile), lambda i: (0, i)),
            whole,
        ],
        out_specs=whole,
        scratch_shapes=[pltpu.VMEM((parts, tokens), WIDE), pltpu.VMEM((128, tokens), LOW)],
        compiler_params=pltpu.CompilerParams(vmem_limit_bytes=32 << 20),
        cost_estimate=pl.CostEstimate(
            flops=2 * 128 * vocab * tokens, bytes_accessed=4 << 20, transcendentals=0
        ),
        name="lookup",
    )(ids, far(table), noise)


def lead_grad_kernel(where_ref, normed_ref, mixed_ref, grads_ref, *refs):
    got_ref, out_refs, (turned_ref, result_ref) = None, refs[:-2], refs[-2:]
    if len(out_refs) > 1:
        got_ref, out_refs = out_refs[0], out_refs[1:]
    role, half, spot = where_ref[0], where_ref[1], where_ref[2]
    step = pl.program_id(0)
    width = normed_ref.shape[1]
    steps = pl.num_programs(0)
    use_mixed = jnp.logical_and(role == 1, half == 1)

    @pl.when(step == 0)
    def _():
        turned_ref[...] = normed_ref[...].T

    @pl.when(jnp.logical_and(step == steps // 2, use_mixed))
    def _():
        turned_ref[...] = mixed_ref[...].T

    result_ref[...] = matmul(turned_ref[...], grads_ref[...])
    unit = width // 16

    def put(block, rows, part):
        if got_ref is not None:
            part = part + got_ref[block, rows, :].astype(WIDE)
        out_ref = out_refs[0].at[block] if got_ref is None else out_refs[block]
        out_ref[rows, :] = part.astype(LOW)

    @pl.when(half == 0)
    def _():
        for block in range(4):
            x = (spot + block) % 4
            put(block, slice(None), result_ref[pl.ds(pl.multiple_of(x * 4 * unit, 4 * unit), 4 * unit)])

    @pl.when(half == 1)
    def _():
        for block in range(4):
            y = (spot + block) % 4
            for x in range(4):
                rows = pl.ds(pl.multiple_of((4 * x + y) * unit, unit), unit)
                put(block, slice(x * unit, (x + 1) * unit), result_ref[rows])


CHEAP = pl.CostEstimate(flops=0, bytes_accessed=1024, transcendentals=0)


def lead_grad(where, normed, saved, grads, got=None):
    tokens, width = normed.shape
    tile = 1024
    whole = pl.BlockSpec((4, width // 4, tile), lambda i, where: (0, 0, i))
    block = pl.BlockSpec((width // 4, tile), lambda i, where: (0, i))
    shape = (width // 4, 2 * width)
    return pl.pallas_call(
        lead_grad_kernel,
        out_shape=[jax.ShapeDtypeStruct((4,) + shape, LOW)]
        if got is None
        else [jax.ShapeDtypeStruct(shape, LOW)] * 4,
        grid_spec=pltpu.PrefetchScalarGridSpec(
            num_scalar_prefetch=1,
            grid=(2 * width // tile,),
            in_specs=[
                pl.BlockSpec((tokens, width), lambda i, where: (0, 0)),
                pl.BlockSpec((tokens, width), lambda i, where: (0, 3)),
                pl.BlockSpec((tokens, tile), lambda i, where: (0, where[1] * (2 * width // tile) + i)),
            ]
            + ([] if got is None else [whole]),
            out_specs=[whole] if got is None else [block] * 4,
            scratch_shapes=[pltpu.VMEM((width, tokens), LOW), pltpu.VMEM((width, tile), WIDE)],
        ),
        compiler_params=pltpu.CompilerParams(vmem_limit_bytes=24 << 20),
        cost_estimate=CHEAP
        if got is None
        else pl.CostEstimate(
            flops=4 * tokens * width * width, bytes_accessed=12 << 20, transcendentals=0
        ),
        name="lead_grad",
    )(where, far(normed), far(saved), far(grads), *([] if got is None else [got]))


def down_grad_kernel(where_ref, saved_ref, nexts_ref, *refs):
    got_ref, out_refs, (buf_ref, got_buf, sems) = None, refs[:-3], refs[-3:]
    if len(out_refs) > 1:
        got_ref, out_refs = out_refs[0], out_refs[1:]
    role, half, spot = where_ref[0], where_ref[1], where_ref[2]
    at = pl.program_id(0)
    unit = saved_ref.shape[1] // 4

    @pl.when(role == 2)
    def _():
        if got_ref is not None:
            bring = pltpu.make_async_copy(got_ref, got_buf, sems.at[4])
            pl.when(at == 0)(bring.start)
        result = matmul_tn(saved_ref[...], nexts_ref[...])
        if got_ref is not None:
            pl.when(at == 0)(bring.wait)

        def put(block, rows, part):
            if got_ref is not None:
                part = part + got_buf[block, rows, :].astype(WIDE)
            buf_ref[block, rows, :] = part.astype(LOW)

        @pl.when(half == 0)
        def _():
            put((at - spot + 4) % 4, slice(None), result)

        @pl.when(half == 1)
        def _():
            rows = pl.ds(pl.multiple_of(at * unit, unit), unit)
            for y in range(4):
                put((y - spot + 4) % 4, rows, result[y * unit : (y + 1) * unit])

        @pl.when(at == pl.num_programs(0) - 1)
        def _():
            copies = [pltpu.make_async_copy(buf_ref, out_refs[0], sems.at[0])]
            if got_ref is not None:
                copies = [
                    pltpu.make_async_copy(buf_ref.at[block], out_ref, sems.at[block])
                    for block, out_ref in enumerate(out_refs)
                ]
            for copy in copies:
                copy.start()
            for copy in copies:
                copy.wait()


def down_grad(where, saved, nexts, got=None):
    tokens, hidden = saved.shape
    width = nexts.shape[1]
    rows = hidden // 8
    live = lambda where: jnp.where(where[0] == 2, 1, 0)
    return pl.pallas_call(
        down_grad_kernel,
        out_shape=[pltpu.HBM((4, rows, width), LOW)]
        if got is None
        else [pltpu.HBM((rows, width), LOW)] * 4,
        grid_spec=pltpu.PrefetchScalarGridSpec(
            num_scalar_prefetch=1,
            grid=(4,),
            in_specs=[
                pl.BlockSpec((tokens, rows), lambda i, where: (0, (where[1] * 4 + i) * live(where))),
                pl.BlockSpec((tokens, width), lambda i, where: (0, 0)),
            ]
            + ([] if got is None else [HBM_SPEC]),
            out_specs=[HBM_SPEC] * (1 if got is None else 4),
            scratch_shapes=[
                pltpu.VMEM((4, rows, width), LOW),
                pltpu.VMEM((4, 16, 128) if got is None else (4, rows, width), LOW),
                pltpu.SemaphoreType.DMA((5,)),
            ],
        ),
        compiler_params=pltpu.CompilerParams(vmem_limit_bytes=28 << 20),
        cost_estimate=CHEAP,
        name="down_grad",
    )(where, far(saved), far(nexts), *([] if got is None else [far(got)]))


def upper_kernel(where_ref, *refs):
    out_ref = refs[4]
    rows = refs[0].shape[0]
    for at, part in enumerate(refs[:4]):
        place = (where_ref[0] - at + 4) % 4
        out_ref[pl.ds(pl.multiple_of(place * rows, rows), rows), :] = part[...]


def upper_half(where, parts):
    rows, width = parts[0].shape
    return pl.pallas_call(
        upper_kernel,
        out_shape=jax.ShapeDtypeStruct((4 * rows, width), LOW),
        in_specs=[SMEM_SPEC] + [VMEM_SPEC] * 4,
        out_specs=VMEM_SPEC,
        compiler_params=pltpu.CompilerParams(vmem_limit_bytes=8 << 20),
        name="upper_half",
    )(where, *parts)


def hold_down_kernel(where_ref, mine_ref, other_ref, own_ref, out_ref, sems):
    rows = mine_ref.shape[0]
    core = where_ref[1]
    spot = lambda at: out_ref.at[pl.ds(pl.multiple_of(at * rows, rows), rows), :]
    copies = [
        pltpu.make_async_copy(mine_ref, spot(core), sems.at[0]),
        pltpu.make_async_copy(other_ref, spot(1 - core), sems.at[1]),
        pltpu.make_async_copy(own_ref, out_ref.at[pl.ds(2 * rows, 2 * rows), :], sems.at[2]),
    ]
    for copy in copies:
        copy.start()
    for copy in copies:
        copy.wait()


def hold_down(where, mine, other, own):
    rows, width = mine.shape
    return pl.pallas_call(
        hold_down_kernel,
        out_shape=pltpu.VMEM((4 * rows, width), LOW),
        in_specs=[SMEM_SPEC] + [VMEM_SPEC] * 2 + [HBM_SPEC],
        out_specs=VMEM_SPEC,
        scratch_shapes=[pltpu.SemaphoreType.DMA((3,))],
        compiler_params=pltpu.CompilerParams(vmem_limit_bytes=8 << 20),
        name="hold_down",
    )(where, mine, other, far(own))


def noise_kernel(spot, plan_ref, ids_ref, *refs):
    candidates, (packed_ref, noise_ref, buf_ref) = refs[:-3], refs[-3:]
    parts = noise_ref.shape[0]
    chosen(plan_ref[spot], candidates, buf_ref)
    packed_ref[:parts] = buf_ref[...]
    noise_ref[...] = buf_ref[...].astype(WIDE)
    ids = ids_ref[...]
    high = jnp.right_shift(ids, 8).astype(WIDE)
    low = jnp.bitwise_and(ids, 255).astype(WIDE)
    at = lax.broadcasted_iota(jnp.int32, (16, ids.shape[1]), 0)
    split = jnp.where(at == 0, high, jnp.where(at == 1, low, 0.0))
    packed_ref[parts:] = split.astype(LOW)


def noise_pack(spot, plan, ids, candidates):
    parts, tokens = candidates[0].shape
    return pl.pallas_call(
        functools.partial(noise_kernel, spot),
        out_shape=[
            jax.ShapeDtypeStruct((parts + 16, tokens), LOW),
            jax.ShapeDtypeStruct((parts, tokens), WIDE),
        ],
        in_specs=[SMEM_SPEC] + [VMEM_SPEC] * (1 + len(candidates)),
        out_specs=[VMEM_SPEC] * 2,
        scratch_shapes=[pltpu.VMEM((parts, tokens), LOW)],
        compiler_params=pltpu.CompilerParams(vmem_limit_bytes=8 << 20),
        cost_estimate=CHEAP,
        name="noise_pack",
    )(plan, ids, *candidates)


def embed_kernel(base_ref, mine_ref, other_ref, out_ref, total_ref):
    step = pl.program_id(0)
    steps = pl.num_programs(0)
    parts = out_ref.shape[0]
    blocks = total_ref.shape[0] // parts

    def add(gathered_ref):
        count, _, tokens = gathered_ref.shape
        term = None
        for at in range(count):
            split = gathered_ref[at, parts : parts + 16].astype(WIDE)
            ids = (split[0:1] * 256.0 + split[1:2]).astype(jnp.int32) - base_ref[0]
            lane = jnp.bitwise_and(ids, 127)
            hits = lax.broadcasted_iota(jnp.int32, (128, tokens), 0) == lane
            hits = jnp.where(hits, 1.0, 0.0).astype(LOW)
            own = jnp.right_shift(ids, 7)
            grads = gathered_ref[at, :parts]
            masked = jnp.concatenate(
                [grads * jnp.where(own == block, 1.0, 0.0).astype(LOW) for block in range(blocks)]
            )
            part = matmul_nt(masked, hits)
            term = part if term is None else term + part

        @pl.when(step == 0)
        def _():
            total_ref[...] = term

        @pl.when(step > 0)
        def _():
            total_ref[...] += term

    pl.when(step < steps // 2)(lambda: add(mine_ref))
    pl.when(step >= steps // 2)(lambda: add(other_ref))

    @pl.when(step == steps - 1)
    def _():
        rows = out_ref.shape[1]
        for block in range(blocks):
            size = min(128, rows - block * 128)
            out_ref[:, block * 128 : block * 128 + size] = total_ref[
                block * parts : (block + 1) * parts, :size
            ]


def embed_sum(base, mine, other, parts, rows):
    count, deep, tokens = mine.shape
    step = 4
    half = count // step
    blocks = -(-rows // 128)
    return pl.pallas_call(
        embed_kernel,
        out_shape=jax.ShapeDtypeStruct((parts, rows), WIDE),
        grid=(2 * half,),
        in_specs=[
            SMEM_SPEC,
            pl.BlockSpec((step, deep, tokens), lambda i: (jnp.minimum(i, half - 1), 0, 0)),
            pl.BlockSpec((step, deep, tokens), lambda i: (jnp.maximum(i - half, 0), 0, 0)),
        ],
        out_specs=pl.BlockSpec((parts, rows), lambda i: (0, 0)),
        scratch_shapes=[pltpu.VMEM((blocks * parts, 128), WIDE)],
        compiler_params=pltpu.CompilerParams(vmem_limit_bytes=32 << 20),
        cost_estimate=CHEAP,
        name="embed_sum",
    )(base, mine, other)


def empty(*kinds):
    return pl.pallas_call(
        lambda *refs: None,
        out_shape=[pltpu.HBM(shape, dtype) for shape, dtype in kinds],
        out_specs=[HBM_SPEC] * len(kinds),
        compiler_params=pltpu.CompilerParams(vmem_limit_bytes=1 << 20),
        name="empty",
    )()


ROW_LEN = 128
SEC, GRP, NX, NY = 4, 2, 4, 4
ALL = ("section", "group", "row")
TURNS = (1, 3, 2)


def route(value, target_of):
    number = lambda s, g, x, y: (s * GRP + g) * NX * NY + x * NY + y
    pairs = []
    for at in itertools.product(range(SEC), range(GRP), range(NX), range(NY)):
        target = target_of(*at)
        if target is not None:
            pairs.append((number(*at), number(*target)))
    return lax.ppermute(value, ALL, pairs)


def link(value, source, target):
    return route(value, lambda s, g, x, y: (target, g, x, y) if s == source else None)


def turn(value, by):
    return route(value, lambda s, g, x, y: ((s + by) % SEC, g, x, y))


def swap_cores(value, sections=range(SEC)):
    return route(value, lambda s, g, x, y: (s, 1 - g, x, y) if s in sections else None)


def plane_route(value, by, first, sections=range(SEC)):
    def target_of(s, g, x, y):
        if s not in sections:
            return None
        if (g == 0) == first:
            return (s, g, (x + by) % NX, y)
        return (s, g, x, (y + by) % NY)

    return route(value, target_of)


def after(value, earlier):
    return lax.optimization_barrier((value, earlier))[0]


def row_block(values, block, count):
    size = values.shape[0] // count
    return lax.dynamic_slice_in_dim(values, block * size, size, 0)


def plane_first(mine, sections=range(SEC)):
    return [mine[0]] + [plane_route(mine[by], by, True, sections) for by in TURNS]


def plane_sum(pieces):
    total = pieces[0].astype(WIDE)
    for piece in pieces[1:]:
        total = total + piece.astype(WIDE)
    return total.astype(LOW)


def plane_second(pieces, second, sections=range(SEC)):
    total = plane_sum(pieces)
    return [row_block(total, second, 4)] + [
        plane_route(row_block(total, (second + by) % 4, 4), by, False, sections) for by in TURNS
    ]


def group_exchange(values, first):
    number = lambda s, g, x, y: (s * GRP + g) * NX * NY + x * NY + y
    groups = []
    for s in range(SEC):
        for g in range(GRP):
            along_x = (g == 0) == first
            for at in range(4):
                groups.append(
                    [number(s, g, i, at) if along_x else number(s, g, at, i) for i in range(4)]
                )
    return lax.all_to_all(values, ALL, 0, 0, axis_index_groups=groups, tiled=True)


def section_exchange(values):
    return lax.all_to_all(values, "section", 0, 0, tiled=True)


def plans(micro, vocab_part):
    last = SEC - 1
    steps = micro + 2 * last
    table = np.zeros((SEC, 6 * steps + 2), np.int32)
    for s in range(SEC):
        for way in range(2):
            depth = s if way == 0 else last - s
            for step in range(steps):
                at = step - 2 * depth
                if 0 <= at < micro:
                    sources = ([0] if step < micro else []) + [
                        d + 1 for d in range(last) if 0 <= step - 2 - 2 * d < micro
                    ]
                    spot = 3 * (way * steps + step)
                    table[s, spot : spot + 3] = (1 + s % 2, at, sources.index(depth))
        table[s, 6 * steps :] = (s * vocab_part, s)
    return table


def local(
    token_ids,
    segment_ids,
    noise_input,
    embed_table,
    input_proj,
    norm_gain,
    lead_weight,
    down_weight,
    final_gain,
    readout_proj,
    head_table,
):
    section = lax.axis_index("section")
    core = lax.axis_index("group")
    row = lax.axis_index("row")
    x_at, y_at = row // NY, row % NY
    first_at = jnp.where(core == 0, x_at, y_at)
    micro, _, tokens = token_ids.shape
    width = input_proj.shape[1]
    hidden = lead_weight.shape[2]
    half_rows = down_weight.shape[1]
    emb_part = input_proj.shape[0]
    vocab_part, emb = head_table.shape
    vocab = embed_table.shape[0]
    all_tokens = micro * tokens
    last = SEC - 1
    gain_half = norm_gain.astype(WIDE)
    lead = lead_weight[0]
    own_down = down_weight[0]
    seg_row = segment_ids
    flat_ids = token_ids.reshape(-1)

    plan = plans(micro, vocab_part)
    steps = micro + 2 * last
    table = lax.dynamic_index_in_dim(jnp.asarray(plan), section, 0, False)
    flat_ids = after(flat_ids, table)
    where_start = jnp.stack((first_at, core)).astype(jnp.int32)
    to_first = lambda v: [v] + [link(v, s, 0) for s in range(1, SEC)]
    eighth = row_block(row_block(own_down, core, 2), first_at, 4)
    eighth = jnp.where(section == 1, link(eighth, 0, 1), link(eighth, 2, 3))
    noise = noise_input[:, 0].transpose(2, 0, 1).reshape(emb_part, -1)
    own_embedded = lookup(flat_ids[None], embed_table.T, noise, 3200)
    parts = to_first(jnp.concatenate((own_embedded, input_proj), axis=1))
    embedded = jnp.concatenate([part[:, :all_tokens] for part in parts])
    input_full = jnp.concatenate([part[:, all_tokens:] for part in parts])
    first_in = matmul_tn(embedded, input_full).astype(LOW).reshape(micro, tokens, width)
    odd = (1, 3)
    eighth = after(eighth, first_in)
    eighths = [eighth] + [plane_route(eighth, by, True, odd) for by in (1, 2, 3)]

    kept = empty(
        ((micro, tokens, width), LOW),
        ((micro, tokens, width), LOW),
        ((micro, tokens, hidden), LOW),
        ((micro, tokens, hidden), WIDE),
    )

    def sources(first, step, hops, order):
        arrived = [hops[step - 2, s] for s in order if (step - 2, s) in hops]
        return ([first[step]] if step < micro else []) + arrived

    outs, hops = [], {}
    for step in range(steps):
        out, *kept = forward_stage(
            3 * step,
            table,
            sources(first_in, step, hops, range(SEC)),
            seg_row,
            gain_half,
            held_lead if step > 0 else lead,
            held_down if step > 1 else None,
            kept,
            step == 0,
        )
        if step == 0:
            held_lead = kept.pop()
            upper = upper_half(where_start, [after(part, out) for part in eighths])
            held_down = hold_down(where_start, upper, swap_cores(upper, odd), own_down)
        outs.append(out)
        for s in range(last):
            if 0 <= step - 2 * s < micro:
                ready = after(out, hops[step - 1, s]) if (step - 1, s) in hops else out
                hops[step, s] = link(ready, s, s + 1)
        if step == 2:
            readout_own = after(readout_proj.T, out)
            readout_full = jnp.concatenate(
                [link(readout_own, s, last) for s in range(last)] + [readout_own]
            )
    entries, normeds, saved, inner = kept

    final_rows = jnp.concatenate(outs[2 * last :]).astype(WIDE)
    normed_f, factor_f = layer_norm(final_rows)
    gain_f = final_gain.astype(WIDE)
    final_low = (normed_f * gain_f).astype(LOW)
    readout = matmul_nt(final_low, readout_full).astype(LOW)
    sent = [link(readout, last, s) for s in range(last)]
    readout, peak, total = head_stats(6 * steps + 1, table, sent + [readout], head_table, 2000)
    stats = jnp.concatenate((peak, total))
    all_stats = section_exchange(jnp.tile(stats, (SEC, 1))).reshape(SEC, 2, all_tokens)
    peak = jnp.max(all_stats[:, 0], axis=0)
    total = jnp.sum(all_stats[:, 1] * jnp.exp(all_stats[:, 0] - peak), axis=0)
    logsum = (peak + jnp.log(total))[None]
    head_grad, grad_readout = head_grads(
        6 * steps, table, readout, head_table, logsum, flat_ids[None]
    )
    grad_low = grad_readout.astype(LOW)
    for s in range(last):
        grad_readout = grad_readout + link(grad_low, s, last).astype(WIDE)
    grad_readout = grad_readout.astype(LOW)
    head_grad = lax.psum_scatter(head_grad, "row", scatter_dimension=0)
    readout_grad = matmul_tn(final_low, grad_readout)
    grad_final = matmul(grad_readout, readout_full)
    final_gain_grad = jnp.sum(grad_final * normed_f, axis=0)
    last_grads = norm_back(grad_final * gain_f, normed_f, factor_f).astype(LOW)
    last_grads = last_grads.reshape(micro, tokens, width)

    lead_turned = turned(6 * steps + 1, table, after(lead, grad_low), 0)
    down_turned = turned(6 * steps + 1, table, after(held_down, grad_low), 1)
    totals = empty(
        ((micro, tokens, width), LOW),
        ((micro, tokens, hidden), LOW),
        ((micro, 8, width), WIDE),
    )
    outs, hops = [], {}
    for step in range(steps):
        out, *totals = backward_stage(
            3 * (steps + step),
            table,
            sources(last_grads, step, hops, range(SEC - 1, -1, -1)),
            seg_row,
            gain_half,
            lead_turned,
            down_turned,
            entries,
            saved,
            inner,
            totals,
        )
        outs.append(out)
        for s in range(1, SEC):
            if 0 <= step - 2 * (last - s) < micro:
                ready = after(out, hops[step - 1, s]) if (step - 1, s) in hops else out
                hops[step, s] = link(ready, s, s - 1)
    section, core, row, readout_grad, final_gain_grad = lax.optimization_barrier(
        (section, core, row, readout_grad, final_gain_grad, out)
    )[:5]
    x_at, y_at = row // NY, row % NY
    first_at, second_at = jnp.where(core == 0, x_at, y_at), jnp.where(core == 0, y_at, x_at)
    is_mlp = section % 2 == 1

    first_grads = jnp.concatenate(outs[2 * last :])
    noise_grad = matmul_nt(input_full, first_grads).astype(LOW)
    pieces = noise_grad.reshape(SEC, emb_part, all_tokens)
    sent = [link(pieces[s], 0, s) for s in range(1, SEC)]

    grad_nexts, grads, gain_grads = totals
    flat = lambda v: v.reshape(all_tokens, v.shape[-1])
    grads = after(grads, head_grad)
    normed, grad_nexts, grads, saved = flat(normeds), flat(grad_nexts), flat(grads), flat(saved)
    role = jnp.where(is_mlp, 2, 1)
    where_other = jnp.stack((role, 1 - core, second_at)).astype(jnp.int32)
    where_mine = jnp.stack((role, core, first_at)).astype(jnp.int32)
    both = lambda mine, other: jnp.where(
        core == 0,
        jnp.concatenate((mine, other), axis=1),
        jnp.concatenate((other, mine), axis=1),
    )
    down_got = swap_cores(down_grad(where_other, saved, grad_nexts)[0], odd)
    lead_other = lead_grad(where_other, normed, saved, grads)[0]
    lead_got = swap_cores(lead_other)
    down_mine = down_grad(after(where_mine, lead_other), saved, grad_nexts, down_got)
    down_first = plane_first(down_mine, odd)
    late_ids = after(flat_ids, down_mine)[None]
    packed, noise_wide = noise_pack(6 * steps + 1, table, late_ids, [pieces[0]] + sent)

    lead_mine = lead_grad(after(where_mine, packed), normed, saved, grads, lead_got)
    lead_first = plane_first(lead_mine)
    first_grads, gain_grads, readout_grad, final_gain_grad = after(
        (first_grads, gain_grads, readout_grad, final_gain_grad), lead_mine
    )
    gain_grad = jnp.sum(gain_grads[:, 0], axis=0)
    input_grad = matmul(embedded, first_grads).reshape(SEC, 16, 4, width)
    input_grad = input_grad.transpose(1, 0, 2, 3).reshape(16, 16, width)
    readout_grad = readout_grad.reshape(16, 16, width)
    vectors = jnp.concatenate(
        (
            gain_grad.reshape(16, 64),
            final_gain_grad.reshape(SEC, 16, 16).transpose(1, 0, 2).reshape(16, 64),
            jnp.zeros((16, width - 128), WIDE),
        ),
        axis=1,
    )
    small = jnp.concatenate(
        (
            jnp.where(section == 0, input_grad, readout_grad),
            vectors[:, None],
            jnp.zeros((16, 15, width), WIDE),
        ),
        axis=1,
    ).astype(LOW)
    half_of = lambda which: lax.dynamic_slice_in_dim(small, which * (width // 2), width // 2, 2)
    small = half_of(core).astype(WIDE) + swap_cores(half_of(1 - core)).astype(WIDE)
    small = small.astype(LOW).reshape(NX, NY, 32, width // 2)
    small = jnp.where(core == 0, small, small.swapaxes(0, 1)).reshape(4, NY * 32, width // 2)
    deep = emb_part + 16

    def exchange(blocks, packed, first):
        rows = blocks.shape[1]
        everywhere = jnp.broadcast_to(packed, (4,) + packed.shape)
        got = group_exchange(jnp.concatenate((blocks, everywhere), axis=1), first)
        return jnp.sum(got[:, :rows].astype(WIDE), axis=0).astype(LOW), got[:, rows:]

    packed = after(packed, lead_mine)
    down_first = after(down_first, lead_mine)
    small, packed = exchange(after(small, down_first), packed, True)
    small, packed = exchange(
        small.reshape(4, 32, width // 2), packed.reshape(4 * deep, all_tokens), False
    )
    packed = packed.reshape(16, deep, all_tokens)
    down_second = plane_second(after(down_first, packed), second_at, odd)
    lead_second = plane_second(after(lead_first, packed), second_at)
    packed_other = swap_cores(packed)
    small = both(small, swap_cores(small))
    embed_grad = embed_sum(
        (row * (vocab // 16)).reshape(1), packed, packed_other, emb_part, vocab // 16
    )
    down_part = plane_sum(after(down_second, embed_grad))
    lead_part = plane_sum(after(lead_second, embed_grad))
    noise_out = noise_wide.reshape(emb_part, micro, tokens).transpose(1, 2, 0)
    lead_out = both(lead_part, swap_cores(lead_part)).astype(WIDE)

    def first_target(s, g, x, y):
        if s % 2 == 0:
            return None
        return (s - 1, 0, x, y) if g == 0 else (s, 0, x, y)

    def second_target(s, g, x, y):
        return (s - 1, 1, x, y) if s % 2 == 1 and g == 0 else None

    to_core_0 = route(down_part, first_target)
    to_core_1 = route(down_part, second_target)
    down_out = jnp.where(
        core == 0, to_core_0, jnp.where(is_mlp, down_part, to_core_1)
    ).astype(WIDE)

    small = after(small, (lead_part, down_part))
    gain_out = small[16, :64].astype(WIDE)
    input_rows = small[:16].reshape(SEC, 4, width)
    readout_rows = small[:16].reshape(64, SEC, 64)
    final_rows = small[16, 64:128].reshape(SEC, 16)

    finals = jnp.pad(final_rows, ((0, 0), (0, width - 16)))[:, None]
    mine = jnp.where(
        section == 0, input_rows, readout_rows.transpose(1, 0, 2).reshape(SEC, 4, width)
    )
    shared = section_exchange(
        jnp.concatenate((mine, finals, jnp.zeros((SEC, 3, width), LOW)), axis=1)
    )
    input_out = shared[0, :4]
    readout_out = shared[last, :4].reshape(64, 64)
    final_out = shared[last, 4, :16]

    head_out = pair_sum(head_grad, swap_cores(head_grad), vocab_part // (NX * NY))
    return (
        noise_out[:, None],
        embed_grad.T,
        input_out.astype(WIDE),
        gain_out[None],
        lead_out[None],
        down_out[None],
        final_out.astype(WIDE),
        readout_out.astype(WIDE),
        head_out,
    )


def solution(mesh):
    in_specs = (
        P(None, ("group", "row"), None),
        P(None, ("group", "row"), None),
        P(None, ("group", "row"), None, "section"),
        P(None, "section"),
        P("section", None),
        P("section", None),
        P("section", None, None),
        P("section", None, None),
        P(),
        P(None, "section"),
        P("section", None),
    )
    out_specs = (
        P(None, ("group", "row"), None, "section"),
        P("row", "section"),
        P(("section", "row"), None),
        P("section", "row"),
        P("section", "row", None),
        P("section", "row", None),
        P(("section", "row")),
        P("row", "section"),
        P(("section", "row"), None),
    )
    return jax.shard_map(local, mesh=mesh, in_specs=in_specs, out_specs=out_specs, check_vma=False)
```

```python
import functools
import itertools

import jax
import jax.numpy as jnp
import numpy as np
from jax import lax
from jax.experimental import pallas as pl
from jax.experimental.pallas import tpu as pltpu
from jax.sharding import PartitionSpec as P

HEADS = 16
HEAD_SIZE = 64
LOW = jnp.bfloat16
WIDE = jnp.float32
EPSILON = 1e-05
MASKED = -1000000000.0
CHUNK = 1024
GELU_A = 0.7978845608028654
GELU_B = 0.044715
HBM_SPEC = pl.BlockSpec(memory_space=pltpu.HBM)
VMEM_SPEC = pl.BlockSpec(memory_space=pltpu.VMEM)
SMEM_SPEC = pl.BlockSpec(memory_space=pltpu.SMEM)


def matmul(former, latter):
    return jnp.dot(former, latter, preferred_element_type=WIDE)


def matmul_nt(former, latter):
    return lax.dot_general(
        former, latter, (((1,), (1,)), ((), ())), preferred_element_type=WIDE
    )


def matmul_tn(former, latter):
    return lax.dot_general(
        former, latter, (((0,), (0,)), ((), ())), preferred_element_type=WIDE
    )


def layer_norm(values):
    centre = jnp.mean(values, axis=-1, keepdims=True)
    centred = values - centre
    variance = jnp.mean(centred * centred, axis=-1, keepdims=True)
    factor = lax.rsqrt(variance + EPSILON)
    return (centred * factor, factor)


def norm_back(grad_normed, normed, factor):
    first_mean = jnp.mean(grad_normed, axis=-1, keepdims=True)
    second_mean = jnp.mean(grad_normed * normed, axis=-1, keepdims=True)
    return factor * (grad_normed - first_mean - normed * second_mean)


def gelu(v):
    return 0.5 * v * (1.0 + jnp.tanh(GELU_A * (v + GELU_B * (v * v * v))))


def gelu_slope(v):
    square = v * v
    bend = jnp.tanh(GELU_A * (v + GELU_B * (square * v)))
    return 0.5 * (1.0 + bend) + 0.5 * v * (1.0 - bend * bend) * (
        GELU_A * (1.0 + 3.0 * GELU_B * square)
    )


def head_probs(scores, same):
    scores = jnp.where(same, scores * HEAD_SIZE ** (-0.5), MASKED)
    expo = jnp.exp(scores - jnp.max(scores, axis=-1, keepdims=True))
    return expo * (1.0 / jnp.sum(expo, axis=-1, keepdims=True))


def same_segment(row):
    across = jnp.broadcast_to(row.astype(WIDE), (row.shape[1], row.shape[1]))
    return across.T == across


def lanes(at, size):
    return pl.ds(pl.multiple_of(at, 128), size)


def turn_kernel(spot, live, plan_ref, value_ref, out_ref):
    @pl.when(jnp.bitwise_and(plan_ref[spot], 1) >= live)
    def _():
        out_ref[...] = value_ref[...].T


def turned(spot, plan, value, live):
    rows, columns = value.shape
    if rows > columns:
        tile = rows // 16
        blocks = (pl.BlockSpec((tile, columns), lambda i: (i, 0)), pl.BlockSpec((columns, tile), lambda i: (0, i)))
    else:
        tile = columns // 16
        blocks = (pl.BlockSpec((rows, tile), lambda i: (0, i)), pl.BlockSpec((tile, rows), lambda i: (i, 0)))
    return pl.pallas_call(
        functools.partial(turn_kernel, spot, live),
        out_shape=pltpu.VMEM((columns, rows), LOW),
        grid=(16,),
        in_specs=[SMEM_SPEC, blocks[0]],
        out_specs=blocks[1],
        compiler_params=pltpu.CompilerParams(vmem_limit_bytes=12 << 20),
        cost_estimate=pl.CostEstimate(flops=0, bytes_accessed=1024, transcendentals=0),
        name="turned",
    )(plan, far(value))


def chosen(choice, candidates, buffer):
    for at, candidate in enumerate(candidates):

        @pl.when(choice == at)
        def _():
            buffer[...] = candidate[...]


def forward_kernel(spot, with_down, loads, count, *refs):
    table_ref, candidates, refs = refs[0], refs[1 : 1 + count], refs[1 + count :]
    if not with_down:
        refs = refs[:3] + (None,) + refs[3:]
    source_ref = load_sems = None
    if loads:
        source_ref, load_sems = refs[2], refs[-1]
        refs = refs[:2] + (refs[13],) + refs[3:13] + refs[14:-1]
    forward_body(spot, table_ref, candidates, source_ref, load_sems, *refs)


def forward_body(
    spot,
    table_ref,
    candidates,
    source_ref,
    load_sems,
    seg_row_ref,
    gain_ref,
    lead_ref,
    down_ref,
    entries_in,
    normeds_in,
    saved_in,
    inner_in,
    out_ref,
    entries_ref,
    normeds_ref,
    saved_ref,
    inner_ref,
    normed_buf,
    saved_buf,
    inner_buf,
    result_buf,
    scores_buf,
    probs_buf,
    entry_ref,
    out_sems,
):
    role, slot = table_ref[spot], table_ref[spot + 1]
    tokens, width = entry_ref.shape
    keeps = [
        pltpu.make_async_copy(entry_ref, entries_ref.at[slot], out_sems.at[0]),
        pltpu.make_async_copy(normed_buf, normeds_ref.at[slot], out_sems.at[1]),
        pltpu.make_async_copy(saved_buf, saved_ref.at[slot], out_sems.at[2]),
    ]
    keep_inner = pltpu.make_async_copy(inner_buf, inner_ref.at[slot], out_sems.at[3])

    def load(j):
        at = lanes(j * CHUNK, CHUNK)
        return pltpu.make_async_copy(source_ref.at[:, at], lead_ref.at[:, at], load_sems.at[j])

    def loaded(j):
        if source_ref is not None:
            load(j).wait()

    if source_ref is not None:
        for j in range(lead_ref.shape[1] // CHUNK):
            load(j).start()

        @pl.when(role != 1)
        def _():
            pl.loop(0, lead_ref.shape[1] // CHUNK)(loaded)

    @pl.when(role > 0)
    def _():
        chosen(table_ref[spot + 2], candidates, entry_ref)
        normed, _ = layer_norm(entry_ref[...].astype(WIDE))
        normed_buf[...] = (normed * gain_ref[...]).astype(LOW)
        keeps[0].start()
        keeps[1].start()

    @pl.when(role == 1)
    def _():
        @pl.loop(0, 3 * width // CHUNK, unroll=3)
        def _(j):
            at = lanes(j * CHUNK, CHUNK)
            loaded(j)
            saved_buf[:, at] = matmul(normed_buf[...], lead_ref[:, at]).astype(LOW)

        left = lax.broadcasted_iota(jnp.int32, (tokens, 128), 1) < HEAD_SIZE
        zero = jnp.zeros((tokens, 128), LOW)

        @pl.loop(0, HEADS // 8, unroll=2)
        def _(group):
            for pair in range(4):
                at = group * 512 + pair * 128
                query = saved_buf[:, lanes(at, 128)]
                key = saved_buf[:, lanes(width + at, 128)]
                scores_buf[group * 8 + 2 * pair] = matmul_nt(jnp.where(left, query, zero), key)
                scores_buf[group * 8 + 2 * pair + 1] = matmul_nt(jnp.where(left, zero, query), key)

        @pl.loop(0, HEADS // 4, unroll=2)
        def _(group):
            same = same_segment(seg_row_ref[slot])
            for head in range(4):
                at = group * 4 + head
                probs_buf[at] = head_probs(scores_buf[at], same).astype(LOW)

        @pl.loop(0, HEADS // 8, unroll=2)
        def _(group):
            for pair in range(4):
                at = group * 512 + pair * 128
                value = saved_buf[:, lanes(2 * width + at, 128)]
                mixed = jnp.where(
                    left,
                    matmul(probs_buf[group * 8 + 2 * pair], value),
                    matmul(probs_buf[group * 8 + 2 * pair + 1], value),
                )
                saved_buf[:, lanes(3 * width + at, 128)] = mixed.astype(LOW)

        keeps[2].start()

        @pl.loop(0, width // CHUNK)
        def _(j):
            at = lanes(j * CHUNK, CHUNK)
            loaded(3 * width // CHUNK + j)
            term = matmul(saved_buf[:, 3 * width :], lead_ref[:, lanes(3 * width + j * CHUNK, CHUNK)])
            out_ref[:, at] = (entry_ref[:, at].astype(WIDE) + term).astype(LOW)

    def feed_forward():
        result_buf[...] = entry_ref[...].astype(WIDE)

        @pl.loop(0, lead_ref.shape[1] // CHUNK, unroll=4)
        def _(j):
            at = lanes(j * CHUNK, CHUNK)
            inner = matmul(normed_buf[...], lead_ref[:, at])
            inner_buf[:, at] = inner
            active = gelu(inner).astype(LOW)
            saved_buf[:, at] = active
            result_buf[...] += matmul(active, down_ref[pl.ds(j * CHUNK, CHUNK), :])

        keeps[2].start()
        keep_inner.start()
        out_ref[...] = result_buf[...].astype(LOW)
        keep_inner.wait()

    if down_ref is not None:
        pl.when(role == 2)(feed_forward)

    @pl.when(role > 0)
    def _():
        for keep in keeps:
            keep.wait()


def pinned(value):
    return pltpu.with_memory_space_constraint(value, pltpu.VMEM)


def far(value):
    return pltpu.with_memory_space_constraint(value, pltpu.HBM)


def forward_stage(spot, table, entries, seg_row, gain, lead, down, kept, loads=False):
    tokens, width = entries[0].shape
    hidden = lead.shape[1]
    count = len(entries) + (3 if down is None else 4)
    given = [VMEM_SPEC] * (len(entries) + 2) + [HBM_SPEC if loads else VMEM_SPEC]
    return pl.pallas_call(
        functools.partial(forward_kernel, spot, down is not None, loads, len(entries)),
        out_shape=[jax.ShapeDtypeStruct((tokens, width), LOW)]
        + [jax.ShapeDtypeStruct(k.shape, k.dtype) for k in kept]
        + ([pltpu.VMEM(lead.shape, LOW)] if loads else []),
        in_specs=[SMEM_SPEC] + given + [VMEM_SPEC] * (down is not None) + [HBM_SPEC] * 4,
        out_specs=[VMEM_SPEC] + [HBM_SPEC] * 4 + [VMEM_SPEC] * loads,
        scratch_shapes=[
            pltpu.VMEM((tokens, width), LOW),
            pltpu.VMEM((tokens, hidden), LOW),
            pltpu.VMEM((tokens, hidden), WIDE),
            pltpu.VMEM((tokens, width), WIDE),
            pltpu.VMEM((HEADS, tokens, tokens), WIDE),
            pltpu.VMEM((HEADS, tokens, tokens), LOW),
            pltpu.VMEM((tokens, width), LOW),
            pltpu.SemaphoreType.DMA((4,)),
        ]
        + ([pltpu.SemaphoreType.DMA((hidden // CHUNK,))] if loads else []),
        input_output_aliases={count + 1 + i: 1 + i for i in range(4)},
        compiler_params=pltpu.CompilerParams(vmem_limit_bytes=18 << 20),
        cost_estimate=pl.CostEstimate(
            flops=4 * tokens * width * hidden, bytes_accessed=20 << 20, transcendentals=0
        ),
        name="forward_stage",
    )(
        table,
        *entries,
        seg_row,
        gain,
        (far if loads else pinned)(lead),
        *([pinned(down)] if down is not None else []),
        *map(far, kept),
    )


def backward_kernel(spot, count, *refs):
    backward_body(spot, refs[0], refs[1 : 1 + count], *refs[1 + count :])


def backward_body(
    spot,
    table_ref,
    candidates,
    seg_row_ref,
    gain_ref,
    lead_ref,
    down_ref,
    entries_ref,
    saved_ref,
    inner_ref,
    nexts_in,
    grads_in,
    gains_in,
    out_ref,
    nexts_ref,
    grads_ref,
    gains_ref,
    saved_buf,
    inner_buf,
    grads_buf,
    mixed_buf,
    gain_buf,
    entry_buf,
    normed_buf,
    scores_buf,
    probs_grad_buf,
    probs_buf,
    scores_grad_buf,
    grad_ref,
    in_sems,
    out_sems,
):
    role, slot = table_ref[spot], table_ref[spot + 1]
    tokens, width = grad_ref.shape
    bring_saved = pltpu.make_async_copy(saved_ref.at[slot], saved_buf, in_sems.at[0])
    bring_inner = pltpu.make_async_copy(inner_ref.at[slot], inner_buf, in_sems.at[1])
    bring_entry = pltpu.make_async_copy(entries_ref.at[slot], entry_buf, in_sems.at[2])
    keep_next = pltpu.make_async_copy(grad_ref, nexts_ref.at[slot], out_sems.at[0])
    keep_grads = pltpu.make_async_copy(grads_buf, grads_ref.at[slot], out_sems.at[1])
    keep_gain = pltpu.make_async_copy(gain_buf, gains_ref.at[slot], out_sems.at[2])

    @pl.when(role == 2)
    def _():
        bring_inner.start()

    @pl.when(role == 1)
    def _():
        bring_saved.start()

    @pl.when(role > 0)
    def _():
        bring_entry.start()
        chosen(table_ref[spot + 2], candidates, grad_ref)
        keep_next.start()
        normed_buf[...] = jnp.zeros_like(normed_buf)

    @pl.when(role == 1)
    def _():
        grads_buf[:, 3 * width :] = grad_ref[...]
        mixed_buf[...] = matmul(grad_ref[...], lead_ref[3 * width :, :]).astype(LOW)
        bring_saved.wait()
        left = lax.broadcasted_iota(jnp.int32, (tokens, 128), 1) < HEAD_SIZE
        zero = jnp.zeros((tokens, 128), LOW)
        scale = HEAD_SIZE ** (-0.5)

        @pl.loop(0, HEADS // 8, unroll=2)
        def _(group):
            for pair in range(4):
                at = group * 512 + pair * 128
                query = saved_buf[:, lanes(at, 128)]
                key = saved_buf[:, lanes(width + at, 128)]
                value = saved_buf[:, lanes(2 * width + at, 128)]
                grad = mixed_buf[:, lanes(at, 128)]
                for own in (0, 1):
                    mine = lambda v: jnp.where(left, v, zero) if own == 0 else jnp.where(left, zero, v)
                    scores_buf[group * 8 + 2 * pair + own] = matmul_nt(mine(query), key)
                    probs_grad_buf[group * 8 + 2 * pair + own] = matmul_nt(mine(grad), value)

        @pl.loop(0, HEADS // 4, unroll=2)
        def _(group):
            same = same_segment(seg_row_ref[slot])
            for head in range(4):
                at = group * 4 + head
                probs = head_probs(scores_buf[at], same)
                probs_buf[at] = probs.astype(LOW)
                grad_probs = probs_grad_buf[at]
                scores_grad_buf[at] = (
                    probs * (grad_probs - jnp.sum(probs * grad_probs, axis=-1, keepdims=True))
                ).astype(LOW)

        @pl.loop(0, HEADS // 4, unroll=2)
        def _(group):
            for pair in range(2):
                at = group * 256 + pair * 128
                query = saved_buf[:, lanes(at, 128)]
                key = saved_buf[:, lanes(width + at, 128)]
                grad = mixed_buf[:, lanes(at, 128)]
                parts = []
                for own in (0, 1):
                    probs = probs_buf[group * 4 + 2 * pair + own]
                    grad_low = scores_grad_buf[group * 4 + 2 * pair + own]
                    parts.append(
                        (
                            matmul(grad_low, key) * scale,
                            matmul_tn(grad_low, query) * scale,
                            matmul_tn(probs, grad),
                        )
                    )
                for which in range(3):
                    grads_buf[:, lanes(which * width + at, 128)] = jnp.where(
                        left, parts[0][which], parts[1][which]
                    ).astype(LOW)

        @pl.loop(0, 3 * width // CHUNK, unroll=3)
        def _(j):
            at = lanes(j * CHUNK, CHUNK)
            normed_buf[...] += matmul(grads_buf[:, at], lead_ref[pl.ds(j * CHUNK, CHUNK), :])

    @pl.when(role == 2)
    def _():
        bring_inner.wait()

        @pl.loop(0, lead_ref.shape[0] // CHUNK, unroll=4)
        def _(j):
            at = lanes(j * CHUNK, CHUNK)
            grad_active = matmul(grad_ref[...], down_ref[:, at])
            grads = (gelu_slope(inner_buf[:, at]) * grad_active).astype(LOW)
            grads_buf[:, at] = grads
            normed_buf[...] += matmul(grads, lead_ref[pl.ds(j * CHUNK, CHUNK), :])

    @pl.when(role > 0)
    def _():
        keep_grads.start()
        bring_entry.wait()
        grad_normed = normed_buf[...]
        normed, factor = layer_norm(entry_buf[...].astype(WIDE))
        gain_buf[...] = jnp.broadcast_to(
            jnp.sum(grad_normed * normed, axis=0, keepdims=True), gain_buf.shape
        )
        keep_gain.start()
        out_ref[...] = (
            grad_ref[...].astype(WIDE) + norm_back(grad_normed * gain_ref[...], normed, factor)
        ).astype(LOW)
        keep_next.wait()
        keep_grads.wait()
        keep_gain.wait()


def backward_stage(
    spot, table, nexts, seg_row, gain, lead, down, entries, saved, inner, totals
):
    tokens, width = nexts[0].shape
    count = len(nexts)
    hidden = lead.shape[0]
    return pl.pallas_call(
        functools.partial(backward_kernel, spot, count),
        out_shape=[jax.ShapeDtypeStruct((tokens, width), LOW)]
        + [jax.ShapeDtypeStruct(k.shape, k.dtype) for k in totals],
        in_specs=[SMEM_SPEC] + [VMEM_SPEC] * (count + 4) + [HBM_SPEC] * 6,
        out_specs=[VMEM_SPEC] + [HBM_SPEC] * 3,
        scratch_shapes=[
            pltpu.VMEM((tokens, hidden), LOW),
            pltpu.VMEM((tokens, hidden), WIDE),
            pltpu.VMEM((tokens, hidden), LOW),
            pltpu.VMEM((tokens, width), LOW),
            pltpu.VMEM((8, width), WIDE),
            pltpu.VMEM((tokens, width), LOW),
            pltpu.VMEM((tokens, width), WIDE),
            pltpu.VMEM((HEADS, tokens, tokens), WIDE),
            pltpu.VMEM((HEADS, tokens, tokens), WIDE),
            pltpu.VMEM((HEADS, tokens, tokens), LOW),
            pltpu.VMEM((HEADS, tokens, tokens), LOW),
            pltpu.VMEM((tokens, width), LOW),
            pltpu.SemaphoreType.DMA((3,)),
            pltpu.SemaphoreType.DMA((3,)),
        ],
        input_output_aliases={count + 8 + i: 1 + i for i in range(3)},
        compiler_params=pltpu.CompilerParams(vmem_limit_bytes=18 << 20),
        cost_estimate=pl.CostEstimate(
            flops=4 * tokens * width * hidden, bytes_accessed=20 << 20, transcendentals=0
        ),
        name="backward_stage",
    )(
        table,
        *nexts,
        seg_row,
        gain,
        pinned(lead),
        pinned(down),
        far(entries),
        far(saved),
        far(inner),
        *map(far, totals),
    )


def stats_kernel(spot, plan_ref, *refs):
    candidates, (table_ref, readout_ref, peak_ref, total_ref) = refs[:-4], refs[-4:]
    step = pl.program_id(0)

    @pl.when(step == 0)
    def _():
        chosen(plan_ref[spot], candidates, readout_ref)

    logits = matmul_nt(table_ref[...], readout_ref[...])
    own_peak = jnp.max(logits, axis=0, keepdims=True)
    own_total = lambda peak: jnp.sum(jnp.exp(logits - peak), axis=0, keepdims=True)

    @pl.when(step == 0)
    def _():
        peak_ref[...] = own_peak
        total_ref[...] = own_total(own_peak)

    @pl.when(step > 0)
    def _():
        peak = jnp.maximum(peak_ref[...], own_peak)
        total_ref[...] = total_ref[...] * jnp.exp(peak_ref[...] - peak) + own_total(peak)
        peak_ref[...] = peak


def head_stats(spot, plan, readouts, table, tile):
    tokens, emb = readouts[0].shape
    vocab = table.shape[0]
    whole = pl.BlockSpec((1, tokens), lambda i: (0, 0))
    rows = pl.BlockSpec((tokens, emb), lambda i: (0, 0))
    return pl.pallas_call(
        functools.partial(stats_kernel, spot),
        out_shape=[jax.ShapeDtypeStruct((tokens, emb), LOW)]
        + [jax.ShapeDtypeStruct((1, tokens), WIDE)] * 2,
        grid=(vocab // tile,),
        in_specs=[SMEM_SPEC]
        + [rows] * len(readouts)
        + [pl.BlockSpec((tile, emb), lambda i: (i, 0))],
        out_specs=[rows, whole, whole],
        compiler_params=pltpu.CompilerParams(vmem_limit_bytes=32 << 20),
        cost_estimate=pl.CostEstimate(
            flops=2 * tokens * vocab * emb, bytes_accessed=5 << 20, transcendentals=tokens * vocab
        ),
        name="head_stats",
    )(plan, *readouts, far(table))


def head_kernel(spot, table_base_ref, readout_ref, table_ref, logsum_ref, ids_ref, head_ref, grad_ref):
    tile = table_ref.shape[0]
    logits = matmul_nt(table_ref[...], readout_ref[...])
    ids = ids_ref[...] - (table_base_ref[spot] + pl.program_id(0) * tile)
    hits = lax.broadcasted_iota(jnp.int32, logits.shape, 0) == ids
    probs = jnp.exp(logits - logsum_ref[...])
    grads = jnp.where(hits, probs - 1.0, probs).astype(LOW)
    head = matmul(grads, readout_ref[...])
    unit = tile // 4
    for shard in range(4):
        head_ref[shard, :unit] = head[shard * unit : (shard + 1) * unit].astype(LOW)
    term = matmul_tn(grads, table_ref[...])

    @pl.when(pl.program_id(0) == 0)
    def _():
        grad_ref[...] = term

    @pl.when(pl.program_id(0) > 0)
    def _():
        grad_ref[...] += term


def head_grads(spot, base, readout, table, logsum, ids):
    tokens, emb = readout.shape
    vocab = table.shape[0]
    row = pl.BlockSpec((1, tokens), lambda i: (0, 0))
    whole = pl.BlockSpec((tokens, emb), lambda i: (0, 0))
    part = pl.BlockSpec((vocab // 4, emb), lambda i: (i, 0))
    return pl.pallas_call(
        functools.partial(head_kernel, spot),
        out_shape=[
            pltpu.HBM((16, 512, emb), LOW),
            jax.ShapeDtypeStruct((tokens, emb), WIDE),
        ],
        grid=(4,),
        in_specs=[SMEM_SPEC, whole, part, row, row],
        out_specs=[pl.BlockSpec((4, 512, emb), lambda i: (i, 0, 0)), whole],
        compiler_params=pltpu.CompilerParams(vmem_limit_bytes=32 << 20),
        cost_estimate=pl.CostEstimate(
            flops=6 * tokens * vocab * emb, bytes_accessed=9 << 20, transcendentals=tokens * vocab
        ),
        name="head_grads",
    )(base, readout, far(table), logsum, ids)


def pair_kernel(former_ref, latter_ref, out_ref):
    rows = out_ref.shape[0]
    out_ref[...] = former_ref[:rows].astype(WIDE) + latter_ref[:rows].astype(WIDE)


def pair_sum(former, latter, rows):
    return pl.pallas_call(
        pair_kernel,
        out_shape=jax.ShapeDtypeStruct((rows, former.shape[1]), WIDE),
        in_specs=[VMEM_SPEC] * 2,
        out_specs=VMEM_SPEC,
        compiler_params=pltpu.CompilerParams(vmem_limit_bytes=8 << 20),
        cost_estimate=pl.CostEstimate(flops=0, bytes_accessed=1024, transcendentals=0),
        name="pair_sum",
    )(former, latter)


def lookup_kernel(ids_ref, table_ref, noise_ref, out_ref, total_ref, low_ref):
    step = pl.program_id(0)
    parts, tile = table_ref.shape
    tokens = ids_ref.shape[1]
    blocks = tile // 128

    @pl.when(step == 0)
    def _():
        lane = jnp.bitwise_and(ids_ref[...], 127)
        hits = lax.broadcasted_iota(jnp.int32, (128, tokens), 0) == lane
        low_ref[...] = jnp.where(hits, 1.0, 0.0).astype(LOW)
        total_ref[...] = noise_ref[...].astype(WIDE)

    stacked = jnp.concatenate(
        [table_ref[:, block * 128 : (block + 1) * 128] for block in range(blocks)]
    )
    found = matmul(stacked, low_ref[...])
    own = jnp.right_shift(ids_ref[...], 7) - step * blocks
    total = jnp.zeros_like(total_ref)
    for block in range(blocks):
        total = jnp.where(own == block, found[block * parts : (block + 1) * parts], total)
    total_ref[...] += total

    @pl.when(step == pl.num_programs(0) - 1)
    def _():
        out_ref[...] = total_ref[...].astype(LOW)


def lookup(ids, table, noise, tile):
    parts, vocab = table.shape
    tokens = ids.shape[1]
    whole = pl.BlockSpec((parts, tokens), lambda i: (0, 0))
    return pl.pallas_call(
        lookup_kernel,
        out_shape=jax.ShapeDtypeStruct((parts, tokens), LOW),
        grid=(vocab // tile,),
        in_specs=[
            pl.BlockSpec((1, tokens), lambda i: (0, 0)),
            pl.BlockSpec((parts, tile), lambda i: (0, i)),
            whole,
        ],
        out_specs=whole,
        scratch_shapes=[pltpu.VMEM((parts, tokens), WIDE), pltpu.VMEM((128, tokens), LOW)],
        compiler_params=pltpu.CompilerParams(vmem_limit_bytes=32 << 20),
        cost_estimate=pl.CostEstimate(
            flops=2 * 128 * vocab * tokens, bytes_accessed=4 << 20, transcendentals=0
        ),
        name="lookup",
    )(ids, far(table), noise)


def lead_grad_kernel(where_ref, normed_ref, mixed_ref, grads_ref, *refs):
    got_ref, out_refs, (turned_ref, result_ref) = None, refs[:-2], refs[-2:]
    if len(out_refs) > 1:
        got_ref, out_refs = out_refs[0], out_refs[1:]
    role, half, spot = where_ref[0], where_ref[1], where_ref[2]
    step = pl.program_id(0)
    width = normed_ref.shape[1]
    steps = pl.num_programs(0)
    use_mixed = jnp.logical_and(role == 1, half == 1)

    @pl.when(step == 0)
    def _():
        turned_ref[...] = normed_ref[...].T

    @pl.when(jnp.logical_and(step == steps // 2, use_mixed))
    def _():
        turned_ref[...] = mixed_ref[...].T

    result_ref[...] = matmul(turned_ref[...], grads_ref[...])
    unit = width // 16

    def put(block, rows, part):
        if got_ref is not None:
            part = part + got_ref[block, rows, :].astype(WIDE)
        out_ref = out_refs[0].at[block] if got_ref is None else out_refs[block]
        out_ref[rows, :] = part.astype(LOW)

    @pl.when(half == 0)
    def _():
        for block in range(4):
            x = (spot + block) % 4
            put(block, slice(None), result_ref[pl.ds(pl.multiple_of(x * 4 * unit, 4 * unit), 4 * unit)])

    @pl.when(half == 1)
    def _():
        for block in range(4):
            y = (spot + block) % 4
            for x in range(4):
                rows = pl.ds(pl.multiple_of((4 * x + y) * unit, unit), unit)
                put(block, slice(x * unit, (x + 1) * unit), result_ref[rows])


CHEAP = pl.CostEstimate(flops=0, bytes_accessed=1024, transcendentals=0)


def lead_grad(where, normed, saved, grads, got=None):
    tokens, width = normed.shape
    tile = 1024
    whole = pl.BlockSpec((4, width // 4, tile), lambda i, where: (0, 0, i))
    block = pl.BlockSpec((width // 4, tile), lambda i, where: (0, i))
    shape = (width // 4, 2 * width)
    return pl.pallas_call(
        lead_grad_kernel,
        out_shape=[jax.ShapeDtypeStruct((4,) + shape, LOW)]
        if got is None
        else [jax.ShapeDtypeStruct(shape, LOW)] * 4,
        grid_spec=pltpu.PrefetchScalarGridSpec(
            num_scalar_prefetch=1,
            grid=(2 * width // tile,),
            in_specs=[
                pl.BlockSpec((tokens, width), lambda i, where: (0, 0)),
                pl.BlockSpec((tokens, width), lambda i, where: (0, 3)),
                pl.BlockSpec((tokens, tile), lambda i, where: (0, where[1] * (2 * width // tile) + i)),
            ]
            + ([] if got is None else [whole]),
            out_specs=[whole] if got is None else [block] * 4,
            scratch_shapes=[pltpu.VMEM((width, tokens), LOW), pltpu.VMEM((width, tile), WIDE)],
        ),
        compiler_params=pltpu.CompilerParams(vmem_limit_bytes=24 << 20),
        cost_estimate=CHEAP
        if got is None
        else pl.CostEstimate(
            flops=4 * tokens * width * width, bytes_accessed=12 << 20, transcendentals=0
        ),
        name="lead_grad",
    )(where, far(normed), far(saved), far(grads), *([] if got is None else [got]))


def down_grad_kernel(where_ref, saved_ref, nexts_ref, *refs):
    got_ref, out_refs, (buf_ref, got_buf, sems) = None, refs[:-3], refs[-3:]
    if len(out_refs) > 1:
        got_ref, out_refs = out_refs[0], out_refs[1:]
    role, half, spot = where_ref[0], where_ref[1], where_ref[2]
    at = pl.program_id(0)
    unit = saved_ref.shape[1] // 4

    @pl.when(role == 2)
    def _():
        if got_ref is not None:
            bring = pltpu.make_async_copy(got_ref, got_buf, sems.at[4])
            pl.when(at == 0)(bring.start)
        result = matmul_tn(saved_ref[...], nexts_ref[...])
        if got_ref is not None:
            pl.when(at == 0)(bring.wait)

        def put(block, rows, part):
            if got_ref is not None:
                part = part + got_buf[block, rows, :].astype(WIDE)
            buf_ref[block, rows, :] = part.astype(LOW)

        @pl.when(half == 0)
        def _():
            put((at - spot + 4) % 4, slice(None), result)

        @pl.when(half == 1)
        def _():
            rows = pl.ds(pl.multiple_of(at * unit, unit), unit)
            for y in range(4):
                put((y - spot + 4) % 4, rows, result[y * unit : (y + 1) * unit])

        @pl.when(at == pl.num_programs(0) - 1)
        def _():
            copies = [pltpu.make_async_copy(buf_ref, out_refs[0], sems.at[0])]
            if got_ref is not None:
                copies = [
                    pltpu.make_async_copy(buf_ref.at[block], out_ref, sems.at[block])
                    for block, out_ref in enumerate(out_refs)
                ]
            for copy in copies:
                copy.start()
            for copy in copies:
                copy.wait()


def down_grad(where, saved, nexts, got=None):
    tokens, hidden = saved.shape
    width = nexts.shape[1]
    rows = hidden // 8
    live = lambda where: jnp.where(where[0] == 2, 1, 0)
    return pl.pallas_call(
        down_grad_kernel,
        out_shape=[pltpu.HBM((4, rows, width), LOW)]
        if got is None
        else [pltpu.HBM((rows, width), LOW)] * 4,
        grid_spec=pltpu.PrefetchScalarGridSpec(
            num_scalar_prefetch=1,
            grid=(4,),
            in_specs=[
                pl.BlockSpec((tokens, rows), lambda i, where: (0, (where[1] * 4 + i) * live(where))),
                pl.BlockSpec((tokens, width), lambda i, where: (0, 0)),
            ]
            + ([] if got is None else [HBM_SPEC]),
            out_specs=[HBM_SPEC] * (1 if got is None else 4),
            scratch_shapes=[
                pltpu.VMEM((4, rows, width), LOW),
                pltpu.VMEM((4, 16, 128) if got is None else (4, rows, width), LOW),
                pltpu.SemaphoreType.DMA((5,)),
            ],
        ),
        compiler_params=pltpu.CompilerParams(vmem_limit_bytes=28 << 20),
        cost_estimate=CHEAP,
        name="down_grad",
    )(where, far(saved), far(nexts), *([] if got is None else [far(got)]))


def upper_kernel(where_ref, *refs):
    out_ref = refs[4]
    rows = refs[0].shape[0]
    for at, part in enumerate(refs[:4]):
        place = (where_ref[0] - at + 4) % 4
        out_ref[pl.ds(pl.multiple_of(place * rows, rows), rows), :] = part[...]


def upper_half(where, parts):
    rows, width = parts[0].shape
    return pl.pallas_call(
        upper_kernel,
        out_shape=jax.ShapeDtypeStruct((4 * rows, width), LOW),
        in_specs=[SMEM_SPEC] + [VMEM_SPEC] * 4,
        out_specs=VMEM_SPEC,
        compiler_params=pltpu.CompilerParams(vmem_limit_bytes=8 << 20),
        name="upper_half",
    )(where, *parts)


def hold_down_kernel(where_ref, mine_ref, other_ref, own_ref, out_ref, sems):
    rows = mine_ref.shape[0]
    core = where_ref[1]
    spot = lambda at: out_ref.at[pl.ds(pl.multiple_of(at * rows, rows), rows), :]
    copies = [
        pltpu.make_async_copy(mine_ref, spot(core), sems.at[0]),
        pltpu.make_async_copy(other_ref, spot(1 - core), sems.at[1]),
        pltpu.make_async_copy(own_ref, out_ref.at[pl.ds(2 * rows, 2 * rows), :], sems.at[2]),
    ]
    for copy in copies:
        copy.start()
    for copy in copies:
        copy.wait()


def hold_down(where, mine, other, own):
    rows, width = mine.shape
    return pl.pallas_call(
        hold_down_kernel,
        out_shape=pltpu.VMEM((4 * rows, width), LOW),
        in_specs=[SMEM_SPEC] + [VMEM_SPEC] * 2 + [HBM_SPEC],
        out_specs=VMEM_SPEC,
        scratch_shapes=[pltpu.SemaphoreType.DMA((3,))],
        compiler_params=pltpu.CompilerParams(vmem_limit_bytes=8 << 20),
        name="hold_down",
    )(where, mine, other, far(own))


def noise_kernel(spot, plan_ref, ids_ref, *refs):
    candidates, (packed_ref, noise_ref, buf_ref) = refs[:-3], refs[-3:]
    parts = noise_ref.shape[0]
    chosen(plan_ref[spot], candidates, buf_ref)
    packed_ref[:parts] = buf_ref[...]
    noise_ref[...] = buf_ref[...].astype(WIDE)
    ids = ids_ref[...]
    high = jnp.right_shift(ids, 8).astype(WIDE)
    low = jnp.bitwise_and(ids, 255).astype(WIDE)
    at = lax.broadcasted_iota(jnp.int32, (16, ids.shape[1]), 0)
    split = jnp.where(at == 0, high, jnp.where(at == 1, low, 0.0))
    packed_ref[parts:] = split.astype(LOW)


def noise_pack(spot, plan, ids, candidates):
    parts, tokens = candidates[0].shape
    return pl.pallas_call(
        functools.partial(noise_kernel, spot),
        out_shape=[
            jax.ShapeDtypeStruct((parts + 16, tokens), LOW),
            jax.ShapeDtypeStruct((parts, tokens), WIDE),
        ],
        in_specs=[SMEM_SPEC] + [VMEM_SPEC] * (1 + len(candidates)),
        out_specs=[VMEM_SPEC] * 2,
        scratch_shapes=[pltpu.VMEM((parts, tokens), LOW)],
        compiler_params=pltpu.CompilerParams(vmem_limit_bytes=8 << 20),
        cost_estimate=CHEAP,
        name="noise_pack",
    )(plan, ids, *candidates)


def embed_kernel(base_ref, mine_ref, other_ref, out_ref, total_ref):
    step = pl.program_id(0)
    steps = pl.num_programs(0)
    parts = out_ref.shape[0]
    blocks = total_ref.shape[0] // parts

    def add(gathered_ref):
        count, _, tokens = gathered_ref.shape
        term = None
        for at in range(count):
            split = gathered_ref[at, parts : parts + 16].astype(WIDE)
            ids = (split[0:1] * 256.0 + split[1:2]).astype(jnp.int32) - base_ref[0]
            lane = jnp.bitwise_and(ids, 127)
            hits = lax.broadcasted_iota(jnp.int32, (128, tokens), 0) == lane
            hits = jnp.where(hits, 1.0, 0.0).astype(LOW)
            own = jnp.right_shift(ids, 7)
            grads = gathered_ref[at, :parts]
            masked = jnp.concatenate(
                [grads * jnp.where(own == block, 1.0, 0.0).astype(LOW) for block in range(blocks)]
            )
            part = matmul_nt(masked, hits)
            term = part if term is None else term + part

        @pl.when(step == 0)
        def _():
            total_ref[...] = term

        @pl.when(step > 0)
        def _():
            total_ref[...] += term

    pl.when(step < steps // 2)(lambda: add(mine_ref))
    pl.when(step >= steps // 2)(lambda: add(other_ref))

    @pl.when(step == steps - 1)
    def _():
        rows = out_ref.shape[1]
        for block in range(blocks):
            size = min(128, rows - block * 128)
            out_ref[:, block * 128 : block * 128 + size] = total_ref[
                block * parts : (block + 1) * parts, :size
            ]


def embed_sum(base, mine, other, parts, rows):
    count, deep, tokens = mine.shape
    step = 4
    half = count // step
    blocks = -(-rows // 128)
    return pl.pallas_call(
        embed_kernel,
        out_shape=jax.ShapeDtypeStruct((parts, rows), WIDE),
        grid=(2 * half,),
        in_specs=[
            SMEM_SPEC,
            pl.BlockSpec((step, deep, tokens), lambda i: (jnp.minimum(i, half - 1), 0, 0)),
            pl.BlockSpec((step, deep, tokens), lambda i: (jnp.maximum(i - half, 0), 0, 0)),
        ],
        out_specs=pl.BlockSpec((parts, rows), lambda i: (0, 0)),
        scratch_shapes=[pltpu.VMEM((blocks * parts, 128), WIDE)],
        compiler_params=pltpu.CompilerParams(vmem_limit_bytes=32 << 20),
        cost_estimate=CHEAP,
        name="embed_sum",
    )(base, mine, other)


def empty(*kinds):
    return pl.pallas_call(
        lambda *refs: None,
        out_shape=[pltpu.HBM(shape, dtype) for shape, dtype in kinds],
        out_specs=[HBM_SPEC] * len(kinds),
        compiler_params=pltpu.CompilerParams(vmem_limit_bytes=1 << 20),
        name="empty",
    )()


ROW_LEN = 128
SEC, GRP, NX, NY = 4, 2, 4, 4
ALL = ("section", "group", "row")
TURNS = (1, 3, 2)


def route(value, target_of):
    number = lambda s, g, x, y: (s * GRP + g) * NX * NY + x * NY + y
    pairs = []
    for at in itertools.product(range(SEC), range(GRP), range(NX), range(NY)):
        target = target_of(*at)
        if target is not None:
            pairs.append((number(*at), number(*target)))
    return lax.ppermute(value, ALL, pairs)


def link(value, source, target):
    return route(value, lambda s, g, x, y: (target, g, x, y) if s == source else None)


def turn(value, by):
    return route(value, lambda s, g, x, y: ((s + by) % SEC, g, x, y))


def swap_cores(value, sections=range(SEC)):
    return route(value, lambda s, g, x, y: (s, 1 - g, x, y) if s in sections else None)


def plane_route(value, by, first, sections=range(SEC)):
    def target_of(s, g, x, y):
        if s not in sections:
            return None
        if (g == 0) == first:
            return (s, g, (x + by) % NX, y)
        return (s, g, x, (y + by) % NY)

    return route(value, target_of)


def after(value, earlier):
    return lax.optimization_barrier((value, earlier))[0]


def row_block(values, block, count):
    size = values.shape[0] // count
    return lax.dynamic_slice_in_dim(values, block * size, size, 0)


def plane_first(mine, sections=range(SEC)):
    return [mine[0]] + [plane_route(mine[by], by, True, sections) for by in TURNS]


def plane_sum(pieces):
    total = pieces[0].astype(WIDE)
    for piece in pieces[1:]:
        total = total + piece.astype(WIDE)
    return total.astype(LOW)


def plane_second(pieces, second, sections=range(SEC)):
    total = plane_sum(pieces)
    return [row_block(total, second, 4)] + [
        plane_route(row_block(total, (second + by) % 4, 4), by, False, sections) for by in TURNS
    ]


def group_exchange(values, first):
    number = lambda s, g, x, y: (s * GRP + g) * NX * NY + x * NY + y
    groups = []
    for s in range(SEC):
        for g in range(GRP):
            along_x = (g == 0) == first
            for at in range(4):
                groups.append(
                    [number(s, g, i, at) if along_x else number(s, g, at, i) for i in range(4)]
                )
    return lax.all_to_all(values, ALL, 0, 0, axis_index_groups=groups, tiled=True)


def section_exchange(values):
    return lax.all_to_all(values, "section", 0, 0, tiled=True)


def plans(micro, vocab_part):
    last = SEC - 1
    steps = micro + 2 * last
    table = np.zeros((SEC, 6 * steps + 2), np.int32)
    for s in range(SEC):
        for way in range(2):
            depth = s if way == 0 else last - s
            for step in range(steps):
                at = step - 2 * depth
                if 0 <= at < micro:
                    sources = ([0] if step < micro else []) + [
                        d + 1 for d in range(last) if 0 <= step - 2 - 2 * d < micro
                    ]
                    spot = 3 * (way * steps + step)
                    table[s, spot : spot + 3] = (1 + s % 2, at, sources.index(depth))
        table[s, 6 * steps :] = (s * vocab_part, s)
    return table


def local(
    token_ids,
    segment_ids,
    noise_input,
    embed_table,
    input_proj,
    norm_gain,
    lead_weight,
    down_weight,
    final_gain,
    readout_proj,
    head_table,
):
    section = lax.axis_index("section")
    core = lax.axis_index("group")
    row = lax.axis_index("row")
    x_at, y_at = row // NY, row % NY
    first_at = jnp.where(core == 0, x_at, y_at)
    micro, _, tokens = token_ids.shape
    width = input_proj.shape[1]
    hidden = lead_weight.shape[2]
    half_rows = down_weight.shape[1]
    emb_part = input_proj.shape[0]
    vocab_part, emb = head_table.shape
    vocab = embed_table.shape[0]
    all_tokens = micro * tokens
    last = SEC - 1
    gain_half = norm_gain.astype(WIDE)
    lead = lead_weight[0]
    own_down = down_weight[0]
    seg_row = segment_ids
    flat_ids = token_ids.reshape(-1)

    plan = plans(micro, vocab_part)
    steps = micro + 2 * last
    table = lax.dynamic_index_in_dim(jnp.asarray(plan), section, 0, False)
    flat_ids = after(flat_ids, table)
    where_start = jnp.stack((first_at, core)).astype(jnp.int32)
    to_first = lambda v: [v] + [link(v, s, 0) for s in range(1, SEC)]
    eighth = row_block(row_block(own_down, core, 2), first_at, 4)
    eighth = jnp.where(section == 1, link(eighth, 0, 1), link(eighth, 2, 3))
    noise = noise_input[:, 0].transpose(2, 0, 1).reshape(emb_part, -1)
    own_embedded = lookup(flat_ids[None], embed_table.T, noise, 3200)
    parts = to_first(jnp.concatenate((own_embedded, input_proj), axis=1))
    embedded = jnp.concatenate([part[:, :all_tokens] for part in parts])
    input_full = jnp.concatenate([part[:, all_tokens:] for part in parts])
    first_in = matmul_tn(embedded, input_full).astype(LOW).reshape(micro, tokens, width)
    odd = (1, 3)
    eighth = after(eighth, first_in)
    eighths = [eighth] + [plane_route(eighth, by, True, odd) for by in (1, 2, 3)]

    kept = empty(
        ((micro, tokens, width), LOW),
        ((micro, tokens, width), LOW),
        ((micro, tokens, hidden), LOW),
        ((micro, tokens, hidden), WIDE),
    )

    def sources(first, step, hops, order):
        arrived = [hops[step - 2, s] for s in order if (step - 2, s) in hops]
        return ([first[step]] if step < micro else []) + arrived

    outs, hops = [], {}
    for step in range(steps):
        out, *kept = forward_stage(
            3 * step,
            table,
            sources(first_in, step, hops, range(SEC)),
            seg_row,
            gain_half,
            held_lead if step > 0 else lead,
            held_down if step > 1 else None,
            kept,
            step == 0,
        )
        if step == 0:
            held_lead = kept.pop()
            upper = upper_half(where_start, [after(part, out) for part in eighths])
            held_down = hold_down(where_start, upper, swap_cores(upper, odd), own_down)
        outs.append(out)
        for s in range(last):
            if 0 <= step - 2 * s < micro:
                ready = after(out, hops[step - 1, s]) if (step - 1, s) in hops else out
                hops[step, s] = link(ready, s, s + 1)
        if step == 2:
            readout_own = after(readout_proj.T, out)
            readout_full = jnp.concatenate(
                [link(readout_own, s, last) for s in range(last)] + [readout_own]
            )
    entries, normeds, saved, inner = kept

    final_rows = jnp.concatenate(outs[2 * last :]).astype(WIDE)
    normed_f, factor_f = layer_norm(final_rows)
    gain_f = final_gain.astype(WIDE)
    final_low = (normed_f * gain_f).astype(LOW)
    readout = matmul_nt(final_low, readout_full).astype(LOW)
    sent = [link(readout, last, s) for s in range(last)]
    readout, peak, total = head_stats(6 * steps + 1, table, sent + [readout], head_table, 2000)
    stats = jnp.concatenate((peak, total))
    all_stats = section_exchange(jnp.tile(stats, (SEC, 1))).reshape(SEC, 2, all_tokens)
    peak = jnp.max(all_stats[:, 0], axis=0)
    total = jnp.sum(all_stats[:, 1] * jnp.exp(all_stats[:, 0] - peak), axis=0)
    logsum = (peak + jnp.log(total))[None]
    head_grad, grad_readout = head_grads(
        6 * steps, table, readout, head_table, logsum, flat_ids[None]
    )
    grad_low = grad_readout.astype(LOW)
    for s in range(last):
        grad_readout = grad_readout + link(grad_low, s, last).astype(WIDE)
    grad_readout = grad_readout.astype(LOW)
    head_grad = lax.psum_scatter(head_grad, "row", scatter_dimension=0)
    readout_grad = matmul_tn(final_low, grad_readout)
    grad_final = matmul(grad_readout, readout_full)
    final_gain_grad = jnp.sum(grad_final * normed_f, axis=0)
    last_grads = norm_back(grad_final * gain_f, normed_f, factor_f).astype(LOW)
    last_grads = last_grads.reshape(micro, tokens, width)

    lead_turned = turned(6 * steps + 1, table, after(lead, grad_low), 0)
    down_turned = turned(6 * steps + 1, table, after(held_down, grad_low), 1)
    totals = empty(
        ((micro, tokens, width), LOW),
        ((micro, tokens, hidden), LOW),
        ((micro, 8, width), WIDE),
    )
    outs, hops = [], {}
    for step in range(steps):
        out, *totals = backward_stage(
            3 * (steps + step),
            table,
            sources(last_grads, step, hops, range(SEC - 1, -1, -1)),
            seg_row,
            gain_half,
            lead_turned,
            down_turned,
            entries,
            saved,
            inner,
            totals,
        )
        outs.append(out)
        for s in range(1, SEC):
            if 0 <= step - 2 * (last - s) < micro:
                ready = after(out, hops[step - 1, s]) if (step - 1, s) in hops else out
                hops[step, s] = link(ready, s, s - 1)
    section, core, row, readout_grad, final_gain_grad = lax.optimization_barrier(
        (section, core, row, readout_grad, final_gain_grad, out)
    )[:5]
    x_at, y_at = row // NY, row % NY
    first_at, second_at = jnp.where(core == 0, x_at, y_at), jnp.where(core == 0, y_at, x_at)
    is_mlp = section % 2 == 1

    first_grads = jnp.concatenate(outs[2 * last :])
    noise_grad = matmul_nt(input_full, first_grads).astype(LOW)
    pieces = noise_grad.reshape(SEC, emb_part, all_tokens)
    sent = [link(pieces[s], 0, s) for s in range(1, SEC)]

    grad_nexts, grads, gain_grads = totals
    flat = lambda v: v.reshape(all_tokens, v.shape[-1])
    grads = after(grads, head_grad)
    normed, grad_nexts, grads, saved = flat(normeds), flat(grad_nexts), flat(grads), flat(saved)
    role = jnp.where(is_mlp, 2, 1)
    where_other = jnp.stack((role, 1 - core, second_at)).astype(jnp.int32)
    where_mine = jnp.stack((role, core, first_at)).astype(jnp.int32)
    both = lambda mine, other: jnp.where(
        core == 0,
        jnp.concatenate((mine, other), axis=1),
        jnp.concatenate((other, mine), axis=1),
    )
    down_got = swap_cores(down_grad(where_other, saved, grad_nexts)[0], odd)
    lead_other = lead_grad(where_other, normed, saved, grads)[0]
    lead_got = swap_cores(lead_other)
    down_mine = down_grad(after(where_mine, lead_other), saved, grad_nexts, down_got)
    down_first = plane_first(down_mine, odd)
    late_ids = after(flat_ids, down_mine)[None]
    packed, noise_wide = noise_pack(6 * steps + 1, table, late_ids, [pieces[0]] + sent)

    lead_mine = lead_grad(after(where_mine, packed), normed, saved, grads, lead_got)
    lead_first = plane_first(lead_mine)
    first_grads, gain_grads, readout_grad, final_gain_grad = after(
        (first_grads, gain_grads, readout_grad, final_gain_grad), lead_mine
    )
    gain_grad = jnp.sum(gain_grads[:, 0], axis=0)
    input_grad = matmul(embedded, first_grads).reshape(SEC, 16, 4, width)
    input_grad = input_grad.transpose(1, 0, 2, 3).reshape(16, 16, width)
    readout_grad = readout_grad.reshape(16, 16, width)
    vectors = jnp.concatenate(
        (
            gain_grad.reshape(16, 64),
            final_gain_grad.reshape(SEC, 16, 16).transpose(1, 0, 2).reshape(16, 64),
            jnp.zeros((16, width - 128), WIDE),
        ),
        axis=1,
    )
    small = jnp.concatenate(
        (
            jnp.where(section == 0, input_grad, readout_grad),
            vectors[:, None],
            jnp.zeros((16, 15, width), WIDE),
        ),
        axis=1,
    ).astype(LOW)
    half_of = lambda which: lax.dynamic_slice_in_dim(small, which * (width // 2), width // 2, 2)
    small = half_of(core).astype(WIDE) + swap_cores(half_of(1 - core)).astype(WIDE)
    small = small.astype(LOW).reshape(NX, NY, 32, width // 2)
    small = jnp.where(core == 0, small, small.swapaxes(0, 1)).reshape(4, NY * 32, width // 2)
    deep = emb_part + 16

    def exchange(blocks, packed, first):
        rows = blocks.shape[1]
        everywhere = jnp.broadcast_to(packed, (4,) + packed.shape)
        got = group_exchange(jnp.concatenate((blocks, everywhere), axis=1), first)
        return jnp.sum(got[:, :rows].astype(WIDE), axis=0).astype(LOW), got[:, rows:]

    packed = after(packed, lead_mine)
    down_first = after(down_first, lead_mine)
    small, packed = exchange(after(small, down_first), packed, True)
    small, packed = exchange(
        small.reshape(4, 32, width // 2), packed.reshape(4 * deep, all_tokens), False
    )
    packed = packed.reshape(16, deep, all_tokens)
    down_second = plane_second(after(down_first, packed), second_at, odd)
    lead_second = plane_second(after(lead_first, packed), second_at)
    packed_other = swap_cores(packed)
    small = both(small, swap_cores(small))
    embed_grad = embed_sum(
        (row * (vocab // 16)).reshape(1), packed, packed_other, emb_part, vocab // 16
    )
    down_part = plane_sum(after(down_second, embed_grad))
    lead_part = plane_sum(after(lead_second, embed_grad))
    noise_out = noise_wide.reshape(emb_part, micro, tokens).transpose(1, 2, 0)
    lead_out = both(lead_part, swap_cores(lead_part)).astype(WIDE)

    def first_target(s, g, x, y):
        if s % 2 == 0:
            return None
        return (s - 1, 0, x, y) if g == 0 else (s, 0, x, y)

    def second_target(s, g, x, y):
        return (s - 1, 1, x, y) if s % 2 == 1 and g == 0 else None

    to_core_0 = route(down_part, first_target)
    to_core_1 = route(down_part, second_target)
    down_out = jnp.where(
        core == 0, to_core_0, jnp.where(is_mlp, down_part, to_core_1)
    ).astype(WIDE)

    small = after(small, (lead_part, down_part))
    gain_out = small[16, :64].astype(WIDE)
    input_rows = small[:16].reshape(SEC, 4, width)
    readout_rows = small[:16].reshape(64, SEC, 64)
    final_rows = small[16, 64:128].reshape(SEC, 16)

    finals = jnp.pad(final_rows, ((0, 0), (0, width - 16)))[:, None]
    mine = jnp.where(
        section == 0, input_rows, readout_rows.transpose(1, 0, 2).reshape(SEC, 4, width)
    )
    shared = section_exchange(
        jnp.concatenate((mine, finals, jnp.zeros((SEC, 3, width), LOW)), axis=1)
    )
    input_out = shared[0, :4]
    readout_out = shared[last, :4].reshape(64, 64)
    final_out = shared[last, 4, :16]

    head_out = pair_sum(head_grad, swap_cores(head_grad), vocab_part // (NX * NY))
    return (
        noise_out[:, None],
        embed_grad.T,
        input_out.astype(WIDE),
        gain_out[None],
        lead_out[None],
        down_out[None],
        final_out.astype(WIDE),
        readout_out.astype(WIDE),
        head_out,
    )


def solution(mesh):
    in_specs = (
        P(None, ("group", "row"), None),
        P(None, ("group", "row"), None),
        P(None, ("group", "row"), None, "section"),
        P(None, "section"),
        P("section", None),
        P("section", None),
        P("section", None, None),
        P("section", None, None),
        P(),
        P(None, "section"),
        P("section", None),
    )
    out_specs = (
        P(None, ("group", "row"), None, "section"),
        P("row", "section"),
        P(("section", "row"), None),
        P("section", "row"),
        P("section", "row", None),
        P("section", "row", None),
        P(("section", "row")),
        P("row", "section"),
        P(("section", "row"), None),
    )
    return jax.shard_map(local, mesh=mesh, in_specs=in_specs, out_specs=out_specs, check_vma=False)
```
